32 devices in a mesh: grp: 1, row: 16 (over z, y, core), col: 2 (over x), ch: 1.
Axes of the slice: x: 2, y: 2, z: 4, core: 2. Of those that a mesh axis runs over, the one named last changes fastest.
Arguments:
- pair: bfloat16 [256, 256, 128], P(('grp', 'row'), 'col'), may hold values from -6 to 6
- cotangent: bfloat16 [256, 256, 128], P(('grp', 'row'), 'col'), may hold values from -6 to 6
- lengths: int32 [1], P('grp'), may hold values from 128 to 256
- norm_gain: float32 [2, 128], replicated, may hold values from 0.25 to 1.75
- norm_bias: float32 [2, 128], replicated, may hold values from -1.5 to 1.5
- proj_weight: bfloat16 [2, 2, 128, 128], P(None, None, None, 'ch'), may hold values from -0.5 to 0.5
- gate_weight: bfloat16 [2, 2, 128, 128], P(None, None, None, 'ch'), may hold values from -0.5 to 0.5
- mid_gain: float32 [2, 128], P(None, 'ch'), may hold values from 0.25 to 1.75
- mid_bias: float32 [2, 128], P(None, 'ch'), may hold values from -1.5 to 1.5
- out_weight: bfloat16 [2, 128, 128], replicated, may hold values from -0.5 to 0.5
- outgate_weight: bfloat16 [2, 128, 128], replicated, may hold values from -0.5 to 0.5
Outputs:
- new_pair: bfloat16 [256, 256, 128], P(('grp', 'row'), 'col')
- grad_pair: bfloat16 [256, 256, 128], P(('grp', 'row'), 'col')
- grad_norm_gain: float32 [2, 128], P('grp')
- grad_norm_bias: float32 [2, 128], P('grp')
- grad_proj_weight: float32 [2, 2, 128, 128], P('grp', None, None, 'ch')
- grad_gate_weight: float32 [2, 2, 128, 128], P('grp', None, None, 'ch')
- grad_mid_gain: float32 [2, 128], P('grp', 'ch')
- grad_mid_bias: float32 [2, 128], P('grp', 'ch')
- grad_out_weight: float32 [2, 128, 128], P('grp')
- grad_outgate_weight: float32 [2, 128, 128], P('grp')
The draws below stay inside these ranges and needn't reach their ends.
Inputs may be any that keep to these rules, and one draw needn't show every extreme that they name: Residues from lengths on are padding of the complex.
All inputs are finite; a program needn't handle non-finite values.
Results may differ from the reference program's by a relative error of at most 0.02.
Values may be sent and summed in bfloat16 or wider, within the bound.
No kernel may reach another device: no remote copies, remote signals or barrier semaphores. Data moves between devices by JAX's collectives and lax.ppermute only.
A program may use at most 64 MiB of HBM per device.

```python
import jax
import jax.numpy as jnp
from jax import lax

C = 128
H = 128
N = 256


def block_levels(own_key, extent, shards, smallest, top_value):
    factor_of = 1.0
    for axis_at, parts in shards:
        draws = jax.random.uniform(jax.random.fold_in(jax.random.fold_in(own_key, 6), axis_at), (parts,), jnp.float32, smallest / len(shards), top_value / len(shards))
        factor_of = factor_of * jnp.repeat(jnp.exp(draws), extent[axis_at] // parts).reshape((-1,) + (1,) * (len(extent) - 1 - axis_at))
    return factor_of


def noise(rng, extent, deviation, reach, split=(), dtype=jnp.bfloat16):
    values = jax.random.normal(rng, extent, jnp.float32) * deviation
    if len(split) > 0:
        values = block_levels(rng, extent, split, -0.22, 0.18) * values
    return jnp.clip(values, min=-reach, max=reach).astype(dtype)


def setup_inputs(seed: int = 0, part: int = 0) -> dict:
    splits = jax.random.split(jax.random.key(seed), 12)
    part_splits = jax.random.split(jax.random.fold_in(splits[11], part), 12)
    pair = noise(part_splits[0], (N, N, C), 1.0, 6.0, ((0, 16), (1, 2)))
    cotangent = noise(part_splits[1], (N, N, C), 1.0, 6.0, ((0, 16), (1, 2)))
    lengths = jax.random.randint(part_splits[2], (1,), N // 2, N + 1).astype(jnp.int32)
    norm_gain = jnp.clip(1.0 + 0.15 * jax.random.normal(splits[3], (2, C), jnp.float32), 0.25, 1.75)
    norm_bias = noise(splits[4], (2, C), 0.3, 1.5, (), jnp.float32)
    proj_weight = noise(splits[5], (2, 2, C, H), C ** -0.5, 0.5)
    gate_weight = noise(splits[6], (2, 2, C, H), C ** -0.5, 0.5)
    mid_gain = jnp.clip(1.0 + 0.15 * jax.random.normal(splits[7], (2, H), jnp.float32), 0.25, 1.75)
    mid_bias = noise(splits[8], (2, H), 0.3, 1.5, (), jnp.float32)
    out_weight = noise(splits[9], (2, H, C), H ** -0.5, 0.5)
    outgate_weight = noise(splits[10], (2, C, C), C ** -0.5, 0.5)
    return dict(pair=pair, cotangent=cotangent, lengths=lengths, norm_gain=norm_gain, norm_bias=norm_bias, proj_weight=proj_weight, gate_weight=gate_weight, mid_gain=mid_gain, mid_bias=mid_bias, out_weight=out_weight, outgate_weight=outgate_weight)


EPS = 1e-05

def as_float(spec, left, right):
    return jnp.einsum(spec, left.astype(jnp.float32), right.astype(jnp.float32))

def norm_channels(values):
    average = lax.optimization_barrier(jnp.mean(values, -1, keepdims=True))
    centred = values - average
    variance = lax.optimization_barrier(jnp.mean(centred * centred, -1, keepdims=True))
    inverse = lax.rsqrt(variance + EPS)
    return (centred * inverse, inverse)

def forward_module(pair_in, pair_mask, weights, incoming):
    gain_in, bias_in, proj_w, gate_w, gain_mid, bias_mid, out_w, outgate_w = weights
    scaled_in, inverse_in = norm_channels(pair_in.astype(jnp.float32))
    normed = (scaled_in * gain_in + bias_in).astype(jnp.bfloat16)
    projected = as_float('ijc,sch->shij', normed, proj_w)
    gating = jax.nn.sigmoid(as_float('ijc,sch->shij', normed, gate_w))
    hidden = (projected * gating * pair_mask).astype(jnp.bfloat16)
    left_side = hidden[0]
    right_side = hidden[1]
    if incoming:
        triangle = as_float('cki,ckj->cij', left_side, right_side)
    else:
        triangle = as_float('cik,cjk->cij', left_side, right_side)
    tri_values = triangle.astype(jnp.bfloat16).astype(jnp.float32)
    average = lax.optimization_barrier(jnp.sum(tri_values, 0)) / H
    inverse_mid = lax.rsqrt(lax.optimization_barrier(jnp.sum(tri_values * tri_values, 0)) / H - average * average + EPS)
    scaled_mid = (tri_values - average) * inverse_mid
    unit = (scaled_mid * gain_mid[:, None, None] + bias_mid[:, None, None]).astype(jnp.bfloat16)
    outer = as_float('hij,hc->ijc', unit, out_w)
    outgate = jax.nn.sigmoid(as_float('ijc,cd->ijd', normed, outgate_w))
    result = (pair_in.astype(jnp.float32) + outer * outgate).astype(jnp.bfloat16)
    saved = (scaled_in, inverse_in, normed, projected, gating, left_side, right_side, scaled_mid, inverse_mid, unit, outer, outgate)
    return (result, saved)

def backward_module(grad_out, pair_mask, weights, saved, incoming):
    gain_in, bias_in, proj_w, gate_w, gain_mid, bias_mid, out_w, outgate_w = weights
    scaled_in, inverse_in, normed, projected, gating, left_side, right_side, scaled_mid, inverse_mid, unit, outer, outgate = saved
    d_outer = (grad_out * outgate).astype(jnp.bfloat16)
    d_gatepre = (grad_out * outer * outgate * (1.0 - outgate)).astype(jnp.bfloat16)
    grad_out_w = as_float('hij,ijc->hc', unit, d_outer)
    grad_outgate_w = as_float('ijc,ijd->cd', normed, d_gatepre)
    d_unit = as_float('ijc,hc->hij', d_outer, out_w)
    d_normed = as_float('ijd,cd->ijc', d_gatepre, outgate_w)
    weighted = d_unit * gain_mid[:, None, None]
    grad_gain_mid = lax.optimization_barrier(jnp.sum(d_unit * scaled_mid, (1, 2)))
    grad_bias_mid = lax.optimization_barrier(jnp.sum(d_unit, (1, 2)))
    first_sum = lax.optimization_barrier(jnp.sum(weighted, 0))
    second_sum = lax.optimization_barrier(jnp.sum(weighted * scaled_mid, 0))
    d_tri = (inverse_mid * (weighted - first_sum / H - scaled_mid * (second_sum / H))).astype(jnp.bfloat16)
    if incoming:
        d_left = as_float('cij,ckj->cki', d_tri, right_side)
        d_right = as_float('cij,cki->ckj', d_tri, left_side)
    else:
        d_left = as_float('cij,cjk->cik', d_tri, right_side)
        d_right = as_float('cij,cik->cjk', d_tri, left_side)
    d_hidden = jnp.stack([d_left.astype(jnp.bfloat16), d_right.astype(jnp.bfloat16)]).astype(jnp.float32)
    d_proj = (d_hidden * gating * pair_mask).astype(jnp.bfloat16)
    d_gate = (d_hidden * projected * gating * (1.0 - gating) * pair_mask).astype(jnp.bfloat16)
    grad_proj_w = as_float('ijc,shij->sch', normed, d_proj)
    grad_gate_w = as_float('ijc,shij->sch', normed, d_gate)
    d_normed = d_normed + as_float('shij,sch->ijc', d_proj, proj_w) + as_float('shij,sch->ijc', d_gate, gate_w)
    weighted_in = d_normed * gain_in
    grad_gain_in = lax.optimization_barrier(jnp.sum(d_normed * scaled_in, (0, 1)))
    grad_bias_in = lax.optimization_barrier(jnp.sum(d_normed, (0, 1)))
    d_pair = inverse_in * (weighted_in - lax.optimization_barrier(jnp.mean(weighted_in, -1, keepdims=True)) - scaled_in * lax.optimization_barrier(jnp.mean(weighted_in * scaled_in, -1, keepdims=True)))
    grads = (grad_gain_in, grad_bias_in, grad_proj_w, grad_gate_w, grad_gain_mid, grad_bias_mid, grad_out_w, grad_outgate_w)
    return (grad_out + d_pair, grads)

def reference(pair, cotangent, lengths, norm_gain, norm_bias, proj_weight, gate_weight, mid_gain, mid_bias, out_weight, outgate_weight):
    positions = lax.iota(jnp.int32, N)
    valid = positions < lengths[0]
    pair_mask = (valid[:, None] & valid[None, :]).astype(jnp.float32)
    state = pair
    stash = []
    for layer in range(2):
        weights = (norm_gain[layer], norm_bias[layer], proj_weight[layer], gate_weight[layer], mid_gain[layer], mid_bias[layer], out_weight[layer], outgate_weight[layer])
        state, saved = forward_module(state, pair_mask, weights, layer == 1)
        stash.append(saved)
    grad_state = cotangent.astype(jnp.float32)
    per_layer = [None, None]
    for layer in (1, 0):
        weights = (norm_gain[layer], norm_bias[layer], proj_weight[layer], gate_weight[layer], mid_gain[layer], mid_bias[layer], out_weight[layer], outgate_weight[layer])
        grad_state, grads = backward_module(grad_state, pair_mask, weights, stash[layer], layer == 1)
        per_layer[layer] = grads
    stacked = [jnp.stack([per_layer[0][index], per_layer[1][index]]) for index in range(8)]
    return (state, grad_state.astype(jnp.bfloat16), stacked[0], stacked[1], stacked[2], stacked[3], stacked[4], stacked[5], stacked[6], stacked[7])
```

```python
import functools

import jax
import jax.numpy as jnp
from jax import lax
from jax.experimental import pallas as pl
from jax.experimental.pallas import tpu as pltpu
from jax.sharding import PartitionSpec as P

H = 128


EPS = 1e-05


def product(spec, left, right):
    return jnp.einsum(spec, left, right, preferred_element_type=jnp.float32)


F32 = jnp.float32
BF16 = jnp.bfloat16


def dot(left, right):
    return lax.dot_general(left, right, (((1,), (0,)), ((), ())), preferred_element_type=F32)


def dot_rt(left, right):
    return lax.dot_general(left, right, (((1,), (1,)), ((), ())), preferred_element_type=F32)


def dot_lt(left, right):
    return lax.dot_general(left, right, (((0,), (0,)), ((), ())), preferred_element_type=F32)


def sigmoid(values):
    return 1.0 / (1.0 + jnp.exp(-values))


def norm_rows(values):
    scale = 1.0 / values.shape[0]
    average = jnp.sum(values, 0, keepdims=True) * scale
    centred = values - average
    variance = jnp.sum(centred * centred, 0, keepdims=True) * scale
    inverse = lax.rsqrt(variance + EPS)
    return centred * inverse, inverse


def turned(weight):
    return jnp.transpose(weight.astype(F32)).astype(BF16)


def column(ref, module, lanes):
    row = ref[module : module + 1, :]
    return jnp.transpose(jnp.broadcast_to(row, (lanes, row.shape[1])))


def as_row(total):
    return jnp.sum(jnp.transpose(total), 0, keepdims=True)


def row_mask(lengths_ref, step, rows, lanes):
    limit = lengths_ref[0]
    row_id = lax.axis_index("row") * rows + step
    col_id = lax.axis_index("col") * lanes + lax.broadcasted_iota(jnp.int32, (1, lanes), 1)
    return jnp.where((row_id < limit) & (col_id < limit), 1.0, 0.0).astype(F32)


def load_in_weights(proj_ref, gate_ref, module, scratch):
    width = proj_ref.shape[-1]
    for side in range(2):
        scratch[side * width : (side + 1) * width, :] = turned(proj_ref[module, side])
        scratch[(2 + side) * width : (3 + side) * width, :] = turned(gate_ref[module, side])


def edges(normed, in_weights, mask):
    pre = dot(in_weights, normed)
    half = pre.shape[0] // 2
    return pre[:half] * sigmoid(pre[half:]) * mask


def put_rows(scratch, values, step, rows):
    scratch[pl.ds(step, values.shape[0], stride=rows), :] = values


def get_rows(scratch, step, channels, rows):
    return scratch[pl.ds(step, channels, stride=rows), :]


def spread_edges(scratch, out_ref):
    shards, sides, group, rows, lanes = out_ref.shape
    block = shards * group * rows
    for side in range(sides):
        part = scratch[side * block : (side + 1) * block, :]
        out_ref[:, side] = part.reshape(shards, group, rows, lanes).astype(BF16)


def collect_edges(in_ref, scratch):
    shards, sides, group, rows, lanes = in_ref.shape
    block = shards * group * rows
    for side in range(sides):
        scratch[side * block : (side + 1) * block, :] = (
            in_ref[:, side].astype(F32).reshape(block, lanes)
        )


def start_kernel(lengths, pair, ngain, nbias, proj_w, gate_w, edge_out, normed_out, wts, scr):
    rows, lanes, channels = pair.shape
    load_in_weights(proj_w, gate_w, 0, wts)
    gain, bias = column(ngain, 0, lanes), column(nbias, 0, lanes)

    def body(step, carry):
        scaled, _ = norm_rows(jnp.transpose(pair[step].astype(F32)))
        normed = (scaled * gain + bias).astype(BF16)
        normed_out[step] = normed
        put_rows(scr, edges(normed, wts[...], row_mask(lengths, step, rows, lanes)), step, rows)
        return carry

    lax.fori_loop(0, rows, body, 0)
    spread_edges(scr, edge_out)


def mid_norm(tri):
    scale = 1.0 / tri.shape[0]
    average = jnp.sum(tri, 0, keepdims=True) * scale
    squares = jnp.sum(tri * tri, 0, keepdims=True) * scale
    inverse = lax.rsqrt(squares - average * average + EPS)
    return (tri - average) * inverse, inverse


def between_kernel(
    lengths, tri, pair, normed0, ngain, nbias, mgain, mbias, out_w, outgate_w, proj_w, gate_w,
    edge_out, mid_out, normed_out, wts, scr,
):
    rows, lanes, channels = pair.shape
    load_in_weights(proj_w, gate_w, 1, wts)
    out_t, outgate_t = turned(out_w[0]), turned(outgate_w[0])
    gain, bias = column(ngain, 1, lanes), column(nbias, 1, lanes)
    gain_mid, bias_mid = column(mgain, 0, lanes), column(mbias, 0, lanes)
    scr[0 : channels * rows, :] = tri[...].astype(F32).reshape(channels * rows, lanes)

    def body(step, carry):
        scaled_mid, _ = mid_norm(get_rows(scr, step, channels, rows))
        unit = (scaled_mid * gain_mid + bias_mid).astype(BF16)
        outer = dot(out_t, unit)
        outgate = sigmoid(dot(outgate_t, normed0[step]))
        mid = (jnp.transpose(pair[step].astype(F32)) + outer * outgate).astype(BF16)
        mid_out[step] = mid
        scaled, _ = norm_rows(mid.astype(F32))
        normed = (scaled * gain + bias).astype(BF16)
        normed_out[step] = normed
        here = edges(normed, wts[...], row_mask(lengths, step, rows, lanes))
        put_rows(scr, here, step, rows)
        return carry

    lax.fori_loop(0, rows, body, 0)
    spread_edges(scr, edge_out)


def triangle_kernel(incoming, edge, tri_out):
    many, few, _, group, rows, lanes = edge.shape

    def whole(side, channel):
        parts = [edge[:, c, side, channel].reshape(many * rows, lanes) for c in range(few)]
        return jnp.concatenate(parts, axis=1)

    for channel in range(group):
        left, right = whole(0, channel), whole(1, channel)
        tri = (dot_lt if incoming else dot_rt)(left, right).astype(BF16)
        for c in range(few):
            part = tri[:, c * lanes : (c + 1) * lanes]
            tri_out[:, c, channel] = part.reshape(many, rows, lanes)


def edge_grad_kernel(incoming, edge, d_tri, grad_out):
    many, few, _, group, rows, lanes = edge.shape

    def whole(ref, *index):
        parts = [ref[(slice(None), c) + index].reshape(many * rows, lanes) for c in range(few)]
        return jnp.concatenate(parts, axis=1)

    for channel in range(group):
        left, right = whole(edge, 0, channel), whole(edge, 1, channel)
        grad = whole(d_tri, channel)
        if incoming:
            d_left, d_right = dot_rt(right, grad), dot(left, grad)
        else:
            d_left, d_right = dot(grad, right), dot_lt(grad, left)
        for side, value in ((0, d_left), (1, d_right)):
            value = value.astype(BF16)
            for c in range(few):
                part = value[:, c * lanes : (c + 1) * lanes]
                grad_out[:, c, side, channel] = part.reshape(many, rows, lanes)


def mid_backward(
    step, grad, tri, normed, gain_mid, bias_mid, out_t, outgate_t, out_w,
    unit_out, d_outer_out, d_gatepre_out, sum_gain, sum_bias,
):
    scaled_mid, inverse_mid = mid_norm(tri)
    unit = (scaled_mid * gain_mid + bias_mid).astype(BF16)
    outer = dot(out_t, unit)
    outgate = sigmoid(dot(outgate_t, normed))
    gated = grad * outgate
    d_outer = gated.astype(BF16)
    d_gatepre = (gated * outer * (1.0 - outgate)).astype(BF16)
    unit_out[step] = unit
    d_outer_out[step] = d_outer
    d_gatepre_out[step] = d_gatepre
    d_unit = dot(out_w, d_outer)
    sum_gain[...] += d_unit * scaled_mid
    sum_bias[...] += d_unit
    weighted = d_unit * gain_mid
    scale = 1.0 / weighted.shape[0]
    first = jnp.sum(weighted, 0, keepdims=True) * scale
    second = jnp.sum(weighted * scaled_mid, 0, keepdims=True) * scale
    d_tri = inverse_mid * (weighted - first - scaled_mid * second)
    return d_tri, outer * outgate


def turn_kernel(
    tri, mid, normed1, cot, mgain, mbias, out_w, outgate_w,
    d_tri_out, new_out, unit_out, d_outer_out, d_gatepre_out, small_out, scr, sum_gain, sum_bias,
):
    rows, channels, lanes = mid.shape
    out_t, outgate_t = turned(out_w[1]), turned(outgate_w[1])
    gain_mid, bias_mid = column(mgain, 1, lanes), column(mbias, 1, lanes)
    scr[...] = tri[...].astype(F32).reshape(channels * rows, lanes)
    sum_gain[...] = jnp.zeros_like(sum_gain)
    sum_bias[...] = jnp.zeros_like(sum_bias)

    def body(step, carry):
        grad = jnp.transpose(cot[step].astype(F32))
        d_tri, update = mid_backward(
            step, grad, get_rows(scr, step, channels, rows), normed1[step], gain_mid, bias_mid,
            out_t, outgate_t, out_w[1], unit_out, d_outer_out, d_gatepre_out, sum_gain, sum_bias,
        )
        new_out[step] = jnp.transpose(mid[step].astype(F32) + update).astype(BF16)
        put_rows(scr, d_tri, step, rows)
        return carry

    lax.fori_loop(0, rows, body, 0)
    d_tri_out[...] = scr[...].reshape(d_tri_out.shape).astype(BF16)
    small_out[0:1, :] = as_row(sum_gain[...])
    small_out[1:2, :] = as_row(sum_bias[...])


def in_backward(
    step, grad, base, d_edges, normed, d_gatepre, mask, gain, wts, proj_w, gate_w, outgate_w,
    d_in_out, sum_gain, sum_bias,
):
    pre = dot(wts[...], normed)
    half = pre.shape[0] // 2
    gating = sigmoid(pre[half:])
    through = d_edges * gating * mask
    d_proj = through.astype(BF16)
    d_gate = (through * pre[:half] * (1.0 - gating)).astype(BF16)
    d_in_out[step, 0:half] = d_proj
    d_in_out[step, half:] = d_gate
    width = half // 2
    d_normed = dot(outgate_w, d_gatepre)
    for side in range(2):
        d_normed += dot(proj_w[side], d_proj[side * width : (side + 1) * width])
        d_normed += dot(gate_w[side], d_gate[side * width : (side + 1) * width])
    scaled, inverse = norm_rows(base)
    sum_gain[...] += d_normed * scaled
    sum_bias[...] += d_normed
    weighted = d_normed * gain
    scale = 1.0 / weighted.shape[0]
    first = jnp.sum(weighted, 0, keepdims=True) * scale
    second = jnp.sum(weighted * scaled, 0, keepdims=True) * scale
    return grad + inverse * (weighted - first - scaled * second)


def middle_kernel(
    lengths, d_edge, mid, normed1, d_gatepre1, cot, tri0, normed0,
    ngain, mgain, mbias, proj_w, gate_w, out_w, outgate_w,
    d_tri_out, grad_out, d_in_out, unit_out, d_outer_out, d_gatepre_out, small_out,
    wts, scr, scr_tri, sums,
):
    rows, channels, lanes = mid.shape
    load_in_weights(proj_w, gate_w, 1, wts)
    out_t, outgate_t = turned(out_w[0]), turned(outgate_w[0])
    gain = column(ngain, 1, lanes)
    gain_mid, bias_mid = column(mgain, 0, lanes), column(mbias, 0, lanes)
    collect_edges(d_edge, scr)
    scr_tri[...] = tri0[...].astype(F32).reshape(channels * rows, lanes)
    sums[...] = jnp.zeros_like(sums)

    def body(step, carry):
        grad = in_backward(
            step, jnp.transpose(cot[step].astype(F32)), mid[step].astype(F32),
            get_rows(scr, step, scr.shape[0] // rows, rows), normed1[step], d_gatepre1[step],
            row_mask(lengths, step, rows, lanes), gain, wts, proj_w[1], gate_w[1], outgate_w[1],
            d_in_out, sums.at[0], sums.at[1],
        )
        grad_out[step] = grad
        d_tri, _ = mid_backward(
            step, grad, get_rows(scr_tri, step, channels, rows), normed0[step], gain_mid, bias_mid,
            out_t, outgate_t, out_w[0], unit_out, d_outer_out, d_gatepre_out,
            sums.at[2], sums.at[3],
        )
        put_rows(scr_tri, d_tri, step, rows)
        return carry

    lax.fori_loop(0, rows, body, 0)
    d_tri_out[...] = scr_tri[...].reshape(d_tri_out.shape).astype(BF16)
    for index in range(4):
        small_out[index : index + 1, :] = as_row(sums[index])


def finish_kernel(
    lengths, d_edge, pair, normed0, d_gatepre0, grad, ngain, proj_w, gate_w, outgate_w,
    grad_out, d_in_out, small_out, wts, scr, sums,
):
    rows, lanes, channels = pair.shape
    load_in_weights(proj_w, gate_w, 0, wts)
    gain = column(ngain, 0, lanes)
    collect_edges(d_edge, scr)
    sums[...] = jnp.zeros_like(sums)

    def body(step, carry):
        total = in_backward(
            step, grad[step], jnp.transpose(pair[step].astype(F32)),
            get_rows(scr, step, scr.shape[0] // rows, rows), normed0[step], d_gatepre0[step],
            row_mask(lengths, step, rows, lanes), gain, wts, proj_w[0], gate_w[0], outgate_w[0],
            d_in_out, sums.at[0], sums.at[1],
        )
        grad_out[step] = jnp.transpose(total).astype(BF16)
        return carry

    lax.fori_loop(0, rows, body, 0)
    for index in range(2):
        small_out[index : index + 1, :] = as_row(sums[index])


def in_weight_kernel(normed, d_in, out_ref):
    rows = normed.shape[0]
    width = normed.shape[1]
    flat = jnp.concatenate([normed[step] for step in range(rows)], axis=1)
    for part in range(d_in.shape[1] // width):
        block = slice(part * width, (part + 1) * width)
        other = jnp.concatenate([d_in[step, block] for step in range(rows)], axis=1)
        out_ref[block, :] = dot_rt(flat, other).astype(out_ref.dtype)


def out_weight_kernel(unit, d_outer, normed, d_gatepre, out_ref):
    rows = normed.shape[0]
    width = normed.shape[1]
    for part, (left, right) in enumerate(((unit, d_outer), (normed, d_gatepre))):
        first = jnp.concatenate([left[step] for step in range(rows)], axis=1)
        second = jnp.concatenate([right[step] for step in range(rows)], axis=1)
        block = slice(part * width, (part + 1) * width)
        out_ref[block, :] = dot_rt(first, second).astype(out_ref.dtype)


SCALARS = pl.BlockSpec(memory_space=pltpu.SMEM)
VECTORS = pl.BlockSpec(memory_space=pltpu.VMEM)


def call(kernel, name, outs, args, scratch=(), flops=0, scalars=0):
    shapes = [jax.ShapeDtypeStruct(shape, dtype) for shape, dtype in outs]
    moved = sum(a.size * a.dtype.itemsize for a in list(args) + shapes)
    result = pl.pallas_call(
        kernel,
        name=name,
        out_shape=shapes,
        in_specs=[SCALARS] * scalars + [VECTORS] * (len(args) - scalars),
        out_specs=[VECTORS] * len(shapes),
        scratch_shapes=[pltpu.VMEM(shape, dtype) for shape, dtype in scratch],
        compiler_params=pltpu.CompilerParams(vmem_limit_bytes=32 * 1024 * 1024),
        cost_estimate=pl.CostEstimate(flops=flops, bytes_accessed=moved, transcendentals=0),
    )(*args)
    return result


def exchange(values):
    return lax.all_to_all(values, ("row", "col"), split_axis=0, concat_axis=0, tiled=True)


def grouped_device(
    pair, cotangent, lengths, ngain, nbias, proj_w, gate_w, mgain, mbias, out_w, outgate_w,
    *, many, few,
):
    rows, lanes, channels = pair.shape
    shards = many * few
    group = H // shards
    edge_shape = (shards, 2, group, rows, lanes)
    grid_shape = (many, few, 2, group, rows, lanes)
    tri_shape = (shards, group, rows, lanes)
    tile = (rows, channels, lanes)
    wts = ((4 * H, channels), BF16)
    big = ((2 * H * rows, lanes), F32)
    mid = ((H * rows, lanes), F32)
    positions = rows * lanes
    triangle = 2 * group * (many * rows) ** 2 * (few * lanes)
    dense = 2 * positions * channels * H

    edge, normed0 = call(
        start_kernel, "start", [(edge_shape, BF16), (tile, BF16)],
        [lengths, pair, ngain, nbias, proj_w, gate_w], [wts, big], 4 * dense, 1,
    )
    edge0 = exchange(edge).reshape(grid_shape)
    (tri,) = call(
        functools.partial(triangle_kernel, False), "outgoing",
        [((many, few, group, rows, lanes), BF16)], [edge0], (), triangle,
    )
    tri0 = exchange(tri.reshape(tri_shape))
    edge, mid_t, normed1 = call(
        between_kernel, "between", [(edge_shape, BF16), (tile, BF16), (tile, BF16)],
        [lengths, tri0, pair, normed0, ngain, nbias, mgain, mbias, out_w, outgate_w, proj_w, gate_w],
        [wts, big], 6 * dense, 1,
    )
    edge1 = exchange(edge).reshape(grid_shape)
    (tri,) = call(
        functools.partial(triangle_kernel, True), "incoming",
        [((many, few, group, rows, lanes), BF16)], [edge1], (), triangle,
    )
    tri1 = exchange(tri.reshape(tri_shape))
    d_tri, new_pair, unit1, d_outer1, d_gatepre1, small_mid1 = call(
        turn_kernel, "turn",
        [(tri_shape, BF16), (pair.shape, BF16), (tile, BF16), (tile, BF16), (tile, BF16),
         ((2, H), F32)],
        [tri1, mid_t, normed1, cotangent, mgain, mbias, out_w, outgate_w],
        [mid, ((H, lanes), F32), ((H, lanes), F32)], 3 * dense,
    )
    d_tri = exchange(d_tri).reshape(many, few, group, rows, lanes)
    (d_edge,) = call(
        functools.partial(edge_grad_kernel, True), "incoming_grad",
        [(grid_shape, BF16)], [edge1, d_tri], (), 2 * triangle,
    )
    d_edge = exchange(d_edge.reshape(edge_shape))
    (out_grads1,) = call(
        out_weight_kernel, "out_weights_upper", [((2 * H, channels), BF16)],
        [unit1, d_outer1, normed1, d_gatepre1], (), 2 * dense,
    )
    d_tri, grad, d_in1, unit0, d_outer0, d_gatepre0, small_mid = call(
        middle_kernel, "middle",
        [(tri_shape, BF16), (tile, F32), ((rows, 4 * H, lanes), BF16), (tile, BF16), (tile, BF16),
         (tile, BF16), ((4, H), F32)],
        [lengths, d_edge, mid_t, normed1, d_gatepre1, cotangent, tri0, normed0,
         ngain, mgain, mbias, proj_w, gate_w, out_w, outgate_w],
        [wts, big, mid, ((4, H, lanes), F32)], 12 * dense, 1,
    )
    d_tri = exchange(d_tri).reshape(many, few, group, rows, lanes)
    (in_grads1,) = call(
        in_weight_kernel, "in_weights_upper", [((4 * H, H), BF16)], [normed1, d_in1], (), 4 * dense,
    )
    (out_grads0,) = call(
        out_weight_kernel, "out_weights_lower", [((2 * H, channels), BF16)],
        [unit0, d_outer0, normed0, d_gatepre0], (), 2 * dense,
    )
    (d_edge,) = call(
        functools.partial(edge_grad_kernel, False), "outgoing_grad",
        [(grid_shape, BF16)], [edge0, d_tri], (), 2 * triangle,
    )
    d_edge = exchange(d_edge.reshape(edge_shape))
    grad_pair, d_in0, small0 = call(
        finish_kernel, "finish",
        [(pair.shape, BF16), ((rows, 4 * H, lanes), BF16), ((2, H), F32)],
        [lengths, d_edge, pair, normed0, d_gatepre0, grad, ngain, proj_w, gate_w, outgate_w],
        [wts, big, ((2, H, lanes), F32)], 9 * dense, 1,
    )
    (in_grads0,) = call(
        in_weight_kernel, "in_weights_lower", [((4 * H, H), BF16)], [normed0, d_in0], (), 4 * dense,
    )
    small = jnp.concatenate([small0, small_mid[2:4], small_mid[0:2], small_mid1], axis=0)
    high = small.astype(BF16)
    low = (small - high.astype(F32)).astype(BF16)
    every = jnp.concatenate([high, low], axis=0)
    weights = jnp.concatenate([in_grads0, out_grads0, in_grads1, out_grads1], axis=0)
    share = weights.shape[0] // shards
    packed = jnp.concatenate(
        [weights.reshape(shards, share, H), jnp.broadcast_to(every[None], (shards,) + every.shape)],
        axis=1,
    )
    summed = jnp.sum(exchange(packed).astype(F32), axis=0)
    small = summed[share : share + 8] + summed[share + 8 :]
    own = summed[:share].astype(BF16)
    weights = exchange(jnp.broadcast_to(own[None], (shards,) + own.shape))
    weights = weights.reshape(2, 6, H, H).astype(F32)
    small = small.reshape(2, 4, H)
    return (
        new_pair,
        grad_pair,
        small[:, 0],
        small[:, 1],
        weights[:, 0:2],
        weights[:, 2:4],
        small[:, 2],
        small[:, 3],
        weights[:, 4],
        weights[:, 5],
    )


def norm_channels(values):
    average = jnp.mean(values, -1, keepdims=True)
    centred = values - average
    variance = jnp.mean(centred * centred, -1, keepdims=True)
    inverse = lax.rsqrt(variance + EPS)
    return (centred * inverse, inverse)


def forward_module(pair_in, pair_mask, weights, incoming):
    gain_in, bias_in, proj_w, gate_w, gain_mid, bias_mid, out_w, outgate_w = weights
    scaled_in, inverse_in = norm_channels(pair_in.astype(jnp.float32))
    normed = (scaled_in * gain_in + bias_in).astype(jnp.bfloat16)
    projected = product("ijc,sch->shij", normed, proj_w)
    gating = jax.nn.sigmoid(product("ijc,sch->shij", normed, gate_w))
    hidden = (projected * gating * pair_mask).astype(jnp.bfloat16)
    left_side, right_side = (
        lax.all_to_all(hidden[0], "row", split_axis=0, concat_axis=1, tiled=True),
        lax.all_to_all(hidden[1], "row", split_axis=0, concat_axis=1, tiled=True),
    )
    if incoming:
        left_side = jnp.swapaxes(left_side, 1, 2)
        right_side = jnp.swapaxes(right_side, 1, 2)
    else:
        left_side, right_side = (
            lax.all_to_all(left_side, "col", split_axis=1, concat_axis=2, tiled=True),
            lax.all_to_all(right_side, "col", split_axis=1, concat_axis=2, tiled=True),
        )
    triangle = product(
        "cik,cjk->cij", left_side, lax.all_gather(right_side, "col", axis=1, tiled=True)
    ).astype(jnp.bfloat16)
    triangle = lax.all_to_all(
        lax.all_to_all(triangle, "col", split_axis=2, concat_axis=1, tiled=True),
        "row",
        split_axis=1,
        concat_axis=0,
        tiled=True,
    )
    tri_values = triangle.astype(jnp.float32)
    total, squares = lax.psum((jnp.sum(tri_values, 0), jnp.sum(tri_values * tri_values, 0)), "ch")
    average = total / H
    inverse_mid = lax.rsqrt(squares / H - average * average + EPS)
    scaled_mid = (tri_values - average) * inverse_mid
    unit = (scaled_mid * gain_mid[:, None, None] + bias_mid[:, None, None]).astype(jnp.bfloat16)
    unit_full = lax.all_gather(unit, "ch", axis=0, tiled=True)
    outer = product("hij,hc->ijc", unit_full, out_w)
    outgate = jax.nn.sigmoid(product("ijc,cd->ijd", normed, outgate_w))
    result = (pair_in.astype(jnp.float32) + outer * outgate).astype(jnp.bfloat16)
    saved = (
        scaled_in,
        inverse_in,
        normed,
        projected,
        gating,
        left_side,
        right_side,
        scaled_mid,
        inverse_mid,
        unit_full,
        outer,
        outgate,
    )
    return (result, saved)


def backward_module(grad_out, pair_mask, weights, saved, incoming):
    gain_in, bias_in, proj_w, gate_w, gain_mid, bias_mid, out_w, outgate_w = weights
    (
        scaled_in,
        inverse_in,
        normed,
        projected,
        gating,
        left_side,
        right_side,
        scaled_mid,
        inverse_mid,
        unit_full,
        outer,
        outgate,
    ) = saved
    d_outer = (grad_out * outgate).astype(jnp.bfloat16)
    d_gatepre = (grad_out * outer * outgate * (1.0 - outgate)).astype(jnp.bfloat16)
    grad_out_w = product("hij,ijc->hc", unit_full, d_outer)
    grad_outgate_w = product("ijc,ijd->cd", normed, d_gatepre)
    width = gain_mid.shape[0]
    own_rows = lax.dynamic_slice_in_dim(out_w, lax.axis_index("ch") * width, width, 0)
    d_unit = product("ijc,hc->hij", d_outer, own_rows)
    d_normed = product("ijd,cd->ijc", d_gatepre, outgate_w)
    weighted = d_unit * gain_mid[:, None, None]
    grad_gain_mid = jnp.sum(d_unit * scaled_mid, (1, 2))
    grad_bias_mid = jnp.sum(d_unit, (1, 2))
    first_sum, second_sum = lax.psum(
        (jnp.sum(weighted, 0), jnp.sum(weighted * scaled_mid, 0)), "ch"
    )
    d_tri = (inverse_mid * (weighted - first_sum / H - scaled_mid * (second_sum / H))).astype(
        jnp.bfloat16
    )
    grad_rows = lax.all_to_all(d_tri, "row", split_axis=0, concat_axis=1, tiled=True)
    grad_cols = lax.all_to_all(grad_rows, "col", split_axis=1, concat_axis=2, tiled=True)
    d_left = product(
        "cij,cjk->cik", grad_cols, lax.all_gather(right_side, "col", axis=1, tiled=True)
    )
    partial_terms = product("cij,cik->cjk", grad_cols, left_side)
    d_right = lax.psum_scatter(
        partial_terms.astype(jnp.bfloat16), "col", scatter_dimension=1, tiled=True
    ).astype(jnp.float32)
    d_left = d_left.astype(jnp.bfloat16)
    d_right = d_right.astype(jnp.bfloat16)
    if incoming:
        d_left = jnp.swapaxes(d_left, 1, 2)
        d_right = jnp.swapaxes(d_right, 1, 2)
    else:
        d_left, d_right = (
            lax.all_to_all(d_left, "col", split_axis=2, concat_axis=1, tiled=True),
            lax.all_to_all(d_right, "col", split_axis=2, concat_axis=1, tiled=True),
        )
    d_left, d_right = (
        lax.all_to_all(d_left, "row", split_axis=1, concat_axis=0, tiled=True),
        lax.all_to_all(d_right, "row", split_axis=1, concat_axis=0, tiled=True),
    )
    d_hidden = jnp.stack([d_left, d_right]).astype(jnp.float32)
    d_proj = (d_hidden * gating * pair_mask).astype(jnp.bfloat16)
    d_gate = (d_hidden * projected * gating * (1.0 - gating) * pair_mask).astype(jnp.bfloat16)
    grad_proj_w = product("ijc,shij->sch", normed, d_proj)
    grad_gate_w = product("ijc,shij->sch", normed, d_gate)
    partial_input = product("shij,sch->ijc", d_proj, proj_w) + product(
        "shij,sch->ijc", d_gate, gate_w
    )
    d_normed = d_normed + lax.psum(partial_input.astype(jnp.bfloat16), "ch").astype(jnp.float32)
    weighted_in = d_normed * gain_in
    grad_gain_in = jnp.sum(d_normed * scaled_in, (0, 1))
    grad_bias_in = jnp.sum(d_normed, (0, 1))
    d_pair = inverse_in * (
        weighted_in
        - jnp.mean(weighted_in, -1, keepdims=True)
        - scaled_in * jnp.mean(weighted_in * scaled_in, -1, keepdims=True)
    )
    grads = (
        grad_gain_in,
        grad_bias_in,
        grad_proj_w,
        grad_gate_w,
        grad_gain_mid,
        grad_bias_mid,
        grad_out_w,
        grad_outgate_w,
    )
    return (grad_out + d_pair, grads)


def per_device(
    pair,
    cotangent,
    lengths,
    norm_gain,
    norm_bias,
    proj_weight,
    gate_weight,
    mid_gain,
    mid_bias,
    out_weight,
    outgate_weight,
):
    rows_here = pair.shape[0]
    cols_here = pair.shape[1]
    row_ids = lax.axis_index("row") * rows_here + lax.iota(jnp.int32, rows_here)
    col_ids = lax.axis_index("col") * cols_here + lax.iota(jnp.int32, cols_here)
    limit = lengths[0]
    pair_mask = ((row_ids[:, None] < limit) & (col_ids[None, :] < limit)).astype(jnp.float32)
    state = pair
    stash = []
    for layer in range(2):
        weights = (
            norm_gain[layer],
            norm_bias[layer],
            proj_weight[layer],
            gate_weight[layer],
            mid_gain[layer],
            mid_bias[layer],
            out_weight[layer],
            outgate_weight[layer],
        )
        state, saved = forward_module(state, pair_mask, weights, layer == 1)
        stash.append(saved)
    grad_state = cotangent.astype(jnp.float32)
    per_layer = [None, None]
    for layer in (1, 0):
        weights = (
            norm_gain[layer],
            norm_bias[layer],
            proj_weight[layer],
            gate_weight[layer],
            mid_gain[layer],
            mid_bias[layer],
            out_weight[layer],
            outgate_weight[layer],
        )
        grad_state, grads = backward_module(
            grad_state, pair_mask, weights, stash[layer], layer == 1
        )
        per_layer[layer] = grads
    lower = per_layer[0]
    upper = per_layer[1]
    summed = lax.psum(
        (
            lower[0],
            lower[1],
            lower[2],
            lower[3],
            lower[4],
            lower[5],
            lower[6],
            lower[7],
            upper[0],
            upper[1],
            upper[2],
            upper[3],
            upper[4],
            upper[5],
            upper[6],
            upper[7],
        ),
        ("row", "col"),
    )
    per_layer = [summed[0:8], summed[8:16]]
    stacked = [jnp.stack([per_layer[0][index], per_layer[1][index]]) for index in range(8)]
    return (
        state,
        grad_state.astype(jnp.bfloat16),
        stacked[0],
        stacked[1],
        stacked[2],
        stacked[3],
        stacked[4],
        stacked[5],
        stacked[6],
        stacked[7],
    )


def solution(mesh):
    in_specs = (
        P(("grp", "row"), "col", None),
        P(("grp", "row"), "col", None),
        P("grp"),
        P(),
        P(),
        P(None, None, None, "ch"),
        P(None, None, None, "ch"),
        P(None, "ch"),
        P(None, "ch"),
        P(),
        P(),
    )
    out_specs = (
        P(("grp", "row"), "col", None),
        P(("grp", "row"), "col", None),
        P("grp", None),
        P("grp", None),
        P("grp", None, None, "ch"),
        P("grp", None, None, "ch"),
        P("grp", "ch"),
        P("grp", "ch"),
        P("grp", None, None),
        P("grp", None, None),
    )
    many, few = mesh.shape["row"], mesh.shape["col"]
    if mesh.shape["ch"] == 1 and H % (many * few) == 0:
        body = functools.partial(grouped_device, many=many, few=few)
    else:
        body = per_device
    return jax.shard_map(
        body, mesh=mesh, in_specs=in_specs, out_specs=out_specs, check_vma=False
    )
```

```python
import functools

import jax
import jax.numpy as jnp
from jax import lax
from jax.experimental import pallas as pl
from jax.experimental.pallas import tpu as pltpu
from jax.sharding import PartitionSpec as P

H = 128


EPS = 1e-05


def product(spec, left, right):
    return jnp.einsum(spec, left, right, preferred_element_type=jnp.float32)


F32 = jnp.float32
BF16 = jnp.bfloat16


def dot(left, right):
    return lax.dot_general(left, right, (((1,), (0,)), ((), ())), preferred_element_type=F32)


def dot_rt(left, right):
    return lax.dot_general(left, right, (((1,), (1,)), ((), ())), preferred_element_type=F32)


def dot_lt(left, right):
    return lax.dot_general(left, right, (((0,), (0,)), ((), ())), preferred_element_type=F32)


def sigmoid(values):
    return 1.0 / (1.0 + jnp.exp(-values))


def norm_rows(values):
    scale = 1.0 / values.shape[0]
    average = jnp.sum(values, 0, keepdims=True) * scale
    centred = values - average
    variance = jnp.sum(centred * centred, 0, keepdims=True) * scale
    inverse = lax.rsqrt(variance + EPS)
    return centred * inverse, inverse


def turned(weight):
    return jnp.transpose(weight.astype(F32)).astype(BF16)


def column(ref, module, lanes):
    row = ref[module : module + 1, :]
    return jnp.transpose(jnp.broadcast_to(row, (lanes, row.shape[1])))


def as_row(total):
    return jnp.sum(jnp.transpose(total), 0, keepdims=True)


def row_mask(lengths_ref, step, rows, lanes):
    limit = lengths_ref[0]
    row_id = lax.axis_index("row") * rows + step
    col_id = lax.axis_index("col") * lanes + lax.broadcasted_iota(jnp.int32, (1, lanes), 1)
    return jnp.where((row_id < limit) & (col_id < limit), 1.0, 0.0).astype(F32)


def load_in_weights(proj_ref, gate_ref, module, scratch):
    width = proj_ref.shape[-1]
    for side in range(2):
        scratch[side * width : (side + 1) * width, :] = turned(proj_ref[module, side])
        scratch[(2 + side) * width : (3 + side) * width, :] = turned(gate_ref[module, side])


def edges(normed, in_weights, mask):
    pre = dot(in_weights, normed)
    half = pre.shape[0] // 2
    return pre[:half] * sigmoid(pre[half:]) * mask


def put_rows(scratch, values, step, rows):
    scratch[pl.ds(step, values.shape[0], stride=rows), :] = values


def get_rows(scratch, step, channels, rows):
    return scratch[pl.ds(step, channels, stride=rows), :]


def spread_edges(scratch, out_refs):
    shards, sides, group, rows, lanes = out_refs[0].shape
    view = scratch.reshape(sides, shards, len(out_refs), group, rows, lanes)
    for chunk, out_ref in enumerate(out_refs):
        for side in range(sides):
            out_ref[:, side] = view[side, :, chunk].astype(BF16)


def collect_edges(in_refs, scratch):
    shards, sides, group, rows, lanes = in_refs[0].shape
    view = scratch.reshape(sides, shards, len(in_refs), group, rows, lanes)
    for chunk, in_ref in enumerate(in_refs):
        for side in range(sides):
            view[side, :, chunk] = in_ref[:, side].astype(F32)


def spread_triangle(scratch, out_refs):
    shards, group, rows, lanes = out_refs[0].shape
    view = scratch.reshape(shards, len(out_refs), group, rows, lanes)
    for chunk, out_ref in enumerate(out_refs):
        out_ref[...] = view[:, chunk].astype(BF16)


def collect_triangle(in_refs, scratch, channels):
    shards, group, rows, lanes = in_refs[0].shape
    view = scratch.at[0 : channels * rows].reshape(shards, len(in_refs), group, rows, lanes)
    for chunk, in_ref in enumerate(in_refs):
        view[:, chunk] = in_ref[...].astype(F32)


def start_kernel(
    lengths, pair, ngain, nbias, proj_w, gate_w, edge_a, edge_b, normed_out, wts, scr
):
    rows, lanes, channels = pair.shape
    load_in_weights(proj_w, gate_w, 0, wts)
    gain, bias = column(ngain, 0, lanes), column(nbias, 0, lanes)

    def body(step, carry):
        scaled, _ = norm_rows(jnp.transpose(pair[step].astype(F32)))
        normed = (scaled * gain + bias).astype(BF16)
        normed_out[step] = normed
        put_rows(scr, edges(normed, wts[...], row_mask(lengths, step, rows, lanes)), step, rows)
        return carry

    lax.fori_loop(0, rows, body, 0, unroll=2)
    spread_edges(scr, (edge_a, edge_b))


def mid_norm(tri):
    scale = 1.0 / tri.shape[0]
    average = jnp.sum(tri, 0, keepdims=True) * scale
    squares = jnp.sum(tri * tri, 0, keepdims=True) * scale
    inverse = lax.rsqrt(squares - average * average + EPS)
    return (tri - average) * inverse, inverse


def between_kernel(
    lengths, tri_a, tri_b, pair, normed0, ngain, nbias, mgain, mbias, out_w, outgate_w, proj_w,
    gate_w, edge_a, edge_b, mid_out, normed_out, wts, scr,
):
    rows, lanes, channels = pair.shape
    load_in_weights(proj_w, gate_w, 1, wts)
    out_t, outgate_t = turned(out_w[0]), turned(outgate_w[0])
    gain, bias = column(ngain, 1, lanes), column(nbias, 1, lanes)
    gain_mid, bias_mid = column(mgain, 0, lanes), column(mbias, 0, lanes)
    collect_triangle((tri_a, tri_b), scr, channels)

    def body(step, carry):
        scaled_mid, _ = mid_norm(get_rows(scr, step, channels, rows))
        unit = (scaled_mid * gain_mid + bias_mid).astype(BF16)
        outer = dot(out_t, unit)
        outgate = sigmoid(dot(outgate_t, normed0[step]))
        mid = (jnp.transpose(pair[step].astype(F32)) + outer * outgate).astype(BF16)
        mid_out[step] = mid
        scaled, _ = norm_rows(mid.astype(F32))
        normed = (scaled * gain + bias).astype(BF16)
        normed_out[step] = normed
        here = edges(normed, wts[...], row_mask(lengths, step, rows, lanes))
        put_rows(scr, here, step, rows)
        return carry

    lax.fori_loop(0, rows, body, 0, unroll=2)
    spread_edges(scr, (edge_a, edge_b))


def triangle_kernel(incoming, edge, tri_out):
    many, few, _, group, rows, lanes = edge.shape

    def whole(side, channel):
        parts = [edge[:, c, side, channel].reshape(many * rows, lanes) for c in range(few)]
        return jnp.concatenate(parts, axis=1)

    for channel in range(group):
        left, right = whole(0, channel), whole(1, channel)
        tri = (dot_lt if incoming else dot_rt)(left, right).astype(BF16)
        for c in range(few):
            part = tri[:, c * lanes : (c + 1) * lanes]
            tri_out[:, c, channel] = part.reshape(many, rows, lanes)


def edge_grad_kernel(incoming, edge, d_tri, grad_out):
    many, few, _, group, rows, lanes = edge.shape

    def whole(ref, *index):
        parts = [ref[(slice(None), c) + index].reshape(many * rows, lanes) for c in range(few)]
        return jnp.concatenate(parts, axis=1)

    for channel in range(group):
        left, right = whole(edge, 0, channel), whole(edge, 1, channel)
        grad = whole(d_tri, channel)
        if incoming:
            d_left, d_right = dot_rt(right, grad), dot(left, grad)
        else:
            d_left, d_right = dot(grad, right), dot_lt(grad, left)
        for side, value in ((0, d_left), (1, d_right)):
            value = value.astype(BF16)
            for c in range(few):
                part = value[:, c * lanes : (c + 1) * lanes]
                grad_out[:, c, side, channel] = part.reshape(many, rows, lanes)


def mid_backward(
    step, grad, tri, normed, gain_mid, bias_mid, out_t, outgate_t, out_w,
    unit_out, d_outer_out, d_gatepre_out, sum_gain, sum_bias,
):
    scaled_mid, inverse_mid = mid_norm(tri)
    unit = (scaled_mid * gain_mid + bias_mid).astype(BF16)
    outer = dot(out_t, unit)
    outgate = sigmoid(dot(outgate_t, normed))
    gated = grad * outgate
    d_outer = gated.astype(BF16)
    d_gatepre = (gated * outer * (1.0 - outgate)).astype(BF16)
    unit_out[step] = unit
    d_outer_out[step] = d_outer
    d_gatepre_out[step] = d_gatepre
    d_unit = dot(out_w, d_outer)
    sum_gain[...] += d_unit * scaled_mid
    sum_bias[...] += d_unit
    weighted = d_unit * gain_mid
    scale = 1.0 / weighted.shape[0]
    first = jnp.sum(weighted, 0, keepdims=True) * scale
    second = jnp.sum(weighted * scaled_mid, 0, keepdims=True) * scale
    d_tri = inverse_mid * (weighted - first - scaled_mid * second)
    return d_tri, outer * outgate


def turn_kernel(
    tri_a, tri_b, mid, normed1, cot, mgain, mbias, out_w, outgate_w,
    d_tri_a, d_tri_b, new_out, unit_out, d_outer_out, d_gatepre_out, small_out, scr, sum_gain, sum_bias,
):
    rows, channels, lanes = mid.shape
    out_t, outgate_t = turned(out_w[1]), turned(outgate_w[1])
    gain_mid, bias_mid = column(mgain, 1, lanes), column(mbias, 1, lanes)
    collect_triangle((tri_a, tri_b), scr, channels)
    sum_gain[...] = jnp.zeros_like(sum_gain)
    sum_bias[...] = jnp.zeros_like(sum_bias)

    def body(step, carry):
        grad = jnp.transpose(cot[step].astype(F32))
        d_tri, update = mid_backward(
            step, grad, get_rows(scr, step, channels, rows), normed1[step], gain_mid, bias_mid,
            out_t, outgate_t, out_w[1], unit_out, d_outer_out, d_gatepre_out, sum_gain, sum_bias,
        )
        new_out[step] = jnp.transpose(mid[step].astype(F32) + update).astype(BF16)
        put_rows(scr, d_tri, step, rows)
        return carry

    lax.fori_loop(0, rows, body, 0, unroll=2)
    spread_triangle(scr, (d_tri_a, d_tri_b))
    small_out[0:1, :] = as_row(sum_gain[...])
    small_out[1:2, :] = as_row(sum_bias[...])


def in_backward(
    step, grad, base, d_edges, normed, d_gatepre, mask, gain, wts, proj_w, gate_w, outgate_w,
    d_in_out, sum_gain, sum_bias,
):
    pre = dot(wts[...], normed)
    half = pre.shape[0] // 2
    gating = sigmoid(pre[half:])
    through = d_edges * gating * mask
    d_proj = through.astype(BF16)
    d_gate = (through * pre[:half] * (1.0 - gating)).astype(BF16)
    d_in_out[step, 0:half] = d_proj
    d_in_out[step, half:] = d_gate
    width = half // 2
    d_normed = dot(outgate_w, d_gatepre)
    for side in range(2):
        d_normed += dot(proj_w[side], d_proj[side * width : (side + 1) * width])
        d_normed += dot(gate_w[side], d_gate[side * width : (side + 1) * width])
    scaled, inverse = norm_rows(base)
    sum_gain[...] += d_normed * scaled
    sum_bias[...] += d_normed
    weighted = d_normed * gain
    scale = 1.0 / weighted.shape[0]
    first = jnp.sum(weighted, 0, keepdims=True) * scale
    second = jnp.sum(weighted * scaled, 0, keepdims=True) * scale
    return grad + inverse * (weighted - first - scaled * second)


def middle_kernel(
    lengths, d_edge_a, d_edge_b, mid, normed1, d_gatepre1, cot, tri_a, tri_b, normed0,
    ngain, mgain, mbias, proj_w, gate_w, out_w, outgate_w,
    d_tri_a, d_tri_b, grad_out, d_in_out, unit_out, d_outer_out, d_gatepre_out, small_out,
    wts, scr, scr_tri, sums,
):
    rows, channels, lanes = mid.shape
    load_in_weights(proj_w, gate_w, 1, wts)
    out_t, outgate_t = turned(out_w[0]), turned(outgate_w[0])
    gain = column(ngain, 1, lanes)
    gain_mid, bias_mid = column(mgain, 0, lanes), column(mbias, 0, lanes)
    collect_edges((d_edge_a, d_edge_b), scr)
    collect_triangle((tri_a, tri_b), scr_tri, channels)
    sums[...] = jnp.zeros_like(sums)

    def body(step, carry):
        grad = in_backward(
            step, jnp.transpose(cot[step].astype(F32)), mid[step].astype(F32),
            get_rows(scr, step, scr.shape[0] // rows, rows), normed1[step], d_gatepre1[step],
            row_mask(lengths, step, rows, lanes), gain, wts, proj_w[1], gate_w[1], outgate_w[1],
            d_in_out, sums.at[0], sums.at[1],
        )
        grad_out[step] = grad
        d_tri, _ = mid_backward(
            step, grad, get_rows(scr_tri, step, channels, rows), normed0[step], gain_mid, bias_mid,
            out_t, outgate_t, out_w[0], unit_out, d_outer_out, d_gatepre_out,
            sums.at[2], sums.at[3],
        )
        put_rows(scr_tri, d_tri, step, rows)
        return carry

    lax.fori_loop(0, rows, body, 0, unroll=2)
    spread_triangle(scr_tri, (d_tri_a, d_tri_b))
    for index in range(4):
        small_out[index : index + 1, :] = as_row(sums[index])


def finish_kernel(
    lengths, d_edge_a, d_edge_b, pair, normed0, d_gatepre0, grad, ngain, proj_w, gate_w, outgate_w,
    grad_out, d_in_out, small_out, wts, scr, sums,
):
    rows, lanes, channels = pair.shape
    load_in_weights(proj_w, gate_w, 0, wts)
    gain = column(ngain, 0, lanes)
    collect_edges((d_edge_a, d_edge_b), scr)
    sums[...] = jnp.zeros_like(sums)

    def body(step, carry):
        total = in_backward(
            step, grad[step], jnp.transpose(pair[step].astype(F32)),
            get_rows(scr, step, scr.shape[0] // rows, rows), normed0[step], d_gatepre0[step],
            row_mask(lengths, step, rows, lanes), gain, wts, proj_w[0], gate_w[0], outgate_w[0],
            d_in_out, sums.at[0], sums.at[1],
        )
        grad_out[step] = jnp.transpose(total).astype(BF16)
        return carry

    lax.fori_loop(0, rows, body, 0, unroll=2)
    for index in range(2):
        small_out[index : index + 1, :] = as_row(sums[index])


def in_weight_kernel(normed, d_in, out_ref):
    rows = normed.shape[0]
    width = normed.shape[1]
    flat = jnp.concatenate([normed[step] for step in range(rows)], axis=1)
    for part in range(d_in.shape[1] // width):
        block = slice(part * width, (part + 1) * width)
        other = jnp.concatenate([d_in[step, block] for step in range(rows)], axis=1)
        out_ref[block, :] = dot_rt(flat, other).astype(out_ref.dtype)


def out_weight_kernel(unit, d_outer, normed, d_gatepre, out_ref):
    rows = normed.shape[0]
    width = normed.shape[1]
    for part, (left, right) in enumerate(((unit, d_outer), (normed, d_gatepre))):
        first = jnp.concatenate([left[step] for step in range(rows)], axis=1)
        second = jnp.concatenate([right[step] for step in range(rows)], axis=1)
        block = slice(part * width, (part + 1) * width)
        out_ref[block, :] = dot_rt(first, second).astype(out_ref.dtype)


SCALARS = pl.BlockSpec(memory_space=pltpu.SMEM)
VECTORS = pl.BlockSpec(memory_space=pltpu.VMEM)


def call(kernel, name, outs, args, scratch=(), flops=0, scalars=0):
    shapes = [jax.ShapeDtypeStruct(shape, dtype) for shape, dtype in outs]
    moved = sum(a.size * a.dtype.itemsize for a in list(args) + shapes)
    result = pl.pallas_call(
        kernel,
        name=name,
        out_shape=shapes,
        in_specs=[SCALARS] * scalars + [VECTORS] * (len(args) - scalars),
        out_specs=[VECTORS] * len(shapes),
        scratch_shapes=[pltpu.VMEM(shape, dtype) for shape, dtype in scratch],
        compiler_params=pltpu.CompilerParams(vmem_limit_bytes=32 * 1024 * 1024),
        cost_estimate=pl.CostEstimate(flops=flops, bytes_accessed=moved, transcendentals=0),
    )(*args)
    return result


def exchange(values):
    return lax.all_to_all(values, ("row", "col"), split_axis=0, concat_axis=0, tiled=True)


def grouped_device(
    pair, cotangent, lengths, ngain, nbias, proj_w, gate_w, mgain, mbias, out_w, outgate_w,
    *, many, few,
):
    rows, lanes, channels = pair.shape
    shards = many * few
    chunks = 2
    group = H // (shards * chunks)
    edge_shape = (shards, 2, group, rows, lanes)
    grid_shape = (many, few, 2, group, rows, lanes)
    tri_shape = (shards, group, rows, lanes)
    tri_grid = (many, few, group, rows, lanes)
    tile = (rows, channels, lanes)
    wts = ((4 * H, channels), BF16)
    big = ((2 * H * rows, lanes), F32)
    mid = ((H * rows, lanes), F32)
    positions = rows * lanes
    triangle = 2 * group * (many * rows) ** 2 * (few * lanes)
    dense = 2 * positions * channels * H

    def triangles(name, incoming, edges_in):
        out = []
        for edge in edges_in:
            (tri,) = call(
                functools.partial(triangle_kernel, incoming), name, [(tri_grid, BF16)], [edge],
                (), triangle,
            )
            out.append(exchange(tri.reshape(tri_shape)))
        return out

    def edge_grads(name, incoming, edges_in, d_tris):
        out = []
        for edge, d_tri in zip(edges_in, d_tris):
            (d_edge,) = call(
                functools.partial(edge_grad_kernel, incoming), name, [(grid_shape, BF16)],
                [edge, exchange(d_tri).reshape(tri_grid)], (), 2 * triangle,
            )
            out.append(exchange(d_edge.reshape(edge_shape)))
        return out

    *edge, normed0 = call(
        start_kernel, "start", [(edge_shape, BF16)] * chunks + [(tile, BF16)],
        [lengths, pair, ngain, nbias, proj_w, gate_w], [wts, big], 4 * dense, 1,
    )
    edge0 = [exchange(part).reshape(grid_shape) for part in edge]
    tri0 = triangles("outgoing", False, edge0)
    *edge, mid_t, normed1 = call(
        between_kernel, "between", [(edge_shape, BF16)] * chunks + [(tile, BF16), (tile, BF16)],
        [lengths, *tri0, pair, normed0, ngain, nbias, mgain, mbias, out_w, outgate_w, proj_w,
         gate_w],
        [wts, big], 6 * dense, 1,
    )
    edge1 = [exchange(part).reshape(grid_shape) for part in edge]
    tri1 = triangles("incoming", True, edge1)
    *d_tri, new_pair, unit1, d_outer1, d_gatepre1, small_mid1 = call(
        turn_kernel, "turn",
        [(tri_shape, BF16)] * chunks
        + [(pair.shape, BF16), (tile, BF16), (tile, BF16), (tile, BF16), ((2, H), F32)],
        [*tri1, mid_t, normed1, cotangent, mgain, mbias, out_w, outgate_w],
        [mid, ((H, lanes), F32), ((H, lanes), F32)], 3 * dense,
    )
    d_edge = edge_grads("incoming_grad", True, edge1, d_tri)
    (out_grads1,) = call(
        out_weight_kernel, "out_weights_upper", [((2 * H, channels), BF16)],
        [unit1, d_outer1, normed1, d_gatepre1], (), 2 * dense,
    )
    *d_tri, grad, d_in1, unit0, d_outer0, d_gatepre0, small_mid = call(
        middle_kernel, "middle",
        [(tri_shape, BF16)] * chunks
        + [(tile, F32), ((rows, 4 * H, lanes), BF16), (tile, BF16), (tile, BF16),
           (tile, BF16), ((4, H), F32)],
        [lengths, *d_edge, mid_t, normed1, d_gatepre1, cotangent, *tri0, normed0,
         ngain, mgain, mbias, proj_w, gate_w, out_w, outgate_w],
        [wts, big, mid, ((4, H, lanes), F32)], 12 * dense, 1,
    )
    d_edge = edge_grads("outgoing_grad", False, edge0, d_tri)
    (in_grads1,) = call(
        in_weight_kernel, "in_weights_upper", [((4 * H, H), BF16)], [normed1, d_in1], (), 4 * dense,
    )
    (out_grads0,) = call(
        out_weight_kernel, "out_weights_lower", [((2 * H, channels), BF16)],
        [unit0, d_outer0, normed0, d_gatepre0], (), 2 * dense,
    )
    early = jnp.concatenate([in_grads1, out_grads1, out_grads0], axis=0)
    early = jnp.sum(exchange(early.reshape(shards, -1, H)).astype(F32), axis=0).astype(BF16)
    grad_pair, d_in0, small0 = call(
        finish_kernel, "finish",
        [(pair.shape, BF16), ((rows, 4 * H, lanes), BF16), ((2, H), F32)],
        [lengths, *d_edge, pair, normed0, d_gatepre0, grad, ngain, proj_w, gate_w, outgate_w],
        [wts, big, ((2, H, lanes), F32)], 9 * dense, 1,
    )
    (in_grads0,) = call(
        in_weight_kernel, "in_weights_lower", [((4 * H, H), BF16)], [normed0, d_in0], (), 4 * dense,
    )
    small = jnp.concatenate([small0, small_mid[2:4], small_mid[0:2], small_mid1], axis=0)
    high = small.astype(BF16)
    low = (small - high.astype(F32)).astype(BF16)
    every = jnp.concatenate([high, low, early], axis=0)
    share = 4 * H // shards
    packed = jnp.concatenate(
        [in_grads0.reshape(shards, share, H), jnp.broadcast_to(every[None], (shards,) + every.shape)],
        axis=1,
    )
    packed = exchange(packed)
    summed = jnp.sum(packed[:, : share + 16].astype(F32), axis=0)
    small = summed[share : share + 8] + summed[share + 8 :]
    early = packed[:, share + 16 :].reshape(8, H, H).astype(F32)
    own = summed[:share].astype(BF16)
    late = exchange(jnp.broadcast_to(own[None], (shards,) + own.shape))
    late = late.reshape(4, H, H).astype(F32)
    small = small.reshape(2, 4, H)
    return (
        new_pair,
        grad_pair,
        small[:, 0],
        small[:, 1],
        jnp.stack([late[0:2], early[0:2]]),
        jnp.stack([late[2:4], early[2:4]]),
        small[:, 2],
        small[:, 3],
        jnp.stack([early[6], early[4]]),
        jnp.stack([early[7], early[5]]),
    )


def norm_channels(values):
    average = jnp.mean(values, -1, keepdims=True)
    centred = values - average
    variance = jnp.mean(centred * centred, -1, keepdims=True)
    inverse = lax.rsqrt(variance + EPS)
    return (centred * inverse, inverse)


def forward_module(pair_in, pair_mask, weights, incoming):
    gain_in, bias_in, proj_w, gate_w, gain_mid, bias_mid, out_w, outgate_w = weights
    scaled_in, inverse_in = norm_channels(pair_in.astype(jnp.float32))
    normed = (scaled_in * gain_in + bias_in).astype(jnp.bfloat16)
    projected = product("ijc,sch->shij", normed, proj_w)
    gating = jax.nn.sigmoid(product("ijc,sch->shij", normed, gate_w))
    hidden = (projected * gating * pair_mask).astype(jnp.bfloat16)
    left_side, right_side = (
        lax.all_to_all(hidden[0], "row", split_axis=0, concat_axis=1, tiled=True),
        lax.all_to_all(hidden[1], "row", split_axis=0, concat_axis=1, tiled=True),
    )
    if incoming:
        left_side = jnp.swapaxes(left_side, 1, 2)
        right_side = jnp.swapaxes(right_side, 1, 2)
    else:
        left_side, right_side = (
            lax.all_to_all(left_side, "col", split_axis=1, concat_axis=2, tiled=True),
            lax.all_to_all(right_side, "col", split_axis=1, concat_axis=2, tiled=True),
        )
    triangle = product(
        "cik,cjk->cij", left_side, lax.all_gather(right_side, "col", axis=1, tiled=True)
    ).astype(jnp.bfloat16)
    triangle = lax.all_to_all(
        lax.all_to_all(triangle, "col", split_axis=2, concat_axis=1, tiled=True),
        "row",
        split_axis=1,
        concat_axis=0,
        tiled=True,
    )
    tri_values = triangle.astype(jnp.float32)
    total, squares = lax.psum((jnp.sum(tri_values, 0), jnp.sum(tri_values * tri_values, 0)), "ch")
    average = total / H
    inverse_mid = lax.rsqrt(squares / H - average * average + EPS)
    scaled_mid = (tri_values - average) * inverse_mid
    unit = (scaled_mid * gain_mid[:, None, None] + bias_mid[:, None, None]).astype(jnp.bfloat16)
    unit_full = lax.all_gather(unit, "ch", axis=0, tiled=True)
    outer = product("hij,hc->ijc", unit_full, out_w)
    outgate = jax.nn.sigmoid(product("ijc,cd->ijd", normed, outgate_w))
    result = (pair_in.astype(jnp.float32) + outer * outgate).astype(jnp.bfloat16)
    saved = (
        scaled_in,
        inverse_in,
        normed,
        projected,
        gating,
        left_side,
        right_side,
        scaled_mid,
        inverse_mid,
        unit_full,
        outer,
        outgate,
    )
    return (result, saved)


def backward_module(grad_out, pair_mask, weights, saved, incoming):
    gain_in, bias_in, proj_w, gate_w, gain_mid, bias_mid, out_w, outgate_w = weights
    (
        scaled_in,
        inverse_in,
        normed,
        projected,
        gating,
        left_side,
        right_side,
        scaled_mid,
        inverse_mid,
        unit_full,
        outer,
        outgate,
    ) = saved
    d_outer = (grad_out * outgate).astype(jnp.bfloat16)
    d_gatepre = (grad_out * outer * outgate * (1.0 - outgate)).astype(jnp.bfloat16)
    grad_out_w = product("hij,ijc->hc", unit_full, d_outer)
    grad_outgate_w = product("ijc,ijd->cd", normed, d_gatepre)
    width = gain_mid.shape[0]
    own_rows = lax.dynamic_slice_in_dim(out_w, lax.axis_index("ch") * width, width, 0)
    d_unit = product("ijc,hc->hij", d_outer, own_rows)
    d_normed = product("ijd,cd->ijc", d_gatepre, outgate_w)
    weighted = d_unit * gain_mid[:, None, None]
    grad_gain_mid = jnp.sum(d_unit * scaled_mid, (1, 2))
    grad_bias_mid = jnp.sum(d_unit, (1, 2))
    first_sum, second_sum = lax.psum(
        (jnp.sum(weighted, 0), jnp.sum(weighted * scaled_mid, 0)), "ch"
    )
    d_tri = (inverse_mid * (weighted - first_sum / H - scaled_mid * (second_sum / H))).astype(
        jnp.bfloat16
    )
    grad_rows = lax.all_to_all(d_tri, "row", split_axis=0, concat_axis=1, tiled=True)
    grad_cols = lax.all_to_all(grad_rows, "col", split_axis=1, concat_axis=2, tiled=True)
    d_left = product(
        "cij,cjk->cik", grad_cols, lax.all_gather(right_side, "col", axis=1, tiled=True)
    )
    partial_terms = product("cij,cik->cjk", grad_cols, left_side)
    d_right = lax.psum_scatter(
        partial_terms.astype(jnp.bfloat16), "col", scatter_dimension=1, tiled=True
    ).astype(jnp.float32)
    d_left = d_left.astype(jnp.bfloat16)
    d_right = d_right.astype(jnp.bfloat16)
    if incoming:
        d_left = jnp.swapaxes(d_left, 1, 2)
        d_right = jnp.swapaxes(d_right, 1, 2)
    else:
        d_left, d_right = (
            lax.all_to_all(d_left, "col", split_axis=2, concat_axis=1, tiled=True),
            lax.all_to_all(d_right, "col", split_axis=2, concat_axis=1, tiled=True),
        )
    d_left, d_right = (
        lax.all_to_all(d_left, "row", split_axis=1, concat_axis=0, tiled=True),
        lax.all_to_all(d_right, "row", split_axis=1, concat_axis=0, tiled=True),
    )
    d_hidden = jnp.stack([d_left, d_right]).astype(jnp.float32)
    d_proj = (d_hidden * gating * pair_mask).astype(jnp.bfloat16)
    d_gate = (d_hidden * projected * gating * (1.0 - gating) * pair_mask).astype(jnp.bfloat16)
    grad_proj_w = product("ijc,shij->sch", normed, d_proj)
    grad_gate_w = product("ijc,shij->sch", normed, d_gate)
    partial_input = product("shij,sch->ijc", d_proj, proj_w) + product(
        "shij,sch->ijc", d_gate, gate_w
    )
    d_normed = d_normed + lax.psum(partial_input.astype(jnp.bfloat16), "ch").astype(jnp.float32)
    weighted_in = d_normed * gain_in
    grad_gain_in = jnp.sum(d_normed * scaled_in, (0, 1))
    grad_bias_in = jnp.sum(d_normed, (0, 1))
    d_pair = inverse_in * (
        weighted_in
        - jnp.mean(weighted_in, -1, keepdims=True)
        - scaled_in * jnp.mean(weighted_in * scaled_in, -1, keepdims=True)
    )
    grads = (
        grad_gain_in,
        grad_bias_in,
        grad_proj_w,
        grad_gate_w,
        grad_gain_mid,
        grad_bias_mid,
        grad_out_w,
        grad_outgate_w,
    )
    return (grad_out + d_pair, grads)


def per_device(
    pair,
    cotangent,
    lengths,
    norm_gain,
    norm_bias,
    proj_weight,
    gate_weight,
    mid_gain,
    mid_bias,
    out_weight,
    outgate_weight,
):
    rows_here = pair.shape[0]
    cols_here = pair.shape[1]
    row_ids = lax.axis_index("row") * rows_here + lax.iota(jnp.int32, rows_here)
    col_ids = lax.axis_index("col") * cols_here + lax.iota(jnp.int32, cols_here)
    limit = lengths[0]
    pair_mask = ((row_ids[:, None] < limit) & (col_ids[None, :] < limit)).astype(jnp.float32)
    state = pair
    stash = []
    for layer in range(2):
        weights = (
            norm_gain[layer],
            norm_bias[layer],
            proj_weight[layer],
            gate_weight[layer],
            mid_gain[layer],
            mid_bias[layer],
            out_weight[layer],
            outgate_weight[layer],
        )
        state, saved = forward_module(state, pair_mask, weights, layer == 1)
        stash.append(saved)
    grad_state = cotangent.astype(jnp.float32)
    per_layer = [None, None]
    for layer in (1, 0):
        weights = (
            norm_gain[layer],
            norm_bias[layer],
            proj_weight[layer],
            gate_weight[layer],
            mid_gain[layer],
            mid_bias[layer],
            out_weight[layer],
            outgate_weight[layer],
        )
        grad_state, grads = backward_module(
            grad_state, pair_mask, weights, stash[layer], layer == 1
        )
        per_layer[layer] = grads
    lower = per_layer[0]
    upper = per_layer[1]
    summed = lax.psum(
        (
            lower[0],
            lower[1],
            lower[2],
            lower[3],
            lower[4],
            lower[5],
            lower[6],
            lower[7],
            upper[0],
            upper[1],
            upper[2],
            upper[3],
            upper[4],
            upper[5],
            upper[6],
            upper[7],
        ),
        ("row", "col"),
    )
    per_layer = [summed[0:8], summed[8:16]]
    stacked = [jnp.stack([per_layer[0][index], per_layer[1][index]]) for index in range(8)]
    return (
        state,
        grad_state.astype(jnp.bfloat16),
        stacked[0],
        stacked[1],
        stacked[2],
        stacked[3],
        stacked[4],
        stacked[5],
        stacked[6],
        stacked[7],
    )


def solution(mesh):
    in_specs = (
        P(("grp", "row"), "col", None),
        P(("grp", "row"), "col", None),
        P("grp"),
        P(),
        P(),
        P(None, None, None, "ch"),
        P(None, None, None, "ch"),
        P(None, "ch"),
        P(None, "ch"),
        P(),
        P(),
    )
    out_specs = (
        P(("grp", "row"), "col", None),
        P(("grp", "row"), "col", None),
        P("grp", None),
        P("grp", None),
        P("grp", None, None, "ch"),
        P("grp", None, None, "ch"),
        P("grp", "ch"),
        P("grp", "ch"),
        P("grp", None, None),
        P("grp", None, None),
    )
    many, few = mesh.shape["row"], mesh.shape["col"]
    if mesh.shape["ch"] == 1 and H % (many * few) == 0:
        body = functools.partial(grouped_device, many=many, few=few)
    else:
        body = per_device
    return jax.shard_map(
        body, mesh=mesh, in_specs=in_specs, out_specs=out_specs, check_vma=False
    )
```

```python
import functools

import jax
import jax.numpy as jnp
from jax import lax
from jax.experimental import pallas as pl
from jax.experimental.pallas import tpu as pltpu
from jax.sharding import PartitionSpec as P

H = 128


EPS = 1e-05


def product(spec, left, right):
    return jnp.einsum(spec, left, right, preferred_element_type=jnp.float32)


F32 = jnp.float32
BF16 = jnp.bfloat16


def dot(left, right):
    return lax.dot_general(left, right, (((1,), (0,)), ((), ())), preferred_element_type=F32)


def dot_rt(left, right):
    return lax.dot_general(left, right, (((1,), (1,)), ((), ())), preferred_element_type=F32)


def dot_lt(left, right):
    return lax.dot_general(left, right, (((0,), (0,)), ((), ())), preferred_element_type=F32)


def sigmoid(values):
    return 1.0 / (1.0 + jnp.exp(-values))


def norm_rows(values):
    scale = 1.0 / values.shape[0]
    average = jnp.sum(values, 0, keepdims=True) * scale
    centred = values - average
    variance = jnp.sum(centred * centred, 0, keepdims=True) * scale
    inverse = lax.rsqrt(variance + EPS)
    return centred * inverse, inverse


def turned(weight):
    return jnp.transpose(weight.astype(F32)).astype(BF16)


def column(ref, module, lanes):
    row = ref[module : module + 1, :]
    return jnp.transpose(jnp.broadcast_to(row, (lanes, row.shape[1])))


def as_row(total):
    return jnp.sum(jnp.transpose(total), 0, keepdims=True)


def row_mask(lengths_ref, step, rows, lanes):
    limit = lengths_ref[0]
    row_id = lax.axis_index("row") * rows + step
    col_id = lax.axis_index("col") * lanes + lax.broadcasted_iota(jnp.int32, (1, lanes), 1)
    return jnp.where((row_id < limit) & (col_id < limit), 1.0, 0.0).astype(F32)


def load_in_weights(proj_ref, gate_ref, module, scratch):
    width = proj_ref.shape[-1]
    for side in range(2):
        scratch[side * width : (side + 1) * width, :] = turned(proj_ref[module, side])
        scratch[(2 + side) * width : (3 + side) * width, :] = turned(gate_ref[module, side])


def put_rows(scratch, values, step, rows):
    scratch[pl.ds(step, values.shape[0], stride=rows), :] = values


def get_rows(scratch, step, channels, rows):
    return scratch[pl.ds(step, channels, stride=rows), :]


def spread_edges(scratch, out_ref):
    shards, sides, group, rows, lanes = out_ref.shape
    block = shards * group * rows
    for side in range(sides):
        part = scratch[side * block : (side + 1) * block, :]
        out_ref[:, side] = part.reshape(shards, group, rows, lanes).astype(BF16)


def collect_edges(in_ref, scratch):
    shards, sides, group, rows, lanes = in_ref.shape
    block = shards * group * rows
    for side in range(sides):
        scratch[side * block : (side + 1) * block, :] = (
            in_ref[:, side].astype(F32).reshape(block, lanes)
        )


def collect_triangle(in_ref, scratch):
    block = in_ref.size // in_ref.shape[-1]
    scratch[0:block, :] = in_ref[...].astype(F32).reshape(block, in_ref.shape[-1])


def each_row(rows, unroll, body):
    def step_body(step, carry):
        body(step)
        return carry

    lax.fori_loop(0, rows, step_body, 0, unroll=unroll)


def mid_norm(tri):
    scale = 1.0 / tri.shape[0]
    average = jnp.sum(tri, 0, keepdims=True) * scale
    squares = jnp.sum(tri * tri, 0, keepdims=True) * scale
    inverse = lax.rsqrt(squares - average * average + EPS)
    return (tri - average) * inverse, inverse


def norm_backward(weighted, scaled, inverse):
    scale = 1.0 / weighted.shape[0]
    first = jnp.sum(weighted, 0, keepdims=True) * scale
    second = jnp.sum(weighted * scaled, 0, keepdims=True) * scale
    return inverse * (weighted - first - scaled * second)


def edges(normed, in_weights, mask):
    pre = dot(in_weights, normed)
    half = pre.shape[0] // 2
    return pre[:half] * sigmoid(pre[half:]) * mask


def start_kernel(
    lengths, pair_far, ngain_far, nbias_far, proj_far, gate_far,
    edge_out, normed_out, pair, ngain, nbias, proj_w, gate_w, sems, wts, scr,
):
    far = (proj_far.at[0], gate_far.at[0], ngain_far, nbias_far, pair_far)
    near = (proj_w.at[0], gate_w.at[0], ngain, nbias, pair)
    copies = [
        pltpu.make_async_copy(source, target, sems.at[index])
        for index, (source, target) in enumerate(zip(far, near))
    ]
    for copy in copies:
        copy.start()
    for copy in copies:
        copy.wait()
    rows, lanes, channels = pair.shape
    load_in_weights(proj_w, gate_w, 0, wts)
    gain, bias = column(ngain, 0, lanes), column(nbias, 0, lanes)

    def body(step):
        scaled, _ = norm_rows(jnp.transpose(pair[step].astype(F32)))
        normed = (scaled * gain + bias).astype(BF16)
        normed_out[step] = normed
        put_rows(scr, edges(normed, wts[...], row_mask(lengths, step, rows, lanes)), step, rows)

    each_row(rows, 4, body)
    spread_edges(scr, edge_out)


def out_gate_kernel(pair, normed, outgate_w, pair_out, gate_out):
    outgate_t = turned(outgate_w[0])

    def body(step):
        pair_out[step] = jnp.transpose(pair[step].astype(F32)).astype(BF16)
        gate_out[step] = sigmoid(dot(outgate_t, normed[step]))

    each_row(pair.shape[0], 2, body)


def between_kernel(
    lengths, tri, pair_t, outgate, ngain, nbias, mgain, mbias, out_w, proj_w, gate_w,
    edge_out, mid_out, normed_out, scaled_mid_out, inverse_mid_out, wts, scr,
):
    rows, channels, lanes = pair_t.shape
    load_in_weights(proj_w, gate_w, 1, wts)
    out_t = turned(out_w[0])
    gain, bias = column(ngain, 1, lanes), column(nbias, 1, lanes)
    gain_mid, bias_mid = column(mgain, 0, lanes), column(mbias, 0, lanes)
    collect_triangle(tri, scr)

    def body(step):
        scaled_mid, inverse_mid = mid_norm(get_rows(scr, step, channels, rows))
        scaled_mid_out[step] = scaled_mid
        inverse_mid_out[pl.ds(step, 1), :] = inverse_mid
        unit = (scaled_mid * gain_mid + bias_mid).astype(BF16)
        outer = dot(out_t, unit)
        mid = (pair_t[step].astype(F32) + outer * outgate[step]).astype(BF16)
        mid_out[step] = mid
        scaled, _ = norm_rows(mid.astype(F32))
        normed = (scaled * gain + bias).astype(BF16)
        normed_out[step] = normed
        here = edges(normed, wts[...], row_mask(lengths, step, rows, lanes))
        put_rows(scr, here, step, rows)

    each_row(rows, 4, body)
    spread_edges(scr, edge_out)


def upstream_kernel(cot, normed, out_w, outgate_w, cot_out, gate_out, d_outer_out, d_unit_out):
    outgate_t = turned(outgate_w[1])

    def body(step):
        grad = jnp.transpose(cot[step].astype(F32))
        outgate = sigmoid(dot(outgate_t, normed[step]))
        d_outer = (grad * outgate).astype(BF16)
        cot_out[step] = grad
        gate_out[step] = outgate
        d_outer_out[step] = d_outer
        d_unit_out[step] = dot(out_w[1], d_outer)

    each_row(cot.shape[0], 2, body)


def turn_kernel(tri, d_unit, mgain, d_tri_out, scr):
    rows, channels, lanes = d_unit.shape
    gain_mid = column(mgain, 1, lanes)
    collect_triangle(tri, scr)

    def body(step):
        scaled_mid, inverse_mid = mid_norm(get_rows(scr, step, channels, rows))
        put_rows(scr, norm_backward(d_unit[step] * gain_mid, scaled_mid, inverse_mid), step, rows)

    each_row(rows, 4, body)
    d_tri_out[...] = scr[...].reshape(d_tri_out.shape).astype(BF16)


def out_weight_grads(unit, d_outer, normed, d_gatepre, out_ref):
    width = unit.shape[0]
    out_ref[0:width, :] = dot_rt(unit[...], d_outer[...]).astype(out_ref.dtype)
    out_ref[width:, :] = dot_rt(normed[...], d_gatepre[...]).astype(out_ref.dtype)


def lane_block(step, lanes):
    return pl.ds(pl.multiple_of(step * lanes, lanes), lanes)


def behind_turn_kernel(
    tri, mid, normed, outgate, grad, d_outer, d_unit, mgain, mbias, out_w, outgate_w,
    new_out, d_normed_out, weights_out, small_out, scr, unit_all, outer_all, normed_all, gate_all,
    sums,
):
    rows, channels, lanes = mid.shape
    out_t = turned(out_w[1])
    gain_mid, bias_mid = column(mgain, 1, lanes), column(mbias, 1, lanes)
    collect_triangle(tri, scr)
    sums[...] = jnp.zeros_like(sums)

    def body(step):
        here = lane_block(step, lanes)
        scaled_mid, _ = mid_norm(get_rows(scr, step, channels, rows))
        unit = (scaled_mid * gain_mid + bias_mid).astype(BF16)
        outer = dot(out_t, unit)
        gate = outgate[step]
        update = outer * gate
        new_out[step] = jnp.transpose(mid[step].astype(F32) + update).astype(BF16)
        d_gatepre = (grad[step] * update * (1.0 - gate)).astype(BF16)
        d_normed_out[step] = dot(outgate_w[1], d_gatepre)
        unit_all[:, here] = unit
        outer_all[:, here] = d_outer[step]
        normed_all[:, here] = normed[step]
        gate_all[:, here] = d_gatepre
        sums[0] += d_unit[step] * scaled_mid
        sums[1] += d_unit[step]

    each_row(rows, 2, body)
    out_weight_grads(unit_all, outer_all, normed_all, gate_all, weights_out)
    for index in range(2):
        small_out[index : index + 1, :] = as_row(sums[index])


def edge_factor_kernel(
    module, lengths, base, normed, proj_w, gate_w,
    proj_out, gate_out, scaled_out, inverse_out, wts,
):
    rows, channels, lanes = base.shape
    load_in_weights(proj_w, gate_w, module, wts)

    def body(step):
        pre = dot(wts[...], normed[step])
        half = pre.shape[0] // 2
        gating = sigmoid(pre[half:])
        factor = gating * row_mask(lengths, step, rows, lanes)
        proj_out[step] = factor
        gate_out[step] = factor * pre[:half] * (1.0 - gating)
        scaled, inverse = norm_rows(base[step].astype(F32))
        scaled_out[step] = scaled
        inverse_out[pl.ds(step, 1), :] = inverse

    each_row(rows, 2, body)


def in_normed(d_in, all_w, proj_w, gate_w):
    width = proj_w.shape[-1]
    total = all_w
    for side in range(2):
        total = total + dot(proj_w[side], d_in[side * width : (side + 1) * width])
        total = total + dot(gate_w[side], d_in[(2 + side) * width : (3 + side) * width])
    return total


def middle_kernel(
    d_edge, proj_factor, gate_factor, d_normed_gate, scaled_in, inverse_in, cot, outgate,
    scaled_mid, inverse_mid, ngain, mgain, proj_w, gate_w, out_w,
    d_tri_out, grad_out, d_in_out, d_normed_out, d_unit_out, scr, scr_tri,
):
    rows, channels, lanes = cot.shape
    gain, gain_mid = column(ngain, 1, lanes), column(mgain, 0, lanes)
    collect_edges(d_edge, scr)
    half = proj_factor.shape[1]

    def body(step):
        here = get_rows(scr, step, half, rows)
        d_proj = (here * proj_factor[step]).astype(BF16)
        d_gate = (here * gate_factor[step]).astype(BF16)
        d_in = jnp.concatenate([d_proj, d_gate], axis=0)
        d_in_out[step] = d_in
        d_normed = in_normed(d_in, d_normed_gate[step], proj_w[1], gate_w[1])
        d_normed_out[step] = d_normed
        grad = cot[step] + norm_backward(
            d_normed * gain, scaled_in[step], inverse_in[pl.ds(step, 1), :]
        )
        grad_out[step] = grad
        d_unit = dot(out_w[0], (grad * outgate[step]).astype(BF16))
        d_unit_out[step] = d_unit
        d_tri = norm_backward(d_unit * gain_mid, scaled_mid[step], inverse_mid[pl.ds(step, 1), :])
        put_rows(scr_tri, d_tri, step, rows)

    each_row(rows, 4, body)
    d_tri_out[...] = scr_tri[...].reshape(d_tri_out.shape).astype(BF16)


def behind_middle_kernel(
    grad, outgate, scaled_mid, d_unit, normed0, d_in1, normed1, d_normed1, scaled1,
    mgain, mbias, out_w, outgate_w,
    d_normed_out, out_weights, in_weights, small_out,
    unit_all, outer_all, normed_all, gate_all, upper_all, d_in_all, sums,
):
    rows, channels, lanes = grad.shape
    out_t = turned(out_w[0])
    gain_mid, bias_mid = column(mgain, 0, lanes), column(mbias, 0, lanes)
    sums[...] = jnp.zeros_like(sums)

    def body(step):
        here = lane_block(step, lanes)
        scaled = scaled_mid[step]
        unit = (scaled * gain_mid + bias_mid).astype(BF16)
        outer = dot(out_t, unit)
        gate = outgate[step]
        gated = grad[step] * gate
        d_gatepre = (gated * outer * (1.0 - gate)).astype(BF16)
        d_normed_out[step] = dot(outgate_w[0], d_gatepre)
        unit_all[:, here] = unit
        outer_all[:, here] = gated.astype(BF16)
        normed_all[:, here] = normed0[step]
        gate_all[:, here] = d_gatepre
        upper_all[:, here] = normed1[step]
        d_in_all[:, here] = d_in1[step]
        sums[0] += d_unit[step] * scaled
        sums[1] += d_unit[step]
        sums[2] += d_normed1[step] * scaled1[step]
        sums[3] += d_normed1[step]

    each_row(rows, 2, body)
    out_weight_grads(unit_all, outer_all, normed_all, gate_all, out_weights)
    in_weight_grads(upper_all, d_in_all, in_weights)
    for index in range(4):
        small_out[index : index + 1, :] = as_row(sums[index])


def in_weight_grads(normed_all, d_in_all, out_ref):
    width = normed_all.shape[0]
    for part in range(d_in_all.shape[0] // width):
        block = slice(part * width, (part + 1) * width)
        out_ref[block, :] = dot_rt(normed_all[...], d_in_all[block, :]).astype(out_ref.dtype)


def finish_kernel(
    d_edge, proj_factor, gate_factor, normed, out0, in1, out1,
    packed_out, d_in_out, scr, normed_all, d_in_all,
):
    rows, half, lanes = proj_factor.shape
    collect_edges(d_edge, scr)

    def body(step):
        place = lane_block(step, lanes)
        here = get_rows(scr, step, half, rows)
        d_proj = (here * proj_factor[step]).astype(BF16)
        d_gate = (here * gate_factor[step]).astype(BF16)
        d_in_out[step, 0:half] = d_proj
        d_in_out[step, half:] = d_gate
        d_in_all[0:half, place] = d_proj
        d_in_all[half:, place] = d_gate
        normed_all[:, place] = normed[step]

    each_row(rows, 4, body)
    first, second, third = d_in_all.shape[0], out0.shape[0], in1.shape[0]
    in_weight_grads(normed_all, d_in_all, packed_out.at[0:first])
    packed_out[first : first + second, :] = out0[...]
    packed_out[first + second : first + second + third, :] = in1[...]
    packed_out[first + second + third :, :] = out1[...]


def behind_finish_kernel(
    d_in, d_normed_gate, grad, scaled_in, inverse_in, ngain, proj_w, gate_w,
    grad_out, small_out, sums,
):
    rows, channels, lanes = grad.shape
    gain = column(ngain, 0, lanes)
    sums[...] = jnp.zeros_like(sums)

    def body(step):
        d_normed = in_normed(d_in[step], d_normed_gate[step], proj_w[0], gate_w[0])
        scaled = scaled_in[step]
        sums[0] += d_normed * scaled
        sums[1] += d_normed
        total = grad[step] + norm_backward(d_normed * gain, scaled, inverse_in[pl.ds(step, 1), :])
        grad_out[step] = jnp.transpose(total).astype(BF16)

    each_row(rows, 2, body)
    for index in range(2):
        small_out[index : index + 1, :] = as_row(sums[index])


def sum_kernel(parts, small0, small_middle, small1, shared_out):
    shards, share, width = parts.shape
    own = jnp.sum(parts[...].astype(F32), axis=0).astype(BF16)
    small = jnp.concatenate(
        [small0[...], small_middle[0:2], small_middle[2:4], small1[...]], axis=0
    )
    high = small.astype(BF16).astype(F32)
    extra = jnp.concatenate([high, small - high], axis=0).astype(BF16)
    for shard in range(shards):
        shared_out[shard, 0:share] = own
        shared_out[shard, share:] = extra


def unpack_kernel(share, shared, proj_out, gate_out, out_out, outgate_out, small_out):
    shards, _, width = shared.shape
    total = jnp.sum(shared[:, share:, :].astype(F32), axis=0)
    small_out[...] = total[0:8] + total[8:16]
    weights = shared[:, 0:share, :].reshape(shards * share, width).astype(F32)
    for module in range(2):
        blocks = [
            weights[(6 * module + part) * width : (6 * module + part + 1) * width]
            for part in range(6)
        ]
        for side in range(2):
            proj_out[module, side] = blocks[side]
            gate_out[module, side] = blocks[2 + side]
        out_out[module] = blocks[4]
        outgate_out[module] = blocks[5]


def triangle_kernel(incoming, edge, tri_out):
    many, few, _, group, rows, lanes = edge.shape

    def whole(side, channel):
        parts = [edge[:, c, side, channel].reshape(many * rows, lanes) for c in range(few)]
        return jnp.concatenate(parts, axis=1)

    for channel in range(group):
        left, right = whole(0, channel), whole(1, channel)
        tri = (dot_lt if incoming else dot_rt)(left, right).astype(BF16)
        for c in range(few):
            part = tri[:, c * lanes : (c + 1) * lanes]
            tri_out[:, c, channel] = part.reshape(many, rows, lanes)


def edge_grad_kernel(incoming, edge, d_tri, grad_out):
    many, few, _, group, rows, lanes = edge.shape

    def whole(ref, *index):
        parts = [ref[(slice(None), c) + index].reshape(many * rows, lanes) for c in range(few)]
        return jnp.concatenate(parts, axis=1)

    for channel in range(group):
        left, right = whole(edge, 0, channel), whole(edge, 1, channel)
        grad = whole(d_tri, channel)
        if incoming:
            d_left, d_right = dot_rt(right, grad), dot(left, grad)
        else:
            d_left, d_right = dot(grad, right), dot_lt(grad, left)
        for side, value in ((0, d_left), (1, d_right)):
            value = value.astype(BF16)
            for c in range(few):
                part = value[:, c * lanes : (c + 1) * lanes]
                grad_out[:, c, side, channel] = part.reshape(many, rows, lanes)


SCALARS = pl.BlockSpec(memory_space=pltpu.SMEM)
VECTORS = pl.BlockSpec(memory_space=pltpu.VMEM)
FAR = pl.BlockSpec(memory_space=pltpu.HBM)


def call(kernel, name, outs, args, scratch=(), flops=0, scalars=0, grant=16, far=False):
    shapes = [jax.ShapeDtypeStruct(shape, dtype) for shape, dtype in outs]
    moved = sum(a.size * a.dtype.itemsize for a in list(args) + shapes)
    rest = FAR if far else VECTORS
    return pl.pallas_call(
        kernel,
        name=name,
        out_shape=shapes,
        in_specs=[SCALARS] * scalars + [rest] * (len(args) - scalars),
        out_specs=[VECTORS] * len(shapes),
        scratch_shapes=[
            pltpu.VMEM(*item) if isinstance(item, tuple) else item for item in scratch
        ],
        compiler_params=pltpu.CompilerParams(vmem_limit_bytes=grant * 1024 * 1024),
        cost_estimate=pl.CostEstimate(flops=flops, bytes_accessed=moved, transcendentals=0),
    )(*args)


def exchange(values):
    return lax.all_to_all(values, ("row", "col"), split_axis=0, concat_axis=0, tiled=True)


def grouped_device(
    pair, cotangent, lengths, ngain, nbias, proj_w, gate_w, mgain, mbias, out_w, outgate_w,
    *, many, few,
):
    rows, lanes, channels = pair.shape
    shards = many * few
    group = H // shards
    edge = ((shards, 2, group, rows, lanes), BF16)
    grid = ((many, few, 2, group, rows, lanes), BF16)
    tri = ((shards, group, rows, lanes), BF16)
    tri_grid = ((many, few, group, rows, lanes), BF16)
    tile = ((rows, channels, lanes), BF16)
    wide = ((rows, channels, lanes), F32)
    row = ((rows, lanes), F32)
    factor = ((rows, 2 * H, lanes), F32)
    d_in = ((rows, 4 * H, lanes), BF16)
    wts = ((4 * H, channels), BF16)
    big = ((2 * H * rows, lanes), F32)
    mid = ((H * rows, lanes), F32)
    positions = rows * lanes
    flat = ((H, positions), BF16)
    flat_in = ((4 * H, positions), BF16)
    out_rows = ((2 * H, channels), BF16)
    in_rows = ((4 * H, H), BF16)
    triangle = 2 * group * (many * rows) ** 2 * (few * lanes)
    dense = 2 * positions * channels * H

    def sums(count):
        return ((count, H, lanes), F32)

    def small(count):
        return ((count, H), F32)

    sent, normed0 = call(
        start_kernel, "start", [edge, tile], [lengths, pair, ngain, nbias, proj_w, gate_w],
        [(pair.shape, BF16), (ngain.shape, F32), (nbias.shape, F32), (proj_w.shape, BF16),
         (gate_w.shape, BF16), pltpu.SemaphoreType.DMA((5,)), wts, big],
        4 * dense, 1, far=True,
    )
    edge0 = exchange(sent).reshape(grid[0])
    pair_t, outgate0 = call(
        out_gate_kernel, "out_gate", [tile, wide], [pair, normed0, outgate_w], (), dense,
    )
    (here,) = call(
        functools.partial(triangle_kernel, False), "outgoing", [tri_grid], [edge0], (), triangle,
    )
    tri0 = exchange(here.reshape(tri[0]))
    sent, mid_t, normed1, scaled_mid0, inverse_mid0 = call(
        between_kernel, "between", [edge, tile, tile, wide, row],
        [lengths, tri0, pair_t, outgate0, ngain, nbias, mgain, mbias, out_w, proj_w, gate_w],
        [wts, big], 5 * dense, 1,
    )
    edge1 = exchange(sent).reshape(grid[0])
    cot_t, outgate1, d_outer1, d_unit1 = call(
        upstream_kernel, "upstream", [wide, wide, tile, wide],
        [cotangent, normed1, out_w, outgate_w], (), 2 * dense,
    )
    (here,) = call(
        functools.partial(triangle_kernel, True), "incoming", [tri_grid], [edge1], (), triangle,
    )
    tri1 = exchange(here.reshape(tri[0]))
    (sent,) = call(turn_kernel, "turn", [tri], [tri1, d_unit1, mgain], [mid], dense)
    d_tri1 = exchange(sent).reshape(tri_grid[0])
    new_pair, d_normed_gate1, out_grads1, small1 = call(
        behind_turn_kernel, "behind_turn", [(pair.shape, BF16), wide, out_rows, small(2)],
        [tri1, mid_t, normed1, outgate1, cot_t, d_outer1, d_unit1, mgain, mbias, out_w, outgate_w],
        [mid, flat, flat, flat, flat, sums(2)], 4 * dense,
    )
    (sent,) = call(
        functools.partial(edge_grad_kernel, True), "incoming_grad", [grid], [edge1, d_tri1],
        (), 2 * triangle,
    )
    d_edge1 = exchange(sent.reshape(edge[0]))
    proj_factor1, gate_factor1, scaled1, inverse1 = call(
        functools.partial(edge_factor_kernel, 1), "edge_factors_upper",
        [factor, factor, wide, row], [lengths, mid_t, normed1, proj_w, gate_w], [wts],
        4 * dense, 1,
    )
    sent, grad, d_in1, d_normed1, d_unit0 = call(
        middle_kernel, "middle", [tri, wide, d_in, wide, wide],
        [d_edge1, proj_factor1, gate_factor1, d_normed_gate1, scaled1, inverse1, cot_t, outgate0,
         scaled_mid0, inverse_mid0, ngain, mgain, proj_w, gate_w, out_w],
        [big, mid], 5 * dense, grant=24,
    )
    d_tri0 = exchange(sent).reshape(tri_grid[0])
    d_normed_gate0, out_grads0, in_grads1, small_middle = call(
        behind_middle_kernel, "behind_middle", [wide, out_rows, in_rows, small(4)],
        [grad, outgate0, scaled_mid0, d_unit0, normed0, d_in1, normed1, d_normed1, scaled1,
         mgain, mbias, out_w, outgate_w],
        [flat, flat, flat, flat, flat, flat_in, sums(4)], 8 * dense, grant=24,
    )
    (sent,) = call(
        functools.partial(edge_grad_kernel, False), "outgoing_grad", [grid], [edge0, d_tri0],
        (), 2 * triangle,
    )
    d_edge0 = exchange(sent.reshape(edge[0]))
    proj_factor0, gate_factor0, scaled0, inverse0 = call(
        functools.partial(edge_factor_kernel, 0), "edge_factors_lower",
        [factor, factor, wide, row], [lengths, pair_t, normed0, proj_w, gate_w], [wts],
        4 * dense, 1,
    )
    share = 12 * H // shards
    packed, d_in0 = call(
        finish_kernel, "finish", [((12 * H, H), BF16), d_in],
        [d_edge0, proj_factor0, gate_factor0, normed0, out_grads0, in_grads1, out_grads1],
        [big, flat, flat_in], 4 * dense,
    )
    parts = exchange(packed.reshape(shards, share, H))
    grad_pair, small0 = call(
        behind_finish_kernel, "behind_finish", [(pair.shape, BF16), small(2)],
        [d_in0, d_normed_gate0, grad, scaled0, inverse0, ngain, proj_w, gate_w], [sums(2)],
        4 * dense,
    )
    (shared,) = call(
        sum_kernel, "sum_weights", [((shards, share + 16, H), BF16)],
        [parts, small0, small_middle, small1],
    )
    shared = exchange(shared)
    grad_proj, grad_gate, grad_out, grad_outgate, small_all = call(
        functools.partial(unpack_kernel, share), "unpack",
        [(proj_w.shape, F32), (gate_w.shape, F32), (out_w.shape, F32), (outgate_w.shape, F32),
         small(8)],
        [shared],
    )
    small_all = small_all.reshape(2, 4, H)
    return (
        new_pair,
        grad_pair,
        small_all[:, 0],
        small_all[:, 1],
        grad_proj,
        grad_gate,
        small_all[:, 2],
        small_all[:, 3],
        grad_out,
        grad_outgate,
    )


def norm_channels(values):
    average = jnp.mean(values, -1, keepdims=True)
    centred = values - average
    variance = jnp.mean(centred * centred, -1, keepdims=True)
    inverse = lax.rsqrt(variance + EPS)
    return (centred * inverse, inverse)


def forward_module(pair_in, pair_mask, weights, incoming):
    gain_in, bias_in, proj_w, gate_w, gain_mid, bias_mid, out_w, outgate_w = weights
    scaled_in, inverse_in = norm_channels(pair_in.astype(jnp.float32))
    normed = (scaled_in * gain_in + bias_in).astype(jnp.bfloat16)
    projected = product("ijc,sch->shij", normed, proj_w)
    gating = jax.nn.sigmoid(product("ijc,sch->shij", normed, gate_w))
    hidden = (projected * gating * pair_mask).astype(jnp.bfloat16)
    left_side, right_side = (
        lax.all_to_all(hidden[0], "row", split_axis=0, concat_axis=1, tiled=True),
        lax.all_to_all(hidden[1], "row", split_axis=0, concat_axis=1, tiled=True),
    )
    if incoming:
        left_side = jnp.swapaxes(left_side, 1, 2)
        right_side = jnp.swapaxes(right_side, 1, 2)
    else:
        left_side, right_side = (
            lax.all_to_all(left_side, "col", split_axis=1, concat_axis=2, tiled=True),
            lax.all_to_all(right_side, "col", split_axis=1, concat_axis=2, tiled=True),
        )
    triangle = product(
        "cik,cjk->cij", left_side, lax.all_gather(right_side, "col", axis=1, tiled=True)
    ).astype(jnp.bfloat16)
    triangle = lax.all_to_all(
        lax.all_to_all(triangle, "col", split_axis=2, concat_axis=1, tiled=True),
        "row",
        split_axis=1,
        concat_axis=0,
        tiled=True,
    )
    tri_values = triangle.astype(jnp.float32)
    total, squares = lax.psum((jnp.sum(tri_values, 0), jnp.sum(tri_values * tri_values, 0)), "ch")
    average = total / H
    inverse_mid = lax.rsqrt(squares / H - average * average + EPS)
    scaled_mid = (tri_values - average) * inverse_mid
    unit = (scaled_mid * gain_mid[:, None, None] + bias_mid[:, None, None]).astype(jnp.bfloat16)
    unit_full = lax.all_gather(unit, "ch", axis=0, tiled=True)
    outer = product("hij,hc->ijc", unit_full, out_w)
    outgate = jax.nn.sigmoid(product("ijc,cd->ijd", normed, outgate_w))
    result = (pair_in.astype(jnp.float32) + outer * outgate).astype(jnp.bfloat16)
    saved = (
        scaled_in,
        inverse_in,
        normed,
        projected,
        gating,
        left_side,
        right_side,
        scaled_mid,
        inverse_mid,
        unit_full,
        outer,
        outgate,
    )
    return (result, saved)


def backward_module(grad_out, pair_mask, weights, saved, incoming):
    gain_in, bias_in, proj_w, gate_w, gain_mid, bias_mid, out_w, outgate_w = weights
    (
        scaled_in,
        inverse_in,
        normed,
        projected,
        gating,
        left_side,
        right_side,
        scaled_mid,
        inverse_mid,
        unit_full,
        outer,
        outgate,
    ) = saved
    d_outer = (grad_out * outgate).astype(jnp.bfloat16)
    d_gatepre = (grad_out * outer * outgate * (1.0 - outgate)).astype(jnp.bfloat16)
    grad_out_w = product("hij,ijc->hc", unit_full, d_outer)
    grad_outgate_w = product("ijc,ijd->cd", normed, d_gatepre)
    width = gain_mid.shape[0]
    own_rows = lax.dynamic_slice_in_dim(out_w, lax.axis_index("ch") * width, width, 0)
    d_unit = product("ijc,hc->hij", d_outer, own_rows)
    d_normed = product("ijd,cd->ijc", d_gatepre, outgate_w)
    weighted = d_unit * gain_mid[:, None, None]
    grad_gain_mid = jnp.sum(d_unit * scaled_mid, (1, 2))
    grad_bias_mid = jnp.sum(d_unit, (1, 2))
    first_sum, second_sum = lax.psum(
        (jnp.sum(weighted, 0), jnp.sum(weighted * scaled_mid, 0)), "ch"
    )
    d_tri = (inverse_mid * (weighted - first_sum / H - scaled_mid * (second_sum / H))).astype(
        jnp.bfloat16
    )
    grad_rows = lax.all_to_all(d_tri, "row", split_axis=0, concat_axis=1, tiled=True)
    grad_cols = lax.all_to_all(grad_rows, "col", split_axis=1, concat_axis=2, tiled=True)
    d_left = product(
        "cij,cjk->cik", grad_cols, lax.all_gather(right_side, "col", axis=1, tiled=True)
    )
    partial_terms = product("cij,cik->cjk", grad_cols, left_side)
    d_right = lax.psum_scatter(
        partial_terms.astype(jnp.bfloat16), "col", scatter_dimension=1, tiled=True
    ).astype(jnp.float32)
    d_left = d_left.astype(jnp.bfloat16)
    d_right = d_right.astype(jnp.bfloat16)
    if incoming:
        d_left = jnp.swapaxes(d_left, 1, 2)
        d_right = jnp.swapaxes(d_right, 1, 2)
    else:
        d_left, d_right = (
            lax.all_to_all(d_left, "col", split_axis=2, concat_axis=1, tiled=True),
            lax.all_to_all(d_right, "col", split_axis=2, concat_axis=1, tiled=True),
        )
    d_left, d_right = (
        lax.all_to_all(d_left, "row", split_axis=1, concat_axis=0, tiled=True),
        lax.all_to_all(d_right, "row", split_axis=1, concat_axis=0, tiled=True),
    )
    d_hidden = jnp.stack([d_left, d_right]).astype(jnp.float32)
    d_proj = (d_hidden * gating * pair_mask).astype(jnp.bfloat16)
    d_gate = (d_hidden * projected * gating * (1.0 - gating) * pair_mask).astype(jnp.bfloat16)
    grad_proj_w = product("ijc,shij->sch", normed, d_proj)
    grad_gate_w = product("ijc,shij->sch", normed, d_gate)
    partial_input = product("shij,sch->ijc", d_proj, proj_w) + product(
        "shij,sch->ijc", d_gate, gate_w
    )
    d_normed = d_normed + lax.psum(partial_input.astype(jnp.bfloat16), "ch").astype(jnp.float32)
    weighted_in = d_normed * gain_in
    grad_gain_in = jnp.sum(d_normed * scaled_in, (0, 1))
    grad_bias_in = jnp.sum(d_normed, (0, 1))
    d_pair = inverse_in * (
        weighted_in
        - jnp.mean(weighted_in, -1, keepdims=True)
        - scaled_in * jnp.mean(weighted_in * scaled_in, -1, keepdims=True)
    )
    grads = (
        grad_gain_in,
        grad_bias_in,
        grad_proj_w,
        grad_gate_w,
        grad_gain_mid,
        grad_bias_mid,
        grad_out_w,
        grad_outgate_w,
    )
    return (grad_out + d_pair, grads)


def per_device(
    pair,
    cotangent,
    lengths,
    norm_gain,
    norm_bias,
    proj_weight,
    gate_weight,
    mid_gain,
    mid_bias,
    out_weight,
    outgate_weight,
):
    rows_here = pair.shape[0]
    cols_here = pair.shape[1]
    row_ids = lax.axis_index("row") * rows_here + lax.iota(jnp.int32, rows_here)
    col_ids = lax.axis_index("col") * cols_here + lax.iota(jnp.int32, cols_here)
    limit = lengths[0]
    pair_mask = ((row_ids[:, None] < limit) & (col_ids[None, :] < limit)).astype(jnp.float32)
    state = pair
    stash = []
    for layer in range(2):
        weights = (
            norm_gain[layer],
            norm_bias[layer],
            proj_weight[layer],
            gate_weight[layer],
            mid_gain[layer],
            mid_bias[layer],
            out_weight[layer],
            outgate_weight[layer],
        )
        state, saved = forward_module(state, pair_mask, weights, layer == 1)
        stash.append(saved)
    grad_state = cotangent.astype(jnp.float32)
    per_layer = [None, None]
    for layer in (1, 0):
        weights = (
            norm_gain[layer],
            norm_bias[layer],
            proj_weight[layer],
            gate_weight[layer],
            mid_gain[layer],
            mid_bias[layer],
            out_weight[layer],
            outgate_weight[layer],
        )
        grad_state, grads = backward_module(
            grad_state, pair_mask, weights, stash[layer], layer == 1
        )
        per_layer[layer] = grads
    lower = per_layer[0]
    upper = per_layer[1]
    summed = lax.psum(
        (
            lower[0],
            lower[1],
            lower[2],
            lower[3],
            lower[4],
            lower[5],
            lower[6],
            lower[7],
            upper[0],
            upper[1],
            upper[2],
            upper[3],
            upper[4],
            upper[5],
            upper[6],
            upper[7],
        ),
        ("row", "col"),
    )
    per_layer = [summed[0:8], summed[8:16]]
    stacked = [jnp.stack([per_layer[0][index], per_layer[1][index]]) for index in range(8)]
    return (
        state,
        grad_state.astype(jnp.bfloat16),
        stacked[0],
        stacked[1],
        stacked[2],
        stacked[3],
        stacked[4],
        stacked[5],
        stacked[6],
        stacked[7],
    )


def solution(mesh):
    in_specs = (
        P(("grp", "row"), "col", None),
        P(("grp", "row"), "col", None),
        P("grp"),
        P(),
        P(),
        P(None, None, None, "ch"),
        P(None, None, None, "ch"),
        P(None, "ch"),
        P(None, "ch"),
        P(),
        P(),
    )
    out_specs = (
        P(("grp", "row"), "col", None),
        P(("grp", "row"), "col", None),
        P("grp", None),
        P("grp", None),
        P("grp", None, None, "ch"),
        P("grp", None, None, "ch"),
        P("grp", "ch"),
        P("grp", "ch"),
        P("grp", None, None),
        P("grp", None, None),
    )
    many, few = mesh.shape["row"], mesh.shape["col"]
    if mesh.shape["ch"] == 1 and H % (many * few) == 0:
        body = functools.partial(grouped_device, many=many, few=few)
    else:
        body = per_device
    return jax.shard_map(
        body, mesh=mesh, in_specs=in_specs, out_specs=out_specs, check_vma=False
    )
```

```python
import functools

import jax
import jax.numpy as jnp
from jax import lax
from jax.experimental import pallas as pl
from jax.experimental.pallas import tpu as pltpu
from jax.sharding import PartitionSpec as P

H = 128


EPS = 1e-05


def product(spec, left, right):
    return jnp.einsum(spec, left, right, preferred_element_type=jnp.float32)


F32 = jnp.float32
BF16 = jnp.bfloat16


def dot(left, right):
    return lax.dot_general(left, right, (((1,), (0,)), ((), ())), preferred_element_type=F32)


def dot_rt(left, right):
    return lax.dot_general(left, right, (((1,), (1,)), ((), ())), preferred_element_type=F32)


def dot_lt(left, right):
    return lax.dot_general(left, right, (((0,), (0,)), ((), ())), preferred_element_type=F32)


def sigmoid(values):
    return 1.0 / (1.0 + jnp.exp(-values))


def norm_rows(values):
    scale = 1.0 / values.shape[0]
    average = jnp.sum(values, 0, keepdims=True) * scale
    centred = values - average
    variance = jnp.sum(centred * centred, 0, keepdims=True) * scale
    inverse = lax.rsqrt(variance + EPS)
    return centred * inverse, inverse


def turned(weight):
    return jnp.transpose(weight.astype(F32)).astype(BF16)


def column(ref, module, lanes):
    row = ref[module : module + 1, :]
    return jnp.transpose(jnp.broadcast_to(row, (lanes, row.shape[1])))


def as_row(total):
    return jnp.sum(jnp.transpose(total), 0, keepdims=True)


def row_mask(lengths_ref, step, rows, lanes):
    limit = lengths_ref[0]
    row_id = lax.axis_index("row") * rows + step
    col_id = lax.axis_index("col") * lanes + lax.broadcasted_iota(jnp.int32, (1, lanes), 1)
    return jnp.where((row_id < limit) & (col_id < limit), 1.0, 0.0).astype(F32)


def load_in_weights(proj_ref, gate_ref, module, scratch):
    width = proj_ref.shape[-1]
    for side in range(2):
        scratch[side * width : (side + 1) * width, :] = turned(proj_ref[module, side])
        scratch[(2 + side) * width : (3 + side) * width, :] = turned(gate_ref[module, side])


def put_rows(scratch, values, step, rows):
    scratch[pl.ds(step, values.shape[0], stride=rows), :] = values


def get_rows(scratch, step, channels, rows):
    return scratch[pl.ds(step, channels, stride=rows), :]


def spread_edges(scratch, out_ref):
    shards, sides, group, rows, lanes = out_ref.shape
    block = shards * group * rows
    for side in range(sides):
        part = scratch[side * block : (side + 1) * block, :]
        out_ref[:, side] = part.reshape(shards, group, rows, lanes).astype(BF16)


def collect_edges(in_ref, scratch):
    shards, sides, group, rows, lanes = in_ref.shape
    block = shards * group * rows
    for side in range(sides):
        scratch[side * block : (side + 1) * block, :] = (
            in_ref[:, side].astype(F32).reshape(block, lanes)
        )


def collect_triangle(in_ref, scratch):
    block = in_ref.size // in_ref.shape[-1]
    scratch[0:block, :] = in_ref[...].astype(F32).reshape(block, in_ref.shape[-1])


def each_row(rows, unroll, body):
    def step_body(step, carry):
        body(step)
        return carry

    lax.fori_loop(0, rows, step_body, 0, unroll=unroll)


def mid_norm(tri):
    scale = 1.0 / tri.shape[0]
    average = jnp.sum(tri, 0, keepdims=True) * scale
    squares = jnp.sum(tri * tri, 0, keepdims=True) * scale
    inverse = lax.rsqrt(squares - average * average + EPS)
    return (tri - average) * inverse, inverse


def norm_backward(weighted, scaled, inverse):
    scale = 1.0 / weighted.shape[0]
    first = jnp.sum(weighted, 0, keepdims=True) * scale
    second = jnp.sum(weighted * scaled, 0, keepdims=True) * scale
    return inverse * (weighted - first - scaled * second)


def save_norm(step, values, scaled_out, inverse_out):
    scaled, inverse = norm_rows(values)
    scaled_out[step] = scaled
    inverse_out[pl.ds(step, 1), :] = inverse
    return scaled


def save_edges(step, normed, in_weights, mask, proj_out, gate_out):
    pre = dot(in_weights, normed)
    half = pre.shape[0] // 2
    gating = sigmoid(pre[half:])
    factor = gating * mask
    value = pre[:half] * factor
    proj_out[step] = factor
    gate_out[step] = value * (1.0 - gating)
    return value


def start_kernel(
    lengths, pair_far, ngain_far, nbias_far, proj_far, gate_far,
    edge_out, normed_out, proj_out, gate_out, scaled_out, inverse_out,
    pair, ngain, nbias, proj_w, gate_w, sems, wts, scr,
):
    far = (proj_far.at[0], gate_far.at[0], ngain_far, nbias_far, pair_far)
    near = (proj_w.at[0], gate_w.at[0], ngain, nbias, pair)
    copies = [
        pltpu.make_async_copy(source, target, sems.at[index])
        for index, (source, target) in enumerate(zip(far, near))
    ]
    for copy in copies:
        copy.start()
    for copy in copies:
        copy.wait()
    rows, lanes, channels = pair.shape
    load_in_weights(proj_w, gate_w, 0, wts)
    gain, bias = column(ngain, 0, lanes), column(nbias, 0, lanes)

    def body(step):
        base = jnp.transpose(pair[step].astype(F32))
        scaled = save_norm(step, base, scaled_out, inverse_out)
        normed = (scaled * gain + bias).astype(BF16)
        normed_out[step] = normed
        mask = row_mask(lengths, step, rows, lanes)
        put_rows(scr, save_edges(step, normed, wts[...], mask, proj_out, gate_out), step, rows)

    each_row(rows, 4, body)
    spread_edges(scr, edge_out)


def between_kernel(
    lengths, tri, pair, normed0, ngain, nbias, mgain, mbias, out_w, outgate_w, proj_w, gate_w,
    edge_out, mid_out, normed_out, proj_out, gate_out, scaled_out, inverse_out,
    outgate_out, scaled_mid_out, inverse_mid_out, wts, scr,
):
    rows, lanes, channels = pair.shape
    load_in_weights(proj_w, gate_w, 1, wts)
    out_t, outgate_t = turned(out_w[0]), turned(outgate_w[0])
    gain, bias = column(ngain, 1, lanes), column(nbias, 1, lanes)
    gain_mid, bias_mid = column(mgain, 0, lanes), column(mbias, 0, lanes)
    collect_triangle(tri, scr)

    def body(step):
        scaled_mid, inverse_mid = mid_norm(get_rows(scr, step, channels, rows))
        scaled_mid_out[step] = scaled_mid
        inverse_mid_out[pl.ds(step, 1), :] = inverse_mid
        unit = (scaled_mid * gain_mid + bias_mid).astype(BF16)
        outer = dot(out_t, unit)
        outgate = sigmoid(dot(outgate_t, normed0[step]))
        outgate_out[step] = outgate
        mid = (jnp.transpose(pair[step].astype(F32)) + outer * outgate).astype(BF16)
        mid_out[step] = mid
        scaled = save_norm(step, mid.astype(F32), scaled_out, inverse_out)
        normed = (scaled * gain + bias).astype(BF16)
        normed_out[step] = normed
        mask = row_mask(lengths, step, rows, lanes)
        put_rows(scr, save_edges(step, normed, wts[...], mask, proj_out, gate_out), step, rows)

    each_row(rows, 4, body)
    spread_edges(scr, edge_out)


def out_weight_grads(unit, d_outer, normed, d_gatepre, out_ref):
    width = unit.shape[0]
    out_ref[0:width, :] = dot_rt(unit[...], d_outer[...]).astype(out_ref.dtype)
    out_ref[width:, :] = dot_rt(normed[...], d_gatepre[...]).astype(out_ref.dtype)


def in_weight_grads(normed_all, d_in_all, out_ref):
    width = normed_all.shape[0]
    for part in range(d_in_all.shape[0] // width):
        block = slice(part * width, (part + 1) * width)
        out_ref[block, :] = dot_rt(normed_all[...], d_in_all[block, :]).astype(out_ref.dtype)


def lane_block(step, lanes):
    return pl.ds(pl.multiple_of(step * lanes, lanes), lanes)


def turn_kernel(
    tri, mid, normed, cot, mgain, mbias, out_w, outgate_w,
    d_tri_out, new_out, grad_out, d_normed_out, weights_out, small_out,
    scr, unit_all, outer_all, normed_all, gate_all, sums,
):
    rows, channels, lanes = mid.shape
    out_t, outgate_t = turned(out_w[1]), turned(outgate_w[1])
    gain_mid, bias_mid = column(mgain, 1, lanes), column(mbias, 1, lanes)
    collect_triangle(tri, scr)
    sums[...] = jnp.zeros_like(sums)

    def body(step):
        here = lane_block(step, lanes)
        grad = jnp.transpose(cot[step].astype(F32))
        grad_out[step] = grad
        outgate = sigmoid(dot(outgate_t, normed[step]))
        gated = grad * outgate
        d_outer = gated.astype(BF16)
        d_unit = dot(out_w[1], d_outer)
        scaled_mid, inverse_mid = mid_norm(get_rows(scr, step, channels, rows))
        put_rows(scr, norm_backward(d_unit * gain_mid, scaled_mid, inverse_mid), step, rows)
        unit = (scaled_mid * gain_mid + bias_mid).astype(BF16)
        outer = dot(out_t, unit)
        new_out[step] = jnp.transpose(mid[step].astype(F32) + outer * outgate).astype(BF16)
        d_gatepre = (gated * outer * (1.0 - outgate)).astype(BF16)
        d_normed_out[step] = dot(outgate_w[1], d_gatepre)
        unit_all[:, here] = unit
        outer_all[:, here] = d_outer
        normed_all[:, here] = normed[step]
        gate_all[:, here] = d_gatepre
        sums[0] += d_unit * scaled_mid
        sums[1] += d_unit

    each_row(rows, 4, body)
    d_tri_out[...] = scr[...].reshape(d_tri_out.shape).astype(BF16)
    out_weight_grads(unit_all, outer_all, normed_all, gate_all, weights_out)
    for index in range(2):
        small_out[index : index + 1, :] = as_row(sums[index])


def in_normed(d_in, all_w, proj_w, gate_w):
    width = proj_w.shape[-1]
    total = all_w
    for side in range(2):
        total = total + dot(proj_w[side], d_in[side * width : (side + 1) * width])
        total = total + dot(gate_w[side], d_in[(2 + side) * width : (3 + side) * width])
    return total


def middle_kernel(
    d_edge, proj_factor, gate_factor, d_normed_gate, scaled_in, inverse_in, cot, outgate,
    scaled_mid, inverse_mid, normed0, normed1, ngain, mgain, mbias, proj_w, gate_w, out_w,
    outgate_w,
    d_tri_out, grad_out, d_normed_out, out_weights, in_weights, small_out,
    scr, scr_tri, unit_all, outer_all, normed_all, gate_all, upper_all, d_in_all, sums,
):
    rows, channels, lanes = cot.shape
    out_t = turned(out_w[0])
    gain = column(ngain, 1, lanes)
    gain_mid, bias_mid = column(mgain, 0, lanes), column(mbias, 0, lanes)
    collect_edges(d_edge, scr)
    sums[...] = jnp.zeros_like(sums)
    half = proj_factor.shape[1]

    def body(step):
        place = lane_block(step, lanes)
        here = get_rows(scr, step, half, rows)
        d_proj = (here * proj_factor[step]).astype(BF16)
        d_gate = (here * gate_factor[step]).astype(BF16)
        d_in = jnp.concatenate([d_proj, d_gate], axis=0)
        d_in_all[:, place] = d_in
        upper_all[:, place] = normed1[step]
        d_normed = in_normed(d_in, d_normed_gate[step], proj_w[1], gate_w[1])
        scaled = scaled_in[step]
        sums[2] += d_normed * scaled
        sums[3] += d_normed
        grad = cot[step] + norm_backward(d_normed * gain, scaled, inverse_in[pl.ds(step, 1), :])
        grad_out[step] = grad
        gate = outgate[step]
        gated = grad * gate
        d_outer = gated.astype(BF16)
        d_unit = dot(out_w[0], d_outer)
        scaled = scaled_mid[step]
        d_tri = norm_backward(d_unit * gain_mid, scaled, inverse_mid[pl.ds(step, 1), :])
        put_rows(scr_tri, d_tri, step, rows)
        unit = (scaled * gain_mid + bias_mid).astype(BF16)
        outer = dot(out_t, unit)
        d_gatepre = (gated * outer * (1.0 - gate)).astype(BF16)
        d_normed_out[step] = dot(outgate_w[0], d_gatepre)
        unit_all[:, place] = unit
        outer_all[:, place] = d_outer
        normed_all[:, place] = normed0[step]
        gate_all[:, place] = d_gatepre
        sums[0] += d_unit * scaled
        sums[1] += d_unit

    each_row(rows, 4, body)
    d_tri_out[...] = scr_tri[...].reshape(d_tri_out.shape).astype(BF16)
    out_weight_grads(unit_all, outer_all, normed_all, gate_all, out_weights)
    in_weight_grads(upper_all, d_in_all, in_weights)
    for index in range(4):
        small_out[index : index + 1, :] = as_row(sums[index])


def finish_kernel(
    d_edge, proj_factor, gate_factor, d_normed_gate, scaled_in, inverse_in, grad, normed,
    ngain, proj_w, gate_w, out0, in1, out1,
    packed_out, grad_out, small_out, scr, normed_all, d_in_all, sums,
):
    rows, half, lanes = proj_factor.shape
    gain = column(ngain, 0, lanes)
    collect_edges(d_edge, scr)
    sums[...] = jnp.zeros_like(sums)

    def body(step):
        place = lane_block(step, lanes)
        here = get_rows(scr, step, half, rows)
        d_proj = (here * proj_factor[step]).astype(BF16)
        d_gate = (here * gate_factor[step]).astype(BF16)
        d_in = jnp.concatenate([d_proj, d_gate], axis=0)
        d_in_all[:, place] = d_in
        normed_all[:, place] = normed[step]
        d_normed = in_normed(d_in, d_normed_gate[step], proj_w[0], gate_w[0])
        scaled = scaled_in[step]
        sums[0] += d_normed * scaled
        sums[1] += d_normed
        total = grad[step] + norm_backward(d_normed * gain, scaled, inverse_in[pl.ds(step, 1), :])
        grad_out[step] = jnp.transpose(total).astype(BF16)

    each_row(rows, 4, body)
    first, second, third = d_in_all.shape[0], out0.shape[0], in1.shape[0]
    in_weight_grads(normed_all, d_in_all, packed_out.at[0:first])
    packed_out[first : first + second, :] = out0[...]
    packed_out[first + second : first + second + third, :] = in1[...]
    packed_out[first + second + third :, :] = out1[...]
    for index in range(2):
        small_out[index : index + 1, :] = as_row(sums[index])


def sum_kernel(parts, small0, small_middle, small1, shared_out):
    shards, share, width = parts.shape
    own = jnp.sum(parts[...].astype(F32), axis=0).astype(BF16)
    small = jnp.concatenate(
        [small0[...], small_middle[0:2], small_middle[2:4], small1[...]], axis=0
    )
    high = small.astype(BF16).astype(F32)
    extra = jnp.concatenate([high, small - high], axis=0).astype(BF16)
    for shard in range(shards):
        shared_out[shard, 0:share] = own
        shared_out[shard, share:] = extra


def unpack_kernel(share, shared, proj_out, gate_out, out_out, outgate_out, small_out):
    shards, _, width = shared.shape
    total = jnp.sum(shared[:, share:, :].astype(F32), axis=0)
    small_out[...] = total[0:8] + total[8:16]
    weights = shared[:, 0:share, :].reshape(shards * share, width).astype(F32)
    for module in range(2):
        blocks = [
            weights[(6 * module + part) * width : (6 * module + part + 1) * width]
            for part in range(6)
        ]
        for side in range(2):
            proj_out[module, side] = blocks[side]
            gate_out[module, side] = blocks[2 + side]
        out_out[module] = blocks[4]
        outgate_out[module] = blocks[5]


def triangle_kernel(incoming, edge, tri_out):
    many, few, _, group, rows, lanes = edge.shape

    def whole(side, channel):
        parts = [edge[:, c, side, channel].reshape(many * rows, lanes) for c in range(few)]
        return jnp.concatenate(parts, axis=1)

    for channel in range(group):
        left, right = whole(0, channel), whole(1, channel)
        tri = (dot_lt if incoming else dot_rt)(left, right).astype(BF16)
        for c in range(few):
            part = tri[:, c * lanes : (c + 1) * lanes]
            tri_out[:, c, channel] = part.reshape(many, rows, lanes)


def edge_grad_kernel(incoming, edge, d_tri, grad_out):
    many, few, _, group, rows, lanes = edge.shape

    def whole(ref, *index):
        parts = [ref[(slice(None), c) + index].reshape(many * rows, lanes) for c in range(few)]
        return jnp.concatenate(parts, axis=1)

    for channel in range(group):
        left, right = whole(edge, 0, channel), whole(edge, 1, channel)
        grad = whole(d_tri, channel)
        if incoming:
            d_left, d_right = dot_rt(right, grad), dot(left, grad)
        else:
            d_left, d_right = dot(grad, right), dot_lt(grad, left)
        for side, value in ((0, d_left), (1, d_right)):
            value = value.astype(BF16)
            for c in range(few):
                part = value[:, c * lanes : (c + 1) * lanes]
                grad_out[:, c, side, channel] = part.reshape(many, rows, lanes)


SCALARS = pl.BlockSpec(memory_space=pltpu.SMEM)
VECTORS = pl.BlockSpec(memory_space=pltpu.VMEM)
FAR = pl.BlockSpec(memory_space=pltpu.HBM)


def call(kernel, name, outs, args, scratch=(), flops=0, scalars=0, grant=16, far=False):
    shapes = [jax.ShapeDtypeStruct(shape, dtype) for shape, dtype in outs]
    moved = sum(a.size * a.dtype.itemsize for a in list(args) + shapes)
    rest = FAR if far else VECTORS
    return pl.pallas_call(
        kernel,
        name=name,
        out_shape=shapes,
        in_specs=[SCALARS] * scalars + [rest] * (len(args) - scalars),
        out_specs=[VECTORS] * len(shapes),
        scratch_shapes=[
            pltpu.VMEM(*item) if isinstance(item, tuple) else item for item in scratch
        ],
        compiler_params=pltpu.CompilerParams(vmem_limit_bytes=grant * 1024 * 1024),
        cost_estimate=pl.CostEstimate(flops=flops, bytes_accessed=moved, transcendentals=0),
    )(*args)


def exchange(values):
    return lax.all_to_all(values, ("row", "col"), split_axis=0, concat_axis=0, tiled=True)


def grouped_device(
    pair, cotangent, lengths, ngain, nbias, proj_w, gate_w, mgain, mbias, out_w, outgate_w,
    *, many, few,
):
    rows, lanes, channels = pair.shape
    shards = many * few
    group = H // shards
    edge = ((shards, 2, group, rows, lanes), BF16)
    grid = ((many, few, 2, group, rows, lanes), BF16)
    tri = ((shards, group, rows, lanes), BF16)
    tri_grid = ((many, few, group, rows, lanes), BF16)
    tile = ((rows, channels, lanes), BF16)
    wide = ((rows, channels, lanes), F32)
    row = ((rows, lanes), F32)
    factor = ((rows, 2 * H, lanes), F32)
    d_in = ((rows, 4 * H, lanes), BF16)
    wts = ((4 * H, channels), BF16)
    big = ((2 * H * rows, lanes), F32)
    mid = ((H * rows, lanes), F32)
    positions = rows * lanes
    flat = ((H, positions), BF16)
    flat_in = ((4 * H, positions), BF16)
    out_rows = ((2 * H, channels), BF16)
    in_rows = ((4 * H, H), BF16)
    triangle = 2 * group * (many * rows) ** 2 * (few * lanes)
    dense = 2 * positions * channels * H

    def sums(count):
        return ((count, H, lanes), F32)

    def small(count):
        return ((count, H), F32)

    saved = [tile, factor, factor, wide, row]
    sent, normed0, *factors0 = call(
        start_kernel, "start", [edge, *saved], [lengths, pair, ngain, nbias, proj_w, gate_w],
        [(pair.shape, BF16), (ngain.shape, F32), (nbias.shape, F32), (proj_w.shape, BF16),
         (gate_w.shape, BF16), pltpu.SemaphoreType.DMA((5,)), wts, big],
        4 * dense, 1, far=True,
    )
    edge0 = exchange(sent).reshape(grid[0])
    (here,) = call(
        functools.partial(triangle_kernel, False), "outgoing", [tri_grid], [edge0], (), triangle,
    )
    tri0 = exchange(here.reshape(tri[0]))
    sent, mid_t, normed1, *factors1, outgate0, scaled_mid0, inverse_mid0 = call(
        between_kernel, "between", [edge, tile, *saved, wide, wide, row],
        [lengths, tri0, pair, normed0, ngain, nbias, mgain, mbias, out_w, outgate_w, proj_w,
         gate_w],
        [wts, big], 6 * dense, 1,
    )
    edge1 = exchange(sent).reshape(grid[0])
    (here,) = call(
        functools.partial(triangle_kernel, True), "incoming", [tri_grid], [edge1], (), triangle,
    )
    tri1 = exchange(here.reshape(tri[0]))
    sent, new_pair, cot_t, d_normed_gate1, out_grads1, small1 = call(
        turn_kernel, "turn", [tri, (pair.shape, BF16), wide, wide, out_rows, small(2)],
        [tri1, mid_t, normed1, cotangent, mgain, mbias, out_w, outgate_w],
        [mid, flat, flat, flat, flat, sums(2)], 6 * dense,
    )
    d_tri1 = exchange(sent).reshape(tri_grid[0])
    (sent,) = call(
        functools.partial(edge_grad_kernel, True), "incoming_grad", [grid], [edge1, d_tri1],
        (), 2 * triangle,
    )
    d_edge1 = exchange(sent.reshape(edge[0]))
    proj_factor1, gate_factor1, scaled1, inverse1 = factors1
    sent, grad, d_normed_gate0, out_grads0, in_grads1, small_middle = call(
        middle_kernel, "middle", [tri, wide, wide, out_rows, in_rows, small(4)],
        [d_edge1, proj_factor1, gate_factor1, d_normed_gate1, scaled1, inverse1, cot_t, outgate0,
         scaled_mid0, inverse_mid0, normed0, normed1, ngain, mgain, mbias, proj_w, gate_w, out_w,
         outgate_w],
        [big, mid, flat, flat, flat, flat, flat, flat_in, sums(4)], 13 * dense,
    )
    d_tri0 = exchange(sent).reshape(tri_grid[0])
    (sent,) = call(
        functools.partial(edge_grad_kernel, False), "outgoing_grad", [grid], [edge0, d_tri0],
        (), 2 * triangle,
    )
    d_edge0 = exchange(sent.reshape(edge[0]))
    share = 12 * H // shards
    proj_factor0, gate_factor0, scaled0, inverse0 = factors0
    packed, grad_pair, small0 = call(
        finish_kernel, "finish", [((12 * H, H), BF16), (pair.shape, BF16), small(2)],
        [d_edge0, proj_factor0, gate_factor0, d_normed_gate0, scaled0, inverse0, grad, normed0,
         ngain, proj_w, gate_w, out_grads0, in_grads1, out_grads1],
        [big, flat, flat_in, sums(2)], 8 * dense,
    )
    parts = exchange(packed.reshape(shards, share, H))
    (shared,) = call(
        sum_kernel, "sum_weights", [((shards, share + 16, H), BF16)],
        [parts, small0, small_middle, small1],
    )
    shared = exchange(shared)
    grad_proj, grad_gate, grad_out, grad_outgate, small_all = call(
        functools.partial(unpack_kernel, share), "unpack",
        [(proj_w.shape, F32), (gate_w.shape, F32), (out_w.shape, F32), (outgate_w.shape, F32),
         small(8)],
        [shared],
    )
    small_all = small_all.reshape(2, 4, H)
    return (
        new_pair,
        grad_pair,
        small_all[:, 0],
        small_all[:, 1],
        grad_proj,
        grad_gate,
        small_all[:, 2],
        small_all[:, 3],
        grad_out,
        grad_outgate,
    )


def norm_channels(values):
    average = jnp.mean(values, -1, keepdims=True)
    centred = values - average
    variance = jnp.mean(centred * centred, -1, keepdims=True)
    inverse = lax.rsqrt(variance + EPS)
    return (centred * inverse, inverse)


def forward_module(pair_in, pair_mask, weights, incoming):
    gain_in, bias_in, proj_w, gate_w, gain_mid, bias_mid, out_w, outgate_w = weights
    scaled_in, inverse_in = norm_channels(pair_in.astype(jnp.float32))
    normed = (scaled_in * gain_in + bias_in).astype(jnp.bfloat16)
    projected = product("ijc,sch->shij", normed, proj_w)
    gating = jax.nn.sigmoid(product("ijc,sch->shij", normed, gate_w))
    hidden = (projected * gating * pair_mask).astype(jnp.bfloat16)
    left_side, right_side = (
        lax.all_to_all(hidden[0], "row", split_axis=0, concat_axis=1, tiled=True),
        lax.all_to_all(hidden[1], "row", split_axis=0, concat_axis=1, tiled=True),
    )
    if incoming:
        left_side = jnp.swapaxes(left_side, 1, 2)
        right_side = jnp.swapaxes(right_side, 1, 2)
    else:
        left_side, right_side = (
            lax.all_to_all(left_side, "col", split_axis=1, concat_axis=2, tiled=True),
            lax.all_to_all(right_side, "col", split_axis=1, concat_axis=2, tiled=True),
        )
    triangle = product(
        "cik,cjk->cij", left_side, lax.all_gather(right_side, "col", axis=1, tiled=True)
    ).astype(jnp.bfloat16)
    triangle = lax.all_to_all(
        lax.all_to_all(triangle, "col", split_axis=2, concat_axis=1, tiled=True),
        "row",
        split_axis=1,
        concat_axis=0,
        tiled=True,
    )
    tri_values = triangle.astype(jnp.float32)
    total, squares = lax.psum((jnp.sum(tri_values, 0), jnp.sum(tri_values * tri_values, 0)), "ch")
    average = total / H
    inverse_mid = lax.rsqrt(squares / H - average * average + EPS)
    scaled_mid = (tri_values - average) * inverse_mid
    unit = (scaled_mid * gain_mid[:, None, None] + bias_mid[:, None, None]).astype(jnp.bfloat16)
    unit_full = lax.all_gather(unit, "ch", axis=0, tiled=True)
    outer = product("hij,hc->ijc", unit_full, out_w)
    outgate = jax.nn.sigmoid(product("ijc,cd->ijd", normed, outgate_w))
    result = (pair_in.astype(jnp.float32) + outer * outgate).astype(jnp.bfloat16)
    saved = (
        scaled_in,
        inverse_in,
        normed,
        projected,
        gating,
        left_side,
        right_side,
        scaled_mid,
        inverse_mid,
        unit_full,
        outer,
        outgate,
    )
    return (result, saved)


def backward_module(grad_out, pair_mask, weights, saved, incoming):
    gain_in, bias_in, proj_w, gate_w, gain_mid, bias_mid, out_w, outgate_w = weights
    (
        scaled_in,
        inverse_in,
        normed,
        projected,
        gating,
        left_side,
        right_side,
        scaled_mid,
        inverse_mid,
        unit_full,
        outer,
        outgate,
    ) = saved
    d_outer = (grad_out * outgate).astype(jnp.bfloat16)
    d_gatepre = (grad_out * outer * outgate * (1.0 - outgate)).astype(jnp.bfloat16)
    grad_out_w = product("hij,ijc->hc", unit_full, d_outer)
    grad_outgate_w = product("ijc,ijd->cd", normed, d_gatepre)
    width = gain_mid.shape[0]
    own_rows = lax.dynamic_slice_in_dim(out_w, lax.axis_index("ch") * width, width, 0)
    d_unit = product("ijc,hc->hij", d_outer, own_rows)
    d_normed = product("ijd,cd->ijc", d_gatepre, outgate_w)
    weighted = d_unit * gain_mid[:, None, None]
    grad_gain_mid = jnp.sum(d_unit * scaled_mid, (1, 2))
    grad_bias_mid = jnp.sum(d_unit, (1, 2))
    first_sum, second_sum = lax.psum(
        (jnp.sum(weighted, 0), jnp.sum(weighted * scaled_mid, 0)), "ch"
    )
    d_tri = (inverse_mid * (weighted - first_sum / H - scaled_mid * (second_sum / H))).astype(
        jnp.bfloat16
    )
    grad_rows = lax.all_to_all(d_tri, "row", split_axis=0, concat_axis=1, tiled=True)
    grad_cols = lax.all_to_all(grad_rows, "col", split_axis=1, concat_axis=2, tiled=True)
    d_left = product(
        "cij,cjk->cik", grad_cols, lax.all_gather(right_side, "col", axis=1, tiled=True)
    )
    partial_terms = product("cij,cik->cjk", grad_cols, left_side)
    d_right = lax.psum_scatter(
        partial_terms.astype(jnp.bfloat16), "col", scatter_dimension=1, tiled=True
    ).astype(jnp.float32)
    d_left = d_left.astype(jnp.bfloat16)
    d_right = d_right.astype(jnp.bfloat16)
    if incoming:
        d_left = jnp.swapaxes(d_left, 1, 2)
        d_right = jnp.swapaxes(d_right, 1, 2)
    else:
        d_left, d_right = (
            lax.all_to_all(d_left, "col", split_axis=2, concat_axis=1, tiled=True),
            lax.all_to_all(d_right, "col", split_axis=2, concat_axis=1, tiled=True),
        )
    d_left, d_right = (
        lax.all_to_all(d_left, "row", split_axis=1, concat_axis=0, tiled=True),
        lax.all_to_all(d_right, "row", split_axis=1, concat_axis=0, tiled=True),
    )
    d_hidden = jnp.stack([d_left, d_right]).astype(jnp.float32)
    d_proj = (d_hidden * gating * pair_mask).astype(jnp.bfloat16)
    d_gate = (d_hidden * projected * gating * (1.0 - gating) * pair_mask).astype(jnp.bfloat16)
    grad_proj_w = product("ijc,shij->sch", normed, d_proj)
    grad_gate_w = product("ijc,shij->sch", normed, d_gate)
    partial_input = product("shij,sch->ijc", d_proj, proj_w) + product(
        "shij,sch->ijc", d_gate, gate_w
    )
    d_normed = d_normed + lax.psum(partial_input.astype(jnp.bfloat16), "ch").astype(jnp.float32)
    weighted_in = d_normed * gain_in
    grad_gain_in = jnp.sum(d_normed * scaled_in, (0, 1))
    grad_bias_in = jnp.sum(d_normed, (0, 1))
    d_pair = inverse_in * (
        weighted_in
        - jnp.mean(weighted_in, -1, keepdims=True)
        - scaled_in * jnp.mean(weighted_in * scaled_in, -1, keepdims=True)
    )
    grads = (
        grad_gain_in,
        grad_bias_in,
        grad_proj_w,
        grad_gate_w,
        grad_gain_mid,
        grad_bias_mid,
        grad_out_w,
        grad_outgate_w,
    )
    return (grad_out + d_pair, grads)


def per_device(
    pair,
    cotangent,
    lengths,
    norm_gain,
    norm_bias,
    proj_weight,
    gate_weight,
    mid_gain,
    mid_bias,
    out_weight,
    outgate_weight,
):
    rows_here = pair.shape[0]
    cols_here = pair.shape[1]
    row_ids = lax.axis_index("row") * rows_here + lax.iota(jnp.int32, rows_here)
    col_ids = lax.axis_index("col") * cols_here + lax.iota(jnp.int32, cols_here)
    limit = lengths[0]
    pair_mask = ((row_ids[:, None] < limit) & (col_ids[None, :] < limit)).astype(jnp.float32)
    state = pair
    stash = []
    for layer in range(2):
        weights = (
            norm_gain[layer],
            norm_bias[layer],
            proj_weight[layer],
            gate_weight[layer],
            mid_gain[layer],
            mid_bias[layer],
            out_weight[layer],
            outgate_weight[layer],
        )
        state, saved = forward_module(state, pair_mask, weights, layer == 1)
        stash.append(saved)
    grad_state = cotangent.astype(jnp.float32)
    per_layer = [None, None]
    for layer in (1, 0):
        weights = (
            norm_gain[layer],
            norm_bias[layer],
            proj_weight[layer],
            gate_weight[layer],
            mid_gain[layer],
            mid_bias[layer],
            out_weight[layer],
            outgate_weight[layer],
        )
        grad_state, grads = backward_module(
            grad_state, pair_mask, weights, stash[layer], layer == 1
        )
        per_layer[layer] = grads
    lower = per_layer[0]
    upper = per_layer[1]
    summed = lax.psum(
        (
            lower[0],
            lower[1],
            lower[2],
            lower[3],
            lower[4],
            lower[5],
            lower[6],
            lower[7],
            upper[0],
            upper[1],
            upper[2],
            upper[3],
            upper[4],
            upper[5],
            upper[6],
            upper[7],
        ),
        ("row", "col"),
    )
    per_layer = [summed[0:8], summed[8:16]]
    stacked = [jnp.stack([per_layer[0][index], per_layer[1][index]]) for index in range(8)]
    return (
        state,
        grad_state.astype(jnp.bfloat16),
        stacked[0],
        stacked[1],
        stacked[2],
        stacked[3],
        stacked[4],
        stacked[5],
        stacked[6],
        stacked[7],
    )


def solution(mesh):
    in_specs = (
        P(("grp", "row"), "col", None),
        P(("grp", "row"), "col", None),
        P("grp"),
        P(),
        P(),
        P(None, None, None, "ch"),
        P(None, None, None, "ch"),
        P(None, "ch"),
        P(None, "ch"),
        P(),
        P(),
    )
    out_specs = (
        P(("grp", "row"), "col", None),
        P(("grp", "row"), "col", None),
        P("grp", None),
        P("grp", None),
        P("grp", None, None, "ch"),
        P("grp", None, None, "ch"),
        P("grp", "ch"),
        P("grp", "ch"),
        P("grp", None, None),
        P("grp", None, None),
    )
    many, few = mesh.shape["row"], mesh.shape["col"]
    if mesh.shape["ch"] == 1 and H % (many * few) == 0:
        body = functools.partial(grouped_device, many=many, few=few)
    else:
        body = per_device
    return jax.shard_map(
        body, mesh=mesh, in_specs=in_specs, out_specs=out_specs, check_vma=False
    )
```

```python
import functools

import jax
import jax.numpy as jnp
from jax import lax
from jax.experimental import pallas as pl
from jax.experimental.pallas import tpu as pltpu
from jax.sharding import PartitionSpec as P

H = 128


EPS = 1e-05


def product(spec, left, right):
    return jnp.einsum(spec, left, right, preferred_element_type=jnp.float32)


F32 = jnp.float32
BF16 = jnp.bfloat16


def dot(left, right):
    return lax.dot_general(left, right, (((1,), (0,)), ((), ())), preferred_element_type=F32)


def dot_rt(left, right):
    return lax.dot_general(left, right, (((1,), (1,)), ((), ())), preferred_element_type=F32)


def dot_lt(left, right):
    return lax.dot_general(left, right, (((0,), (0,)), ((), ())), preferred_element_type=F32)


def sigmoid(values):
    return 1.0 / (1.0 + jnp.exp(-values))


def norm_rows(values):
    scale = 1.0 / values.shape[0]
    average = jnp.sum(values, 0, keepdims=True) * scale
    centred = values - average
    variance = jnp.sum(centred * centred, 0, keepdims=True) * scale
    inverse = lax.rsqrt(variance + EPS)
    return centred * inverse, inverse


def turned(weight):
    return jnp.transpose(weight.astype(F32)).astype(BF16)


def column(ref, module, lanes):
    row = ref[module : module + 1, :]
    return jnp.transpose(jnp.broadcast_to(row, (lanes, row.shape[1])))


def as_row(total):
    return jnp.sum(jnp.transpose(total), 0, keepdims=True)


def row_mask(lengths_ref, step, rows, lanes):
    limit = lengths_ref[0]
    row_id = lax.axis_index("row") * rows + step
    col_id = lax.axis_index("col") * lanes + lax.broadcasted_iota(jnp.int32, (1, lanes), 1)
    return jnp.where((row_id < limit) & (col_id < limit), 1.0, 0.0).astype(F32)


def load_in_weights(proj_ref, gate_ref, module, scratch):
    width = proj_ref.shape[-1]
    for side in range(2):
        scratch[side * width : (side + 1) * width, :] = turned(proj_ref[module, side])
        scratch[(2 + side) * width : (3 + side) * width, :] = turned(gate_ref[module, side])


def put_rows(scratch, values, step, rows):
    scratch[pl.ds(step, values.shape[0], stride=rows), :] = values


def get_rows(scratch, step, channels, rows):
    return scratch[pl.ds(step, channels, stride=rows), :]


def spread_edges(scratch, out_ref):
    shards, sides, group, rows, lanes = out_ref.shape
    block = shards * group * rows
    for side in range(sides):
        part = scratch[side * block : (side + 1) * block, :]
        out_ref[:, side] = part.reshape(shards, group, rows, lanes).astype(BF16)


def collect_edges(in_ref, scratch):
    shards, sides, group, rows, lanes = in_ref.shape
    block = shards * group * rows
    for side in range(sides):
        scratch[side * block : (side + 1) * block, :] = (
            in_ref[:, side].astype(F32).reshape(block, lanes)
        )


def collect_triangle(in_ref, scratch):
    block = in_ref.size // in_ref.shape[-1]
    scratch[0:block, :] = in_ref[...].astype(F32).reshape(block, in_ref.shape[-1])


def each_row(rows, unroll, body):
    def step_body(step, carry):
        body(step)
        return carry

    lax.fori_loop(0, rows, step_body, 0, unroll=unroll)


def mid_norm(tri):
    scale = 1.0 / tri.shape[0]
    average = jnp.sum(tri, 0, keepdims=True) * scale
    squares = jnp.sum(tri * tri, 0, keepdims=True) * scale
    inverse = lax.rsqrt(squares - average * average + EPS)
    return (tri - average) * inverse, inverse


def norm_backward(weighted, scaled, inverse):
    scale = 1.0 / weighted.shape[0]
    first = jnp.sum(weighted, 0, keepdims=True) * scale
    second = jnp.sum(weighted * scaled, 0, keepdims=True) * scale
    return inverse * (weighted - first - scaled * second)


def save_norm(step, values, scaled_out, inverse_out):
    scaled, inverse = norm_rows(values)
    scaled_out[step] = scaled
    inverse_out[pl.ds(step, 1), :] = inverse
    return scaled


def save_edges(step, normed, in_weights, mask, proj_out, gate_out):
    pre = dot(in_weights, normed)
    half = pre.shape[0] // 2
    gating = sigmoid(pre[half:])
    factor = gating * mask
    value = pre[:half] * factor
    proj_out[step] = factor
    gate_out[step] = value * (1.0 - gating)
    return value


def start_kernel(
    lengths, pair_far, ngain_far, nbias_far, proj_far, gate_far,
    edge_out, normed_out, proj_out, gate_out, scaled_out, inverse_out,
    pair, ngain, nbias, proj_w, gate_w, sems, wts, scr,
):
    far = (proj_far.at[0], gate_far.at[0], ngain_far, nbias_far, pair_far)
    near = (proj_w.at[0], gate_w.at[0], ngain, nbias, pair)
    copies = [
        pltpu.make_async_copy(source, target, sems.at[index])
        for index, (source, target) in enumerate(zip(far, near))
    ]
    for copy in copies:
        copy.start()
    for copy in copies:
        copy.wait()
    rows, lanes, channels = pair.shape
    load_in_weights(proj_w, gate_w, 0, wts)
    gain, bias = column(ngain, 0, lanes), column(nbias, 0, lanes)

    def body(step):
        base = jnp.transpose(pair[step].astype(F32))
        scaled = save_norm(step, base, scaled_out, inverse_out)
        normed = (scaled * gain + bias).astype(BF16)
        normed_out[step] = normed
        mask = row_mask(lengths, step, rows, lanes)
        put_rows(scr, save_edges(step, normed, wts[...], mask, proj_out, gate_out), step, rows)

    each_row(rows, 4, body)
    spread_edges(scr, edge_out)


def between_kernel(
    lengths, tri, pair, normed0, ngain, nbias, mgain, mbias, out_w, outgate_w, proj_w, gate_w,
    edge_out, mid_out, normed_out, proj_out, gate_out, scaled_out, inverse_out,
    outgate_out, scaled_mid_out, inverse_mid_out, wts, scr,
):
    rows, lanes, channels = pair.shape
    load_in_weights(proj_w, gate_w, 1, wts)
    out_t, outgate_t = turned(out_w[0]), turned(outgate_w[0])
    gain, bias = column(ngain, 1, lanes), column(nbias, 1, lanes)
    gain_mid, bias_mid = column(mgain, 0, lanes), column(mbias, 0, lanes)
    collect_triangle(tri, scr)

    def body(step):
        scaled_mid, inverse_mid = mid_norm(get_rows(scr, step, channels, rows))
        scaled_mid_out[step] = scaled_mid
        inverse_mid_out[pl.ds(step, 1), :] = inverse_mid
        unit = (scaled_mid * gain_mid + bias_mid).astype(BF16)
        outer = dot(out_t, unit)
        outgate = sigmoid(dot(outgate_t, normed0[step]))
        outgate_out[step] = outgate
        mid = (jnp.transpose(pair[step].astype(F32)) + outer * outgate).astype(BF16)
        mid_out[step] = mid
        scaled = save_norm(step, mid.astype(F32), scaled_out, inverse_out)
        normed = (scaled * gain + bias).astype(BF16)
        normed_out[step] = normed
        mask = row_mask(lengths, step, rows, lanes)
        put_rows(scr, save_edges(step, normed, wts[...], mask, proj_out, gate_out), step, rows)

    each_row(rows, 4, body)
    spread_edges(scr, edge_out)


def out_weight_grads(unit, d_outer, normed, d_gatepre, out_ref):
    width = unit.shape[0]
    out_ref[0:width, :] = dot_rt(unit[...], d_outer[...]).astype(out_ref.dtype)
    out_ref[width:, :] = dot_rt(normed[...], d_gatepre[...]).astype(out_ref.dtype)


def in_weight_grads(normed_all, d_in_all, out_ref):
    width = normed_all.shape[0]
    for part in range(d_in_all.shape[0] // width):
        block = slice(part * width, (part + 1) * width)
        out_ref[block, :] = dot_rt(normed_all[...], d_in_all[block, :]).astype(out_ref.dtype)


def lane_block(step, lanes):
    return pl.ds(pl.multiple_of(step * lanes, lanes), lanes)


def turn_kernel(
    tri, mid, normed, cot, mgain, mbias, out_w, outgate_w,
    d_tri_out, new_out, grad_out, d_normed_out, weights_out, small_out,
    scr, unit_all, outer_all, normed_all, gate_all, sums,
):
    rows, channels, lanes = mid.shape
    out_t, outgate_t = turned(out_w[1]), turned(outgate_w[1])
    gain_mid, bias_mid = column(mgain, 1, lanes), column(mbias, 1, lanes)
    collect_triangle(tri, scr)
    sums[...] = jnp.zeros_like(sums)

    def body(step):
        here = lane_block(step, lanes)
        grad = jnp.transpose(cot[step].astype(F32))
        grad_out[step] = grad
        outgate = sigmoid(dot(outgate_t, normed[step]))
        gated = grad * outgate
        d_outer = gated.astype(BF16)
        d_unit = dot(out_w[1], d_outer)
        scaled_mid, inverse_mid = mid_norm(get_rows(scr, step, channels, rows))
        put_rows(scr, norm_backward(d_unit * gain_mid, scaled_mid, inverse_mid), step, rows)
        unit = (scaled_mid * gain_mid + bias_mid).astype(BF16)
        outer = dot(out_t, unit)
        new_out[step] = jnp.transpose(mid[step].astype(F32) + outer * outgate).astype(BF16)
        d_gatepre = (gated * outer * (1.0 - outgate)).astype(BF16)
        d_normed_out[step] = dot(outgate_w[1], d_gatepre)
        unit_all[:, here] = unit
        outer_all[:, here] = d_outer
        normed_all[:, here] = normed[step]
        gate_all[:, here] = d_gatepre
        sums[0] += d_unit * scaled_mid
        sums[1] += d_unit

    each_row(rows, 4, body)
    d_tri_out[...] = scr[...].reshape(d_tri_out.shape).astype(BF16)
    out_weight_grads(unit_all, outer_all, normed_all, gate_all, weights_out)
    for index in range(2):
        small_out[index : index + 1, :] = as_row(sums[index])


def in_normed(d_in, all_w, proj_w, gate_w):
    width = proj_w.shape[-1]
    total = all_w
    for side in range(2):
        total = total + dot(proj_w[side], d_in[side * width : (side + 1) * width])
        total = total + dot(gate_w[side], d_in[(2 + side) * width : (3 + side) * width])
    return total


def middle_kernel(
    d_edge, proj_factor, gate_factor, d_normed_gate, scaled_in, inverse_in, cot, outgate,
    scaled_mid, inverse_mid, normed0, normed1, ngain, mgain, mbias, proj_w, gate_w, out_w,
    outgate_w,
    d_tri_out, grad_out, d_normed_out, out_weights, in_weights, small_out,
    scr, scr_tri, unit_all, outer_all, normed_all, gate_all, upper_all, d_in_all, sums,
):
    rows, channels, lanes = cot.shape
    out_t = turned(out_w[0])
    gain = column(ngain, 1, lanes)
    gain_mid, bias_mid = column(mgain, 0, lanes), column(mbias, 0, lanes)
    collect_edges(d_edge, scr)
    sums[...] = jnp.zeros_like(sums)
    half = proj_factor.shape[1]

    def body(step):
        place = lane_block(step, lanes)
        here = get_rows(scr, step, half, rows)
        d_proj = (here * proj_factor[step]).astype(BF16)
        d_gate = (here * gate_factor[step]).astype(BF16)
        d_in = jnp.concatenate([d_proj, d_gate], axis=0)
        d_in_all[:, place] = d_in
        upper_all[:, place] = normed1[step]
        d_normed = in_normed(d_in, d_normed_gate[step], proj_w[1], gate_w[1])
        scaled = scaled_in[step]
        sums[2] += d_normed * scaled
        sums[3] += d_normed
        grad = cot[step] + norm_backward(d_normed * gain, scaled, inverse_in[pl.ds(step, 1), :])
        grad_out[step] = grad
        gate = outgate[step]
        gated = grad * gate
        d_outer = gated.astype(BF16)
        d_unit = dot(out_w[0], d_outer)
        scaled = scaled_mid[step]
        d_tri = norm_backward(d_unit * gain_mid, scaled, inverse_mid[pl.ds(step, 1), :])
        put_rows(scr_tri, d_tri, step, rows)
        unit = (scaled * gain_mid + bias_mid).astype(BF16)
        outer = dot(out_t, unit)
        d_gatepre = (gated * outer * (1.0 - gate)).astype(BF16)
        d_normed_out[step] = dot(outgate_w[0], d_gatepre)
        unit_all[:, place] = unit
        outer_all[:, place] = d_outer
        normed_all[:, place] = normed0[step]
        gate_all[:, place] = d_gatepre
        sums[0] += d_unit * scaled
        sums[1] += d_unit

    each_row(rows, 2, body)
    d_tri_out[...] = scr_tri[...].reshape(d_tri_out.shape).astype(BF16)
    out_weight_grads(unit_all, outer_all, normed_all, gate_all, out_weights)
    in_weight_grads(upper_all, d_in_all, in_weights)
    for index in range(4):
        small_out[index : index + 1, :] = as_row(sums[index])


def finish_kernel(
    d_edge, proj_factor, gate_factor, d_normed_gate, scaled_in, inverse_in, grad, normed,
    ngain, proj_w, gate_w, out0, in1, out1,
    packed_out, grad_out, small_out, scr, normed_all, d_in_all, sums,
):
    rows, half, lanes = proj_factor.shape
    gain = column(ngain, 0, lanes)
    collect_edges(d_edge, scr)
    sums[...] = jnp.zeros_like(sums)

    def body(step):
        place = lane_block(step, lanes)
        here = get_rows(scr, step, half, rows)
        d_proj = (here * proj_factor[step]).astype(BF16)
        d_gate = (here * gate_factor[step]).astype(BF16)
        d_in = jnp.concatenate([d_proj, d_gate], axis=0)
        d_in_all[:, place] = d_in
        normed_all[:, place] = normed[step]
        d_normed = in_normed(d_in, d_normed_gate[step], proj_w[0], gate_w[0])
        scaled = scaled_in[step]
        sums[0] += d_normed * scaled
        sums[1] += d_normed
        total = grad[step] + norm_backward(d_normed * gain, scaled, inverse_in[pl.ds(step, 1), :])
        grad_out[step] = jnp.transpose(total).astype(BF16)

    each_row(rows, 4, body)
    first, second, third = d_in_all.shape[0], out0.shape[0], in1.shape[0]
    in_weight_grads(normed_all, d_in_all, packed_out.at[0:first])
    packed_out[first : first + second, :] = out0[...]
    packed_out[first + second : first + second + third, :] = in1[...]
    packed_out[first + second + third :, :] = out1[...]
    for index in range(2):
        small_out[index : index + 1, :] = as_row(sums[index])


def sum_kernel(parts, small0, small_middle, small1, own_out):
    share = parts.shape[1]
    own_out[0:share, :] = jnp.sum(parts[...].astype(F32), axis=0).astype(BF16)
    small = jnp.concatenate(
        [small0[...], small_middle[0:2], small_middle[2:4], small1[...]], axis=0
    )
    high = small.astype(BF16).astype(F32)
    own_out[share:, :] = jnp.concatenate([high, small - high], axis=0).astype(BF16)


def unpack_kernel(
    share, steps, few, shared, proj_out, gate_out, out_out, outgate_out, small_out, weights
):
    shards, _, width = shared.shape
    me = lax.axis_index("row") * few + lax.axis_index("col")
    total = jnp.zeros(small_out.shape, F32)
    for shard in range(shards):
        apart = me ^ shard
        place = 0
        for order, mask in enumerate(steps):
            place = place + jnp.where((apart & mask) != 0, 1 << order, 0)
        weights[shard * share : (shard + 1) * share, :] = shared[place, 0:share].astype(F32)
        extra = shared[place, share:].astype(F32)
        total = total + extra[0:8] + extra[8:16]
    small_out[...] = total
    for module in range(2):
        blocks = [
            weights[(6 * module + part) * width : (6 * module + part + 1) * width, :]
            for part in range(6)
        ]
        for side in range(2):
            proj_out[module, side] = blocks[side]
            gate_out[module, side] = blocks[2 + side]
        out_out[module] = blocks[4]
        outgate_out[module] = blocks[5]


def triangle_kernel(incoming, edge, tri_out):
    many, few, _, group, rows, lanes = edge.shape

    def whole(side, channel):
        parts = [edge[:, c, side, channel].reshape(many * rows, lanes) for c in range(few)]
        return jnp.concatenate(parts, axis=1)

    for channel in range(group):
        left, right = whole(0, channel), whole(1, channel)
        tri = (dot_lt if incoming else dot_rt)(left, right).astype(BF16)
        for c in range(few):
            part = tri[:, c * lanes : (c + 1) * lanes]
            tri_out[:, c, channel] = part.reshape(many, rows, lanes)


def edge_grad_kernel(incoming, edge, d_tri, grad_out):
    many, few, _, group, rows, lanes = edge.shape

    def whole(ref, *index):
        parts = [ref[(slice(None), c) + index].reshape(many * rows, lanes) for c in range(few)]
        return jnp.concatenate(parts, axis=1)

    for channel in range(group):
        left, right = whole(edge, 0, channel), whole(edge, 1, channel)
        grad = whole(d_tri, channel)
        if incoming:
            d_left, d_right = dot_rt(right, grad), dot(left, grad)
        else:
            d_left, d_right = dot(grad, right), dot_lt(grad, left)
        for side, value in ((0, d_left), (1, d_right)):
            value = value.astype(BF16)
            for c in range(few):
                part = value[:, c * lanes : (c + 1) * lanes]
                grad_out[:, c, side, channel] = part.reshape(many, rows, lanes)


SCALARS = pl.BlockSpec(memory_space=pltpu.SMEM)
VECTORS = pl.BlockSpec(memory_space=pltpu.VMEM)
FAR = pl.BlockSpec(memory_space=pltpu.HBM)


def call(kernel, name, outs, args, scratch=(), flops=0, scalars=0, grant=16, far=False):
    shapes = [jax.ShapeDtypeStruct(shape, dtype) for shape, dtype in outs]
    moved = sum(a.size * a.dtype.itemsize for a in list(args) + shapes)
    rest = FAR if far else VECTORS
    return pl.pallas_call(
        kernel,
        name=name,
        out_shape=shapes,
        in_specs=[SCALARS] * scalars + [rest] * (len(args) - scalars),
        out_specs=[VECTORS] * len(shapes),
        scratch_shapes=[
            pltpu.VMEM(*item) if isinstance(item, tuple) else item for item in scratch
        ],
        compiler_params=pltpu.CompilerParams(vmem_limit_bytes=grant * 1024 * 1024),
        cost_estimate=pl.CostEstimate(flops=flops, bytes_accessed=moved, transcendentals=0),
    )(*args)


def exchange(values):
    return lax.all_to_all(values, ("row", "col"), split_axis=0, concat_axis=0, tiled=True)


def doubling_steps(many, few):
    far = [("row", 1 << bit) for bit in range(many.bit_length() - 2, 0, -1)]
    return far + [("col", 1 << bit) for bit in range(few.bit_length() - 1)] + [("row", 1)]


def gather_apart(own, many, few):
    have = own[None]
    for axis, mask in doubling_steps(many, few):
        size = many if axis == "row" else few
        pairs = [(index, index ^ mask) for index in range(size)]
        have = jnp.concatenate([have, lax.ppermute(have, axis, pairs)], axis=0)
    return have


def grouped_device(
    pair, cotangent, lengths, ngain, nbias, proj_w, gate_w, mgain, mbias, out_w, outgate_w,
    *, many, few,
):
    rows, lanes, channels = pair.shape
    shards = many * few
    group = H // shards
    edge = ((shards, 2, group, rows, lanes), BF16)
    grid = ((many, few, 2, group, rows, lanes), BF16)
    tri = ((shards, group, rows, lanes), BF16)
    tri_grid = ((many, few, group, rows, lanes), BF16)
    tile = ((rows, channels, lanes), BF16)
    wide = ((rows, channels, lanes), F32)
    row = ((rows, lanes), F32)
    factor = ((rows, 2 * H, lanes), F32)
    d_in = ((rows, 4 * H, lanes), BF16)
    wts = ((4 * H, channels), BF16)
    big = ((2 * H * rows, lanes), F32)
    mid = ((H * rows, lanes), F32)
    positions = rows * lanes
    flat = ((H, positions), BF16)
    flat_in = ((4 * H, positions), BF16)
    out_rows = ((2 * H, channels), BF16)
    in_rows = ((4 * H, H), BF16)
    triangle = 2 * group * (many * rows) ** 2 * (few * lanes)
    dense = 2 * positions * channels * H

    def sums(count):
        return ((count, H, lanes), F32)

    def small(count):
        return ((count, H), F32)

    saved = [tile, factor, factor, wide, row]
    far = [
        pltpu.with_memory_space_constraint(item, pltpu.HBM)
        for item in (pair, ngain, nbias, proj_w, gate_w)
    ]
    sent, normed0, *factors0 = call(
        start_kernel, "start", [edge, *saved], [lengths, *far],
        [(pair.shape, BF16), (ngain.shape, F32), (nbias.shape, F32), (proj_w.shape, BF16),
         (gate_w.shape, BF16), pltpu.SemaphoreType.DMA((5,)), wts, big],
        4 * dense, 1, far=True,
    )
    edge0 = exchange(sent).reshape(grid[0])
    (here,) = call(
        functools.partial(triangle_kernel, False), "outgoing", [tri_grid], [edge0], (), triangle,
    )
    tri0 = exchange(here.reshape(tri[0]))
    sent, mid_t, normed1, *factors1, outgate0, scaled_mid0, inverse_mid0 = call(
        between_kernel, "between", [edge, tile, *saved, wide, wide, row],
        [lengths, tri0, pair, normed0, ngain, nbias, mgain, mbias, out_w, outgate_w, proj_w,
         gate_w],
        [wts, big], 6 * dense, 1,
    )
    edge1 = exchange(sent).reshape(grid[0])
    (here,) = call(
        functools.partial(triangle_kernel, True), "incoming", [tri_grid], [edge1], (), triangle,
    )
    tri1 = exchange(here.reshape(tri[0]))
    sent, new_pair, cot_t, d_normed_gate1, out_grads1, small1 = call(
        turn_kernel, "turn", [tri, (pair.shape, BF16), wide, wide, out_rows, small(2)],
        [tri1, mid_t, normed1, cotangent, mgain, mbias, out_w, outgate_w],
        [mid, flat, flat, flat, flat, sums(2)], 6 * dense,
    )
    d_tri1 = exchange(sent).reshape(tri_grid[0])
    (sent,) = call(
        functools.partial(edge_grad_kernel, True), "incoming_grad", [grid], [edge1, d_tri1],
        (), 2 * triangle,
    )
    d_edge1 = exchange(sent.reshape(edge[0]))
    proj_factor1, gate_factor1, scaled1, inverse1 = factors1
    sent, grad, d_normed_gate0, out_grads0, in_grads1, small_middle = call(
        middle_kernel, "middle", [tri, wide, wide, out_rows, in_rows, small(4)],
        [d_edge1, proj_factor1, gate_factor1, d_normed_gate1, scaled1, inverse1, cot_t, outgate0,
         scaled_mid0, inverse_mid0, normed0, normed1, ngain, mgain, mbias, proj_w, gate_w, out_w,
         outgate_w],
        [big, mid, flat, flat, flat, flat, flat, flat_in, sums(4)], 13 * dense,
    )
    d_tri0 = exchange(sent).reshape(tri_grid[0])
    (sent,) = call(
        functools.partial(edge_grad_kernel, False), "outgoing_grad", [grid], [edge0, d_tri0],
        (), 2 * triangle,
    )
    d_edge0 = exchange(sent.reshape(edge[0]))
    share = 12 * H // shards
    proj_factor0, gate_factor0, scaled0, inverse0 = factors0
    packed, grad_pair, small0 = call(
        finish_kernel, "finish", [((12 * H, H), BF16), (pair.shape, BF16), small(2)],
        [d_edge0, proj_factor0, gate_factor0, d_normed_gate0, scaled0, inverse0, grad, normed0,
         ngain, proj_w, gate_w, out_grads0, in_grads1, out_grads1],
        [big, flat, flat_in, sums(2)], 8 * dense,
    )
    parts = exchange(packed.reshape(shards, share, H))
    (own,) = call(
        sum_kernel, "sum_weights", [((share + 16, H), BF16)],
        [parts, small0, small_middle, small1],
    )
    shared = gather_apart(own, many, few)
    steps = [mask * few if axis == "row" else mask for axis, mask in doubling_steps(many, few)]
    grad_proj, grad_gate, grad_out, grad_outgate, small_all = call(
        functools.partial(unpack_kernel, share, steps, few), "unpack",
        [(proj_w.shape, F32), (gate_w.shape, F32), (out_w.shape, F32), (outgate_w.shape, F32),
         small(8)],
        [shared], [((shards * share, H), F32)],
    )
    small_all = small_all.reshape(2, 4, H)
    return (
        new_pair,
        grad_pair,
        small_all[:, 0],
        small_all[:, 1],
        grad_proj,
        grad_gate,
        small_all[:, 2],
        small_all[:, 3],
        grad_out,
        grad_outgate,
    )


def norm_channels(values):
    average = jnp.mean(values, -1, keepdims=True)
    centred = values - average
    variance = jnp.mean(centred * centred, -1, keepdims=True)
    inverse = lax.rsqrt(variance + EPS)
    return (centred * inverse, inverse)


def forward_module(pair_in, pair_mask, weights, incoming):
    gain_in, bias_in, proj_w, gate_w, gain_mid, bias_mid, out_w, outgate_w = weights
    scaled_in, inverse_in = norm_channels(pair_in.astype(jnp.float32))
    normed = (scaled_in * gain_in + bias_in).astype(jnp.bfloat16)
    projected = product("ijc,sch->shij", normed, proj_w)
    gating = jax.nn.sigmoid(product("ijc,sch->shij", normed, gate_w))
    hidden = (projected * gating * pair_mask).astype(jnp.bfloat16)
    left_side, right_side = (
        lax.all_to_all(hidden[0], "row", split_axis=0, concat_axis=1, tiled=True),
        lax.all_to_all(hidden[1], "row", split_axis=0, concat_axis=1, tiled=True),
    )
    if incoming:
        left_side = jnp.swapaxes(left_side, 1, 2)
        right_side = jnp.swapaxes(right_side, 1, 2)
    else:
        left_side, right_side = (
            lax.all_to_all(left_side, "col", split_axis=1, concat_axis=2, tiled=True),
            lax.all_to_all(right_side, "col", split_axis=1, concat_axis=2, tiled=True),
        )
    triangle = product(
        "cik,cjk->cij", left_side, lax.all_gather(right_side, "col", axis=1, tiled=True)
    ).astype(jnp.bfloat16)
    triangle = lax.all_to_all(
        lax.all_to_all(triangle, "col", split_axis=2, concat_axis=1, tiled=True),
        "row",
        split_axis=1,
        concat_axis=0,
        tiled=True,
    )
    tri_values = triangle.astype(jnp.float32)
    total, squares = lax.psum((jnp.sum(tri_values, 0), jnp.sum(tri_values * tri_values, 0)), "ch")
    average = total / H
    inverse_mid = lax.rsqrt(squares / H - average * average + EPS)
    scaled_mid = (tri_values - average) * inverse_mid
    unit = (scaled_mid * gain_mid[:, None, None] + bias_mid[:, None, None]).astype(jnp.bfloat16)
    unit_full = lax.all_gather(unit, "ch", axis=0, tiled=True)
    outer = product("hij,hc->ijc", unit_full, out_w)
    outgate = jax.nn.sigmoid(product("ijc,cd->ijd", normed, outgate_w))
    result = (pair_in.astype(jnp.float32) + outer * outgate).astype(jnp.bfloat16)
    saved = (
        scaled_in,
        inverse_in,
        normed,
        projected,
        gating,
        left_side,
        right_side,
        scaled_mid,
        inverse_mid,
        unit_full,
        outer,
        outgate,
    )
    return (result, saved)


def backward_module(grad_out, pair_mask, weights, saved, incoming):
    gain_in, bias_in, proj_w, gate_w, gain_mid, bias_mid, out_w, outgate_w = weights
    (
        scaled_in,
        inverse_in,
        normed,
        projected,
        gating,
        left_side,
        right_side,
        scaled_mid,
        inverse_mid,
        unit_full,
        outer,
        outgate,
    ) = saved
    d_outer = (grad_out * outgate).astype(jnp.bfloat16)
    d_gatepre = (grad_out * outer * outgate * (1.0 - outgate)).astype(jnp.bfloat16)
    grad_out_w = product("hij,ijc->hc", unit_full, d_outer)
    grad_outgate_w = product("ijc,ijd->cd", normed, d_gatepre)
    width = gain_mid.shape[0]
    own_rows = lax.dynamic_slice_in_dim(out_w, lax.axis_index("ch") * width, width, 0)
    d_unit = product("ijc,hc->hij", d_outer, own_rows)
    d_normed = product("ijd,cd->ijc", d_gatepre, outgate_w)
    weighted = d_unit * gain_mid[:, None, None]
    grad_gain_mid = jnp.sum(d_unit * scaled_mid, (1, 2))
    grad_bias_mid = jnp.sum(d_unit, (1, 2))
    first_sum, second_sum = lax.psum(
        (jnp.sum(weighted, 0), jnp.sum(weighted * scaled_mid, 0)), "ch"
    )
    d_tri = (inverse_mid * (weighted - first_sum / H - scaled_mid * (second_sum / H))).astype(
        jnp.bfloat16
    )
    grad_rows = lax.all_to_all(d_tri, "row", split_axis=0, concat_axis=1, tiled=True)
    grad_cols = lax.all_to_all(grad_rows, "col", split_axis=1, concat_axis=2, tiled=True)
    d_left = product(
        "cij,cjk->cik", grad_cols, lax.all_gather(right_side, "col", axis=1, tiled=True)
    )
    partial_terms = product("cij,cik->cjk", grad_cols, left_side)
    d_right = lax.psum_scatter(
        partial_terms.astype(jnp.bfloat16), "col", scatter_dimension=1, tiled=True
    ).astype(jnp.float32)
    d_left = d_left.astype(jnp.bfloat16)
    d_right = d_right.astype(jnp.bfloat16)
    if incoming:
        d_left = jnp.swapaxes(d_left, 1, 2)
        d_right = jnp.swapaxes(d_right, 1, 2)
    else:
        d_left, d_right = (
            lax.all_to_all(d_left, "col", split_axis=2, concat_axis=1, tiled=True),
            lax.all_to_all(d_right, "col", split_axis=2, concat_axis=1, tiled=True),
        )
    d_left, d_right = (
        lax.all_to_all(d_left, "row", split_axis=1, concat_axis=0, tiled=True),
        lax.all_to_all(d_right, "row", split_axis=1, concat_axis=0, tiled=True),
    )
    d_hidden = jnp.stack([d_left, d_right]).astype(jnp.float32)
    d_proj = (d_hidden * gating * pair_mask).astype(jnp.bfloat16)
    d_gate = (d_hidden * projected * gating * (1.0 - gating) * pair_mask).astype(jnp.bfloat16)
    grad_proj_w = product("ijc,shij->sch", normed, d_proj)
    grad_gate_w = product("ijc,shij->sch", normed, d_gate)
    partial_input = product("shij,sch->ijc", d_proj, proj_w) + product(
        "shij,sch->ijc", d_gate, gate_w
    )
    d_normed = d_normed + lax.psum(partial_input.astype(jnp.bfloat16), "ch").astype(jnp.float32)
    weighted_in = d_normed * gain_in
    grad_gain_in = jnp.sum(d_normed * scaled_in, (0, 1))
    grad_bias_in = jnp.sum(d_normed, (0, 1))
    d_pair = inverse_in * (
        weighted_in
        - jnp.mean(weighted_in, -1, keepdims=True)
        - scaled_in * jnp.mean(weighted_in * scaled_in, -1, keepdims=True)
    )
    grads = (
        grad_gain_in,
        grad_bias_in,
        grad_proj_w,
        grad_gate_w,
        grad_gain_mid,
        grad_bias_mid,
        grad_out_w,
        grad_outgate_w,
    )
    return (grad_out + d_pair, grads)


def per_device(
    pair,
    cotangent,
    lengths,
    norm_gain,
    norm_bias,
    proj_weight,
    gate_weight,
    mid_gain,
    mid_bias,
    out_weight,
    outgate_weight,
):
    rows_here = pair.shape[0]
    cols_here = pair.shape[1]
    row_ids = lax.axis_index("row") * rows_here + lax.iota(jnp.int32, rows_here)
    col_ids = lax.axis_index("col") * cols_here + lax.iota(jnp.int32, cols_here)
    limit = lengths[0]
    pair_mask = ((row_ids[:, None] < limit) & (col_ids[None, :] < limit)).astype(jnp.float32)
    state = pair
    stash = []
    for layer in range(2):
        weights = (
            norm_gain[layer],
            norm_bias[layer],
            proj_weight[layer],
            gate_weight[layer],
            mid_gain[layer],
            mid_bias[layer],
            out_weight[layer],
            outgate_weight[layer],
        )
        state, saved = forward_module(state, pair_mask, weights, layer == 1)
        stash.append(saved)
    grad_state = cotangent.astype(jnp.float32)
    per_layer = [None, None]
    for layer in (1, 0):
        weights = (
            norm_gain[layer],
            norm_bias[layer],
            proj_weight[layer],
            gate_weight[layer],
            mid_gain[layer],
            mid_bias[layer],
            out_weight[layer],
            outgate_weight[layer],
        )
        grad_state, grads = backward_module(
            grad_state, pair_mask, weights, stash[layer], layer == 1
        )
        per_layer[layer] = grads
    lower = per_layer[0]
    upper = per_layer[1]
    summed = lax.psum(
        (
            lower[0],
            lower[1],
            lower[2],
            lower[3],
            lower[4],
            lower[5],
            lower[6],
            lower[7],
            upper[0],
            upper[1],
            upper[2],
            upper[3],
            upper[4],
            upper[5],
            upper[6],
            upper[7],
        ),
        ("row", "col"),
    )
    per_layer = [summed[0:8], summed[8:16]]
    stacked = [jnp.stack([per_layer[0][index], per_layer[1][index]]) for index in range(8)]
    return (
        state,
        grad_state.astype(jnp.bfloat16),
        stacked[0],
        stacked[1],
        stacked[2],
        stacked[3],
        stacked[4],
        stacked[5],
        stacked[6],
        stacked[7],
    )


def solution(mesh):
    in_specs = (
        P(("grp", "row"), "col", None),
        P(("grp", "row"), "col", None),
        P("grp"),
        P(),
        P(),
        P(None, None, None, "ch"),
        P(None, None, None, "ch"),
        P(None, "ch"),
        P(None, "ch"),
        P(),
        P(),
    )
    out_specs = (
        P(("grp", "row"), "col", None),
        P(("grp", "row"), "col", None),
        P("grp", None),
        P("grp", None),
        P("grp", None, None, "ch"),
        P("grp", None, None, "ch"),
        P("grp", "ch"),
        P("grp", "ch"),
        P("grp", None, None),
        P("grp", None, None),
    )
    many, few = mesh.shape["row"], mesh.shape["col"]
    if mesh.shape["ch"] == 1 and H % (many * few) == 0 and many & (many - 1) == 0:
        body = functools.partial(grouped_device, many=many, few=few)
    else:
        body = per_device
    return jax.shard_map(
        body, mesh=mesh, in_specs=in_specs, out_specs=out_specs, check_vma=False
    )
```

```python
import functools

import jax
import jax.numpy as jnp
from jax import lax
from jax.experimental import pallas as pl
from jax.experimental.pallas import tpu as pltpu
from jax.sharding import PartitionSpec as P

H = 128


EPS = 1e-05


def product(spec, left, right):
    return jnp.einsum(spec, left, right, preferred_element_type=jnp.float32)


F32 = jnp.float32
BF16 = jnp.bfloat16


def dot(left, right):
    return lax.dot_general(left, right, (((1,), (0,)), ((), ())), preferred_element_type=F32)


def dot_rt(left, right):
    return lax.dot_general(left, right, (((1,), (1,)), ((), ())), preferred_element_type=F32)


def dot_lt(left, right):
    return lax.dot_general(left, right, (((0,), (0,)), ((), ())), preferred_element_type=F32)


def sigmoid(values):
    return 1.0 / (1.0 + jnp.exp(-values))


def norm_rows(values):
    scale = 1.0 / values.shape[0]
    average = jnp.sum(values, 0, keepdims=True) * scale
    centred = values - average
    variance = jnp.sum(centred * centred, 0, keepdims=True) * scale
    inverse = lax.rsqrt(variance + EPS)
    return centred * inverse, inverse


def turned(weight):
    return jnp.transpose(weight.astype(F32)).astype(BF16)


def column(ref, module, lanes):
    row = ref[module : module + 1, :]
    return jnp.transpose(jnp.broadcast_to(row, (lanes, row.shape[1])))


def as_row(total):
    return jnp.sum(jnp.transpose(total), 0, keepdims=True)


def row_mask(lengths_ref, step, rows, lanes):
    limit = lengths_ref[0]
    row_id = lax.axis_index("row") * rows + step
    col_id = lax.axis_index("col") * lanes + lax.broadcasted_iota(jnp.int32, (1, lanes), 1)
    return jnp.where((row_id < limit) & (col_id < limit), 1.0, 0.0).astype(F32)


def load_in_weights(proj_ref, gate_ref, module, scratch):
    width = proj_ref.shape[-1]
    for side in range(2):
        scratch[side * width : (side + 1) * width, :] = turned(proj_ref[module, side])
        scratch[(2 + side) * width : (3 + side) * width, :] = turned(gate_ref[module, side])


def put_rows(scratch, values, step, rows):
    scratch[pl.ds(step, values.shape[0], stride=rows), :] = values


def get_rows(scratch, step, channels, rows):
    return scratch[pl.ds(step, channels, stride=rows), :]


def own_number(few):
    return lax.axis_index("row") * few + lax.axis_index("col")


def core_bit(few):
    return few


def chip_offsets(shards, few):
    return [mask for mask in range(shards) if mask & core_bit(few) == 0]


def sources(pieces, few):
    me = own_number(few)
    for offset, piece in zip(chip_offsets(2 * len(pieces), few), pieces):
        for core in range(2):
            yield me ^ (offset | core * core_bit(few)), piece.at[core]


def rows_at(place, size):
    return pl.ds(pl.multiple_of(place * size, size), size)


def spread_edges(scratch, out_ref, few):
    shards, sides, group, rows, lanes = out_ref.shape
    size = group * rows
    me = own_number(few)
    for mask in range(shards):
        for side in range(sides):
            part = scratch[rows_at(side * shards + (me ^ mask), size), :]
            out_ref[mask, side] = part.astype(BF16).reshape(group, rows, lanes)


def collect_edges(pieces, scratch, few):
    _, sides, group, rows, lanes = pieces[0].shape
    size, shards = group * rows, 2 * len(pieces)
    for source, part in sources(pieces, few):
        for side in range(sides):
            scratch[rows_at(side * shards + source, size), :] = (
                part[side].astype(F32).reshape(size, lanes)
            )


def spread_triangle(scratch, out_ref, few):
    shards, group, rows, lanes = out_ref.shape
    me = own_number(few)
    for mask in range(shards):
        part = scratch[rows_at(me ^ mask, group * rows), :]
        out_ref[mask] = part.astype(BF16).reshape(group, rows, lanes)


def collect_triangle(pieces, scratch, few):
    _, group, rows, lanes = pieces[0].shape
    for source, part in sources(pieces, few):
        scratch[rows_at(source, group * rows), :] = (
            part[...].astype(F32).reshape(group * rows, lanes)
        )


def each_row(rows, unroll, body):
    def step_body(step, carry):
        body(step)
        return carry

    lax.fori_loop(0, rows, step_body, 0, unroll=unroll)


def mid_norm(tri):
    scale = 1.0 / tri.shape[0]
    average = jnp.sum(tri, 0, keepdims=True) * scale
    squares = jnp.sum(tri * tri, 0, keepdims=True) * scale
    inverse = lax.rsqrt(squares - average * average + EPS)
    return (tri - average) * inverse, inverse


def norm_backward(weighted, scaled, inverse):
    scale = 1.0 / weighted.shape[0]
    first = jnp.sum(weighted, 0, keepdims=True) * scale
    second = jnp.sum(weighted * scaled, 0, keepdims=True) * scale
    return inverse * (weighted - first - scaled * second)


def save_norm(step, values, scaled_out, inverse_out):
    scaled, inverse = norm_rows(values)
    scaled_out[step] = scaled
    inverse_out[pl.ds(step, 1), :] = inverse
    return scaled


def save_edges(step, normed, in_weights, mask, proj_out, gate_out):
    pre = dot(in_weights, normed)
    half = pre.shape[0] // 2
    gating = sigmoid(pre[half:])
    factor = gating * mask
    value = pre[:half] * factor
    proj_out[step] = factor
    gate_out[step] = value * (1.0 - gating)
    return value


def start_kernel(
    few, lengths, pair_far, ngain_far, nbias_far, proj_far, gate_far,
    edge_out, normed_out, proj_out, gate_out, scaled_out, inverse_out,
    pair, ngain, nbias, proj_w, gate_w, sems, wts, scr,
):
    far = (proj_far.at[0], gate_far.at[0], ngain_far, nbias_far, pair_far)
    near = (proj_w.at[0], gate_w.at[0], ngain, nbias, pair)
    copies = [
        pltpu.make_async_copy(source, target, sems.at[index])
        for index, (source, target) in enumerate(zip(far, near))
    ]
    for copy in copies:
        copy.start()
    for copy in copies:
        copy.wait()
    rows, lanes, channels = pair.shape
    load_in_weights(proj_w, gate_w, 0, wts)
    gain, bias = column(ngain, 0, lanes), column(nbias, 0, lanes)

    def body(step):
        base = jnp.transpose(pair[step].astype(F32))
        scaled = save_norm(step, base, scaled_out, inverse_out)
        normed = (scaled * gain + bias).astype(BF16)
        normed_out[step] = normed
        mask = row_mask(lengths, step, rows, lanes)
        put_rows(scr, save_edges(step, normed, wts[...], mask, proj_out, gate_out), step, rows)

    each_row(rows, 4, body)
    spread_edges(scr, edge_out, few)


def between_kernel(
    few, count, lengths, *refs,
):
    tri, rest = refs[:count], refs[count:]
    between_body(few, lengths, tri, *rest)


def between_body(
    few, lengths, tri, pair, normed0, ngain, nbias, mgain, mbias, out_w, outgate_w, proj_w, gate_w,
    edge_out, mid_out, normed_out, proj_out, gate_out, scaled_out, inverse_out,
    outgate_out, scaled_mid_out, inverse_mid_out, wts, scr,
):
    rows, lanes, channels = pair.shape
    load_in_weights(proj_w, gate_w, 1, wts)
    out_t, outgate_t = turned(out_w[0]), turned(outgate_w[0])
    gain, bias = column(ngain, 1, lanes), column(nbias, 1, lanes)
    gain_mid, bias_mid = column(mgain, 0, lanes), column(mbias, 0, lanes)
    collect_triangle(tri, scr, few)

    def body(step):
        scaled_mid, inverse_mid = mid_norm(get_rows(scr, step, channels, rows))
        scaled_mid_out[step] = scaled_mid
        inverse_mid_out[pl.ds(step, 1), :] = inverse_mid
        unit = (scaled_mid * gain_mid + bias_mid).astype(BF16)
        outer = dot(out_t, unit)
        outgate = sigmoid(dot(outgate_t, normed0[step]))
        outgate_out[step] = outgate
        mid = (jnp.transpose(pair[step].astype(F32)) + outer * outgate).astype(BF16)
        mid_out[step] = mid
        scaled = save_norm(step, mid.astype(F32), scaled_out, inverse_out)
        normed = (scaled * gain + bias).astype(BF16)
        normed_out[step] = normed
        mask = row_mask(lengths, step, rows, lanes)
        put_rows(scr, save_edges(step, normed, wts[...], mask, proj_out, gate_out), step, rows)

    each_row(rows, 4, body)
    spread_edges(scr, edge_out, few)


def out_weight_grads(unit, d_outer, normed, d_gatepre, out_ref):
    width = unit.shape[0]
    out_ref[0:width, :] = dot_rt(unit[...], d_outer[...]).astype(out_ref.dtype)
    out_ref[width:, :] = dot_rt(normed[...], d_gatepre[...]).astype(out_ref.dtype)


def in_weight_grads(normed_all, d_in_all, out_ref):
    width = normed_all.shape[0]
    for part in range(d_in_all.shape[0] // width):
        block = slice(part * width, (part + 1) * width)
        out_ref[block, :] = dot_rt(normed_all[...], d_in_all[block, :]).astype(out_ref.dtype)


def lane_block(step, lanes):
    return pl.ds(pl.multiple_of(step * lanes, lanes), lanes)


def turn_kernel(few, count, *refs):
    turn_body(few, refs[:count], *refs[count:])


def turn_body(
    few, tri, mid, normed, cot, mgain, mbias, out_w, outgate_w,
    d_tri_out, new_out, grad_out, d_normed_out, weights_out, small_out,
    scr, unit_all, outer_all, normed_all, gate_all, sums,
):
    rows, channels, lanes = mid.shape
    out_t, outgate_t = turned(out_w[1]), turned(outgate_w[1])
    gain_mid, bias_mid = column(mgain, 1, lanes), column(mbias, 1, lanes)
    collect_triangle(tri, scr, few)
    sums[...] = jnp.zeros_like(sums)

    def body(step):
        here = lane_block(step, lanes)
        grad = jnp.transpose(cot[step].astype(F32))
        grad_out[step] = grad
        outgate = sigmoid(dot(outgate_t, normed[step]))
        gated = grad * outgate
        d_outer = gated.astype(BF16)
        d_unit = dot(out_w[1], d_outer)
        scaled_mid, inverse_mid = mid_norm(get_rows(scr, step, channels, rows))
        put_rows(scr, norm_backward(d_unit * gain_mid, scaled_mid, inverse_mid), step, rows)
        unit = (scaled_mid * gain_mid + bias_mid).astype(BF16)
        outer = dot(out_t, unit)
        new_out[step] = jnp.transpose(mid[step].astype(F32) + outer * outgate).astype(BF16)
        d_gatepre = (gated * outer * (1.0 - outgate)).astype(BF16)
        d_normed_out[step] = dot(outgate_w[1], d_gatepre)
        unit_all[:, here] = unit
        outer_all[:, here] = d_outer
        normed_all[:, here] = normed[step]
        gate_all[:, here] = d_gatepre
        sums[0] += d_unit * scaled_mid
        sums[1] += d_unit

    each_row(rows, 4, body)
    spread_triangle(scr, d_tri_out, few)
    out_weight_grads(unit_all, outer_all, normed_all, gate_all, weights_out)
    for index in range(2):
        small_out[index : index + 1, :] = as_row(sums[index])


def in_normed(d_in, all_w, proj_w, gate_w):
    width = proj_w.shape[-1]
    total = all_w
    for side in range(2):
        total = total + dot(proj_w[side], d_in[side * width : (side + 1) * width])
        total = total + dot(gate_w[side], d_in[(2 + side) * width : (3 + side) * width])
    return total


def middle_kernel(few, count, *refs):
    middle_body(few, refs[:count], *refs[count:])


def middle_body(
    few, d_edge, proj_factor, gate_factor, d_normed_gate, scaled_in, inverse_in, cot, outgate,
    scaled_mid, inverse_mid, normed0, normed1, ngain, mgain, mbias, proj_w, gate_w, out_w,
    outgate_w,
    d_tri_out, grad_out, d_normed_out, out_weights, in_weights, small_out,
    scr, scr_tri, unit_all, outer_all, normed_all, gate_all, upper_all, d_in_all, sums,
):
    rows, channels, lanes = cot.shape
    out_t = turned(out_w[0])
    gain = column(ngain, 1, lanes)
    gain_mid, bias_mid = column(mgain, 0, lanes), column(mbias, 0, lanes)
    collect_edges(d_edge, scr, few)
    sums[...] = jnp.zeros_like(sums)
    half = proj_factor.shape[1]

    def body(step):
        place = lane_block(step, lanes)
        here = get_rows(scr, step, half, rows)
        d_proj = (here * proj_factor[step]).astype(BF16)
        d_gate = (here * gate_factor[step]).astype(BF16)
        d_in = jnp.concatenate([d_proj, d_gate], axis=0)
        d_in_all[:, place] = d_in
        upper_all[:, place] = normed1[step]
        d_normed = in_normed(d_in, d_normed_gate[step], proj_w[1], gate_w[1])
        scaled = scaled_in[step]
        sums[2] += d_normed * scaled
        sums[3] += d_normed
        grad = cot[step] + norm_backward(d_normed * gain, scaled, inverse_in[pl.ds(step, 1), :])
        grad_out[step] = grad
        gate = outgate[step]
        gated = grad * gate
        d_outer = gated.astype(BF16)
        d_unit = dot(out_w[0], d_outer)
        scaled = scaled_mid[step]
        d_tri = norm_backward(d_unit * gain_mid, scaled, inverse_mid[pl.ds(step, 1), :])
        put_rows(scr_tri, d_tri, step, rows)
        unit = (scaled * gain_mid + bias_mid).astype(BF16)
        outer = dot(out_t, unit)
        d_gatepre = (gated * outer * (1.0 - gate)).astype(BF16)
        d_normed_out[step] = dot(outgate_w[0], d_gatepre)
        unit_all[:, place] = unit
        outer_all[:, place] = d_outer
        normed_all[:, place] = normed0[step]
        gate_all[:, place] = d_gatepre
        sums[0] += d_unit * scaled
        sums[1] += d_unit

    each_row(rows, 4, body)
    spread_triangle(scr_tri, d_tri_out, few)
    out_weight_grads(unit_all, outer_all, normed_all, gate_all, out_weights)
    in_weight_grads(upper_all, d_in_all, in_weights)
    for index in range(4):
        small_out[index : index + 1, :] = as_row(sums[index])


def finish_kernel(few, count, *refs):
    finish_body(few, refs[:count], *refs[count:])


def finish_body(
    few, d_edge, proj_factor, gate_factor, d_normed_gate, scaled_in, inverse_in, grad, normed,
    ngain, proj_w, gate_w, out0, in1, out1,
    packed_out, grad_out, small_out, scr, normed_all, d_in_all, sums,
):
    rows, half, lanes = proj_factor.shape
    gain = column(ngain, 0, lanes)
    collect_edges(d_edge, scr, few)
    sums[...] = jnp.zeros_like(sums)

    def body(step):
        place = lane_block(step, lanes)
        here = get_rows(scr, step, half, rows)
        d_proj = (here * proj_factor[step]).astype(BF16)
        d_gate = (here * gate_factor[step]).astype(BF16)
        d_in = jnp.concatenate([d_proj, d_gate], axis=0)
        d_in_all[:, place] = d_in
        normed_all[:, place] = normed[step]
        d_normed = in_normed(d_in, d_normed_gate[step], proj_w[0], gate_w[0])
        scaled = scaled_in[step]
        sums[0] += d_normed * scaled
        sums[1] += d_normed
        total = grad[step] + norm_backward(d_normed * gain, scaled, inverse_in[pl.ds(step, 1), :])
        grad_out[step] = jnp.transpose(total).astype(BF16)

    each_row(rows, 4, body)
    first, second, third = d_in_all.shape[0], out0.shape[0], in1.shape[0]
    in_weight_grads(normed_all, d_in_all, packed_out.at[0:first])
    packed_out[first : first + second, :] = out0[...]
    packed_out[first + second : first + second + third, :] = in1[...]
    packed_out[first + second + third :, :] = out1[...]
    for index in range(2):
        small_out[index : index + 1, :] = as_row(sums[index])


def sum_kernel(parts, small0, small_middle, small1, shared_out):
    shards, share, width = parts.shape
    own = jnp.sum(parts[...].astype(F32), axis=0).astype(BF16)
    small = jnp.concatenate(
        [small0[...], small_middle[0:2], small_middle[2:4], small1[...]], axis=0
    )
    high = small.astype(BF16).astype(F32)
    extra = jnp.concatenate([high, small - high], axis=0).astype(BF16)
    for shard in range(shards):
        shared_out[shard, 0:share] = own
        shared_out[shard, share:] = extra


def unpack_kernel(share, shared, proj_out, gate_out, out_out, outgate_out, small_out):
    shards, _, width = shared.shape
    total = jnp.sum(shared[:, share:, :].astype(F32), axis=0)
    small_out[...] = total[0:8] + total[8:16]
    weights = shared[:, 0:share, :].reshape(shards * share, width).astype(F32)
    for module in range(2):
        blocks = [
            weights[(6 * module + part) * width : (6 * module + part + 1) * width]
            for part in range(6)
        ]
        for side in range(2):
            proj_out[module, side] = blocks[side]
            gate_out[module, side] = blocks[2 + side]
        out_out[module] = blocks[4]
        outgate_out[module] = blocks[5]


def triangle_kernel(incoming, few, count, *refs):
    pieces, (edge_out, tri_out, tri_all) = refs[:count], refs[count:]
    shards, _, group, rows, lanes = edge_out.shape
    many = shards // few
    for source, part in sources(pieces, few):
        edge_out[source] = part[...]
    edge = edge_out.reshape(many, few, 2, group, rows, lanes)

    def whole(side, channel):
        parts = [edge[:, c, side, channel].reshape(many * rows, lanes) for c in range(few)]
        return jnp.concatenate(parts, axis=1)

    for channel in range(group):
        left, right = whole(0, channel), whole(1, channel)
        tri = (dot_lt if incoming else dot_rt)(left, right).astype(BF16)
        for c in range(few):
            part = tri[:, c * lanes : (c + 1) * lanes]
            tri_all[:, c, channel] = part.reshape(many, rows, lanes)
    place = tri_all.reshape(shards, group, rows, lanes)
    me = own_number(few)
    for mask in range(shards):
        tri_out[mask] = place[me ^ mask]


def edge_grad_kernel(incoming, few, count, *refs):
    pieces, (edge_all, grad_out, tri_all, grad_all) = refs[:count], refs[count:]
    shards, _, group, rows, lanes = edge_all.shape
    many = shards // few
    for source, part in sources(pieces, few):
        tri_all[source] = part[...]
    edge = edge_all.reshape(many, few, 2, group, rows, lanes)
    d_tri = tri_all.reshape(many, few, group, rows, lanes)

    def whole(ref, *index):
        parts = [ref[(slice(None), c) + index].reshape(many * rows, lanes) for c in range(few)]
        return jnp.concatenate(parts, axis=1)

    for channel in range(group):
        left, right = whole(edge, 0, channel), whole(edge, 1, channel)
        grad = whole(d_tri, channel)
        if incoming:
            d_left, d_right = dot_rt(right, grad), dot(left, grad)
        else:
            d_left, d_right = dot(grad, right), dot_lt(grad, left)
        for side, value in ((0, d_left), (1, d_right)):
            value = value.astype(BF16)
            for c in range(few):
                part = value[:, c * lanes : (c + 1) * lanes]
                grad_all[:, c, side, channel] = part.reshape(many, rows, lanes)
    place = grad_all.reshape(shards, 2, group, rows, lanes)
    me = own_number(few)
    for mask in range(shards):
        grad_out[mask] = place[me ^ mask]


SCALARS = pl.BlockSpec(memory_space=pltpu.SMEM)
VECTORS = pl.BlockSpec(memory_space=pltpu.VMEM)
FAR = pl.BlockSpec(memory_space=pltpu.HBM)


def call(kernel, name, outs, args, scratch=(), flops=0, scalars=0, grant=16, far=False):
    shapes = [jax.ShapeDtypeStruct(shape, dtype) for shape, dtype in outs]
    moved = sum(a.size * a.dtype.itemsize for a in list(args) + shapes)
    rest = FAR if far else VECTORS
    return pl.pallas_call(
        kernel,
        name=name,
        out_shape=shapes,
        in_specs=[SCALARS] * scalars + [rest] * (len(args) - scalars),
        out_specs=[VECTORS] * len(shapes),
        scratch_shapes=[
            pltpu.VMEM(*item) if isinstance(item, tuple) else item for item in scratch
        ],
        compiler_params=pltpu.CompilerParams(vmem_limit_bytes=grant * 1024 * 1024),
        cost_estimate=pl.CostEstimate(flops=flops, bytes_accessed=moved, transcendentals=0),
    )(*args)


def exchange(values):
    return lax.all_to_all(values, ("row", "col"), split_axis=0, concat_axis=0, tiled=True)


def swap(values, mask, shards):
    pairs = [(index, index ^ mask) for index in range(shards)]
    return lax.ppermute(values, ("row", "col"), pairs)


def trade(sent, few):
    shards = sent.shape[0]
    core = core_bit(few)
    offsets = chip_offsets(shards, few)
    given = jnp.stack([sent[offset | core] for offset in offsets])
    got = swap(given, core, shards)
    pieces = {}
    for place, offset in sorted(enumerate(offsets), key=lambda item: -item[1]):
        both = jnp.stack([sent[offset], got[place]])
        pieces[offset] = swap(both, offset, shards) if offset else both
    return [pieces[offset] for offset in offsets]


def grouped_device(
    pair, cotangent, lengths, ngain, nbias, proj_w, gate_w, mgain, mbias, out_w, outgate_w,
    *, many, few,
):
    rows, lanes, channels = pair.shape
    shards = many * few
    group = H // shards
    edge = ((shards, 2, group, rows, lanes), BF16)
    grid = ((many, few, 2, group, rows, lanes), BF16)
    tri = ((shards, group, rows, lanes), BF16)
    tri_grid = ((many, few, group, rows, lanes), BF16)
    tile = ((rows, channels, lanes), BF16)
    wide = ((rows, channels, lanes), F32)
    row = ((rows, lanes), F32)
    factor = ((rows, 2 * H, lanes), F32)
    d_in = ((rows, 4 * H, lanes), BF16)
    wts = ((4 * H, channels), BF16)
    big = ((2 * H * rows, lanes), F32)
    mid = ((H * rows, lanes), F32)
    positions = rows * lanes
    flat = ((H, positions), BF16)
    flat_in = ((4 * H, positions), BF16)
    out_rows = ((2 * H, channels), BF16)
    in_rows = ((4 * H, H), BF16)
    triangle = 2 * group * (many * rows) ** 2 * (few * lanes)
    dense = 2 * positions * channels * H

    def sums(count):
        return ((count, H, lanes), F32)

    def small(count):
        return ((count, H), F32)

    saved = [tile, factor, factor, wide, row]
    count = shards // 2
    far = [
        pltpu.with_memory_space_constraint(item, pltpu.HBM)
        for item in (pair, ngain, nbias, proj_w, gate_w)
    ]
    sent, normed0, *factors0 = call(
        functools.partial(start_kernel, few), "start", [edge, *saved], [lengths, *far],
        [(pair.shape, BF16), (ngain.shape, F32), (nbias.shape, F32), (proj_w.shape, BF16),
         (gate_w.shape, BF16), pltpu.SemaphoreType.DMA((5,)), wts, big],
        4 * dense, 1, far=True,
    )
    edge0, sent = call(
        functools.partial(triangle_kernel, False, few, count), "outgoing", [edge, tri],
        trade(sent, few), [tri_grid], triangle,
    )
    tri0 = trade(sent, few)
    sent, mid_t, normed1, *factors1, outgate0, scaled_mid0, inverse_mid0 = call(
        functools.partial(between_kernel, few, count), "between",
        [edge, tile, *saved, wide, wide, row],
        [lengths, *tri0, pair, normed0, ngain, nbias, mgain, mbias, out_w, outgate_w, proj_w,
         gate_w],
        [wts, big], 6 * dense, 1,
    )
    edge1, sent = call(
        functools.partial(triangle_kernel, True, few, count), "incoming", [edge, tri],
        trade(sent, few), [tri_grid], triangle,
    )
    tri1 = trade(sent, few)
    sent, new_pair, cot_t, d_normed_gate1, out_grads1, small1 = call(
        functools.partial(turn_kernel, few, count), "turn",
        [tri, (pair.shape, BF16), wide, wide, out_rows, small(2)],
        [*tri1, mid_t, normed1, cotangent, mgain, mbias, out_w, outgate_w],
        [mid, flat, flat, flat, flat, sums(2)], 6 * dense,
    )
    (sent,) = call(
        functools.partial(edge_grad_kernel, True, few, count), "incoming_grad", [edge],
        [*trade(sent, few), edge1], [tri, grid], 2 * triangle,
    )
    d_edge1 = trade(sent, few)
    proj_factor1, gate_factor1, scaled1, inverse1 = factors1
    sent, grad, d_normed_gate0, out_grads0, in_grads1, small_middle = call(
        functools.partial(middle_kernel, few, count), "middle",
        [tri, wide, wide, out_rows, in_rows, small(4)],
        [*d_edge1, proj_factor1, gate_factor1, d_normed_gate1, scaled1, inverse1, cot_t, outgate0,
         scaled_mid0, inverse_mid0, normed0, normed1, ngain, mgain, mbias, proj_w, gate_w, out_w,
         outgate_w],
        [big, mid, flat, flat, flat, flat, flat, flat_in, sums(4)], 13 * dense,
    )
    (sent,) = call(
        functools.partial(edge_grad_kernel, False, few, count), "outgoing_grad", [edge],
        [*trade(sent, few), edge0], [tri, grid], 2 * triangle,
    )
    d_edge0 = trade(sent, few)
    share = 12 * H // shards
    proj_factor0, gate_factor0, scaled0, inverse0 = factors0
    packed, grad_pair, small0 = call(
        functools.partial(finish_kernel, few, count), "finish",
        [((12 * H, H), BF16), (pair.shape, BF16), small(2)],
        [*d_edge0, proj_factor0, gate_factor0, d_normed_gate0, scaled0, inverse0, grad, normed0,
         ngain, proj_w, gate_w, out_grads0, in_grads1, out_grads1],
        [big, flat, flat_in, sums(2)], 8 * dense,
    )
    parts = exchange(packed.reshape(shards, share, H))
    (shared,) = call(
        sum_kernel, "sum_weights", [((shards, share + 16, H), BF16)],
        [parts, small0, small_middle, small1],
    )
    shared = exchange(shared)
    grad_proj, grad_gate, grad_out, grad_outgate, small_all = call(
        functools.partial(unpack_kernel, share), "unpack",
        [(proj_w.shape, F32), (gate_w.shape, F32), (out_w.shape, F32), (outgate_w.shape, F32),
         small(8)],
        [shared],
    )
    small_all = small_all.reshape(2, 4, H)
    return (
        new_pair,
        grad_pair,
        small_all[:, 0],
        small_all[:, 1],
        grad_proj,
        grad_gate,
        small_all[:, 2],
        small_all[:, 3],
        grad_out,
        grad_outgate,
    )


def norm_channels(values):
    average = jnp.mean(values, -1, keepdims=True)
    centred = values - average
    variance = jnp.mean(centred * centred, -1, keepdims=True)
    inverse = lax.rsqrt(variance + EPS)
    return (centred * inverse, inverse)


def forward_module(pair_in, pair_mask, weights, incoming):
    gain_in, bias_in, proj_w, gate_w, gain_mid, bias_mid, out_w, outgate_w = weights
    scaled_in, inverse_in = norm_channels(pair_in.astype(jnp.float32))
    normed = (scaled_in * gain_in + bias_in).astype(jnp.bfloat16)
    projected = product("ijc,sch->shij", normed, proj_w)
    gating = jax.nn.sigmoid(product("ijc,sch->shij", normed, gate_w))
    hidden = (projected * gating * pair_mask).astype(jnp.bfloat16)
    left_side, right_side = (
        lax.all_to_all(hidden[0], "row", split_axis=0, concat_axis=1, tiled=True),
        lax.all_to_all(hidden[1], "row", split_axis=0, concat_axis=1, tiled=True),
    )
    if incoming:
        left_side = jnp.swapaxes(left_side, 1, 2)
        right_side = jnp.swapaxes(right_side, 1, 2)
    else:
        left_side, right_side = (
            lax.all_to_all(left_side, "col", split_axis=1, concat_axis=2, tiled=True),
            lax.all_to_all(right_side, "col", split_axis=1, concat_axis=2, tiled=True),
        )
    triangle = product(
        "cik,cjk->cij", left_side, lax.all_gather(right_side, "col", axis=1, tiled=True)
    ).astype(jnp.bfloat16)
    triangle = lax.all_to_all(
        lax.all_to_all(triangle, "col", split_axis=2, concat_axis=1, tiled=True),
        "row",
        split_axis=1,
        concat_axis=0,
        tiled=True,
    )
    tri_values = triangle.astype(jnp.float32)
    total, squares = lax.psum((jnp.sum(tri_values, 0), jnp.sum(tri_values * tri_values, 0)), "ch")
    average = total / H
    inverse_mid = lax.rsqrt(squares / H - average * average + EPS)
    scaled_mid = (tri_values - average) * inverse_mid
    unit = (scaled_mid * gain_mid[:, None, None] + bias_mid[:, None, None]).astype(jnp.bfloat16)
    unit_full = lax.all_gather(unit, "ch", axis=0, tiled=True)
    outer = product("hij,hc->ijc", unit_full, out_w)
    outgate = jax.nn.sigmoid(product("ijc,cd->ijd", normed, outgate_w))
    result = (pair_in.astype(jnp.float32) + outer * outgate).astype(jnp.bfloat16)
    saved = (
        scaled_in,
        inverse_in,
        normed,
        projected,
        gating,
        left_side,
        right_side,
        scaled_mid,
        inverse_mid,
        unit_full,
        outer,
        outgate,
    )
    return (result, saved)


def backward_module(grad_out, pair_mask, weights, saved, incoming):
    gain_in, bias_in, proj_w, gate_w, gain_mid, bias_mid, out_w, outgate_w = weights
    (
        scaled_in,
        inverse_in,
        normed,
        projected,
        gating,
        left_side,
        right_side,
        scaled_mid,
        inverse_mid,
        unit_full,
        outer,
        outgate,
    ) = saved
    d_outer = (grad_out * outgate).astype(jnp.bfloat16)
    d_gatepre = (grad_out * outer * outgate * (1.0 - outgate)).astype(jnp.bfloat16)
    grad_out_w = product("hij,ijc->hc", unit_full, d_outer)
    grad_outgate_w = product("ijc,ijd->cd", normed, d_gatepre)
    width = gain_mid.shape[0]
    own_rows = lax.dynamic_slice_in_dim(out_w, lax.axis_index("ch") * width, width, 0)
    d_unit = product("ijc,hc->hij", d_outer, own_rows)
    d_normed = product("ijd,cd->ijc", d_gatepre, outgate_w)
    weighted = d_unit * gain_mid[:, None, None]
    grad_gain_mid = jnp.sum(d_unit * scaled_mid, (1, 2))
    grad_bias_mid = jnp.sum(d_unit, (1, 2))
    first_sum, second_sum = lax.psum(
        (jnp.sum(weighted, 0), jnp.sum(weighted * scaled_mid, 0)), "ch"
    )
    d_tri = (inverse_mid * (weighted - first_sum / H - scaled_mid * (second_sum / H))).astype(
        jnp.bfloat16
    )
    grad_rows = lax.all_to_all(d_tri, "row", split_axis=0, concat_axis=1, tiled=True)
    grad_cols = lax.all_to_all(grad_rows, "col", split_axis=1, concat_axis=2, tiled=True)
    d_left = product(
        "cij,cjk->cik", grad_cols, lax.all_gather(right_side, "col", axis=1, tiled=True)
    )
    partial_terms = product("cij,cik->cjk", grad_cols, left_side)
    d_right = lax.psum_scatter(
        partial_terms.astype(jnp.bfloat16), "col", scatter_dimension=1, tiled=True
    ).astype(jnp.float32)
    d_left = d_left.astype(jnp.bfloat16)
    d_right = d_right.astype(jnp.bfloat16)
    if incoming:
        d_left = jnp.swapaxes(d_left, 1, 2)
        d_right = jnp.swapaxes(d_right, 1, 2)
    else:
        d_left, d_right = (
            lax.all_to_all(d_left, "col", split_axis=2, concat_axis=1, tiled=True),
            lax.all_to_all(d_right, "col", split_axis=2, concat_axis=1, tiled=True),
        )
    d_left, d_right = (
        lax.all_to_all(d_left, "row", split_axis=1, concat_axis=0, tiled=True),
        lax.all_to_all(d_right, "row", split_axis=1, concat_axis=0, tiled=True),
    )
    d_hidden = jnp.stack([d_left, d_right]).astype(jnp.float32)
    d_proj = (d_hidden * gating * pair_mask).astype(jnp.bfloat16)
    d_gate = (d_hidden * projected * gating * (1.0 - gating) * pair_mask).astype(jnp.bfloat16)
    grad_proj_w = product("ijc,shij->sch", normed, d_proj)
    grad_gate_w = product("ijc,shij->sch", normed, d_gate)
    partial_input = product("shij,sch->ijc", d_proj, proj_w) + product(
        "shij,sch->ijc", d_gate, gate_w
    )
    d_normed = d_normed + lax.psum(partial_input.astype(jnp.bfloat16), "ch").astype(jnp.float32)
    weighted_in = d_normed * gain_in
    grad_gain_in = jnp.sum(d_normed * scaled_in, (0, 1))
    grad_bias_in = jnp.sum(d_normed, (0, 1))
    d_pair = inverse_in * (
        weighted_in
        - jnp.mean(weighted_in, -1, keepdims=True)
        - scaled_in * jnp.mean(weighted_in * scaled_in, -1, keepdims=True)
    )
    grads = (
        grad_gain_in,
        grad_bias_in,
        grad_proj_w,
        grad_gate_w,
        grad_gain_mid,
        grad_bias_mid,
        grad_out_w,
        grad_outgate_w,
    )
    return (grad_out + d_pair, grads)


def per_device(
    pair,
    cotangent,
    lengths,
    norm_gain,
    norm_bias,
    proj_weight,
    gate_weight,
    mid_gain,
    mid_bias,
    out_weight,
    outgate_weight,
):
    rows_here = pair.shape[0]
    cols_here = pair.shape[1]
    row_ids = lax.axis_index("row") * rows_here + lax.iota(jnp.int32, rows_here)
    col_ids = lax.axis_index("col") * cols_here + lax.iota(jnp.int32, cols_here)
    limit = lengths[0]
    pair_mask = ((row_ids[:, None] < limit) & (col_ids[None, :] < limit)).astype(jnp.float32)
    state = pair
    stash = []
    for layer in range(2):
        weights = (
            norm_gain[layer],
            norm_bias[layer],
            proj_weight[layer],
            gate_weight[layer],
            mid_gain[layer],
            mid_bias[layer],
            out_weight[layer],
            outgate_weight[layer],
        )
        state, saved = forward_module(state, pair_mask, weights, layer == 1)
        stash.append(saved)
    grad_state = cotangent.astype(jnp.float32)
    per_layer = [None, None]
    for layer in (1, 0):
        weights = (
            norm_gain[layer],
            norm_bias[layer],
            proj_weight[layer],
            gate_weight[layer],
            mid_gain[layer],
            mid_bias[layer],
            out_weight[layer],
            outgate_weight[layer],
        )
        grad_state, grads = backward_module(
            grad_state, pair_mask, weights, stash[layer], layer == 1
        )
        per_layer[layer] = grads
    lower = per_layer[0]
    upper = per_layer[1]
    summed = lax.psum(
        (
            lower[0],
            lower[1],
            lower[2],
            lower[3],
            lower[4],
            lower[5],
            lower[6],
            lower[7],
            upper[0],
            upper[1],
            upper[2],
            upper[3],
            upper[4],
            upper[5],
            upper[6],
            upper[7],
        ),
        ("row", "col"),
    )
    per_layer = [summed[0:8], summed[8:16]]
    stacked = [jnp.stack([per_layer[0][index], per_layer[1][index]]) for index in range(8)]
    return (
        state,
        grad_state.astype(jnp.bfloat16),
        stacked[0],
        stacked[1],
        stacked[2],
        stacked[3],
        stacked[4],
        stacked[5],
        stacked[6],
        stacked[7],
    )


def power_of_two(many, few):
    return many > 1 and many & (many - 1) == 0 and few & (few - 1) == 0


def solution(mesh):
    in_specs = (
        P(("grp", "row"), "col", None),
        P(("grp", "row"), "col", None),
        P("grp"),
        P(),
        P(),
        P(None, None, None, "ch"),
        P(None, None, None, "ch"),
        P(None, "ch"),
        P(None, "ch"),
        P(),
        P(),
    )
    out_specs = (
        P(("grp", "row"), "col", None),
        P(("grp", "row"), "col", None),
        P("grp", None),
        P("grp", None),
        P("grp", None, None, "ch"),
        P("grp", None, None, "ch"),
        P("grp", "ch"),
        P("grp", "ch"),
        P("grp", None, None),
        P("grp", None, None),
    )
    many, few = mesh.shape["row"], mesh.shape["col"]
    if mesh.shape["ch"] == 1 and H % (many * few) == 0 and power_of_two(many, few):
        body = functools.partial(grouped_device, many=many, few=few)
    else:
        body = per_device
    return jax.shard_map(
        body, mesh=mesh, in_specs=in_specs, out_specs=out_specs, check_vma=False
    )
```

```python
import functools

import jax
import jax.numpy as jnp
from jax import lax
from jax.experimental import pallas as pl
from jax.experimental.pallas import tpu as pltpu
from jax.sharding import PartitionSpec as P

H = 128


EPS = 1e-05


def product(spec, left, right):
    return jnp.einsum(spec, left, right, preferred_element_type=jnp.float32)


F32 = jnp.float32
BF16 = jnp.bfloat16


def dot(left, right):
    return lax.dot_general(left, right, (((1,), (0,)), ((), ())), preferred_element_type=F32)


def dot_rt(left, right):
    return lax.dot_general(left, right, (((1,), (1,)), ((), ())), preferred_element_type=F32)


def dot_lt(left, right):
    return lax.dot_general(left, right, (((0,), (0,)), ((), ())), preferred_element_type=F32)


def sigmoid(values):
    return 1.0 / (1.0 + jnp.exp(-values))


def norm_rows(values):
    scale = 1.0 / values.shape[0]
    average = jnp.sum(values, 0, keepdims=True) * scale
    centred = values - average
    variance = jnp.sum(centred * centred, 0, keepdims=True) * scale
    inverse = lax.rsqrt(variance + EPS)
    return centred * inverse, inverse


def turned(weight):
    return jnp.transpose(weight.astype(F32)).astype(BF16)


def column(ref, module, lanes):
    row = ref[module : module + 1, :]
    return jnp.transpose(jnp.broadcast_to(row, (lanes, row.shape[1])))


def as_row(total):
    return jnp.sum(jnp.transpose(total), 0, keepdims=True)


def row_mask(lengths_ref, step, rows, lanes):
    limit = lengths_ref[0]
    row_id = lax.axis_index("row") * rows + step
    col_id = lax.axis_index("col") * lanes + lax.broadcasted_iota(jnp.int32, (1, lanes), 1)
    return jnp.where((row_id < limit) & (col_id < limit), 1.0, 0.0).astype(F32)


def load_in_weights(proj_ref, gate_ref, module, scratch):
    width = proj_ref.shape[-1]
    for side in range(2):
        scratch[side * width : (side + 1) * width, :] = turned(proj_ref[module, side])
        scratch[(2 + side) * width : (3 + side) * width, :] = turned(gate_ref[module, side])


def put_rows(scratch, values, step, rows):
    scratch[pl.ds(step, values.shape[0], stride=rows), :] = values


def get_rows(scratch, step, channels, rows):
    return scratch[pl.ds(step, channels, stride=rows), :]


def spread_edges(scratch, out_ref):
    shards, sides, group, rows, lanes = out_ref.shape
    block = shards * group * rows
    for side in range(sides):
        part = scratch[side * block : (side + 1) * block, :]
        out_ref[:, side] = part.reshape(shards, group, rows, lanes).astype(BF16)


def collect_edges(in_ref, scratch):
    shards, sides, group, rows, lanes = in_ref.shape
    block = shards * group * rows
    for side in range(sides):
        scratch[side * block : (side + 1) * block, :] = (
            in_ref[:, side].astype(F32).reshape(block, lanes)
        )


def collect_triangle(in_ref, scratch):
    block = in_ref.size // in_ref.shape[-1]
    scratch[0:block, :] = in_ref[...].astype(F32).reshape(block, in_ref.shape[-1])


def each_row(rows, unroll, body):
    def step_body(step, carry):
        body(step)
        return carry

    lax.fori_loop(0, rows, step_body, 0, unroll=unroll)


def mid_norm(tri):
    scale = 1.0 / tri.shape[0]
    average = jnp.sum(tri, 0, keepdims=True) * scale
    squares = jnp.sum(tri * tri, 0, keepdims=True) * scale
    inverse = lax.rsqrt(squares - average * average + EPS)
    return (tri - average) * inverse, inverse


def norm_backward(weighted, scaled, inverse):
    scale = 1.0 / weighted.shape[0]
    first = jnp.sum(weighted, 0, keepdims=True) * scale
    second = jnp.sum(weighted * scaled, 0, keepdims=True) * scale
    return inverse * (weighted - first - scaled * second)


def save_norm(step, values, scaled_out, inverse_out):
    scaled, inverse = norm_rows(values)
    scaled_out[step] = scaled
    inverse_out[pl.ds(step, 1), :] = inverse
    return scaled


def save_edges(step, normed, in_weights, mask, proj_out, gate_out):
    pre = dot(in_weights, normed)
    half = pre.shape[0] // 2
    gating = sigmoid(pre[half:])
    factor = gating * mask
    value = pre[:half] * factor
    proj_out[step] = factor
    gate_out[step] = value * (1.0 - gating)
    return value


def start_kernel(
    lengths, pair_far, ngain_far, nbias_far, proj_far, gate_far,
    edge_out, normed_out, proj_out, gate_out, scaled_out, inverse_out,
    pair, ngain, nbias, proj_w, gate_w, sems, wts, scr,
):
    far = (proj_far.at[0], gate_far.at[0], ngain_far, nbias_far, pair_far)
    near = (proj_w.at[0], gate_w.at[0], ngain, nbias, pair)
    copies = [
        pltpu.make_async_copy(source, target, sems.at[index])
        for index, (source, target) in enumerate(zip(far, near))
    ]
    for copy in copies:
        copy.start()
    for copy in copies:
        copy.wait()
    rows, lanes, channels = pair.shape
    load_in_weights(proj_w, gate_w, 0, wts)
    gain, bias = column(ngain, 0, lanes), column(nbias, 0, lanes)

    def body(step):
        base = jnp.transpose(pair[step].astype(F32))
        scaled = save_norm(step, base, scaled_out, inverse_out)
        normed = (scaled * gain + bias).astype(BF16)
        normed_out[step] = normed
        mask = row_mask(lengths, step, rows, lanes)
        put_rows(scr, save_edges(step, normed, wts[...], mask, proj_out, gate_out), step, rows)

    each_row(rows, 4, body)
    spread_edges(scr, edge_out)


def between_kernel(
    lengths, tri, pair, normed0, ngain, nbias, mgain, mbias, out_w, outgate_w, proj_w, gate_w,
    edge_out, mid_out, normed_out, proj_out, gate_out, scaled_out, inverse_out,
    outgate_out, scaled_mid_out, inverse_mid_out, wts, scr,
):
    rows, lanes, channels = pair.shape
    load_in_weights(proj_w, gate_w, 1, wts)
    out_t, outgate_t = turned(out_w[0]), turned(outgate_w[0])
    gain, bias = column(ngain, 1, lanes), column(nbias, 1, lanes)
    gain_mid, bias_mid = column(mgain, 0, lanes), column(mbias, 0, lanes)
    collect_triangle(tri, scr)

    def body(step):
        scaled_mid, inverse_mid = mid_norm(get_rows(scr, step, channels, rows))
        scaled_mid_out[step] = scaled_mid
        inverse_mid_out[pl.ds(step, 1), :] = inverse_mid
        unit = (scaled_mid * gain_mid + bias_mid).astype(BF16)
        outer = dot(out_t, unit)
        outgate = sigmoid(dot(outgate_t, normed0[step]))
        outgate_out[step] = outgate
        mid = (jnp.transpose(pair[step].astype(F32)) + outer * outgate).astype(BF16)
        mid_out[step] = mid
        scaled = save_norm(step, mid.astype(F32), scaled_out, inverse_out)
        normed = (scaled * gain + bias).astype(BF16)
        normed_out[step] = normed
        mask = row_mask(lengths, step, rows, lanes)
        put_rows(scr, save_edges(step, normed, wts[...], mask, proj_out, gate_out), step, rows)

    each_row(rows, 4, body)
    spread_edges(scr, edge_out)


def out_weight_grads(unit, d_outer, normed, d_gatepre, out_ref):
    width = unit.shape[0]
    out_ref[0:width, :] = dot_rt(unit[...], d_outer[...]).astype(out_ref.dtype)
    out_ref[width:, :] = dot_rt(normed[...], d_gatepre[...]).astype(out_ref.dtype)


def in_weight_grads(normed_all, d_in_all, out_ref):
    width = normed_all.shape[0]
    for part in range(d_in_all.shape[0] // width):
        block = slice(part * width, (part + 1) * width)
        out_ref[block, :] = dot_rt(normed_all[...], d_in_all[block, :]).astype(out_ref.dtype)


def lane_block(step, lanes):
    return pl.ds(pl.multiple_of(step * lanes, lanes), lanes)


def turn_kernel(
    tri, mid, normed, cot, mgain, mbias, out_w, outgate_w,
    d_tri_out, new_out, grad_out, d_normed_out, weights_out, small_out,
    scr, unit_all, outer_all, normed_all, gate_all, sums,
):
    rows, channels, lanes = mid.shape
    out_t, outgate_t = turned(out_w[1]), turned(outgate_w[1])
    gain_mid, bias_mid = column(mgain, 1, lanes), column(mbias, 1, lanes)
    collect_triangle(tri, scr)
    sums[...] = jnp.zeros_like(sums)

    def body(step):
        here = lane_block(step, lanes)
        grad = jnp.transpose(cot[step].astype(F32))
        grad_out[step] = grad
        outgate = sigmoid(dot(outgate_t, normed[step]))
        gated = grad * outgate
        d_outer = gated.astype(BF16)
        d_unit = dot(out_w[1], d_outer)
        scaled_mid, inverse_mid = mid_norm(get_rows(scr, step, channels, rows))
        put_rows(scr, norm_backward(d_unit * gain_mid, scaled_mid, inverse_mid), step, rows)
        unit = (scaled_mid * gain_mid + bias_mid).astype(BF16)
        outer = dot(out_t, unit)
        new_out[step] = jnp.transpose(mid[step].astype(F32) + outer * outgate).astype(BF16)
        d_gatepre = (gated * outer * (1.0 - outgate)).astype(BF16)
        d_normed_out[step] = dot(outgate_w[1], d_gatepre)
        unit_all[:, here] = unit
        outer_all[:, here] = d_outer
        normed_all[:, here] = normed[step]
        gate_all[:, here] = d_gatepre
        sums[0] += d_unit * scaled_mid
        sums[1] += d_unit

    each_row(rows, 4, body)
    d_tri_out[...] = scr[...].reshape(d_tri_out.shape).astype(BF16)
    out_weight_grads(unit_all, outer_all, normed_all, gate_all, weights_out)
    for index in range(2):
        small_out[index : index + 1, :] = as_row(sums[index])


def in_normed(d_in, all_w, proj_w, gate_w):
    width = proj_w.shape[-1]
    total = all_w
    for side in range(2):
        total = total + dot(proj_w[side], d_in[side * width : (side + 1) * width])
        total = total + dot(gate_w[side], d_in[(2 + side) * width : (3 + side) * width])
    return total


def middle_kernel(
    d_edge, proj_factor, gate_factor, d_normed_gate, scaled_in, inverse_in, cot, outgate,
    scaled_mid, inverse_mid, normed0, normed1, ngain, mgain, mbias, proj_w, gate_w, out_w,
    outgate_w,
    d_tri_out, grad_out, d_normed_out, out_weights, in_weights, small_out,
    scr, scr_tri, unit_all, outer_all, normed_all, gate_all, upper_all, d_in_all, sums,
):
    rows, channels, lanes = cot.shape
    out_t = turned(out_w[0])
    gain = column(ngain, 1, lanes)
    gain_mid, bias_mid = column(mgain, 0, lanes), column(mbias, 0, lanes)
    collect_edges(d_edge, scr)
    sums[...] = jnp.zeros_like(sums)
    half = proj_factor.shape[1]

    def upper(step):
        place = lane_block(step, lanes)
        here = get_rows(scr, step, half, rows)
        d_proj = (here * proj_factor[step]).astype(BF16)
        d_gate = (here * gate_factor[step]).astype(BF16)
        d_in = jnp.concatenate([d_proj, d_gate], axis=0)
        d_in_all[:, place] = d_in
        upper_all[:, place] = normed1[step]
        d_normed = in_normed(d_in, d_normed_gate[step], proj_w[1], gate_w[1])
        scaled = scaled_in[step]
        sums[2] += d_normed * scaled
        sums[3] += d_normed
        grad_out[step] = cot[step] + norm_backward(
            d_normed * gain, scaled, inverse_in[pl.ds(step, 1), :]
        )

    def lower(step):
        place = lane_block(step, lanes)
        gate = outgate[step]
        gated = grad_out[step] * gate
        d_outer = gated.astype(BF16)
        d_unit = dot(out_w[0], d_outer)
        scaled = scaled_mid[step]
        d_tri = norm_backward(d_unit * gain_mid, scaled, inverse_mid[pl.ds(step, 1), :])
        put_rows(scr_tri, d_tri, step, rows)
        unit = (scaled * gain_mid + bias_mid).astype(BF16)
        outer = dot(out_t, unit)
        d_gatepre = (gated * outer * (1.0 - gate)).astype(BF16)
        d_normed_out[step] = dot(outgate_w[0], d_gatepre)
        unit_all[:, place] = unit
        outer_all[:, place] = d_outer
        normed_all[:, place] = normed0[step]
        gate_all[:, place] = d_gatepre
        sums[0] += d_unit * scaled
        sums[1] += d_unit

    each_row(rows, 4, upper)
    each_row(rows, 4, lower)
    d_tri_out[...] = scr_tri[...].reshape(d_tri_out.shape).astype(BF16)
    out_weight_grads(unit_all, outer_all, normed_all, gate_all, out_weights)
    in_weight_grads(upper_all, d_in_all, in_weights)
    for index in range(4):
        small_out[index : index + 1, :] = as_row(sums[index])


def split_cores(all_rows, own_out, other_out, few):
    chips, share, width = own_out.shape
    view = all_rows.reshape(chips // few, 2, few, share, width)
    core = lax.rem(lax.axis_index("row"), 2)
    own_out[...] = view[:, core].reshape(own_out.shape)
    other_out[...] = view[:, 1 - core].reshape(other_out.shape)


def finish_kernel(
    few, d_edge, proj_factor, gate_factor, normed, out0, in1, out1,
    own_out, other_out, d_in_out, scr, normed_all, d_in_all, packed,
):
    rows, half, lanes = proj_factor.shape
    collect_edges(d_edge, scr)

    def body(step):
        place = lane_block(step, lanes)
        here = get_rows(scr, step, half, rows)
        d_proj = (here * proj_factor[step]).astype(BF16)
        d_gate = (here * gate_factor[step]).astype(BF16)
        d_in = jnp.concatenate([d_proj, d_gate], axis=0)
        d_in_out[step] = d_in
        d_in_all[:, place] = d_in
        normed_all[:, place] = normed[step]

    each_row(rows, 4, body)
    first, second, third = d_in_all.shape[0], out0.shape[0], in1.shape[0]
    in_weight_grads(normed_all, d_in_all, packed.at[0:first])
    packed[first : first + second, :] = out0[...]
    packed[first + second : first + second + third, :] = in1[...]
    packed[first + second + third :, :] = out1[...]
    split_cores(packed, own_out, other_out, few)


def behind_finish_kernel(
    d_in, d_normed_gate, scaled_in, inverse_in, grad, ngain, proj_w, gate_w,
    grad_out, small_out, sums,
):
    rows, channels, lanes = grad.shape
    gain = column(ngain, 0, lanes)
    sums[...] = jnp.zeros_like(sums)

    def body(step):
        d_normed = in_normed(d_in[step], d_normed_gate[step], proj_w[0], gate_w[0])
        scaled = scaled_in[step]
        sums[0] += d_normed * scaled
        sums[1] += d_normed
        total = grad[step] + norm_backward(d_normed * gain, scaled, inverse_in[pl.ds(step, 1), :])
        grad_out[step] = jnp.transpose(total).astype(BF16)

    each_row(rows, 4, body)
    for index in range(2):
        small_out[index : index + 1, :] = as_row(sums[index])


def add_kernel(first, second, out_ref):
    out_ref[...] = (first[...].astype(F32) + second[...].astype(F32)).astype(BF16)


def sum_kernel(parts, small0, small_middle, small1, shared_out):
    chips, share, width = parts.shape
    own = jnp.sum(parts[...].astype(F32), axis=0).astype(BF16)
    small = jnp.concatenate(
        [small0[...], small_middle[0:2], small_middle[2:4], small1[...]], axis=0
    )
    high = small.astype(BF16).astype(F32)
    extra = jnp.concatenate([high, small - high], axis=0).astype(BF16)
    for chip in range(chips):
        shared_out[chip, 0:share] = own
        shared_out[chip, share:] = extra


def unpack_kernel(
    share, few, own, other, proj_out, gate_out, out_out, outgate_out,
    norm_gain_out, norm_bias_out, mid_gain_out, mid_bias_out, weights,
):
    chips, _, width = own.shape
    core = lax.rem(lax.axis_index("row"), 2)
    view = weights.reshape(chips // few, 2, few, share, width)
    block = (chips // few, few, share, width)
    view[:, core] = own[:, 0:share].astype(F32).reshape(block)
    view[:, 1 - core] = other[:, 0:share].astype(F32).reshape(block)
    mine = jnp.sum(own[:, share:].astype(F32), axis=0)
    theirs = jnp.sum(other[:, share:].astype(F32), axis=0)
    total = mine + theirs
    total = total[0:8] + total[8:16]
    for module in range(2):
        for index, out in enumerate((norm_gain_out, norm_bias_out, mid_gain_out, mid_bias_out)):
            at = 4 * module + index
            out[module : module + 1, :] = total[at : at + 1]
        blocks = [
            weights[(6 * module + part) * width : (6 * module + part + 1) * width, :]
            for part in range(6)
        ]
        for side in range(2):
            proj_out[module, side] = blocks[side]
            gate_out[module, side] = blocks[2 + side]
        out_out[module] = blocks[4]
        outgate_out[module] = blocks[5]


def triangle_kernel(incoming, edge, tri_out):
    many, few, _, group, rows, lanes = edge.shape

    def whole(side, channel):
        parts = [edge[:, c, side, channel].reshape(many * rows, lanes) for c in range(few)]
        return jnp.concatenate(parts, axis=1)

    for channel in range(group):
        left, right = whole(0, channel), whole(1, channel)
        tri = (dot_lt if incoming else dot_rt)(left, right).astype(BF16)
        for c in range(few):
            part = tri[:, c * lanes : (c + 1) * lanes]
            tri_out[:, c, channel] = part.reshape(many, rows, lanes)


def edge_grad_kernel(incoming, edge, d_tri, grad_out):
    many, few, _, group, rows, lanes = edge.shape

    def whole(ref, *index):
        parts = [ref[(slice(None), c) + index].reshape(many * rows, lanes) for c in range(few)]
        return jnp.concatenate(parts, axis=1)

    for channel in range(group):
        left, right = whole(edge, 0, channel), whole(edge, 1, channel)
        grad = whole(d_tri, channel)
        if incoming:
            d_left, d_right = dot_rt(right, grad), dot(left, grad)
        else:
            d_left, d_right = dot(grad, right), dot_lt(grad, left)
        for side, value in ((0, d_left), (1, d_right)):
            value = value.astype(BF16)
            for c in range(few):
                part = value[:, c * lanes : (c + 1) * lanes]
                grad_out[:, c, side, channel] = part.reshape(many, rows, lanes)


SCALARS = pl.BlockSpec(memory_space=pltpu.SMEM)
VECTORS = pl.BlockSpec(memory_space=pltpu.VMEM)
FAR = pl.BlockSpec(memory_space=pltpu.HBM)


def call(kernel, name, outs, args, scratch=(), flops=0, scalars=0, grant=16, far=False):
    shapes = [jax.ShapeDtypeStruct(shape, dtype) for shape, dtype in outs]
    moved = sum(a.size * a.dtype.itemsize for a in list(args) + shapes)
    rest = FAR if far else VECTORS
    return pl.pallas_call(
        kernel,
        name=name,
        out_shape=shapes,
        in_specs=[SCALARS] * scalars + [rest] * (len(args) - scalars),
        out_specs=[VECTORS] * len(shapes),
        scratch_shapes=[
            pltpu.VMEM(*item) if isinstance(item, tuple) else item for item in scratch
        ],
        compiler_params=pltpu.CompilerParams(vmem_limit_bytes=grant * 1024 * 1024),
        cost_estimate=pl.CostEstimate(flops=flops, bytes_accessed=moved, transcendentals=0),
    )(*args)


def exchange(values):
    return lax.all_to_all(values, ("row", "col"), split_axis=0, concat_axis=0, tiled=True)


def swap_cores(values, many, few):
    pairs = [(index, index ^ few) for index in range(many * few)]
    return lax.ppermute(values, ("row", "col"), pairs)


def exchange_chips(values, many, few):
    groups = [
        [row * few + col for row in range(core, many, 2) for col in range(few)] for core in range(2)
    ]
    return lax.all_to_all(
        values, ("row", "col"), split_axis=0, concat_axis=0, axis_index_groups=groups, tiled=True
    )


def grouped_device(
    pair, cotangent, lengths, ngain, nbias, proj_w, gate_w, mgain, mbias, out_w, outgate_w,
    *, many, few,
):
    rows, lanes, channels = pair.shape
    shards = many * few
    group = H // shards
    edge = ((shards, 2, group, rows, lanes), BF16)
    grid = ((many, few, 2, group, rows, lanes), BF16)
    tri = ((shards, group, rows, lanes), BF16)
    tri_grid = ((many, few, group, rows, lanes), BF16)
    tile = ((rows, channels, lanes), BF16)
    wide = ((rows, channels, lanes), F32)
    row = ((rows, lanes), F32)
    factor = ((rows, 2 * H, lanes), F32)
    d_in = ((rows, 4 * H, lanes), BF16)
    wts = ((4 * H, channels), BF16)
    big = ((2 * H * rows, lanes), F32)
    mid = ((H * rows, lanes), F32)
    positions = rows * lanes
    flat = ((H, positions), BF16)
    flat_in = ((4 * H, positions), BF16)
    out_rows = ((2 * H, channels), BF16)
    in_rows = ((4 * H, H), BF16)
    triangle = 2 * group * (many * rows) ** 2 * (few * lanes)
    dense = 2 * positions * channels * H

    def sums(count):
        return ((count, H, lanes), F32)

    def small(count):
        return ((count, H), F32)

    saved = [tile, factor, factor, wide, row]
    far = [
        pltpu.with_memory_space_constraint(item, pltpu.HBM)
        for item in (pair, ngain, nbias, proj_w, gate_w)
    ]
    sent, normed0, *factors0 = call(
        start_kernel, "start", [edge, *saved], [lengths, *far],
        [(pair.shape, BF16), (ngain.shape, F32), (nbias.shape, F32), (proj_w.shape, BF16),
         (gate_w.shape, BF16), pltpu.SemaphoreType.DMA((5,)), wts, big],
        4 * dense, 1, far=True,
    )
    edge0 = exchange(sent).reshape(grid[0])
    (here,) = call(
        functools.partial(triangle_kernel, False), "outgoing", [tri_grid], [edge0], (), triangle,
    )
    tri0 = exchange(here.reshape(tri[0]))
    sent, mid_t, normed1, *factors1, outgate0, scaled_mid0, inverse_mid0 = call(
        between_kernel, "between", [edge, tile, *saved, wide, wide, row],
        [lengths, tri0, pair, normed0, ngain, nbias, mgain, mbias, out_w, outgate_w, proj_w,
         gate_w],
        [wts, big], 6 * dense, 1,
    )
    edge1 = exchange(sent).reshape(grid[0])
    (here,) = call(
        functools.partial(triangle_kernel, True), "incoming", [tri_grid], [edge1], (), triangle,
    )
    tri1 = exchange(here.reshape(tri[0]))
    sent, new_pair, cot_t, d_normed_gate1, out_grads1, small1 = call(
        turn_kernel, "turn", [tri, (pair.shape, BF16), wide, wide, out_rows, small(2)],
        [tri1, mid_t, normed1, cotangent, mgain, mbias, out_w, outgate_w],
        [mid, flat, flat, flat, flat, sums(2)], 6 * dense,
    )
    d_tri1 = exchange(sent).reshape(tri_grid[0])
    (sent,) = call(
        functools.partial(edge_grad_kernel, True), "incoming_grad", [grid], [edge1, d_tri1],
        (), 2 * triangle,
    )
    d_edge1 = exchange(sent.reshape(edge[0]))
    proj_factor1, gate_factor1, scaled1, inverse1 = factors1
    sent, grad, d_normed_gate0, out_grads0, in_grads1, small_middle = call(
        middle_kernel, "middle", [tri, wide, wide, out_rows, in_rows, small(4)],
        [d_edge1, proj_factor1, gate_factor1, d_normed_gate1, scaled1, inverse1, cot_t, outgate0,
         scaled_mid0, inverse_mid0, normed0, normed1, ngain, mgain, mbias, proj_w, gate_w, out_w,
         outgate_w],
        [big, mid, flat, flat, flat, flat, flat, flat_in, sums(4)], 13 * dense,
    )
    d_tri0 = exchange(sent).reshape(tri_grid[0])
    (sent,) = call(
        functools.partial(edge_grad_kernel, False), "outgoing_grad", [grid], [edge0, d_tri0],
        (), 2 * triangle,
    )
    d_edge0 = exchange(sent.reshape(edge[0]))
    share = 12 * H // shards
    chips = shards // 2
    proj_factor0, gate_factor0, scaled0, inverse0 = factors0
    held = ((chips, share, H), BF16)
    own, other, d_in0 = call(
        functools.partial(finish_kernel, few), "finish", [held, held, d_in],
        [d_edge0, proj_factor0, gate_factor0, normed0, out_grads0, in_grads1, out_grads1],
        [big, flat, flat_in, ((12 * H, H), BF16)], 4 * dense,
    )
    other = swap_cores(other, many, few)
    grad_pair, small0 = call(
        behind_finish_kernel, "behind_finish", [(pair.shape, BF16), small(2)],
        [d_in0, d_normed_gate0, scaled0, inverse0, grad, ngain, proj_w, gate_w], [sums(2)],
        4 * dense,
    )
    (own,) = call(add_kernel, "add_cores", [held], [own, other])
    parts = exchange_chips(own, many, few)
    (shared,) = call(
        sum_kernel, "sum_weights", [((chips, share + 16, H), BF16)],
        [parts, small0, small_middle, small1],
    )
    shared = exchange_chips(shared, many, few)
    other = swap_cores(shared, many, few)
    grad_proj, grad_gate, grad_out, grad_outgate, *vectors = call(
        functools.partial(unpack_kernel, share, few), "unpack",
        [(proj_w.shape, F32), (gate_w.shape, F32), (out_w.shape, F32), (outgate_w.shape, F32),
         (ngain.shape, F32), (nbias.shape, F32), (mgain.shape, F32), (mbias.shape, F32)],
        [shared, other], [((12 * H, H), F32)],
    )
    return (
        new_pair,
        grad_pair,
        vectors[0],
        vectors[1],
        grad_proj,
        grad_gate,
        vectors[2],
        vectors[3],
        grad_out,
        grad_outgate,
    )


def norm_channels(values):
    average = jnp.mean(values, -1, keepdims=True)
    centred = values - average
    variance = jnp.mean(centred * centred, -1, keepdims=True)
    inverse = lax.rsqrt(variance + EPS)
    return (centred * inverse, inverse)


def forward_module(pair_in, pair_mask, weights, incoming):
    gain_in, bias_in, proj_w, gate_w, gain_mid, bias_mid, out_w, outgate_w = weights
    scaled_in, inverse_in = norm_channels(pair_in.astype(jnp.float32))
    normed = (scaled_in * gain_in + bias_in).astype(jnp.bfloat16)
    projected = product("ijc,sch->shij", normed, proj_w)
    gating = jax.nn.sigmoid(product("ijc,sch->shij", normed, gate_w))
    hidden = (projected * gating * pair_mask).astype(jnp.bfloat16)
    left_side, right_side = (
        lax.all_to_all(hidden[0], "row", split_axis=0, concat_axis=1, tiled=True),
        lax.all_to_all(hidden[1], "row", split_axis=0, concat_axis=1, tiled=True),
    )
    if incoming:
        left_side = jnp.swapaxes(left_side, 1, 2)
        right_side = jnp.swapaxes(right_side, 1, 2)
    else:
        left_side, right_side = (
            lax.all_to_all(left_side, "col", split_axis=1, concat_axis=2, tiled=True),
            lax.all_to_all(right_side, "col", split_axis=1, concat_axis=2, tiled=True),
        )
    triangle = product(
        "cik,cjk->cij", left_side, lax.all_gather(right_side, "col", axis=1, tiled=True)
    ).astype(jnp.bfloat16)
    triangle = lax.all_to_all(
        lax.all_to_all(triangle, "col", split_axis=2, concat_axis=1, tiled=True),
        "row",
        split_axis=1,
        concat_axis=0,
        tiled=True,
    )
    tri_values = triangle.astype(jnp.float32)
    total, squares = lax.psum((jnp.sum(tri_values, 0), jnp.sum(tri_values * tri_values, 0)), "ch")
    average = total / H
    inverse_mid = lax.rsqrt(squares / H - average * average + EPS)
    scaled_mid = (tri_values - average) * inverse_mid
    unit = (scaled_mid * gain_mid[:, None, None] + bias_mid[:, None, None]).astype(jnp.bfloat16)
    unit_full = lax.all_gather(unit, "ch", axis=0, tiled=True)
    outer = product("hij,hc->ijc", unit_full, out_w)
    outgate = jax.nn.sigmoid(product("ijc,cd->ijd", normed, outgate_w))
    result = (pair_in.astype(jnp.float32) + outer * outgate).astype(jnp.bfloat16)
    saved = (
        scaled_in,
        inverse_in,
        normed,
        projected,
        gating,
        left_side,
        right_side,
        scaled_mid,
        inverse_mid,
        unit_full,
        outer,
        outgate,
    )
    return (result, saved)


def backward_module(grad_out, pair_mask, weights, saved, incoming):
    gain_in, bias_in, proj_w, gate_w, gain_mid, bias_mid, out_w, outgate_w = weights
    (
        scaled_in,
        inverse_in,
        normed,
        projected,
        gating,
        left_side,
        right_side,
        scaled_mid,
        inverse_mid,
        unit_full,
        outer,
        outgate,
    ) = saved
    d_outer = (grad_out * outgate).astype(jnp.bfloat16)
    d_gatepre = (grad_out * outer * outgate * (1.0 - outgate)).astype(jnp.bfloat16)
    grad_out_w = product("hij,ijc->hc", unit_full, d_outer)
    grad_outgate_w = product("ijc,ijd->cd", normed, d_gatepre)
    width = gain_mid.shape[0]
    own_rows = lax.dynamic_slice_in_dim(out_w, lax.axis_index("ch") * width, width, 0)
    d_unit = product("ijc,hc->hij", d_outer, own_rows)
    d_normed = product("ijd,cd->ijc", d_gatepre, outgate_w)
    weighted = d_unit * gain_mid[:, None, None]
    grad_gain_mid = jnp.sum(d_unit * scaled_mid, (1, 2))
    grad_bias_mid = jnp.sum(d_unit, (1, 2))
    first_sum, second_sum = lax.psum(
        (jnp.sum(weighted, 0), jnp.sum(weighted * scaled_mid, 0)), "ch"
    )
    d_tri = (inverse_mid * (weighted - first_sum / H - scaled_mid * (second_sum / H))).astype(
        jnp.bfloat16
    )
    grad_rows = lax.all_to_all(d_tri, "row", split_axis=0, concat_axis=1, tiled=True)
    grad_cols = lax.all_to_all(grad_rows, "col", split_axis=1, concat_axis=2, tiled=True)
    d_left = product(
        "cij,cjk->cik", grad_cols, lax.all_gather(right_side, "col", axis=1, tiled=True)
    )
    partial_terms = product("cij,cik->cjk", grad_cols, left_side)
    d_right = lax.psum_scatter(
        partial_terms.astype(jnp.bfloat16), "col", scatter_dimension=1, tiled=True
    ).astype(jnp.float32)
    d_left = d_left.astype(jnp.bfloat16)
    d_right = d_right.astype(jnp.bfloat16)
    if incoming:
        d_left = jnp.swapaxes(d_left, 1, 2)
        d_right = jnp.swapaxes(d_right, 1, 2)
    else:
        d_left, d_right = (
            lax.all_to_all(d_left, "col", split_axis=2, concat_axis=1, tiled=True),
            lax.all_to_all(d_right, "col", split_axis=2, concat_axis=1, tiled=True),
        )
    d_left, d_right = (
        lax.all_to_all(d_left, "row", split_axis=1, concat_axis=0, tiled=True),
        lax.all_to_all(d_right, "row", split_axis=1, concat_axis=0, tiled=True),
    )
    d_hidden = jnp.stack([d_left, d_right]).astype(jnp.float32)
    d_proj = (d_hidden * gating * pair_mask).astype(jnp.bfloat16)
    d_gate = (d_hidden * projected * gating * (1.0 - gating) * pair_mask).astype(jnp.bfloat16)
    grad_proj_w = product("ijc,shij->sch", normed, d_proj)
    grad_gate_w = product("ijc,shij->sch", normed, d_gate)
    partial_input = product("shij,sch->ijc", d_proj, proj_w) + product(
        "shij,sch->ijc", d_gate, gate_w
    )
    d_normed = d_normed + lax.psum(partial_input.astype(jnp.bfloat16), "ch").astype(jnp.float32)
    weighted_in = d_normed * gain_in
    grad_gain_in = jnp.sum(d_normed * scaled_in, (0, 1))
    grad_bias_in = jnp.sum(d_normed, (0, 1))
    d_pair = inverse_in * (
        weighted_in
        - jnp.mean(weighted_in, -1, keepdims=True)
        - scaled_in * jnp.mean(weighted_in * scaled_in, -1, keepdims=True)
    )
    grads = (
        grad_gain_in,
        grad_bias_in,
        grad_proj_w,
        grad_gate_w,
        grad_gain_mid,
        grad_bias_mid,
        grad_out_w,
        grad_outgate_w,
    )
    return (grad_out + d_pair, grads)


def per_device(
    pair,
    cotangent,
    lengths,
    norm_gain,
    norm_bias,
    proj_weight,
    gate_weight,
    mid_gain,
    mid_bias,
    out_weight,
    outgate_weight,
):
    rows_here = pair.shape[0]
    cols_here = pair.shape[1]
    row_ids = lax.axis_index("row") * rows_here + lax.iota(jnp.int32, rows_here)
    col_ids = lax.axis_index("col") * cols_here + lax.iota(jnp.int32, cols_here)
    limit = lengths[0]
    pair_mask = ((row_ids[:, None] < limit) & (col_ids[None, :] < limit)).astype(jnp.float32)
    state = pair
    stash = []
    for layer in range(2):
        weights = (
            norm_gain[layer],
            norm_bias[layer],
            proj_weight[layer],
            gate_weight[layer],
            mid_gain[layer],
            mid_bias[layer],
            out_weight[layer],
            outgate_weight[layer],
        )
        state, saved = forward_module(state, pair_mask, weights, layer == 1)
        stash.append(saved)
    grad_state = cotangent.astype(jnp.float32)
    per_layer = [None, None]
    for layer in (1, 0):
        weights = (
            norm_gain[layer],
            norm_bias[layer],
            proj_weight[layer],
            gate_weight[layer],
            mid_gain[layer],
            mid_bias[layer],
            out_weight[layer],
            outgate_weight[layer],
        )
        grad_state, grads = backward_module(
            grad_state, pair_mask, weights, stash[layer], layer == 1
        )
        per_layer[layer] = grads
    lower = per_layer[0]
    upper = per_layer[1]
    summed = lax.psum(
        (
            lower[0],
            lower[1],
            lower[2],
            lower[3],
            lower[4],
            lower[5],
            lower[6],
            lower[7],
            upper[0],
            upper[1],
            upper[2],
            upper[3],
            upper[4],
            upper[5],
            upper[6],
            upper[7],
        ),
        ("row", "col"),
    )
    per_layer = [summed[0:8], summed[8:16]]
    stacked = [jnp.stack([per_layer[0][index], per_layer[1][index]]) for index in range(8)]
    return (
        state,
        grad_state.astype(jnp.bfloat16),
        stacked[0],
        stacked[1],
        stacked[2],
        stacked[3],
        stacked[4],
        stacked[5],
        stacked[6],
        stacked[7],
    )


def solution(mesh):
    in_specs = (
        P(("grp", "row"), "col", None),
        P(("grp", "row"), "col", None),
        P("grp"),
        P(),
        P(),
        P(None, None, None, "ch"),
        P(None, None, None, "ch"),
        P(None, "ch"),
        P(None, "ch"),
        P(),
        P(),
    )
    out_specs = (
        P(("grp", "row"), "col", None),
        P(("grp", "row"), "col", None),
        P("grp", None),
        P("grp", None),
        P("grp", None, None, "ch"),
        P("grp", None, None, "ch"),
        P("grp", "ch"),
        P("grp", "ch"),
        P("grp", None, None),
        P("grp", None, None),
    )
    many, few = mesh.shape["row"], mesh.shape["col"]
    if mesh.shape["ch"] == 1 and H % (many * few) == 0 and many % 2 == 0 and few & (few - 1) == 0:
        body = functools.partial(grouped_device, many=many, few=few)
    else:
        body = per_device
    return jax.shard_map(
        body, mesh=mesh, in_specs=in_specs, out_specs=out_specs, check_vma=False
    )
```

```python
import functools

import jax
import jax.numpy as jnp
from jax import lax
from jax.experimental import pallas as pl
from jax.experimental.pallas import tpu as pltpu
from jax.sharding import PartitionSpec as P

H = 128


EPS = 1e-05


def product(spec, left, right):
    return jnp.einsum(spec, left, right, preferred_element_type=jnp.float32)


F32 = jnp.float32
BF16 = jnp.bfloat16


def dot(left, right):
    return lax.dot_general(left, right, (((1,), (0,)), ((), ())), preferred_element_type=F32)


def dot_rt(left, right):
    return lax.dot_general(left, right, (((1,), (1,)), ((), ())), preferred_element_type=F32)


def dot_lt(left, right):
    return lax.dot_general(left, right, (((0,), (0,)), ((), ())), preferred_element_type=F32)


def sigmoid(values):
    return 0.5 * jnp.tanh(0.5 * values) + 0.5


def norm_rows(values):
    scale = 1.0 / values.shape[0]
    average = jnp.sum(values, 0, keepdims=True) * scale
    centred = values - average
    variance = jnp.sum(centred * centred, 0, keepdims=True) * scale
    inverse = lax.rsqrt(variance + EPS)
    return centred * inverse, inverse


def turned(weight):
    return jnp.transpose(weight.astype(F32)).astype(BF16)


def column(ref, module, lanes):
    row = ref[module : module + 1, :]
    return jnp.transpose(jnp.broadcast_to(row, (lanes, row.shape[1])))


def as_row(total):
    return jnp.sum(jnp.transpose(total), 0, keepdims=True)


def row_mask(lengths_ref, step, rows, lanes):
    limit = lengths_ref[0]
    row_id = lax.axis_index("row") * rows + step
    col_id = lax.axis_index("col") * lanes + lax.broadcasted_iota(jnp.int32, (1, lanes), 1)
    return jnp.where((row_id < limit) & (col_id < limit), 1.0, 0.0).astype(F32)


def load_in_weights(proj_ref, gate_ref, module, scratch):
    width = proj_ref.shape[-1]
    for side in range(2):
        scratch[side * width : (side + 1) * width, :] = turned(proj_ref[module, side])
        scratch[(2 + side) * width : (3 + side) * width, :] = turned(gate_ref[module, side])


def put_rows(scratch, values, step, rows):
    scratch[pl.ds(step, values.shape[0], stride=rows), :] = values


def get_rows(scratch, step, channels, rows):
    return scratch[pl.ds(step, channels, stride=rows), :]


def spread_edges(scratch, out_ref):
    shards, sides, group, rows, lanes = out_ref.shape
    block = shards * group * rows
    for side in range(sides):
        part = scratch[side * block : (side + 1) * block, :]
        out_ref[:, side] = part.reshape(shards, group, rows, lanes).astype(BF16)


def collect_edges(in_ref, scratch):
    shards, sides, group, rows, lanes = in_ref.shape
    block = shards * group * rows
    for side in range(sides):
        scratch[side * block : (side + 1) * block, :] = (
            in_ref[:, side].astype(F32).reshape(block, lanes)
        )


def collect_triangle(in_ref, scratch):
    block = in_ref.size // in_ref.shape[-1]
    scratch[0:block, :] = in_ref[...].astype(F32).reshape(block, in_ref.shape[-1])


def each_row(rows, unroll, body, sums=None):
    def several(block, carry):
        parts = [body(block * unroll + step) for step in range(unroll)]
        for index in range(0 if sums is None else sums.shape[0]):
            total = parts[0][index]
            for part in parts[1:]:
                total = total + part[index]
            sums[index] += total
        return carry

    lax.fori_loop(0, rows // unroll, several, 0)


def mid_norm(tri):
    scale = 1.0 / tri.shape[0]
    average = jnp.sum(tri, 0, keepdims=True) * scale
    squares = jnp.sum(tri * tri, 0, keepdims=True) * scale
    inverse = lax.rsqrt(squares - average * average + EPS)
    return (tri - average) * inverse, inverse


def norm_backward(weighted, scaled, inverse):
    scale = 1.0 / weighted.shape[0]
    first = jnp.sum(weighted, 0, keepdims=True) * scale
    second = jnp.sum(weighted * scaled, 0, keepdims=True) * scale
    return inverse * (weighted - first - scaled * second)


def save_norm(step, values, scaled_out, inverse_out):
    scaled, inverse = norm_rows(values)
    scaled_out[step] = scaled
    inverse_out[pl.ds(step, 1), :] = inverse
    return scaled


def save_edges(step, normed, in_weights, mask, proj_out, gate_out):
    pre = dot(in_weights, normed)
    half = pre.shape[0] // 2
    gating = sigmoid(pre[half:])
    factor = gating * mask
    value = pre[:half] * factor
    proj_out[step] = factor
    gate_out[step] = value * (1.0 - gating)
    return value


def start_kernel(
    lengths, pair_far, ngain_far, nbias_far, proj_far, gate_far,
    edge_out, normed_out, proj_out, gate_out, scaled_out, inverse_out, mask_out,
    pair, ngain, nbias, proj_w, gate_w, sems, wts, scr,
):
    far = (proj_far.at[0], gate_far.at[0], ngain_far, nbias_far, pair_far)
    near = (proj_w.at[0], gate_w.at[0], ngain, nbias, pair)
    copies = [
        pltpu.make_async_copy(source, target, sems.at[index])
        for index, (source, target) in enumerate(zip(far, near))
    ]
    for copy in copies:
        copy.start()
    for copy in copies:
        copy.wait()
    rows, lanes, channels = pair.shape
    load_in_weights(proj_w, gate_w, 0, wts)
    gain, bias = column(ngain, 0, lanes), column(nbias, 0, lanes)

    def body(step):
        base = jnp.transpose(pair[step].astype(F32))
        scaled = save_norm(step, base, scaled_out, inverse_out)
        normed = (scaled * gain + bias).astype(BF16)
        normed_out[step] = normed
        mask = row_mask(lengths, step, rows, lanes)
        mask_out[pl.ds(step, 1), :] = mask
        put_rows(scr, save_edges(step, normed, wts[...], mask, proj_out, gate_out), step, rows)

    each_row(rows, 4, body)
    spread_edges(scr, edge_out)


def between_kernel(
    mask_all, tri, pair, normed0, ngain, nbias, mgain, mbias, out_w, outgate_w, proj_w, gate_w,
    edge_out, mid_out, normed_out, proj_out, gate_out, scaled_out, inverse_out,
    outgate_out, scaled_mid_out, inverse_mid_out, wts, scr,
):
    rows, lanes, channels = pair.shape
    load_in_weights(proj_w, gate_w, 1, wts)
    out_t, outgate_t = turned(out_w[0]), turned(outgate_w[0])
    gain, bias = column(ngain, 1, lanes), column(nbias, 1, lanes)
    gain_mid, bias_mid = column(mgain, 0, lanes), column(mbias, 0, lanes)
    collect_triangle(tri, scr)

    def body(step):
        scaled_mid, inverse_mid = mid_norm(get_rows(scr, step, channels, rows))
        scaled_mid_out[step] = scaled_mid
        inverse_mid_out[pl.ds(step, 1), :] = inverse_mid
        unit = (scaled_mid * gain_mid + bias_mid).astype(BF16)
        outer = dot(out_t, unit)
        outgate = sigmoid(dot(outgate_t, normed0[step]))
        outgate_out[step] = outgate
        mid = (jnp.transpose(pair[step].astype(F32)) + outer * outgate).astype(BF16)
        mid_out[step] = mid
        scaled = save_norm(step, mid.astype(F32), scaled_out, inverse_out)
        normed = (scaled * gain + bias).astype(BF16)
        normed_out[step] = normed
        mask = mask_all[pl.ds(step, 1), :]
        put_rows(scr, save_edges(step, normed, wts[...], mask, proj_out, gate_out), step, rows)

    each_row(rows, 4, body)
    spread_edges(scr, edge_out)


def out_weight_grads(unit, d_outer, normed, d_gatepre, out_ref):
    width = unit.shape[0]
    out_ref[0:width, :] = dot_rt(unit[...], d_outer[...]).astype(out_ref.dtype)
    out_ref[width:, :] = dot_rt(normed[...], d_gatepre[...]).astype(out_ref.dtype)


def in_weight_grads(normed_all, d_in_all, out_ref):
    width = normed_all.shape[0]
    for part in range(d_in_all.shape[0] // width):
        block = slice(part * width, (part + 1) * width)
        out_ref[block, :] = dot_rt(normed_all[...], d_in_all[block, :]).astype(out_ref.dtype)


def lane_block(step, lanes):
    return pl.ds(pl.multiple_of(step * lanes, lanes), lanes)


def turn_kernel(
    tri, mid, normed, cot, mgain, mbias, out_w, outgate_w,
    d_tri_out, new_out, grad_out, d_normed_out, weights_out, small_out,
    scr, unit_all, outer_all, normed_all, gate_all, sums,
):
    rows, channels, lanes = mid.shape
    out_t, outgate_t = turned(out_w[1]), turned(outgate_w[1])
    gain_mid, bias_mid = column(mgain, 1, lanes), column(mbias, 1, lanes)
    collect_triangle(tri, scr)
    sums[...] = jnp.zeros_like(sums)

    def body(step):
        here = lane_block(step, lanes)
        grad = jnp.transpose(cot[step].astype(F32))
        grad_out[step] = grad
        outgate = sigmoid(dot(outgate_t, normed[step]))
        gated = grad * outgate
        d_outer = gated.astype(BF16)
        d_unit = dot(out_w[1], d_outer)
        scaled_mid, inverse_mid = mid_norm(get_rows(scr, step, channels, rows))
        put_rows(scr, norm_backward(d_unit * gain_mid, scaled_mid, inverse_mid), step, rows)
        unit = (scaled_mid * gain_mid + bias_mid).astype(BF16)
        outer = dot(out_t, unit)
        new_out[step] = jnp.transpose(mid[step].astype(F32) + outer * outgate).astype(BF16)
        d_gatepre = (gated * outer * (1.0 - outgate)).astype(BF16)
        d_normed_out[step] = dot(outgate_w[1], d_gatepre)
        unit_all[:, here] = unit
        outer_all[:, here] = d_outer
        normed_all[:, here] = normed[step]
        gate_all[:, here] = d_gatepre
        return d_unit * scaled_mid, d_unit

    each_row(rows, 4, body, sums)
    d_tri_out[...] = scr[...].reshape(d_tri_out.shape).astype(BF16)
    out_weight_grads(unit_all, outer_all, normed_all, gate_all, weights_out)
    for index in range(2):
        small_out[index : index + 1, :] = as_row(sums[index])


def in_normed(d_in, all_w, proj_w, gate_w):
    width = proj_w.shape[-1]
    total = all_w
    for side in range(2):
        total = total + dot(proj_w[side], d_in[side * width : (side + 1) * width])
        total = total + dot(gate_w[side], d_in[(2 + side) * width : (3 + side) * width])
    return total


def middle_kernel(
    d_edge, proj_factor, gate_factor, d_normed_gate, scaled_in, inverse_in, cot, outgate,
    scaled_mid, inverse_mid, normed0, normed1, ngain, mgain, mbias, proj_w, gate_w, out_w,
    outgate_w,
    d_tri_out, grad_out, d_normed_out, out_weights, in_weights, small_out,
    scr, scr_tri, unit_all, outer_all, normed_all, gate_all, upper_all, d_in_all, sums,
):
    rows, channels, lanes = cot.shape
    out_t = turned(out_w[0])
    gain = column(ngain, 1, lanes)
    gain_mid, bias_mid = column(mgain, 0, lanes), column(mbias, 0, lanes)
    collect_edges(d_edge, scr)
    sums[...] = jnp.zeros_like(sums)
    half = proj_factor.shape[1]

    def upper(step):
        place = lane_block(step, lanes)
        here = get_rows(scr, step, half, rows)
        d_proj = (here * proj_factor[step]).astype(BF16)
        d_gate = (here * gate_factor[step]).astype(BF16)
        d_in = jnp.concatenate([d_proj, d_gate], axis=0)
        d_in_all[:, place] = d_in
        upper_all[:, place] = normed1[step]
        d_normed = in_normed(d_in, d_normed_gate[step], proj_w[1], gate_w[1])
        scaled = scaled_in[step]
        grad_out[step] = cot[step] + norm_backward(
            d_normed * gain, scaled, inverse_in[pl.ds(step, 1), :]
        )
        return d_normed * scaled, d_normed

    def lower(step):
        place = lane_block(step, lanes)
        gate = outgate[step]
        gated = grad_out[step] * gate
        d_outer = gated.astype(BF16)
        d_unit = dot(out_w[0], d_outer)
        scaled = scaled_mid[step]
        d_tri = norm_backward(d_unit * gain_mid, scaled, inverse_mid[pl.ds(step, 1), :])
        put_rows(scr_tri, d_tri, step, rows)
        unit = (scaled * gain_mid + bias_mid).astype(BF16)
        outer = dot(out_t, unit)
        d_gatepre = (gated * outer * (1.0 - gate)).astype(BF16)
        d_normed_out[step] = dot(outgate_w[0], d_gatepre)
        unit_all[:, place] = unit
        outer_all[:, place] = d_outer
        normed_all[:, place] = normed0[step]
        gate_all[:, place] = d_gatepre
        return d_unit * scaled, d_unit

    each_row(rows, 4, upper, sums.at[2:4])
    each_row(rows, 4, lower, sums.at[0:2])
    d_tri_out[...] = scr_tri[...].reshape(d_tri_out.shape).astype(BF16)
    out_weight_grads(unit_all, outer_all, normed_all, gate_all, out_weights)
    in_weight_grads(upper_all, d_in_all, in_weights)
    for index in range(4):
        small_out[index : index + 1, :] = as_row(sums[index])


def split_cores(all_rows, own_out, other_out, few):
    chips, share, width = own_out.shape
    view = all_rows.reshape(chips // few, 2, few, share, width)
    core = lax.rem(lax.axis_index("row"), 2)
    own_out[...] = view[:, core].reshape(own_out.shape)
    other_out[...] = view[:, 1 - core].reshape(other_out.shape)


def finish_kernel(
    few, d_edge, proj_factor, gate_factor, normed, out0, in1, out1,
    own_out, other_out, d_in_out, scr, normed_all, d_in_all, packed,
):
    rows, half, lanes = proj_factor.shape
    collect_edges(d_edge, scr)

    def body(step):
        place = lane_block(step, lanes)
        here = get_rows(scr, step, half, rows)
        d_proj = (here * proj_factor[step]).astype(BF16)
        d_gate = (here * gate_factor[step]).astype(BF16)
        d_in = jnp.concatenate([d_proj, d_gate], axis=0)
        d_in_out[step] = d_in
        d_in_all[:, place] = d_in
        normed_all[:, place] = normed[step]

    each_row(rows, 4, body)
    first, second, third = d_in_all.shape[0], out0.shape[0], in1.shape[0]
    in_weight_grads(normed_all, d_in_all, packed.at[0:first])
    packed[first : first + second, :] = out0[...]
    packed[first + second : first + second + third, :] = in1[...]
    packed[first + second + third :, :] = out1[...]
    split_cores(packed, own_out, other_out, few)


def norm_sums_kernel(
    d_in, d_normed_gate, scaled_in, proj_w, gate_w, small_middle, small1,
    d_normed_out, extra_out, sums,
):
    rows = d_in.shape[0]
    sums[...] = jnp.zeros_like(sums)

    def body(step):
        d_normed = in_normed(d_in[step], d_normed_gate[step], proj_w[0], gate_w[0])
        d_normed_out[step] = d_normed
        return d_normed * scaled_in[step], d_normed

    each_row(rows, 4, body, sums)
    small = jnp.concatenate(
        [as_row(sums[0]), as_row(sums[1]), small_middle[0:2], small_middle[2:4], small1[...]],
        axis=0,
    )
    high = small.astype(BF16).astype(F32)
    extra_out[...] = jnp.concatenate([high, small - high], axis=0).astype(BF16)


def add_kernel(first, second, extra, out_ref, extra_out):
    out_ref[...] = (first[...].astype(F32) + second[...].astype(F32)).astype(BF16)
    extra_out[...] = extra[...]


def sum_kernel(parts, extra, shared_out):
    chips, share, width = parts.shape
    own = jnp.sum(parts[...].astype(F32), axis=0).astype(BF16)
    for chip in range(chips):
        shared_out[chip, 0:share] = own
        shared_out[chip, share:] = extra[...]


def grad_pair_kernel(
    share, shared, d_normed, scaled_in, inverse_in, grad, ngain, grad_out, mine_out
):
    rows, channels, lanes = grad.shape
    gain = column(ngain, 0, lanes)
    mine_out[...] = jnp.sum(shared[:, share:].astype(F32), axis=0)

    def body(step):
        total = grad[step] + norm_backward(
            d_normed[step] * gain, scaled_in[step], inverse_in[pl.ds(step, 1), :]
        )
        grad_out[step] = jnp.transpose(total).astype(BF16)

    each_row(rows, 4, body)


def unpack_kernel(
    share, few, own, other, mine, proj_out, gate_out, out_out, outgate_out,
    norm_gain_out, norm_bias_out, mid_gain_out, mid_bias_out, weights,
):
    chips, _, width = own.shape
    core = lax.rem(lax.axis_index("row"), 2)
    view = weights.reshape(chips // few, 2, few, share, width)
    block = (chips // few, few, share, width)
    view[:, core] = own[:, 0:share].astype(F32).reshape(block)
    view[:, 1 - core] = other[:, 0:share].astype(F32).reshape(block)
    total = mine[...] + jnp.sum(other[:, share:].astype(F32), axis=0)
    total = total[0:8] + total[8:16]
    for module in range(2):
        for index, out in enumerate((norm_gain_out, norm_bias_out, mid_gain_out, mid_bias_out)):
            at = 4 * module + index
            out[module : module + 1, :] = total[at : at + 1]
        blocks = [
            weights[(6 * module + part) * width : (6 * module + part + 1) * width, :]
            for part in range(6)
        ]
        for side in range(2):
            proj_out[module, side] = blocks[side]
            gate_out[module, side] = blocks[2 + side]
        out_out[module] = blocks[4]
        outgate_out[module] = blocks[5]


def triangle_kernel(incoming, edge, tri_out):
    many, few, _, group, rows, lanes = edge.shape

    def whole(side, channel):
        parts = [edge[:, c, side, channel].reshape(many * rows, lanes) for c in range(few)]
        return jnp.concatenate(parts, axis=1)

    for channel in range(group):
        left, right = whole(0, channel), whole(1, channel)
        tri = (dot_lt if incoming else dot_rt)(left, right).astype(BF16)
        for c in range(few):
            part = tri[:, c * lanes : (c + 1) * lanes]
            tri_out[:, c, channel] = part.reshape(many, rows, lanes)


def edge_grad_kernel(incoming, edge, d_tri, grad_out):
    many, few, _, group, rows, lanes = edge.shape

    def whole(ref, *index):
        parts = [ref[(slice(None), c) + index].reshape(many * rows, lanes) for c in range(few)]
        return jnp.concatenate(parts, axis=1)

    for channel in range(group):
        left, right = whole(edge, 0, channel), whole(edge, 1, channel)
        grad = whole(d_tri, channel)
        if incoming:
            d_left, d_right = dot_rt(right, grad), dot(left, grad)
        else:
            d_left, d_right = dot(grad, right), dot_lt(grad, left)
        for side, value in ((0, d_left), (1, d_right)):
            value = value.astype(BF16)
            for c in range(few):
                part = value[:, c * lanes : (c + 1) * lanes]
                grad_out[:, c, side, channel] = part.reshape(many, rows, lanes)


SCALARS = pl.BlockSpec(memory_space=pltpu.SMEM)
VECTORS = pl.BlockSpec(memory_space=pltpu.VMEM)
FAR = pl.BlockSpec(memory_space=pltpu.HBM)


def call(kernel, name, outs, args, scratch=(), flops=0, grant=16, specs=None):
    shapes = [jax.ShapeDtypeStruct(shape, dtype) for shape, dtype in outs]
    moved = sum(a.size * a.dtype.itemsize for a in list(args) + shapes)
    return pl.pallas_call(
        kernel,
        name=name,
        out_shape=shapes,
        in_specs=specs or [VECTORS] * len(args),
        out_specs=[VECTORS] * len(shapes),
        scratch_shapes=[
            pltpu.VMEM(*item) if isinstance(item, tuple) else item for item in scratch
        ],
        compiler_params=pltpu.CompilerParams(vmem_limit_bytes=grant * 1024 * 1024),
        cost_estimate=pl.CostEstimate(flops=flops, bytes_accessed=moved, transcendentals=0),
    )(*args)


def exchange(values):
    return lax.all_to_all(values, ("row", "col"), split_axis=0, concat_axis=0, tiled=True)


def swap_cores(values, many, few):
    pairs = [(index, index ^ few) for index in range(many * few)]
    return lax.ppermute(values, ("row", "col"), pairs)


def exchange_chips(values, many, few):
    groups = [
        [row * few + col for row in range(core, many, 2) for col in range(few)] for core in range(2)
    ]
    return lax.all_to_all(
        values, ("row", "col"), split_axis=0, concat_axis=0, axis_index_groups=groups, tiled=True
    )


def grouped_device(
    pair, cotangent, lengths, ngain, nbias, proj_w, gate_w, mgain, mbias, out_w, outgate_w,
    *, many, few,
):
    rows, lanes, channels = pair.shape
    shards = many * few
    group = H // shards
    edge = ((shards, 2, group, rows, lanes), BF16)
    grid = ((many, few, 2, group, rows, lanes), BF16)
    tri = ((shards, group, rows, lanes), BF16)
    tri_grid = ((many, few, group, rows, lanes), BF16)
    tile = ((rows, channels, lanes), BF16)
    wide = ((rows, channels, lanes), F32)
    row = ((rows, lanes), F32)
    factor = ((rows, 2 * H, lanes), F32)
    d_in = ((rows, 4 * H, lanes), BF16)
    wts = ((4 * H, channels), BF16)
    big = ((2 * H * rows, lanes), F32)
    mid = ((H * rows, lanes), F32)
    positions = rows * lanes
    flat = ((H, positions), BF16)
    flat_in = ((4 * H, positions), BF16)
    out_rows = ((2 * H, channels), BF16)
    in_rows = ((4 * H, H), BF16)
    triangle = 2 * group * (many * rows) ** 2 * (few * lanes)
    dense = 2 * positions * channels * H

    def sums(count):
        return ((count, H, lanes), F32)

    def small(count):
        return ((count, H), F32)

    saved = [tile, factor, factor, wide, row]
    far = [
        pltpu.with_memory_space_constraint(item, pltpu.HBM)
        for item in (pair, ngain, nbias, proj_w, gate_w)
    ]
    sent, normed0, *factors0, mask = call(
        start_kernel, "start", [edge, *saved, row], [lengths, *far],
        [(pair.shape, BF16), (ngain.shape, F32), (nbias.shape, F32), (proj_w.shape, BF16),
         (gate_w.shape, BF16), pltpu.SemaphoreType.DMA((5,)), wts, big],
        4 * dense, specs=[SCALARS] + [FAR] * len(far),
    )
    edge0 = exchange(sent).reshape(grid[0])
    (here,) = call(
        functools.partial(triangle_kernel, False), "outgoing", [tri_grid], [edge0], (), triangle,
    )
    tri0 = exchange(here.reshape(tri[0]))
    sent, mid_t, normed1, *factors1, outgate0, scaled_mid0, inverse_mid0 = call(
        between_kernel, "between", [edge, tile, *saved, wide, wide, row],
        [mask, tri0, pair, normed0, ngain, nbias, mgain, mbias, out_w, outgate_w, proj_w,
         gate_w],
        [wts, big], 6 * dense,
    )
    edge1 = exchange(sent).reshape(grid[0])
    (here,) = call(
        functools.partial(triangle_kernel, True), "incoming", [tri_grid], [edge1], (), triangle,
    )
    tri1 = exchange(here.reshape(tri[0]))
    sent, new_pair, cot_t, d_normed_gate1, out_grads1, small1 = call(
        turn_kernel, "turn", [tri, (pair.shape, BF16), wide, wide, out_rows, small(2)],
        [tri1, mid_t, normed1, cotangent, mgain, mbias, out_w, outgate_w],
        [mid, flat, flat, flat, flat, sums(2)], 6 * dense,
    )
    d_tri1 = exchange(sent).reshape(tri_grid[0])
    (sent,) = call(
        functools.partial(edge_grad_kernel, True), "incoming_grad", [grid], [edge1, d_tri1],
        (), 2 * triangle,
    )
    d_edge1 = exchange(sent.reshape(edge[0]))
    proj_factor1, gate_factor1, scaled1, inverse1 = factors1
    sent, grad, d_normed_gate0, out_grads0, in_grads1, small_middle = call(
        middle_kernel, "middle", [tri, wide, wide, out_rows, in_rows, small(4)],
        [d_edge1, proj_factor1, gate_factor1, d_normed_gate1, scaled1, inverse1, cot_t, outgate0,
         scaled_mid0, inverse_mid0, normed0, normed1, ngain, mgain, mbias, proj_w, gate_w, out_w,
         outgate_w],
        [big, mid, flat, flat, flat, flat, flat, flat_in, sums(4)], 13 * dense,
    )
    d_tri0 = exchange(sent).reshape(tri_grid[0])
    (sent,) = call(
        functools.partial(edge_grad_kernel, False), "outgoing_grad", [grid], [edge0, d_tri0],
        (), 2 * triangle,
    )
    d_edge0 = exchange(sent.reshape(edge[0]))
    share = 12 * H // shards
    chips = shards // 2
    proj_factor0, gate_factor0, scaled0, inverse0 = factors0
    held = ((chips, share, H), BF16)
    own, other, d_in0 = call(
        functools.partial(finish_kernel, few), "finish", [held, held, d_in],
        [d_edge0, proj_factor0, gate_factor0, normed0, out_grads0, in_grads1, out_grads1],
        [big, flat, flat_in, ((12 * H, H), BF16)], 4 * dense,
    )
    other = swap_cores(other, many, few)
    d_normed0, extra = call(
        norm_sums_kernel, "norm_sums", [wide, ((16, H), BF16)],
        [d_in0, d_normed_gate0, scaled0, proj_w, gate_w, small_middle, small1], [sums(2)],
        4 * dense,
    )
    own, extra = call(add_kernel, "add_cores", [held, ((16, H), BF16)], [own, other, extra])
    parts = exchange_chips(own, many, few)
    (shared,) = call(
        sum_kernel, "sum_weights", [((chips, share + 16, H), BF16)], [parts, extra]
    )
    shared = exchange_chips(shared, many, few)
    other = swap_cores(shared, many, few)
    grad_pair, mine = call(
        functools.partial(grad_pair_kernel, share), "grad_pair",
        [(pair.shape, BF16), ((16, H), F32)],
        [shared, d_normed0, scaled0, inverse0, grad, ngain],
    )
    grad_proj, grad_gate, grad_out, grad_outgate, *vectors = call(
        functools.partial(unpack_kernel, share, few), "unpack",
        [(proj_w.shape, F32), (gate_w.shape, F32), (out_w.shape, F32), (outgate_w.shape, F32),
         (ngain.shape, F32), (nbias.shape, F32), (mgain.shape, F32), (mbias.shape, F32)],
        [shared, other, mine], [((12 * H, H), F32)],
    )
    return (
        new_pair,
        grad_pair,
        vectors[0],
        vectors[1],
        grad_proj,
        grad_gate,
        vectors[2],
        vectors[3],
        grad_out,
        grad_outgate,
    )


def norm_channels(values):
    average = jnp.mean(values, -1, keepdims=True)
    centred = values - average
    variance = jnp.mean(centred * centred, -1, keepdims=True)
    inverse = lax.rsqrt(variance + EPS)
    return (centred * inverse, inverse)


def forward_module(pair_in, pair_mask, weights, incoming):
    gain_in, bias_in, proj_w, gate_w, gain_mid, bias_mid, out_w, outgate_w = weights
    scaled_in, inverse_in = norm_channels(pair_in.astype(jnp.float32))
    normed = (scaled_in * gain_in + bias_in).astype(jnp.bfloat16)
    projected = product("ijc,sch->shij", normed, proj_w)
    gating = jax.nn.sigmoid(product("ijc,sch->shij", normed, gate_w))
    hidden = (projected * gating * pair_mask).astype(jnp.bfloat16)
    left_side, right_side = (
        lax.all_to_all(hidden[0], "row", split_axis=0, concat_axis=1, tiled=True),
        lax.all_to_all(hidden[1], "row", split_axis=0, concat_axis=1, tiled=True),
    )
    if incoming:
        left_side = jnp.swapaxes(left_side, 1, 2)
        right_side = jnp.swapaxes(right_side, 1, 2)
    else:
        left_side, right_side = (
            lax.all_to_all(left_side, "col", split_axis=1, concat_axis=2, tiled=True),
            lax.all_to_all(right_side, "col", split_axis=1, concat_axis=2, tiled=True),
        )
    triangle = product(
        "cik,cjk->cij", left_side, lax.all_gather(right_side, "col", axis=1, tiled=True)
    ).astype(jnp.bfloat16)
    triangle = lax.all_to_all(
        lax.all_to_all(triangle, "col", split_axis=2, concat_axis=1, tiled=True),
        "row",
        split_axis=1,
        concat_axis=0,
        tiled=True,
    )
    tri_values = triangle.astype(jnp.float32)
    total, squares = lax.psum((jnp.sum(tri_values, 0), jnp.sum(tri_values * tri_values, 0)), "ch")
    average = total / H
    inverse_mid = lax.rsqrt(squares / H - average * average + EPS)
    scaled_mid = (tri_values - average) * inverse_mid
    unit = (scaled_mid * gain_mid[:, None, None] + bias_mid[:, None, None]).astype(jnp.bfloat16)
    unit_full = lax.all_gather(unit, "ch", axis=0, tiled=True)
    outer = product("hij,hc->ijc", unit_full, out_w)
    outgate = jax.nn.sigmoid(product("ijc,cd->ijd", normed, outgate_w))
    result = (pair_in.astype(jnp.float32) + outer * outgate).astype(jnp.bfloat16)
    saved = (
        scaled_in,
        inverse_in,
        normed,
        projected,
        gating,
        left_side,
        right_side,
        scaled_mid,
        inverse_mid,
        unit_full,
        outer,
        outgate,
    )
    return (result, saved)


def backward_module(grad_out, pair_mask, weights, saved, incoming):
    gain_in, bias_in, proj_w, gate_w, gain_mid, bias_mid, out_w, outgate_w = weights
    (
        scaled_in,
        inverse_in,
        normed,
        projected,
        gating,
        left_side,
        right_side,
        scaled_mid,
        inverse_mid,
        unit_full,
        outer,
        outgate,
    ) = saved
    d_outer = (grad_out * outgate).astype(jnp.bfloat16)
    d_gatepre = (grad_out * outer * outgate * (1.0 - outgate)).astype(jnp.bfloat16)
    grad_out_w = product("hij,ijc->hc", unit_full, d_outer)
    grad_outgate_w = product("ijc,ijd->cd", normed, d_gatepre)
    width = gain_mid.shape[0]
    own_rows = lax.dynamic_slice_in_dim(out_w, lax.axis_index("ch") * width, width, 0)
    d_unit = product("ijc,hc->hij", d_outer, own_rows)
    d_normed = product("ijd,cd->ijc", d_gatepre, outgate_w)
    weighted = d_unit * gain_mid[:, None, None]
    grad_gain_mid = jnp.sum(d_unit * scaled_mid, (1, 2))
    grad_bias_mid = jnp.sum(d_unit, (1, 2))
    first_sum, second_sum = lax.psum(
        (jnp.sum(weighted, 0), jnp.sum(weighted * scaled_mid, 0)), "ch"
    )
    d_tri = (inverse_mid * (weighted - first_sum / H - scaled_mid * (second_sum / H))).astype(
        jnp.bfloat16
    )
    grad_rows = lax.all_to_all(d_tri, "row", split_axis=0, concat_axis=1, tiled=True)
    grad_cols = lax.all_to_all(grad_rows, "col", split_axis=1, concat_axis=2, tiled=True)
    d_left = product(
        "cij,cjk->cik", grad_cols, lax.all_gather(right_side, "col", axis=1, tiled=True)
    )
    partial_terms = product("cij,cik->cjk", grad_cols, left_side)
    d_right = lax.psum_scatter(
        partial_terms.astype(jnp.bfloat16), "col", scatter_dimension=1, tiled=True
    ).astype(jnp.float32)
    d_left = d_left.astype(jnp.bfloat16)
    d_right = d_right.astype(jnp.bfloat16)
    if incoming:
        d_left = jnp.swapaxes(d_left, 1, 2)
        d_right = jnp.swapaxes(d_right, 1, 2)
    else:
        d_left, d_right = (
            lax.all_to_all(d_left, "col", split_axis=2, concat_axis=1, tiled=True),
            lax.all_to_all(d_right, "col", split_axis=2, concat_axis=1, tiled=True),
        )
    d_left, d_right = (
        lax.all_to_all(d_left, "row", split_axis=1, concat_axis=0, tiled=True),
        lax.all_to_all(d_right, "row", split_axis=1, concat_axis=0, tiled=True),
    )
    d_hidden = jnp.stack([d_left, d_right]).astype(jnp.float32)
    d_proj = (d_hidden * gating * pair_mask).astype(jnp.bfloat16)
    d_gate = (d_hidden * projected * gating * (1.0 - gating) * pair_mask).astype(jnp.bfloat16)
    grad_proj_w = product("ijc,shij->sch", normed, d_proj)
    grad_gate_w = product("ijc,shij->sch", normed, d_gate)
    partial_input = product("shij,sch->ijc", d_proj, proj_w) + product(
        "shij,sch->ijc", d_gate, gate_w
    )
    d_normed = d_normed + lax.psum(partial_input.astype(jnp.bfloat16), "ch").astype(jnp.float32)
    weighted_in = d_normed * gain_in
    grad_gain_in = jnp.sum(d_normed * scaled_in, (0, 1))
    grad_bias_in = jnp.sum(d_normed, (0, 1))
    d_pair = inverse_in * (
        weighted_in
        - jnp.mean(weighted_in, -1, keepdims=True)
        - scaled_in * jnp.mean(weighted_in * scaled_in, -1, keepdims=True)
    )
    grads = (
        grad_gain_in,
        grad_bias_in,
        grad_proj_w,
        grad_gate_w,
        grad_gain_mid,
        grad_bias_mid,
        grad_out_w,
        grad_outgate_w,
    )
    return (grad_out + d_pair, grads)


def per_device(
    pair,
    cotangent,
    lengths,
    norm_gain,
    norm_bias,
    proj_weight,
    gate_weight,
    mid_gain,
    mid_bias,
    out_weight,
    outgate_weight,
):
    rows_here = pair.shape[0]
    cols_here = pair.shape[1]
    row_ids = lax.axis_index("row") * rows_here + lax.iota(jnp.int32, rows_here)
    col_ids = lax.axis_index("col") * cols_here + lax.iota(jnp.int32, cols_here)
    limit = lengths[0]
    pair_mask = ((row_ids[:, None] < limit) & (col_ids[None, :] < limit)).astype(jnp.float32)
    state = pair
    stash = []
    for layer in range(2):
        weights = (
            norm_gain[layer],
            norm_bias[layer],
            proj_weight[layer],
            gate_weight[layer],
            mid_gain[layer],
            mid_bias[layer],
            out_weight[layer],
            outgate_weight[layer],
        )
        state, saved = forward_module(state, pair_mask, weights, layer == 1)
        stash.append(saved)
    grad_state = cotangent.astype(jnp.float32)
    per_layer = [None, None]
    for layer in (1, 0):
        weights = (
            norm_gain[layer],
            norm_bias[layer],
            proj_weight[layer],
            gate_weight[layer],
            mid_gain[layer],
            mid_bias[layer],
            out_weight[layer],
            outgate_weight[layer],
        )
        grad_state, grads = backward_module(
            grad_state, pair_mask, weights, stash[layer], layer == 1
        )
        per_layer[layer] = grads
    lower = per_layer[0]
    upper = per_layer[1]
    summed = lax.psum(
        (
            lower[0],
            lower[1],
            lower[2],
            lower[3],
            lower[4],
            lower[5],
            lower[6],
            lower[7],
            upper[0],
            upper[1],
            upper[2],
            upper[3],
            upper[4],
            upper[5],
            upper[6],
            upper[7],
        ),
        ("row", "col"),
    )
    per_layer = [summed[0:8], summed[8:16]]
    stacked = [jnp.stack([per_layer[0][index], per_layer[1][index]]) for index in range(8)]
    return (
        state,
        grad_state.astype(jnp.bfloat16),
        stacked[0],
        stacked[1],
        stacked[2],
        stacked[3],
        stacked[4],
        stacked[5],
        stacked[6],
        stacked[7],
    )


def solution(mesh):
    in_specs = (
        P(("grp", "row"), "col", None),
        P(("grp", "row"), "col", None),
        P("grp"),
        P(),
        P(),
        P(None, None, None, "ch"),
        P(None, None, None, "ch"),
        P(None, "ch"),
        P(None, "ch"),
        P(),
        P(),
    )
    out_specs = (
        P(("grp", "row"), "col", None),
        P(("grp", "row"), "col", None),
        P("grp", None),
        P("grp", None),
        P("grp", None, None, "ch"),
        P("grp", None, None, "ch"),
        P("grp", "ch"),
        P("grp", "ch"),
        P("grp", None, None),
        P("grp", None, None),
    )
    many, few = mesh.shape["row"], mesh.shape["col"]
    if mesh.shape["ch"] == 1 and H % (many * few) == 0 and many % 2 == 0 and few & (few - 1) == 0:
        body = functools.partial(grouped_device, many=many, few=few)
    else:
        body = per_device
    return jax.shard_map(
        body, mesh=mesh, in_specs=in_specs, out_specs=out_specs, check_vma=False
    )
```

```python
import functools

import jax
import jax.numpy as jnp
from jax import lax
from jax.experimental import pallas as pl
from jax.experimental.pallas import tpu as pltpu
from jax.sharding import PartitionSpec as P

H = 128


EPS = 1e-05


def product(spec, left, right):
    return jnp.einsum(spec, left, right, preferred_element_type=jnp.float32)


F32 = jnp.float32
BF16 = jnp.bfloat16


def dot(left, right):
    return lax.dot_general(left, right, (((1,), (0,)), ((), ())), preferred_element_type=F32)


def dot_rt(left, right):
    return lax.dot_general(left, right, (((1,), (1,)), ((), ())), preferred_element_type=F32)


def dot_lt(left, right):
    return lax.dot_general(left, right, (((0,), (0,)), ((), ())), preferred_element_type=F32)


def sigmoid(values):
    return 0.5 * jnp.tanh(0.5 * values) + 0.5


def norm_rows(values):
    scale = 1.0 / values.shape[0]
    average = jnp.sum(values, 0, keepdims=True) * scale
    centred = values - average
    variance = jnp.sum(centred * centred, 0, keepdims=True) * scale
    inverse = lax.rsqrt(variance + EPS)
    return centred * inverse, inverse


def turned(weight):
    return jnp.transpose(weight.astype(F32)).astype(BF16)


def column(ref, module, lanes):
    row = ref[module : module + 1, :]
    return jnp.transpose(jnp.broadcast_to(row, (lanes, row.shape[1])))


def as_row(total):
    return jnp.sum(jnp.transpose(total), 0, keepdims=True)


def row_mask(lengths_ref, step, rows, lanes):
    limit = lengths_ref[0]
    row_id = lax.axis_index("row") * rows + step
    col_id = lax.axis_index("col") * lanes + lax.broadcasted_iota(jnp.int32, (1, lanes), 1)
    return jnp.where((row_id < limit) & (col_id < limit), 1.0, 0.0).astype(F32)


def load_in_weights(proj_ref, gate_ref, module, scratch):
    width = proj_ref.shape[-1]
    for side in range(2):
        scratch[side * width : (side + 1) * width, :] = turned(proj_ref[module, side])
        scratch[(2 + side) * width : (3 + side) * width, :] = turned(gate_ref[module, side])


BLOCK = 16


def turn_matrix(rows):
    size = BLOCK * rows
    out = lax.broadcasted_iota(jnp.int32, (size, size), 0)
    source = lax.broadcasted_iota(jnp.int32, (size, size), 1)
    return jnp.where(source == (out % rows) * BLOCK + out // rows, 1.0, 0.0).astype(BF16)


def spread_block(matrix, scratch, start, group):
    rows, _, lanes = scratch.shape
    block = scratch[:, start : start + BLOCK, :].reshape(rows * BLOCK, lanes)
    return dot(matrix, block).astype(BF16).reshape(BLOCK // group, group, rows, lanes)


def collect_block(matrix, values, scratch, start):
    rows, _, lanes = scratch.shape
    turned_block = dot(matrix, values.reshape(BLOCK * rows, lanes)).astype(BF16)
    scratch[:, start : start + BLOCK, :] = turned_block.reshape(rows, BLOCK, lanes)


def spread_edges(scratch, out_ref):
    shards, sides, group, rows, lanes = out_ref.shape
    matrix, step = turn_matrix(rows), BLOCK // group
    for side in range(sides):
        for shard in range(0, shards, step):
            start = (side * shards + shard) * group
            out_ref[shard : shard + step, side] = spread_block(matrix, scratch, start, group)


def collect_edges(in_ref, scratch):
    shards, sides, group, rows, lanes = in_ref.shape
    matrix, step = turn_matrix(rows), BLOCK // group
    for side in range(sides):
        for shard in range(0, shards, step):
            start = (side * shards + shard) * group
            collect_block(matrix, in_ref[shard : shard + step, side], scratch, start)


def spread_triangle(scratch, out_ref):
    shards, group, rows, lanes = out_ref.shape
    matrix, step = turn_matrix(rows), BLOCK // group
    for shard in range(0, shards, step):
        out_ref[shard : shard + step] = spread_block(matrix, scratch, shard * group, group)


def collect_triangle(in_ref, scratch):
    shards, group, rows, lanes = in_ref.shape
    matrix, step = turn_matrix(rows), BLOCK // group
    for shard in range(0, shards, step):
        collect_block(matrix, in_ref[shard : shard + step], scratch, shard * group)


def each_row(rows, unroll, body, sums=None):
    def several(block, carry):
        parts = [body(block * unroll + step) for step in range(unroll)]
        for index in range(0 if sums is None else sums.shape[0]):
            total = parts[0][index]
            for part in parts[1:]:
                total = total + part[index]
            sums[index] += total
        return carry

    lax.fori_loop(0, rows // unroll, several, 0)


def mid_norm(tri):
    scale = 1.0 / tri.shape[0]
    average = jnp.sum(tri, 0, keepdims=True) * scale
    squares = jnp.sum(tri * tri, 0, keepdims=True) * scale
    inverse = lax.rsqrt(squares - average * average + EPS)
    return (tri - average) * inverse, inverse


def norm_backward(weighted, scaled, inverse):
    scale = 1.0 / weighted.shape[0]
    first = jnp.sum(weighted, 0, keepdims=True) * scale
    second = jnp.sum(weighted * scaled, 0, keepdims=True) * scale
    return inverse * (weighted - first - scaled * second)


def save_norm(step, values, scaled_out, inverse_out):
    scaled, inverse = norm_rows(values)
    scaled_out[step] = scaled
    inverse_out[pl.ds(step, 1), :] = inverse
    return scaled


def save_edges(step, normed, in_weights, mask, proj_out, gate_out):
    pre = dot(in_weights, normed)
    half = pre.shape[0] // 2
    gating = sigmoid(pre[half:])
    factor = gating * mask
    value = pre[:half] * factor
    proj_out[step] = factor
    gate_out[step] = value * (1.0 - gating)
    return value


def start_kernel(
    lengths, pair_far, ngain_far, nbias_far, proj_far, gate_far,
    edge_out, normed_out, proj_out, gate_out, scaled_out, inverse_out, mask_out,
    pair, ngain, nbias, proj_w, gate_w, sems, wts, scr,
):
    far = (proj_far.at[0], gate_far.at[0], ngain_far, nbias_far, pair_far)
    near = (proj_w.at[0], gate_w.at[0], ngain, nbias, pair)
    copies = [
        pltpu.make_async_copy(source, target, sems.at[index])
        for index, (source, target) in enumerate(zip(far, near))
    ]
    for copy in copies:
        copy.start()
    for copy in copies:
        copy.wait()
    rows, lanes, channels = pair.shape
    load_in_weights(proj_w, gate_w, 0, wts)
    gain, bias = column(ngain, 0, lanes), column(nbias, 0, lanes)

    def body(step):
        base = jnp.transpose(pair[step].astype(F32))
        scaled = save_norm(step, base, scaled_out, inverse_out)
        normed = (scaled * gain + bias).astype(BF16)
        normed_out[step] = normed
        mask = row_mask(lengths, step, rows, lanes)
        mask_out[pl.ds(step, 1), :] = mask
        scr[step] = save_edges(step, normed, wts[...], mask, proj_out, gate_out).astype(BF16)

    each_row(rows, 4, body)
    spread_edges(scr, edge_out)


def between_kernel(
    mask_all, tri, pair, normed0, ngain, nbias, mgain, mbias, out_w, outgate_w, proj_w, gate_w,
    edge_out, mid_out, normed_out, proj_out, gate_out, scaled_out, inverse_out,
    outgate_out, scaled_mid_out, inverse_mid_out, wts, scr,
):
    rows, lanes, channels = pair.shape
    load_in_weights(proj_w, gate_w, 1, wts)
    out_t, outgate_t = turned(out_w[0]), turned(outgate_w[0])
    gain, bias = column(ngain, 1, lanes), column(nbias, 1, lanes)
    gain_mid, bias_mid = column(mgain, 0, lanes), column(mbias, 0, lanes)
    collect_triangle(tri, scr)

    def body(step):
        scaled_mid, inverse_mid = mid_norm(scr[step, 0:channels].astype(F32))
        scaled_mid_out[step] = scaled_mid
        inverse_mid_out[pl.ds(step, 1), :] = inverse_mid
        unit = (scaled_mid * gain_mid + bias_mid).astype(BF16)
        outer = dot(out_t, unit)
        outgate = sigmoid(dot(outgate_t, normed0[step]))
        outgate_out[step] = outgate
        mid = (jnp.transpose(pair[step].astype(F32)) + outer * outgate).astype(BF16)
        mid_out[step] = mid
        scaled = save_norm(step, mid.astype(F32), scaled_out, inverse_out)
        normed = (scaled * gain + bias).astype(BF16)
        normed_out[step] = normed
        mask = mask_all[pl.ds(step, 1), :]
        scr[step] = save_edges(step, normed, wts[...], mask, proj_out, gate_out).astype(BF16)

    each_row(rows, 4, body)
    spread_edges(scr, edge_out)


def out_weight_grads(unit, d_outer, normed, d_gatepre, out_ref):
    width = unit.shape[0]
    out_ref[0:width, :] = dot_rt(unit[...], d_outer[...]).astype(out_ref.dtype)
    out_ref[width:, :] = dot_rt(normed[...], d_gatepre[...]).astype(out_ref.dtype)


def in_weight_grads(normed_all, d_in_all, out_ref):
    width = normed_all.shape[0]
    for part in range(d_in_all.shape[0] // width):
        block = slice(part * width, (part + 1) * width)
        out_ref[block, :] = dot_rt(normed_all[...], d_in_all[block, :]).astype(out_ref.dtype)


def lane_block(step, lanes):
    return pl.ds(pl.multiple_of(step * lanes, lanes), lanes)


def turn_kernel(
    tri, mid, normed, cot, mgain, mbias, out_w, outgate_w,
    d_tri_out, new_out, grad_out, d_normed_out, weights_out, small_out,
    scr, unit_all, outer_all, normed_all, gate_all, sums,
):
    rows, channels, lanes = mid.shape
    out_t, outgate_t = turned(out_w[1]), turned(outgate_w[1])
    gain_mid, bias_mid = column(mgain, 1, lanes), column(mbias, 1, lanes)
    collect_triangle(tri, scr)
    sums[...] = jnp.zeros_like(sums)

    def body(step):
        here = lane_block(step, lanes)
        grad = jnp.transpose(cot[step].astype(F32))
        grad_out[step] = grad
        outgate = sigmoid(dot(outgate_t, normed[step]))
        gated = grad * outgate
        d_outer = gated.astype(BF16)
        d_unit = dot(out_w[1], d_outer)
        scaled_mid, inverse_mid = mid_norm(scr[step, 0:channels].astype(F32))
        scr[step] = norm_backward(d_unit * gain_mid, scaled_mid, inverse_mid).astype(BF16)
        unit = (scaled_mid * gain_mid + bias_mid).astype(BF16)
        outer = dot(out_t, unit)
        new_out[step] = jnp.transpose(mid[step].astype(F32) + outer * outgate).astype(BF16)
        d_gatepre = (gated * outer * (1.0 - outgate)).astype(BF16)
        d_normed_out[step] = dot(outgate_w[1], d_gatepre)
        unit_all[:, here] = unit
        outer_all[:, here] = d_outer
        normed_all[:, here] = normed[step]
        gate_all[:, here] = d_gatepre
        return d_unit * scaled_mid, d_unit

    each_row(rows, 4, body, sums)
    spread_triangle(scr, d_tri_out)
    out_weight_grads(unit_all, outer_all, normed_all, gate_all, weights_out)
    for index in range(2):
        small_out[index : index + 1, :] = as_row(sums[index])


def in_normed(d_in, all_w, proj_w, gate_w):
    width = proj_w.shape[-1]
    total = all_w
    for side in range(2):
        total = total + dot(proj_w[side], d_in[side * width : (side + 1) * width])
        total = total + dot(gate_w[side], d_in[(2 + side) * width : (3 + side) * width])
    return total


def middle_kernel(
    d_edge, proj_factor, gate_factor, d_normed_gate, scaled_in, inverse_in, cot, outgate,
    scaled_mid, inverse_mid, normed0, normed1, ngain, mgain, mbias, proj_w, gate_w, out_w,
    outgate_w,
    d_tri_out, grad_out, d_normed_out, out_weights, in_weights, small_out,
    scr, scr_tri, unit_all, outer_all, normed_all, gate_all, upper_all, d_in_all, sums,
):
    rows, channels, lanes = cot.shape
    out_t = turned(out_w[0])
    gain = column(ngain, 1, lanes)
    gain_mid, bias_mid = column(mgain, 0, lanes), column(mbias, 0, lanes)
    collect_edges(d_edge, scr)
    sums[...] = jnp.zeros_like(sums)
    half = proj_factor.shape[1]

    def upper(step):
        place = lane_block(step, lanes)
        here = scr[step].astype(F32)
        d_proj = (here * proj_factor[step]).astype(BF16)
        d_gate = (here * gate_factor[step]).astype(BF16)
        d_in = jnp.concatenate([d_proj, d_gate], axis=0)
        d_in_all[:, place] = d_in
        upper_all[:, place] = normed1[step]
        d_normed = in_normed(d_in, d_normed_gate[step], proj_w[1], gate_w[1])
        scaled = scaled_in[step]
        grad_out[step] = cot[step] + norm_backward(
            d_normed * gain, scaled, inverse_in[pl.ds(step, 1), :]
        )
        return d_normed * scaled, d_normed

    def lower(step):
        place = lane_block(step, lanes)
        gate = outgate[step]
        gated = grad_out[step] * gate
        d_outer = gated.astype(BF16)
        d_unit = dot(out_w[0], d_outer)
        scaled = scaled_mid[step]
        d_tri = norm_backward(d_unit * gain_mid, scaled, inverse_mid[pl.ds(step, 1), :])
        scr_tri[step] = d_tri.astype(BF16)
        unit = (scaled * gain_mid + bias_mid).astype(BF16)
        outer = dot(out_t, unit)
        d_gatepre = (gated * outer * (1.0 - gate)).astype(BF16)
        d_normed_out[step] = dot(outgate_w[0], d_gatepre)
        unit_all[:, place] = unit
        outer_all[:, place] = d_outer
        normed_all[:, place] = normed0[step]
        gate_all[:, place] = d_gatepre
        return d_unit * scaled, d_unit

    each_row(rows, 4, upper, sums.at[2:4])
    each_row(rows, 4, lower, sums.at[0:2])
    spread_triangle(scr_tri, d_tri_out)
    out_weight_grads(unit_all, outer_all, normed_all, gate_all, out_weights)
    in_weight_grads(upper_all, d_in_all, in_weights)
    for index in range(4):
        small_out[index : index + 1, :] = as_row(sums[index])


def split_cores(all_rows, own_out, other_out, few):
    chips, share, width = own_out.shape
    view = all_rows.reshape(chips // few, 2, few, share, width)
    core = lax.rem(lax.axis_index("row"), 2)
    own_out[...] = view[:, core].reshape(own_out.shape)
    other_out[...] = view[:, 1 - core].reshape(other_out.shape)


def finish_kernel(
    few, d_edge, proj_factor, gate_factor, normed, out0, in1, out1,
    own_out, other_out, d_in_out, scr, normed_all, d_in_all, packed,
):
    rows, half, lanes = proj_factor.shape
    collect_edges(d_edge, scr)

    def body(step):
        place = lane_block(step, lanes)
        here = scr[step].astype(F32)
        d_proj = (here * proj_factor[step]).astype(BF16)
        d_gate = (here * gate_factor[step]).astype(BF16)
        d_in = jnp.concatenate([d_proj, d_gate], axis=0)
        d_in_out[step] = d_in
        d_in_all[:, place] = d_in
        normed_all[:, place] = normed[step]

    each_row(rows, 4, body)
    first, second, third = d_in_all.shape[0], out0.shape[0], in1.shape[0]
    in_weight_grads(normed_all, d_in_all, packed.at[0:first])
    packed[first : first + second, :] = out0[...]
    packed[first + second : first + second + third, :] = in1[...]
    packed[first + second + third :, :] = out1[...]
    split_cores(packed, own_out, other_out, few)


def norm_sums_kernel(
    d_in, d_normed_gate, scaled_in, proj_w, gate_w, small_middle, small1,
    d_normed_out, extra_out, sums,
):
    rows = d_in.shape[0]
    sums[...] = jnp.zeros_like(sums)

    def body(step):
        d_normed = in_normed(d_in[step], d_normed_gate[step], proj_w[0], gate_w[0])
        d_normed_out[step] = d_normed
        return d_normed * scaled_in[step], d_normed

    each_row(rows, 4, body, sums)
    small = jnp.concatenate(
        [as_row(sums[0]), as_row(sums[1]), small_middle[0:2], small_middle[2:4], small1[...]],
        axis=0,
    )
    high = small.astype(BF16).astype(F32)
    extra_out[...] = jnp.concatenate([high, small - high], axis=0).astype(BF16)


def add_kernel(first, second, extra, out_ref, extra_out):
    out_ref[...] = (first[...].astype(F32) + second[...].astype(F32)).astype(BF16)
    extra_out[...] = extra[...]


def sum_kernel(parts, extra, shared_out):
    chips, share, width = parts.shape
    own = jnp.sum(parts[...].astype(F32), axis=0).astype(BF16)
    for chip in range(chips):
        shared_out[chip, 0:share] = own
        shared_out[chip, share:] = extra[...]


def grad_pair_kernel(
    share, shared, d_normed, scaled_in, inverse_in, grad, ngain, grad_out, mine_out
):
    rows, channels, lanes = grad.shape
    gain = column(ngain, 0, lanes)
    mine_out[...] = jnp.sum(shared[:, share:].astype(F32), axis=0)

    def body(step):
        total = grad[step] + norm_backward(
            d_normed[step] * gain, scaled_in[step], inverse_in[pl.ds(step, 1), :]
        )
        grad_out[step] = jnp.transpose(total).astype(BF16)

    each_row(rows, 4, body)


def unpack_kernel(
    share, few, own, other, mine, proj_out, gate_out, out_out, outgate_out,
    norm_gain_out, norm_bias_out, mid_gain_out, mid_bias_out, weights,
):
    chips, _, width = own.shape
    core = lax.rem(lax.axis_index("row"), 2)
    view = weights.reshape(chips // few, 2, few, share, width)
    block = (chips // few, few, share, width)
    view[:, core] = own[:, 0:share].astype(F32).reshape(block)
    view[:, 1 - core] = other[:, 0:share].astype(F32).reshape(block)
    total = mine[...] + jnp.sum(other[:, share:].astype(F32), axis=0)
    total = total[0:8] + total[8:16]
    for module in range(2):
        for index, out in enumerate((norm_gain_out, norm_bias_out, mid_gain_out, mid_bias_out)):
            at = 4 * module + index
            out[module : module + 1, :] = total[at : at + 1]
        blocks = [
            weights[(6 * module + part) * width : (6 * module + part + 1) * width, :]
            for part in range(6)
        ]
        for side in range(2):
            proj_out[module, side] = blocks[side]
            gate_out[module, side] = blocks[2 + side]
        out_out[module] = blocks[4]
        outgate_out[module] = blocks[5]


def triangle_kernel(incoming, edge, tri_out):
    many, few, _, group, rows, lanes = edge.shape

    def whole(side, channel):
        parts = [edge[:, c, side, channel].reshape(many * rows, lanes) for c in range(few)]
        return jnp.concatenate(parts, axis=1)

    for channel in range(group):
        left, right = whole(0, channel), whole(1, channel)
        tri = (dot_lt if incoming else dot_rt)(left, right).astype(BF16)
        for c in range(few):
            part = tri[:, c * lanes : (c + 1) * lanes]
            tri_out[:, c, channel] = part.reshape(many, rows, lanes)


def edge_grad_kernel(incoming, edge, d_tri, grad_out):
    many, few, _, group, rows, lanes = edge.shape

    def whole(ref, *index):
        parts = [ref[(slice(None), c) + index].reshape(many * rows, lanes) for c in range(few)]
        return jnp.concatenate(parts, axis=1)

    for channel in range(group):
        left, right = whole(edge, 0, channel), whole(edge, 1, channel)
        grad = whole(d_tri, channel)
        if incoming:
            d_left, d_right = dot_rt(right, grad), dot(left, grad)
        else:
            d_left, d_right = dot(grad, right), dot_lt(grad, left)
        for side, value in ((0, d_left), (1, d_right)):
            value = value.astype(BF16)
            for c in range(few):
                part = value[:, c * lanes : (c + 1) * lanes]
                grad_out[:, c, side, channel] = part.reshape(many, rows, lanes)


SCALARS = pl.BlockSpec(memory_space=pltpu.SMEM)
VECTORS = pl.BlockSpec(memory_space=pltpu.VMEM)
FAR = pl.BlockSpec(memory_space=pltpu.HBM)


def call(kernel, name, outs, args, scratch=(), flops=0, grant=16, specs=None):
    shapes = [jax.ShapeDtypeStruct(shape, dtype) for shape, dtype in outs]
    moved = sum(a.size * a.dtype.itemsize for a in list(args) + shapes)
    return pl.pallas_call(
        kernel,
        name=name,
        out_shape=shapes,
        in_specs=specs or [VECTORS] * len(args),
        out_specs=[VECTORS] * len(shapes),
        scratch_shapes=[
            pltpu.VMEM(*item) if isinstance(item, tuple) else item for item in scratch
        ],
        compiler_params=pltpu.CompilerParams(vmem_limit_bytes=grant * 1024 * 1024),
        cost_estimate=pl.CostEstimate(flops=flops, bytes_accessed=moved, transcendentals=0),
    )(*args)


def exchange(values):
    return lax.all_to_all(values, ("row", "col"), split_axis=0, concat_axis=0, tiled=True)


def swap_cores(values, many, few):
    pairs = [(index, index ^ few) for index in range(many * few)]
    return lax.ppermute(values, ("row", "col"), pairs)


def exchange_chips(values, many, few):
    groups = [
        [row * few + col for row in range(core, many, 2) for col in range(few)] for core in range(2)
    ]
    return lax.all_to_all(
        values, ("row", "col"), split_axis=0, concat_axis=0, axis_index_groups=groups, tiled=True
    )


def grouped_device(
    pair, cotangent, lengths, ngain, nbias, proj_w, gate_w, mgain, mbias, out_w, outgate_w,
    *, many, few,
):
    rows, lanes, channels = pair.shape
    shards = many * few
    group = H // shards
    edge = ((shards, 2, group, rows, lanes), BF16)
    grid = ((many, few, 2, group, rows, lanes), BF16)
    tri = ((shards, group, rows, lanes), BF16)
    tri_grid = ((many, few, group, rows, lanes), BF16)
    tile = ((rows, channels, lanes), BF16)
    wide = ((rows, channels, lanes), F32)
    row = ((rows, lanes), F32)
    factor = ((rows, 2 * H, lanes), F32)
    d_in = ((rows, 4 * H, lanes), BF16)
    wts = ((4 * H, channels), BF16)
    big = ((rows, 2 * H, lanes), BF16)
    mid = ((rows, H, lanes), BF16)
    positions = rows * lanes
    flat = ((H, positions), BF16)
    flat_in = ((4 * H, positions), BF16)
    out_rows = ((2 * H, channels), BF16)
    in_rows = ((4 * H, H), BF16)
    triangle = 2 * group * (many * rows) ** 2 * (few * lanes)
    dense = 2 * positions * channels * H

    def sums(count):
        return ((count, H, lanes), F32)

    def small(count):
        return ((count, H), F32)

    saved = [tile, factor, factor, wide, row]
    far = [
        pltpu.with_memory_space_constraint(item, pltpu.HBM)
        for item in (pair, ngain, nbias, proj_w, gate_w)
    ]
    sent, normed0, *factors0, mask = call(
        start_kernel, "start", [edge, *saved, row], [lengths, *far],
        [(pair.shape, BF16), (ngain.shape, F32), (nbias.shape, F32), (proj_w.shape, BF16),
         (gate_w.shape, BF16), pltpu.SemaphoreType.DMA((5,)), wts, big],
        4 * dense, specs=[SCALARS] + [FAR] * len(far),
    )
    edge0 = exchange(sent).reshape(grid[0])
    (here,) = call(
        functools.partial(triangle_kernel, False), "outgoing", [tri_grid], [edge0], (), triangle,
    )
    tri0 = exchange(here.reshape(tri[0]))
    sent, mid_t, normed1, *factors1, outgate0, scaled_mid0, inverse_mid0 = call(
        between_kernel, "between", [edge, tile, *saved, wide, wide, row],
        [mask, tri0, pair, normed0, ngain, nbias, mgain, mbias, out_w, outgate_w, proj_w,
         gate_w],
        [wts, big], 6 * dense,
    )
    edge1 = exchange(sent).reshape(grid[0])
    (here,) = call(
        functools.partial(triangle_kernel, True), "incoming", [tri_grid], [edge1], (), triangle,
    )
    tri1 = exchange(here.reshape(tri[0]))
    sent, new_pair, cot_t, d_normed_gate1, out_grads1, small1 = call(
        turn_kernel, "turn", [tri, (pair.shape, BF16), wide, wide, out_rows, small(2)],
        [tri1, mid_t, normed1, cotangent, mgain, mbias, out_w, outgate_w],
        [mid, flat, flat, flat, flat, sums(2)], 6 * dense,
    )
    d_tri1 = exchange(sent).reshape(tri_grid[0])
    (sent,) = call(
        functools.partial(edge_grad_kernel, True), "incoming_grad", [grid], [edge1, d_tri1],
        (), 2 * triangle,
    )
    d_edge1 = exchange(sent.reshape(edge[0]))
    proj_factor1, gate_factor1, scaled1, inverse1 = factors1
    sent, grad, d_normed_gate0, out_grads0, in_grads1, small_middle = call(
        middle_kernel, "middle", [tri, wide, wide, out_rows, in_rows, small(4)],
        [d_edge1, proj_factor1, gate_factor1, d_normed_gate1, scaled1, inverse1, cot_t, outgate0,
         scaled_mid0, inverse_mid0, normed0, normed1, ngain, mgain, mbias, proj_w, gate_w, out_w,
         outgate_w],
        [big, mid, flat, flat, flat, flat, flat, flat_in, sums(4)], 13 * dense,
    )
    d_tri0 = exchange(sent).reshape(tri_grid[0])
    (sent,) = call(
        functools.partial(edge_grad_kernel, False), "outgoing_grad", [grid], [edge0, d_tri0],
        (), 2 * triangle,
    )
    d_edge0 = exchange(sent.reshape(edge[0]))
    share = 12 * H // shards
    chips = shards // 2
    proj_factor0, gate_factor0, scaled0, inverse0 = factors0
    held = ((chips, share, H), BF16)
    own, other, d_in0 = call(
        functools.partial(finish_kernel, few), "finish", [held, held, d_in],
        [d_edge0, proj_factor0, gate_factor0, normed0, out_grads0, in_grads1, out_grads1],
        [big, flat, flat_in, ((12 * H, H), BF16)], 4 * dense,
    )
    other = swap_cores(other, many, few)
    d_normed0, extra = call(
        norm_sums_kernel, "norm_sums", [wide, ((16, H), BF16)],
        [d_in0, d_normed_gate0, scaled0, proj_w, gate_w, small_middle, small1], [sums(2)],
        4 * dense,
    )
    own, extra = call(add_kernel, "add_cores", [held, ((16, H), BF16)], [own, other, extra])
    parts = exchange_chips(own, many, few)
    (shared,) = call(
        sum_kernel, "sum_weights", [((chips, share + 16, H), BF16)], [parts, extra]
    )
    shared = exchange_chips(shared, many, few)
    other = swap_cores(shared, many, few)
    grad_pair, mine = call(
        functools.partial(grad_pair_kernel, share), "grad_pair",
        [(pair.shape, BF16), ((16, H), F32)],
        [shared, d_normed0, scaled0, inverse0, grad, ngain],
    )
    grad_proj, grad_gate, grad_out, grad_outgate, *vectors = call(
        functools.partial(unpack_kernel, share, few), "unpack",
        [(proj_w.shape, F32), (gate_w.shape, F32), (out_w.shape, F32), (outgate_w.shape, F32),
         (ngain.shape, F32), (nbias.shape, F32), (mgain.shape, F32), (mbias.shape, F32)],
        [shared, other, mine], [((12 * H, H), F32)],
    )
    return (
        new_pair,
        grad_pair,
        vectors[0],
        vectors[1],
        grad_proj,
        grad_gate,
        vectors[2],
        vectors[3],
        grad_out,
        grad_outgate,
    )


def norm_channels(values):
    average = jnp.mean(values, -1, keepdims=True)
    centred = values - average
    variance = jnp.mean(centred * centred, -1, keepdims=True)
    inverse = lax.rsqrt(variance + EPS)
    return (centred * inverse, inverse)


def forward_module(pair_in, pair_mask, weights, incoming):
    gain_in, bias_in, proj_w, gate_w, gain_mid, bias_mid, out_w, outgate_w = weights
    scaled_in, inverse_in = norm_channels(pair_in.astype(jnp.float32))
    normed = (scaled_in * gain_in + bias_in).astype(jnp.bfloat16)
    projected = product("ijc,sch->shij", normed, proj_w)
    gating = jax.nn.sigmoid(product("ijc,sch->shij", normed, gate_w))
    hidden = (projected * gating * pair_mask).astype(jnp.bfloat16)
    left_side, right_side = (
        lax.all_to_all(hidden[0], "row", split_axis=0, concat_axis=1, tiled=True),
        lax.all_to_all(hidden[1], "row", split_axis=0, concat_axis=1, tiled=True),
    )
    if incoming:
        left_side = jnp.swapaxes(left_side, 1, 2)
        right_side = jnp.swapaxes(right_side, 1, 2)
    else:
        left_side, right_side = (
            lax.all_to_all(left_side, "col", split_axis=1, concat_axis=2, tiled=True),
            lax.all_to_all(right_side, "col", split_axis=1, concat_axis=2, tiled=True),
        )
    triangle = product(
        "cik,cjk->cij", left_side, lax.all_gather(right_side, "col", axis=1, tiled=True)
    ).astype(jnp.bfloat16)
    triangle = lax.all_to_all(
        lax.all_to_all(triangle, "col", split_axis=2, concat_axis=1, tiled=True),
        "row",
        split_axis=1,
        concat_axis=0,
        tiled=True,
    )
    tri_values = triangle.astype(jnp.float32)
    total, squares = lax.psum((jnp.sum(tri_values, 0), jnp.sum(tri_values * tri_values, 0)), "ch")
    average = total / H
    inverse_mid = lax.rsqrt(squares / H - average * average + EPS)
    scaled_mid = (tri_values - average) * inverse_mid
    unit = (scaled_mid * gain_mid[:, None, None] + bias_mid[:, None, None]).astype(jnp.bfloat16)
    unit_full = lax.all_gather(unit, "ch", axis=0, tiled=True)
    outer = product("hij,hc->ijc", unit_full, out_w)
    outgate = jax.nn.sigmoid(product("ijc,cd->ijd", normed, outgate_w))
    result = (pair_in.astype(jnp.float32) + outer * outgate).astype(jnp.bfloat16)
    saved = (
        scaled_in,
        inverse_in,
        normed,
        projected,
        gating,
        left_side,
        right_side,
        scaled_mid,
        inverse_mid,
        unit_full,
        outer,
        outgate,
    )
    return (result, saved)


def backward_module(grad_out, pair_mask, weights, saved, incoming):
    gain_in, bias_in, proj_w, gate_w, gain_mid, bias_mid, out_w, outgate_w = weights
    (
        scaled_in,
        inverse_in,
        normed,
        projected,
        gating,
        left_side,
        right_side,
        scaled_mid,
        inverse_mid,
        unit_full,
        outer,
        outgate,
    ) = saved
    d_outer = (grad_out * outgate).astype(jnp.bfloat16)
    d_gatepre = (grad_out * outer * outgate * (1.0 - outgate)).astype(jnp.bfloat16)
    grad_out_w = product("hij,ijc->hc", unit_full, d_outer)
    grad_outgate_w = product("ijc,ijd->cd", normed, d_gatepre)
    width = gain_mid.shape[0]
    own_rows = lax.dynamic_slice_in_dim(out_w, lax.axis_index("ch") * width, width, 0)
    d_unit = product("ijc,hc->hij", d_outer, own_rows)
    d_normed = product("ijd,cd->ijc", d_gatepre, outgate_w)
    weighted = d_unit * gain_mid[:, None, None]
    grad_gain_mid = jnp.sum(d_unit * scaled_mid, (1, 2))
    grad_bias_mid = jnp.sum(d_unit, (1, 2))
    first_sum, second_sum = lax.psum(
        (jnp.sum(weighted, 0), jnp.sum(weighted * scaled_mid, 0)), "ch"
    )
    d_tri = (inverse_mid * (weighted - first_sum / H - scaled_mid * (second_sum / H))).astype(
        jnp.bfloat16
    )
    grad_rows = lax.all_to_all(d_tri, "row", split_axis=0, concat_axis=1, tiled=True)
    grad_cols = lax.all_to_all(grad_rows, "col", split_axis=1, concat_axis=2, tiled=True)
    d_left = product(
        "cij,cjk->cik", grad_cols, lax.all_gather(right_side, "col", axis=1, tiled=True)
    )
    partial_terms = product("cij,cik->cjk", grad_cols, left_side)
    d_right = lax.psum_scatter(
        partial_terms.astype(jnp.bfloat16), "col", scatter_dimension=1, tiled=True
    ).astype(jnp.float32)
    d_left = d_left.astype(jnp.bfloat16)
    d_right = d_right.astype(jnp.bfloat16)
    if incoming:
        d_left = jnp.swapaxes(d_left, 1, 2)
        d_right = jnp.swapaxes(d_right, 1, 2)
    else:
        d_left, d_right = (
            lax.all_to_all(d_left, "col", split_axis=2, concat_axis=1, tiled=True),
            lax.all_to_all(d_right, "col", split_axis=2, concat_axis=1, tiled=True),
        )
    d_left, d_right = (
        lax.all_to_all(d_left, "row", split_axis=1, concat_axis=0, tiled=True),
        lax.all_to_all(d_right, "row", split_axis=1, concat_axis=0, tiled=True),
    )
    d_hidden = jnp.stack([d_left, d_right]).astype(jnp.float32)
    d_proj = (d_hidden * gating * pair_mask).astype(jnp.bfloat16)
    d_gate = (d_hidden * projected * gating * (1.0 - gating) * pair_mask).astype(jnp.bfloat16)
    grad_proj_w = product("ijc,shij->sch", normed, d_proj)
    grad_gate_w = product("ijc,shij->sch", normed, d_gate)
    partial_input = product("shij,sch->ijc", d_proj, proj_w) + product(
        "shij,sch->ijc", d_gate, gate_w
    )
    d_normed = d_normed + lax.psum(partial_input.astype(jnp.bfloat16), "ch").astype(jnp.float32)
    weighted_in = d_normed * gain_in
    grad_gain_in = jnp.sum(d_normed * scaled_in, (0, 1))
    grad_bias_in = jnp.sum(d_normed, (0, 1))
    d_pair = inverse_in * (
        weighted_in
        - jnp.mean(weighted_in, -1, keepdims=True)
        - scaled_in * jnp.mean(weighted_in * scaled_in, -1, keepdims=True)
    )
    grads = (
        grad_gain_in,
        grad_bias_in,
        grad_proj_w,
        grad_gate_w,
        grad_gain_mid,
        grad_bias_mid,
        grad_out_w,
        grad_outgate_w,
    )
    return (grad_out + d_pair, grads)


def per_device(
    pair,
    cotangent,
    lengths,
    norm_gain,
    norm_bias,
    proj_weight,
    gate_weight,
    mid_gain,
    mid_bias,
    out_weight,
    outgate_weight,
):
    rows_here = pair.shape[0]
    cols_here = pair.shape[1]
    row_ids = lax.axis_index("row") * rows_here + lax.iota(jnp.int32, rows_here)
    col_ids = lax.axis_index("col") * cols_here + lax.iota(jnp.int32, cols_here)
    limit = lengths[0]
    pair_mask = ((row_ids[:, None] < limit) & (col_ids[None, :] < limit)).astype(jnp.float32)
    state = pair
    stash = []
    for layer in range(2):
        weights = (
            norm_gain[layer],
            norm_bias[layer],
            proj_weight[layer],
            gate_weight[layer],
            mid_gain[layer],
            mid_bias[layer],
            out_weight[layer],
            outgate_weight[layer],
        )
        state, saved = forward_module(state, pair_mask, weights, layer == 1)
        stash.append(saved)
    grad_state = cotangent.astype(jnp.float32)
    per_layer = [None, None]
    for layer in (1, 0):
        weights = (
            norm_gain[layer],
            norm_bias[layer],
            proj_weight[layer],
            gate_weight[layer],
            mid_gain[layer],
            mid_bias[layer],
            out_weight[layer],
            outgate_weight[layer],
        )
        grad_state, grads = backward_module(
            grad_state, pair_mask, weights, stash[layer], layer == 1
        )
        per_layer[layer] = grads
    lower = per_layer[0]
    upper = per_layer[1]
    summed = lax.psum(
        (
            lower[0],
            lower[1],
            lower[2],
            lower[3],
            lower[4],
            lower[5],
            lower[6],
            lower[7],
            upper[0],
            upper[1],
            upper[2],
            upper[3],
            upper[4],
            upper[5],
            upper[6],
            upper[7],
        ),
        ("row", "col"),
    )
    per_layer = [summed[0:8], summed[8:16]]
    stacked = [jnp.stack([per_layer[0][index], per_layer[1][index]]) for index in range(8)]
    return (
        state,
        grad_state.astype(jnp.bfloat16),
        stacked[0],
        stacked[1],
        stacked[2],
        stacked[3],
        stacked[4],
        stacked[5],
        stacked[6],
        stacked[7],
    )


def on_device(pair, *rest, many, few, split):
    rows, lanes, channels = pair.shape
    shards = many * few
    whole_channels = split == 1 and H % shards == 0 and BLOCK % (H // shards) == 0
    tiles = rows == BLOCK and lanes % 128 == 0 and channels == H
    if whole_channels and tiles and many % 2 == 0 and few & (few - 1) == 0:
        return grouped_device(pair, *rest, many=many, few=few)
    return per_device(pair, *rest)


def solution(mesh):
    in_specs = (
        P(("grp", "row"), "col", None),
        P(("grp", "row"), "col", None),
        P("grp"),
        P(),
        P(),
        P(None, None, None, "ch"),
        P(None, None, None, "ch"),
        P(None, "ch"),
        P(None, "ch"),
        P(),
        P(),
    )
    out_specs = (
        P(("grp", "row"), "col", None),
        P(("grp", "row"), "col", None),
        P("grp", None),
        P("grp", None),
        P("grp", None, None, "ch"),
        P("grp", None, None, "ch"),
        P("grp", "ch"),
        P("grp", "ch"),
        P("grp", None, None),
        P("grp", None, None),
    )
    body = functools.partial(
        on_device, many=mesh.shape["row"], few=mesh.shape["col"], split=mesh.shape["ch"]
    )
    return jax.shard_map(
        body, mesh=mesh, in_specs=in_specs, out_specs=out_specs, check_vma=False
    )
```

```python
import functools

import jax
import jax.numpy as jnp
from jax import lax
from jax.experimental import pallas as pl
from jax.experimental.pallas import tpu as pltpu
from jax.sharding import PartitionSpec as P

H = 128


EPS = 1e-05


def product(spec, left, right):
    return jnp.einsum(spec, left, right, preferred_element_type=jnp.float32)


F32 = jnp.float32
BF16 = jnp.bfloat16


def dot(left, right):
    return lax.dot_general(left, right, (((1,), (0,)), ((), ())), preferred_element_type=F32)


def dot_rt(left, right):
    return lax.dot_general(left, right, (((1,), (1,)), ((), ())), preferred_element_type=F32)


def dot_lt(left, right):
    return lax.dot_general(left, right, (((0,), (0,)), ((), ())), preferred_element_type=F32)


def sigmoid(values):
    return 0.5 * jnp.tanh(0.5 * values) + 0.5


def norm_rows(values):
    scale = 1.0 / values.shape[0]
    average = jnp.sum(values, 0, keepdims=True) * scale
    centred = values - average
    variance = jnp.sum(centred * centred, 0, keepdims=True) * scale
    inverse = lax.rsqrt(variance + EPS)
    return centred * inverse, inverse


def turned(weight):
    return jnp.transpose(weight.astype(F32)).astype(BF16)


def column(ref, module, lanes):
    row = ref[module : module + 1, :]
    return jnp.transpose(jnp.broadcast_to(row, (lanes, row.shape[1])))


def as_row(total):
    return jnp.sum(jnp.transpose(total), 0, keepdims=True)


def row_mask(lengths_ref, step, rows, lanes):
    limit = lengths_ref[0]
    row_id = lax.axis_index("row") * rows + step
    col_id = lax.axis_index("col") * lanes + lax.broadcasted_iota(jnp.int32, (1, lanes), 1)
    return jnp.where((row_id < limit) & (col_id < limit), 1.0, 0.0).astype(F32)


EDGE_BLOCK = 64


def load_in_weights(proj_ref, gate_ref, module, scratch):
    width = proj_ref.shape[-1]
    for side in range(2):
        proj, gate = turned(proj_ref[module, side]), turned(gate_ref[module, side])
        for start in range(0, width, EDGE_BLOCK):
            at = 2 * (side * width + start)
            scratch[at : at + EDGE_BLOCK, :] = proj[start : start + EDGE_BLOCK]
            scratch[at + EDGE_BLOCK : at + 2 * EDGE_BLOCK, :] = gate[start : start + EDGE_BLOCK]


def load_back_weights(proj_ref, gate_ref, module, scratch):
    width = proj_ref.shape[-1]
    for side in range(2):
        scratch[:, side * width : (side + 1) * width] = proj_ref[module, side]
        scratch[:, (2 + side) * width : (3 + side) * width] = gate_ref[module, side]


BLOCK = 16


def turn_matrix(rows):
    size = BLOCK * rows
    out = lax.broadcasted_iota(jnp.int32, (size, size), 0)
    source = lax.broadcasted_iota(jnp.int32, (size, size), 1)
    return jnp.where(source == (out % rows) * BLOCK + out // rows, 1.0, 0.0).astype(BF16)


def spread_block(matrix, scratch, start, group):
    rows, _, lanes = scratch.shape
    block = scratch[:, start : start + BLOCK, :].reshape(rows * BLOCK, lanes)
    return dot(matrix, block).astype(BF16).reshape(BLOCK // group, group, rows, lanes)


def collect_block(matrix, values, scratch, start):
    rows, _, lanes = scratch.shape
    turned_block = dot(matrix, values.reshape(BLOCK * rows, lanes)).astype(BF16)
    scratch[:, start : start + BLOCK, :] = turned_block.reshape(rows, BLOCK, lanes)


def spread_edges(scratch, out_ref):
    shards, sides, group, rows, lanes = out_ref.shape
    matrix, step = turn_matrix(rows), BLOCK // group
    for side in range(sides):
        for shard in range(0, shards, step):
            start = (side * shards + shard) * group
            out_ref[shard : shard + step, side] = spread_block(matrix, scratch, start, group)


def collect_edges(in_ref, scratch):
    shards, sides, group, rows, lanes = in_ref.shape
    matrix, step = turn_matrix(rows), BLOCK // group
    for side in range(sides):
        for shard in range(0, shards, step):
            start = (side * shards + shard) * group
            collect_block(matrix, in_ref[shard : shard + step, side], scratch, start)


def spread_triangle(scratch, out_ref):
    shards, group, rows, lanes = out_ref.shape
    matrix, step = turn_matrix(rows), BLOCK // group
    for shard in range(0, shards, step):
        out_ref[shard : shard + step] = spread_block(matrix, scratch, shard * group, group)


def collect_triangle(in_ref, scratch):
    shards, group, rows, lanes = in_ref.shape
    matrix, step = turn_matrix(rows), BLOCK // group
    for shard in range(0, shards, step):
        collect_block(matrix, in_ref[shard : shard + step], scratch, shard * group)


def each_row(rows, unroll, body, sums=None):
    def several(block, carry):
        parts = [body(block * unroll + step) for step in range(unroll)]
        for index in range(0 if sums is None else sums.shape[0]):
            total = parts[0][index]
            for part in parts[1:]:
                total = total + part[index]
            sums[index] += total
        return carry

    lax.fori_loop(0, rows // unroll, several, 0)


def mid_norm(tri):
    scale = 1.0 / tri.shape[0]
    average = jnp.sum(tri, 0, keepdims=True) * scale
    squares = jnp.sum(tri * tri, 0, keepdims=True) * scale
    inverse = lax.rsqrt(squares - average * average + EPS)
    return (tri - average) * inverse, inverse


def norm_backward(weighted, scaled, inverse):
    scale = 1.0 / weighted.shape[0]
    first = jnp.sum(weighted, 0, keepdims=True) * scale
    second = jnp.sum(weighted * scaled, 0, keepdims=True) * scale
    return inverse * (weighted - first - scaled * second)


def save_norm(step, values, scaled_out, inverse_out):
    scaled, inverse = norm_rows(values)
    scaled_out[step] = scaled
    inverse_out[pl.ds(step, 1), :] = inverse
    return scaled


def save_edges(step, normed, wts, mask, proj_out, gate_out, edge_scr):
    for start in range(0, proj_out.shape[1], EDGE_BLOCK):
        block = slice(start, start + EDGE_BLOCK)
        pre = dot(wts[2 * start : 2 * (start + EDGE_BLOCK), :], normed)
        gating = sigmoid(pre[EDGE_BLOCK:])
        factor = gating * mask
        value = pre[:EDGE_BLOCK] * factor
        proj_out[step, block] = factor
        gate_out[step, block] = value * (1.0 - gating)
        edge_scr[step, block] = value.astype(BF16)


def start_kernel(
    lengths, pair_far, ngain_far, nbias_far, proj_far, gate_far,
    edge_out, normed_out, proj_out, gate_out, scaled_out, inverse_out, mask_out,
    pair, ngain, nbias, proj_w, gate_w, sems, wts, scr,
):
    far = (proj_far.at[0], gate_far.at[0], ngain_far, nbias_far, pair_far)
    near = (proj_w.at[0], gate_w.at[0], ngain, nbias, pair)
    copies = [
        pltpu.make_async_copy(source, target, sems.at[index])
        for index, (source, target) in enumerate(zip(far, near))
    ]
    for copy in copies:
        copy.start()
    for copy in copies:
        copy.wait()
    rows, lanes, channels = pair.shape
    load_in_weights(proj_w, gate_w, 0, wts)
    gain, bias = column(ngain, 0, lanes), column(nbias, 0, lanes)

    def body(step):
        base = jnp.transpose(pair[step].astype(F32))
        scaled = save_norm(step, base, scaled_out, inverse_out)
        normed = (scaled * gain + bias).astype(BF16)
        normed_out[step] = normed
        mask = row_mask(lengths, step, rows, lanes)
        mask_out[pl.ds(step, 1), :] = mask
        save_edges(step, normed, wts, mask, proj_out, gate_out, scr)

    each_row(rows, 4, body)
    spread_edges(scr, edge_out)


def between_kernel(
    mask_all, tri, pair, normed0, ngain, nbias, mgain, mbias, out_w, outgate_w, proj_w, gate_w,
    edge_out, mid_out, normed_out, proj_out, gate_out, scaled_out, inverse_out,
    outgate_out, scaled_mid_out, inverse_mid_out, wts, scr,
):
    rows, lanes, channels = pair.shape
    load_in_weights(proj_w, gate_w, 1, wts)
    out_t, outgate_t = turned(out_w[0]), turned(outgate_w[0])
    gain, bias = column(ngain, 1, lanes), column(nbias, 1, lanes)
    gain_mid, bias_mid = column(mgain, 0, lanes), column(mbias, 0, lanes)
    collect_triangle(tri, scr)

    def body(step):
        scaled_mid, inverse_mid = mid_norm(scr[step, 0:channels].astype(F32))
        scaled_mid_out[step] = scaled_mid
        inverse_mid_out[pl.ds(step, 1), :] = inverse_mid
        unit = (scaled_mid * gain_mid + bias_mid).astype(BF16)
        outer = dot(out_t, unit)
        outgate = sigmoid(dot(outgate_t, normed0[step]))
        outgate_out[step] = outgate
        mid = (jnp.transpose(pair[step].astype(F32)) + outer * outgate).astype(BF16)
        mid_out[step] = mid
        scaled = save_norm(step, mid.astype(F32), scaled_out, inverse_out)
        normed = (scaled * gain + bias).astype(BF16)
        normed_out[step] = normed
        mask = mask_all[pl.ds(step, 1), :]
        save_edges(step, normed, wts, mask, proj_out, gate_out, scr)

    each_row(rows, 4, body)
    spread_edges(scr, edge_out)


def out_weight_grads(unit, d_outer, normed, d_gatepre, out_ref):
    width = unit.shape[0]
    out_ref[0:width, :] = dot_rt(unit[...], d_outer[...]).astype(out_ref.dtype)
    out_ref[width:, :] = dot_rt(normed[...], d_gatepre[...]).astype(out_ref.dtype)


def in_weight_grads(normed_all, d_in_all, out_ref):
    width = normed_all.shape[0]
    for part in range(d_in_all.shape[0] // width):
        block = slice(part * width, (part + 1) * width)
        out_ref[block, :] = dot_rt(normed_all[...], d_in_all[block, :]).astype(out_ref.dtype)


def lane_block(step, lanes):
    return pl.ds(pl.multiple_of(step * lanes, lanes), lanes)


def turn_kernel(
    tri, mid, normed, cot, mgain, mbias, out_w, outgate_w,
    d_tri_out, new_out, grad_out, d_normed_out, weights_out, small_out,
    scr, unit_all, outer_all, normed_all, gate_all, sums,
):
    rows, channels, lanes = mid.shape
    out_t, outgate_t = turned(out_w[1]), turned(outgate_w[1])
    gain_mid, bias_mid = column(mgain, 1, lanes), column(mbias, 1, lanes)
    collect_triangle(tri, scr)
    sums[...] = jnp.zeros_like(sums)

    def body(step):
        here = lane_block(step, lanes)
        grad = jnp.transpose(cot[step].astype(F32))
        grad_out[step] = grad
        outgate = sigmoid(dot(outgate_t, normed[step]))
        gated = grad * outgate
        d_outer = gated.astype(BF16)
        d_unit = dot(out_w[1], d_outer)
        scaled_mid, inverse_mid = mid_norm(scr[step, 0:channels].astype(F32))
        scr[step] = norm_backward(d_unit * gain_mid, scaled_mid, inverse_mid).astype(BF16)
        unit = (scaled_mid * gain_mid + bias_mid).astype(BF16)
        outer = dot(out_t, unit)
        new_out[step] = jnp.transpose(mid[step].astype(F32) + outer * outgate).astype(BF16)
        d_gatepre = (gated * outer * (1.0 - outgate)).astype(BF16)
        d_normed_out[step] = dot(outgate_w[1], d_gatepre)
        unit_all[:, here] = unit
        outer_all[:, here] = d_outer
        normed_all[:, here] = normed[step]
        gate_all[:, here] = d_gatepre
        return d_unit * scaled_mid, d_unit

    each_row(rows, 4, body, sums)
    spread_triangle(scr, d_tri_out)
    out_weight_grads(unit_all, outer_all, normed_all, gate_all, weights_out)
    for index in range(2):
        small_out[index : index + 1, :] = as_row(sums[index])


def edge_backward(step, scratch, proj_factor, gate_factor, d_in_out):
    half = proj_factor.shape[1]
    for start in range(0, half, EDGE_BLOCK):
        block = slice(start, start + EDGE_BLOCK)
        here = scratch[step, block].astype(F32)
        d_in_out[start : start + EDGE_BLOCK, :] = (here * proj_factor[step, block]).astype(BF16)
        d_in_out[half + start : half + start + EDGE_BLOCK, :] = (
            here * gate_factor[step, block]
        ).astype(BF16)


def middle_kernel(
    d_edge, proj_factor, gate_factor, d_normed_gate, scaled_in, inverse_in, cot, outgate,
    scaled_mid, inverse_mid, normed0, normed1, ngain, mgain, mbias, proj_w, gate_w, out_w,
    outgate_w,
    d_tri_out, grad_out, d_normed_out, out_weights, in_weights, small_out,
    scr, scr_tri, unit_all, outer_all, normed_all, gate_all, upper_all, d_in_all, back, sums,
):
    rows, channels, lanes = cot.shape
    out_t = turned(out_w[0])
    gain = column(ngain, 1, lanes)
    gain_mid, bias_mid = column(mgain, 0, lanes), column(mbias, 0, lanes)
    collect_edges(d_edge, scr)
    sums[...] = jnp.zeros_like(sums)
    load_back_weights(proj_w, gate_w, 1, back)

    def upper(step):
        place = lane_block(step, lanes)
        edge_backward(step, scr, proj_factor, gate_factor, d_in_all.at[:, place])
        upper_all[:, place] = normed1[step]
        d_normed = d_normed_gate[step] + dot(back[...], d_in_all[:, place])
        scaled = scaled_in[step]
        grad_out[step] = cot[step] + norm_backward(
            d_normed * gain, scaled, inverse_in[pl.ds(step, 1), :]
        )
        return d_normed * scaled, d_normed

    def lower(step):
        place = lane_block(step, lanes)
        gate = outgate[step]
        gated = grad_out[step] * gate
        d_outer = gated.astype(BF16)
        d_unit = dot(out_w[0], d_outer)
        scaled = scaled_mid[step]
        d_tri = norm_backward(d_unit * gain_mid, scaled, inverse_mid[pl.ds(step, 1), :])
        scr_tri[step] = d_tri.astype(BF16)
        unit = (scaled * gain_mid + bias_mid).astype(BF16)
        outer = dot(out_t, unit)
        d_gatepre = (gated * outer * (1.0 - gate)).astype(BF16)
        d_normed_out[step] = dot(outgate_w[0], d_gatepre)
        unit_all[:, place] = unit
        outer_all[:, place] = d_outer
        normed_all[:, place] = normed0[step]
        gate_all[:, place] = d_gatepre
        return d_unit * scaled, d_unit

    each_row(rows, 4, upper, sums.at[2:4])
    each_row(rows, 4, lower, sums.at[0:2])
    spread_triangle(scr_tri, d_tri_out)
    out_weight_grads(unit_all, outer_all, normed_all, gate_all, out_weights)
    in_weight_grads(upper_all, d_in_all, in_weights)
    for index in range(4):
        small_out[index : index + 1, :] = as_row(sums[index])


def split_cores(all_rows, own_out, other_out, few):
    chips, share, width = own_out.shape
    view = all_rows.reshape(chips // few, 2, few, share, width)
    core = lax.rem(lax.axis_index("row"), 2)
    own_out[...] = view[:, core].reshape(own_out.shape)
    other_out[...] = view[:, 1 - core].reshape(other_out.shape)


def finish_kernel(
    few, d_edge, proj_factor, gate_factor, normed, out0, in1, out1,
    own_out, other_out, d_in_all, scr, normed_all, packed,
):
    rows, half, lanes = proj_factor.shape
    collect_edges(d_edge, scr)

    def body(step):
        place = lane_block(step, lanes)
        edge_backward(step, scr, proj_factor, gate_factor, d_in_all.at[:, place])
        normed_all[:, place] = normed[step]

    each_row(rows, 4, body)
    first, second, third = d_in_all.shape[0], out0.shape[0], in1.shape[0]
    in_weight_grads(normed_all, d_in_all, packed.at[0:first])
    packed[first : first + second, :] = out0[...]
    packed[first + second : first + second + third, :] = in1[...]
    packed[first + second + third :, :] = out1[...]
    split_cores(packed, own_out, other_out, few)


def norm_sums_kernel(
    d_in, d_normed_gate, scaled_in, proj_w, gate_w, small_middle, small1,
    d_normed_out, extra_out, back, sums,
):
    rows, channels, lanes = scaled_in.shape
    sums[...] = jnp.zeros_like(sums)
    load_back_weights(proj_w, gate_w, 0, back)

    def body(step):
        d_normed = d_normed_gate[step] + dot(back[...], d_in[:, lane_block(step, lanes)])
        d_normed_out[step] = d_normed
        return d_normed * scaled_in[step], d_normed

    each_row(rows, 4, body, sums)
    small = jnp.concatenate(
        [as_row(sums[0]), as_row(sums[1]), small_middle[0:2], small_middle[2:4], small1[...]],
        axis=0,
    )
    high = small.astype(BF16).astype(F32)
    extra_out[...] = jnp.concatenate([high, small - high], axis=0).astype(BF16)


def add_kernel(first, second, extra, out_ref, extra_out):
    out_ref[...] = (first[...].astype(F32) + second[...].astype(F32)).astype(BF16)
    extra_out[...] = extra[...]


def sum_kernel(parts, extra, shared_out):
    chips, share, width = parts.shape
    own = jnp.sum(parts[...].astype(F32), axis=0).astype(BF16)
    for chip in range(chips):
        shared_out[chip, 0:share] = own
        shared_out[chip, share:] = extra[...]


def grad_pair_kernel(
    share, shared, d_normed, scaled_in, inverse_in, grad, ngain, grad_out, mine_out
):
    rows, channels, lanes = grad.shape
    gain = column(ngain, 0, lanes)
    mine_out[...] = jnp.sum(shared[:, share:].astype(F32), axis=0)

    def body(step):
        total = grad[step] + norm_backward(
            d_normed[step] * gain, scaled_in[step], inverse_in[pl.ds(step, 1), :]
        )
        grad_out[step] = jnp.transpose(total).astype(BF16)

    each_row(rows, 4, body)


def unpack_kernel(
    share, few, own, other, mine, proj_out, gate_out, out_out, outgate_out,
    norm_gain_out, norm_bias_out, mid_gain_out, mid_bias_out, weights,
):
    chips, _, width = own.shape
    core = lax.rem(lax.axis_index("row"), 2)
    view = weights.reshape(chips // few, 2, few, share, width)
    block = (chips // few, few, share, width)
    view[:, core] = own[:, 0:share].astype(F32).reshape(block)
    view[:, 1 - core] = other[:, 0:share].astype(F32).reshape(block)
    total = mine[...] + jnp.sum(other[:, share:].astype(F32), axis=0)
    total = total[0:8] + total[8:16]
    for module in range(2):
        for index, out in enumerate((norm_gain_out, norm_bias_out, mid_gain_out, mid_bias_out)):
            at = 4 * module + index
            out[module : module + 1, :] = total[at : at + 1]
        blocks = [
            weights[(6 * module + part) * width : (6 * module + part + 1) * width, :]
            for part in range(6)
        ]
        for side in range(2):
            proj_out[module, side] = blocks[side]
            gate_out[module, side] = blocks[2 + side]
        out_out[module] = blocks[4]
        outgate_out[module] = blocks[5]


def triangle_kernel(incoming, edge, tri_out):
    many, few, _, group, rows, lanes = edge.shape

    def whole(side, channel):
        parts = [edge[:, c, side, channel].reshape(many * rows, lanes) for c in range(few)]
        return jnp.concatenate(parts, axis=1)

    for channel in range(group):
        left, right = whole(0, channel), whole(1, channel)
        tri = (dot_lt if incoming else dot_rt)(left, right).astype(BF16)
        for c in range(few):
            part = tri[:, c * lanes : (c + 1) * lanes]
            tri_out[:, c, channel] = part.reshape(many, rows, lanes)


def edge_grad_kernel(incoming, edge, d_tri, grad_out):
    many, few, _, group, rows, lanes = edge.shape

    def whole(ref, *index):
        parts = [ref[(slice(None), c) + index].reshape(many * rows, lanes) for c in range(few)]
        return jnp.concatenate(parts, axis=1)

    for channel in range(group):
        left, right = whole(edge, 0, channel), whole(edge, 1, channel)
        grad = whole(d_tri, channel)
        if incoming:
            d_left, d_right = dot_rt(right, grad), dot(left, grad)
        else:
            d_left, d_right = dot(grad, right), dot_lt(grad, left)
        for side, value in ((0, d_left), (1, d_right)):
            value = value.astype(BF16)
            for c in range(few):
                part = value[:, c * lanes : (c + 1) * lanes]
                grad_out[:, c, side, channel] = part.reshape(many, rows, lanes)


SCALARS = pl.BlockSpec(memory_space=pltpu.SMEM)
VECTORS = pl.BlockSpec(memory_space=pltpu.VMEM)
FAR = pl.BlockSpec(memory_space=pltpu.HBM)


def call(kernel, name, outs, args, scratch=(), flops=0, grant=16, specs=None):
    shapes = [jax.ShapeDtypeStruct(shape, dtype) for shape, dtype in outs]
    moved = sum(a.size * a.dtype.itemsize for a in list(args) + shapes)
    return pl.pallas_call(
        kernel,
        name=name,
        out_shape=shapes,
        in_specs=specs or [VECTORS] * len(args),
        out_specs=[VECTORS] * len(shapes),
        scratch_shapes=[
            pltpu.VMEM(*item) if isinstance(item, tuple) else item for item in scratch
        ],
        compiler_params=pltpu.CompilerParams(vmem_limit_bytes=grant * 1024 * 1024),
        cost_estimate=pl.CostEstimate(flops=flops, bytes_accessed=moved, transcendentals=0),
    )(*args)


def exchange(values):
    return lax.all_to_all(values, ("row", "col"), split_axis=0, concat_axis=0, tiled=True)


def swap_cores(values, many, few):
    pairs = [(index, index ^ few) for index in range(many * few)]
    return lax.ppermute(values, ("row", "col"), pairs)


def exchange_chips(values, many, few):
    groups = [
        [row * few + col for row in range(core, many, 2) for col in range(few)] for core in range(2)
    ]
    return lax.all_to_all(
        values, ("row", "col"), split_axis=0, concat_axis=0, axis_index_groups=groups, tiled=True
    )


def grouped_device(
    pair, cotangent, lengths, ngain, nbias, proj_w, gate_w, mgain, mbias, out_w, outgate_w,
    *, many, few,
):
    rows, lanes, channels = pair.shape
    shards = many * few
    group = H // shards
    edge = ((shards, 2, group, rows, lanes), BF16)
    grid = ((many, few, 2, group, rows, lanes), BF16)
    tri = ((shards, group, rows, lanes), BF16)
    tri_grid = ((many, few, group, rows, lanes), BF16)
    tile = ((rows, channels, lanes), BF16)
    wide = ((rows, channels, lanes), F32)
    row = ((rows, lanes), F32)
    factor = ((rows, 2 * H, lanes), F32)
    back = ((channels, 4 * H), BF16)
    wts = ((4 * H, channels), BF16)
    big = ((rows, 2 * H, lanes), BF16)
    mid = ((rows, H, lanes), BF16)
    positions = rows * lanes
    flat = ((H, positions), BF16)
    flat_in = ((4 * H, positions), BF16)
    out_rows = ((2 * H, channels), BF16)
    in_rows = ((4 * H, H), BF16)
    triangle = 2 * group * (many * rows) ** 2 * (few * lanes)
    dense = 2 * positions * channels * H

    def sums(count):
        return ((count, H, lanes), F32)

    def small(count):
        return ((count, H), F32)

    saved = [tile, factor, factor, wide, row]
    far = [
        pltpu.with_memory_space_constraint(item, pltpu.HBM)
        for item in (pair, ngain, nbias, proj_w, gate_w)
    ]
    sent, normed0, *factors0, mask = call(
        start_kernel, "start", [edge, *saved, row], [lengths, *far],
        [(pair.shape, BF16), (ngain.shape, F32), (nbias.shape, F32), (proj_w.shape, BF16),
         (gate_w.shape, BF16), pltpu.SemaphoreType.DMA((5,)), wts, big],
        4 * dense, specs=[SCALARS] + [FAR] * len(far),
    )
    edge0 = exchange(sent).reshape(grid[0])
    (here,) = call(
        functools.partial(triangle_kernel, False), "outgoing", [tri_grid], [edge0], (), triangle,
    )
    tri0 = exchange(here.reshape(tri[0]))
    sent, mid_t, normed1, *factors1, outgate0, scaled_mid0, inverse_mid0 = call(
        between_kernel, "between", [edge, tile, *saved, wide, wide, row],
        [mask, tri0, pair, normed0, ngain, nbias, mgain, mbias, out_w, outgate_w, proj_w,
         gate_w],
        [wts, big], 6 * dense,
    )
    edge1 = exchange(sent).reshape(grid[0])
    (here,) = call(
        functools.partial(triangle_kernel, True), "incoming", [tri_grid], [edge1], (), triangle,
    )
    tri1 = exchange(here.reshape(tri[0]))
    sent, new_pair, cot_t, d_normed_gate1, out_grads1, small1 = call(
        turn_kernel, "turn", [tri, (pair.shape, BF16), wide, wide, out_rows, small(2)],
        [tri1, mid_t, normed1, cotangent, mgain, mbias, out_w, outgate_w],
        [mid, flat, flat, flat, flat, sums(2)], 6 * dense,
    )
    d_tri1 = exchange(sent).reshape(tri_grid[0])
    (sent,) = call(
        functools.partial(edge_grad_kernel, True), "incoming_grad", [grid], [edge1, d_tri1],
        (), 2 * triangle,
    )
    d_edge1 = exchange(sent.reshape(edge[0]))
    proj_factor1, gate_factor1, scaled1, inverse1 = factors1
    sent, grad, d_normed_gate0, out_grads0, in_grads1, small_middle = call(
        middle_kernel, "middle", [tri, wide, wide, out_rows, in_rows, small(4)],
        [d_edge1, proj_factor1, gate_factor1, d_normed_gate1, scaled1, inverse1, cot_t, outgate0,
         scaled_mid0, inverse_mid0, normed0, normed1, ngain, mgain, mbias, proj_w, gate_w, out_w,
         outgate_w],
        [big, mid, flat, flat, flat, flat, flat, flat_in, back, sums(4)], 13 * dense,
    )
    d_tri0 = exchange(sent).reshape(tri_grid[0])
    (sent,) = call(
        functools.partial(edge_grad_kernel, False), "outgoing_grad", [grid], [edge0, d_tri0],
        (), 2 * triangle,
    )
    d_edge0 = exchange(sent.reshape(edge[0]))
    share = 12 * H // shards
    chips = shards // 2
    proj_factor0, gate_factor0, scaled0, inverse0 = factors0
    held = ((chips, share, H), BF16)
    own, other, d_in0 = call(
        functools.partial(finish_kernel, few), "finish", [held, held, flat_in],
        [d_edge0, proj_factor0, gate_factor0, normed0, out_grads0, in_grads1, out_grads1],
        [big, flat, ((12 * H, H), BF16)], 4 * dense,
    )
    other = swap_cores(other, many, few)
    d_normed0, extra = call(
        norm_sums_kernel, "norm_sums", [wide, ((16, H), BF16)],
        [d_in0, d_normed_gate0, scaled0, proj_w, gate_w, small_middle, small1], [back, sums(2)],
        4 * dense,
    )
    own, extra = call(add_kernel, "add_cores", [held, ((16, H), BF16)], [own, other, extra])
    parts = exchange_chips(own, many, few)
    (shared,) = call(
        sum_kernel, "sum_weights", [((chips, share + 16, H), BF16)], [parts, extra]
    )
    shared = exchange_chips(shared, many, few)
    other = swap_cores(shared, many, few)
    grad_pair, mine = call(
        functools.partial(grad_pair_kernel, share), "grad_pair",
        [(pair.shape, BF16), ((16, H), F32)],
        [shared, d_normed0, scaled0, inverse0, grad, ngain],
    )
    grad_proj, grad_gate, grad_out, grad_outgate, *vectors = call(
        functools.partial(unpack_kernel, share, few), "unpack",
        [(proj_w.shape, F32), (gate_w.shape, F32), (out_w.shape, F32), (outgate_w.shape, F32),
         (ngain.shape, F32), (nbias.shape, F32), (mgain.shape, F32), (mbias.shape, F32)],
        [shared, other, mine], [((12 * H, H), F32)],
    )
    return (
        new_pair,
        grad_pair,
        vectors[0],
        vectors[1],
        grad_proj,
        grad_gate,
        vectors[2],
        vectors[3],
        grad_out,
        grad_outgate,
    )


def norm_channels(values):
    average = jnp.mean(values, -1, keepdims=True)
    centred = values - average
    variance = jnp.mean(centred * centred, -1, keepdims=True)
    inverse = lax.rsqrt(variance + EPS)
    return (centred * inverse, inverse)


def forward_module(pair_in, pair_mask, weights, incoming):
    gain_in, bias_in, proj_w, gate_w, gain_mid, bias_mid, out_w, outgate_w = weights
    scaled_in, inverse_in = norm_channels(pair_in.astype(jnp.float32))
    normed = (scaled_in * gain_in + bias_in).astype(jnp.bfloat16)
    projected = product("ijc,sch->shij", normed, proj_w)
    gating = jax.nn.sigmoid(product("ijc,sch->shij", normed, gate_w))
    hidden = (projected * gating * pair_mask).astype(jnp.bfloat16)
    left_side, right_side = (
        lax.all_to_all(hidden[0], "row", split_axis=0, concat_axis=1, tiled=True),
        lax.all_to_all(hidden[1], "row", split_axis=0, concat_axis=1, tiled=True),
    )
    if incoming:
        left_side = jnp.swapaxes(left_side, 1, 2)
        right_side = jnp.swapaxes(right_side, 1, 2)
    else:
        left_side, right_side = (
            lax.all_to_all(left_side, "col", split_axis=1, concat_axis=2, tiled=True),
            lax.all_to_all(right_side, "col", split_axis=1, concat_axis=2, tiled=True),
        )
    triangle = product(
        "cik,cjk->cij", left_side, lax.all_gather(right_side, "col", axis=1, tiled=True)
    ).astype(jnp.bfloat16)
    triangle = lax.all_to_all(
        lax.all_to_all(triangle, "col", split_axis=2, concat_axis=1, tiled=True),
        "row",
        split_axis=1,
        concat_axis=0,
        tiled=True,
    )
    tri_values = triangle.astype(jnp.float32)
    total, squares = lax.psum((jnp.sum(tri_values, 0), jnp.sum(tri_values * tri_values, 0)), "ch")
    average = total / H
    inverse_mid = lax.rsqrt(squares / H - average * average + EPS)
    scaled_mid = (tri_values - average) * inverse_mid
    unit = (scaled_mid * gain_mid[:, None, None] + bias_mid[:, None, None]).astype(jnp.bfloat16)
    unit_full = lax.all_gather(unit, "ch", axis=0, tiled=True)
    outer = product("hij,hc->ijc", unit_full, out_w)
    outgate = jax.nn.sigmoid(product("ijc,cd->ijd", normed, outgate_w))
    result = (pair_in.astype(jnp.float32) + outer * outgate).astype(jnp.bfloat16)
    saved = (
        scaled_in,
        inverse_in,
        normed,
        projected,
        gating,
        left_side,
        right_side,
        scaled_mid,
        inverse_mid,
        unit_full,
        outer,
        outgate,
    )
    return (result, saved)


def backward_module(grad_out, pair_mask, weights, saved, incoming):
    gain_in, bias_in, proj_w, gate_w, gain_mid, bias_mid, out_w, outgate_w = weights
    (
        scaled_in,
        inverse_in,
        normed,
        projected,
        gating,
        left_side,
        right_side,
        scaled_mid,
        inverse_mid,
        unit_full,
        outer,
        outgate,
    ) = saved
    d_outer = (grad_out * outgate).astype(jnp.bfloat16)
    d_gatepre = (grad_out * outer * outgate * (1.0 - outgate)).astype(jnp.bfloat16)
    grad_out_w = product("hij,ijc->hc", unit_full, d_outer)
    grad_outgate_w = product("ijc,ijd->cd", normed, d_gatepre)
    width = gain_mid.shape[0]
    own_rows = lax.dynamic_slice_in_dim(out_w, lax.axis_index("ch") * width, width, 0)
    d_unit = product("ijc,hc->hij", d_outer, own_rows)
    d_normed = product("ijd,cd->ijc", d_gatepre, outgate_w)
    weighted = d_unit * gain_mid[:, None, None]
    grad_gain_mid = jnp.sum(d_unit * scaled_mid, (1, 2))
    grad_bias_mid = jnp.sum(d_unit, (1, 2))
    first_sum, second_sum = lax.psum(
        (jnp.sum(weighted, 0), jnp.sum(weighted * scaled_mid, 0)), "ch"
    )
    d_tri = (inverse_mid * (weighted - first_sum / H - scaled_mid * (second_sum / H))).astype(
        jnp.bfloat16
    )
    grad_rows = lax.all_to_all(d_tri, "row", split_axis=0, concat_axis=1, tiled=True)
    grad_cols = lax.all_to_all(grad_rows, "col", split_axis=1, concat_axis=2, tiled=True)
    d_left = product(
        "cij,cjk->cik", grad_cols, lax.all_gather(right_side, "col", axis=1, tiled=True)
    )
    partial_terms = product("cij,cik->cjk", grad_cols, left_side)
    d_right = lax.psum_scatter(
        partial_terms.astype(jnp.bfloat16), "col", scatter_dimension=1, tiled=True
    ).astype(jnp.float32)
    d_left = d_left.astype(jnp.bfloat16)
    d_right = d_right.astype(jnp.bfloat16)
    if incoming:
        d_left = jnp.swapaxes(d_left, 1, 2)
        d_right = jnp.swapaxes(d_right, 1, 2)
    else:
        d_left, d_right = (
            lax.all_to_all(d_left, "col", split_axis=2, concat_axis=1, tiled=True),
            lax.all_to_all(d_right, "col", split_axis=2, concat_axis=1, tiled=True),
        )
    d_left, d_right = (
        lax.all_to_all(d_left, "row", split_axis=1, concat_axis=0, tiled=True),
        lax.all_to_all(d_right, "row", split_axis=1, concat_axis=0, tiled=True),
    )
    d_hidden = jnp.stack([d_left, d_right]).astype(jnp.float32)
    d_proj = (d_hidden * gating * pair_mask).astype(jnp.bfloat16)
    d_gate = (d_hidden * projected * gating * (1.0 - gating) * pair_mask).astype(jnp.bfloat16)
    grad_proj_w = product("ijc,shij->sch", normed, d_proj)
    grad_gate_w = product("ijc,shij->sch", normed, d_gate)
    partial_input = product("shij,sch->ijc", d_proj, proj_w) + product(
        "shij,sch->ijc", d_gate, gate_w
    )
    d_normed = d_normed + lax.psum(partial_input.astype(jnp.bfloat16), "ch").astype(jnp.float32)
    weighted_in = d_normed * gain_in
    grad_gain_in = jnp.sum(d_normed * scaled_in, (0, 1))
    grad_bias_in = jnp.sum(d_normed, (0, 1))
    d_pair = inverse_in * (
        weighted_in
        - jnp.mean(weighted_in, -1, keepdims=True)
        - scaled_in * jnp.mean(weighted_in * scaled_in, -1, keepdims=True)
    )
    grads = (
        grad_gain_in,
        grad_bias_in,
        grad_proj_w,
        grad_gate_w,
        grad_gain_mid,
        grad_bias_mid,
        grad_out_w,
        grad_outgate_w,
    )
    return (grad_out + d_pair, grads)


def per_device(
    pair,
    cotangent,
    lengths,
    norm_gain,
    norm_bias,
    proj_weight,
    gate_weight,
    mid_gain,
    mid_bias,
    out_weight,
    outgate_weight,
):
    rows_here = pair.shape[0]
    cols_here = pair.shape[1]
    row_ids = lax.axis_index("row") * rows_here + lax.iota(jnp.int32, rows_here)
    col_ids = lax.axis_index("col") * cols_here + lax.iota(jnp.int32, cols_here)
    limit = lengths[0]
    pair_mask = ((row_ids[:, None] < limit) & (col_ids[None, :] < limit)).astype(jnp.float32)
    state = pair
    stash = []
    for layer in range(2):
        weights = (
            norm_gain[layer],
            norm_bias[layer],
            proj_weight[layer],
            gate_weight[layer],
            mid_gain[layer],
            mid_bias[layer],
            out_weight[layer],
            outgate_weight[layer],
        )
        state, saved = forward_module(state, pair_mask, weights, layer == 1)
        stash.append(saved)
    grad_state = cotangent.astype(jnp.float32)
    per_layer = [None, None]
    for layer in (1, 0):
        weights = (
            norm_gain[layer],
            norm_bias[layer],
            proj_weight[layer],
            gate_weight[layer],
            mid_gain[layer],
            mid_bias[layer],
            out_weight[layer],
            outgate_weight[layer],
        )
        grad_state, grads = backward_module(
            grad_state, pair_mask, weights, stash[layer], layer == 1
        )
        per_layer[layer] = grads
    lower = per_layer[0]
    upper = per_layer[1]
    summed = lax.psum(
        (
            lower[0],
            lower[1],
            lower[2],
            lower[3],
            lower[4],
            lower[5],
            lower[6],
            lower[7],
            upper[0],
            upper[1],
            upper[2],
            upper[3],
            upper[4],
            upper[5],
            upper[6],
            upper[7],
        ),
        ("row", "col"),
    )
    per_layer = [summed[0:8], summed[8:16]]
    stacked = [jnp.stack([per_layer[0][index], per_layer[1][index]]) for index in range(8)]
    return (
        state,
        grad_state.astype(jnp.bfloat16),
        stacked[0],
        stacked[1],
        stacked[2],
        stacked[3],
        stacked[4],
        stacked[5],
        stacked[6],
        stacked[7],
    )


def on_device(pair, *rest, many, few, split):
    rows, lanes, channels = pair.shape
    shards = many * few
    whole_channels = split == 1 and H % shards == 0 and BLOCK % (H // shards) == 0
    tiles = rows == BLOCK and lanes % 128 == 0 and channels == H
    if whole_channels and tiles and many % 2 == 0 and few & (few - 1) == 0:
        return grouped_device(pair, *rest, many=many, few=few)
    return per_device(pair, *rest)


def solution(mesh):
    in_specs = (
        P(("grp", "row"), "col", None),
        P(("grp", "row"), "col", None),
        P("grp"),
        P(),
        P(),
        P(None, None, None, "ch"),
        P(None, None, None, "ch"),
        P(None, "ch"),
        P(None, "ch"),
        P(),
        P(),
    )
    out_specs = (
        P(("grp", "row"), "col", None),
        P(("grp", "row"), "col", None),
        P("grp", None),
        P("grp", None),
        P("grp", None, None, "ch"),
        P("grp", None, None, "ch"),
        P("grp", "ch"),
        P("grp", "ch"),
        P("grp", None, None),
        P("grp", None, None),
    )
    body = functools.partial(
        on_device, many=mesh.shape["row"], few=mesh.shape["col"], split=mesh.shape["ch"]
    )
    return jax.shard_map(
        body, mesh=mesh, in_specs=in_specs, out_specs=out_specs, check_vma=False
    )
```

```python
import functools

import jax
import jax.numpy as jnp
from jax import lax
from jax.experimental import pallas as pl
from jax.experimental.pallas import tpu as pltpu
from jax.sharding import PartitionSpec as P

H = 128


EPS = 1e-05


def product(spec, left, right):
    return jnp.einsum(spec, left, right, preferred_element_type=jnp.float32)


F32 = jnp.float32
BF16 = jnp.bfloat16


def dot(left, right):
    return lax.dot_general(left, right, (((1,), (0,)), ((), ())), preferred_element_type=F32)


def dot_rt(left, right):
    return lax.dot_general(left, right, (((1,), (1,)), ((), ())), preferred_element_type=F32)


def dot_lt(left, right):
    return lax.dot_general(left, right, (((0,), (0,)), ((), ())), preferred_element_type=F32)


def sigmoid(values):
    return 0.5 * jnp.tanh(0.5 * values) + 0.5


def norm_rows(values):
    scale = 1.0 / values.shape[0]
    average = jnp.sum(values, 0, keepdims=True) * scale
    centred = values - average
    variance = jnp.sum(centred * centred, 0, keepdims=True) * scale
    inverse = lax.rsqrt(variance + EPS)
    return centred * inverse, inverse


def turned(weight):
    return jnp.transpose(weight.astype(F32)).astype(BF16)


def column(ref, module, lanes):
    row = ref[module : module + 1, :]
    return jnp.transpose(jnp.broadcast_to(row, (lanes, row.shape[1])))


def as_row(total):
    return jnp.sum(jnp.transpose(total), 0, keepdims=True)


def row_mask(lengths_ref, step, rows, lanes):
    limit = lengths_ref[0]
    row_id = lax.axis_index("row") * rows + step
    col_id = lax.axis_index("col") * lanes + lax.broadcasted_iota(jnp.int32, (1, lanes), 1)
    return jnp.where((row_id < limit) & (col_id < limit), 1.0, 0.0).astype(F32)


def load_in_weights(proj_ref, gate_ref, module, scratch):
    width = proj_ref.shape[-1]
    for side in range(2):
        scratch[side * width : (side + 1) * width, :] = turned(proj_ref[module, side])
        scratch[(2 + side) * width : (3 + side) * width, :] = turned(gate_ref[module, side])


def load_back_weights(proj_ref, gate_ref, module, scratch):
    width = proj_ref.shape[-1]
    for side in range(2):
        scratch[:, side * width : (side + 1) * width] = proj_ref[module, side]
        scratch[:, (2 + side) * width : (3 + side) * width] = gate_ref[module, side]


BLOCK = 16


def turn_matrix(rows):
    size = BLOCK * rows
    out = lax.broadcasted_iota(jnp.int32, (size, size), 0)
    source = lax.broadcasted_iota(jnp.int32, (size, size), 1)
    return jnp.where(source == (out % rows) * BLOCK + out // rows, 1.0, 0.0).astype(BF16)


def spread_block(matrix, scratch, start, group):
    rows, _, lanes = scratch.shape
    block = scratch[:, start : start + BLOCK, :].reshape(rows * BLOCK, lanes)
    return dot(matrix, block).astype(BF16).reshape(BLOCK // group, group, rows, lanes)


def collect_block(matrix, values, scratch, start):
    rows, _, lanes = scratch.shape
    turned_block = dot(matrix, values.reshape(BLOCK * rows, lanes)).astype(BF16)
    scratch[:, start : start + BLOCK, :] = turned_block.reshape(rows, BLOCK, lanes)


def spread_edges(scratch, out_ref):
    shards, sides, group, rows, lanes = out_ref.shape
    matrix, step = turn_matrix(rows), BLOCK // group
    for side in range(sides):
        for shard in range(0, shards, step):
            start = (side * shards + shard) * group
            out_ref[shard : shard + step, side] = spread_block(matrix, scratch, start, group)


def collect_edges(in_ref, scratch):
    shards, sides, group, rows, lanes = in_ref.shape
    matrix, step = turn_matrix(rows), BLOCK // group
    for side in range(sides):
        for shard in range(0, shards, step):
            start = (side * shards + shard) * group
            collect_block(matrix, in_ref[shard : shard + step, side], scratch, start)


def spread_triangle(scratch, out_ref):
    shards, group, rows, lanes = out_ref.shape
    matrix, step = turn_matrix(rows), BLOCK // group
    for shard in range(0, shards, step):
        out_ref[shard : shard + step] = spread_block(matrix, scratch, shard * group, group)


def collect_triangle(in_ref, scratch):
    shards, group, rows, lanes = in_ref.shape
    matrix, step = turn_matrix(rows), BLOCK // group
    for shard in range(0, shards, step):
        collect_block(matrix, in_ref[shard : shard + step], scratch, shard * group)


def each_row(rows, unroll, body, sums=None):
    for block in range(0, rows, unroll):
        parts = [body(block + step) for step in range(unroll)]
        for index in range(0 if sums is None else sums.shape[0]):
            total = parts[0][index]
            for part in parts[1:]:
                total = total + part[index]
            sums[index] += total


def mid_norm(tri):
    scale = 1.0 / tri.shape[0]
    average = jnp.sum(tri, 0, keepdims=True) * scale
    squares = jnp.sum(tri * tri, 0, keepdims=True) * scale
    inverse = lax.rsqrt(squares - average * average + EPS)
    return (tri - average) * inverse, inverse


def norm_backward(weighted, scaled, inverse):
    scale = 1.0 / weighted.shape[0]
    first = jnp.sum(weighted, 0, keepdims=True) * scale
    second = jnp.sum(weighted * scaled, 0, keepdims=True) * scale
    return inverse * (weighted - first - scaled * second)


def save_norm(step, values, scaled_out, inverse_out):
    scaled, inverse = norm_rows(values)
    scaled_out[step] = scaled
    inverse_out[pl.ds(step, 1), :] = inverse
    return scaled


def save_edges(step, normed, in_weights, mask, proj_out, gate_out):
    pre = dot(in_weights, normed)
    half = pre.shape[0] // 2
    gating = sigmoid(pre[half:])
    factor = gating * mask
    value = pre[:half] * factor
    proj_out[step] = factor
    gate_out[step] = value * (1.0 - gating)
    return value.astype(BF16)


def start_kernel(
    lengths, pair_far, ngain_far, nbias_far, proj_far, gate_far,
    edge_out, normed_out, proj_out, gate_out, scaled_out, inverse_out, mask_out,
    pair, ngain, nbias, proj_w, gate_w, sems, wts, scr,
):
    far = (proj_far.at[0], gate_far.at[0], ngain_far, nbias_far, pair_far)
    near = (proj_w.at[0], gate_w.at[0], ngain, nbias, pair)
    copies = [
        pltpu.make_async_copy(source, target, sems.at[index])
        for index, (source, target) in enumerate(zip(far, near))
    ]
    for copy in copies:
        copy.start()
    for copy in copies:
        copy.wait()
    rows, lanes, channels = pair.shape
    load_in_weights(proj_w, gate_w, 0, wts)
    gain, bias = column(ngain, 0, lanes), column(nbias, 0, lanes)

    def body(step):
        base = jnp.transpose(pair[step].astype(F32))
        scaled = save_norm(step, base, scaled_out, inverse_out)
        normed = (scaled * gain + bias).astype(BF16)
        normed_out[step] = normed
        mask = row_mask(lengths, step, rows, lanes)
        mask_out[pl.ds(step, 1), :] = mask
        scr[step] = save_edges(step, normed, wts[...], mask, proj_out, gate_out)

    each_row(rows, 4, body)
    spread_edges(scr, edge_out)


def between_kernel(
    mask_all, tri, pair, normed0, ngain, nbias, mgain, mbias, out_w, outgate_w, proj_w, gate_w,
    edge_out, mid_out, normed_out, proj_out, gate_out, scaled_out, inverse_out,
    outgate_out, scaled_mid_out, inverse_mid_out, wts, tri_in, scr,
):
    rows, lanes, channels = pair.shape
    load_in_weights(proj_w, gate_w, 1, wts)
    out_t, outgate_t = turned(out_w[0]), turned(outgate_w[0])
    gain, bias = column(ngain, 1, lanes), column(nbias, 1, lanes)
    gain_mid, bias_mid = column(mgain, 0, lanes), column(mbias, 0, lanes)
    collect_triangle(tri, tri_in)

    def body(step):
        scaled_mid, inverse_mid = mid_norm(tri_in[step].astype(F32))
        scaled_mid_out[step] = scaled_mid
        inverse_mid_out[pl.ds(step, 1), :] = inverse_mid
        unit = (scaled_mid * gain_mid + bias_mid).astype(BF16)
        outer = dot(out_t, unit)
        outgate = sigmoid(dot(outgate_t, normed0[step]))
        outgate_out[step] = outgate
        mid = (jnp.transpose(pair[step].astype(F32)) + outer * outgate).astype(BF16)
        mid_out[step] = mid
        scaled = save_norm(step, mid.astype(F32), scaled_out, inverse_out)
        normed = (scaled * gain + bias).astype(BF16)
        normed_out[step] = normed
        mask = mask_all[pl.ds(step, 1), :]
        scr[step] = save_edges(step, normed, wts[...], mask, proj_out, gate_out)

    each_row(rows, 4, body)
    spread_edges(scr, edge_out)


def out_weight_grads(unit, d_outer, normed, d_gatepre, out_ref):
    width = unit.shape[0]
    out_ref[0:width, :] = dot_rt(unit[...], d_outer[...]).astype(out_ref.dtype)
    out_ref[width:, :] = dot_rt(normed[...], d_gatepre[...]).astype(out_ref.dtype)


def in_weight_grads(normed_all, d_in_all, out_ref):
    width = normed_all.shape[0]
    for part in range(d_in_all.shape[0] // width):
        block = slice(part * width, (part + 1) * width)
        out_ref[block, :] = dot_rt(normed_all[...], d_in_all[block, :]).astype(out_ref.dtype)


def lane_block(step, lanes):
    return pl.ds(step * lanes, lanes)


def turn_kernel(
    tri, mid, normed, cot, mgain, mbias, out_w, outgate_w,
    d_tri_out, new_out, grad_out, d_normed_out, weights_out, small_out,
    tri_in, scr, unit_all, outer_all, normed_all, gate_all, sums,
):
    rows, channels, lanes = mid.shape
    out_t, outgate_t = turned(out_w[1]), turned(outgate_w[1])
    gain_mid, bias_mid = column(mgain, 1, lanes), column(mbias, 1, lanes)
    collect_triangle(tri, tri_in)
    sums[...] = jnp.zeros_like(sums)

    def body(step):
        here = lane_block(step, lanes)
        grad = jnp.transpose(cot[step].astype(F32))
        grad_out[step] = grad
        outgate = sigmoid(dot(outgate_t, normed[step]))
        gated = grad * outgate
        d_outer = gated.astype(BF16)
        d_unit = dot(out_w[1], d_outer)
        scaled_mid, inverse_mid = mid_norm(tri_in[step].astype(F32))
        scr[step] = norm_backward(d_unit * gain_mid, scaled_mid, inverse_mid).astype(BF16)
        unit = (scaled_mid * gain_mid + bias_mid).astype(BF16)
        outer = dot(out_t, unit)
        new_out[step] = jnp.transpose(mid[step].astype(F32) + outer * outgate).astype(BF16)
        d_gatepre = (gated * outer * (1.0 - outgate)).astype(BF16)
        d_normed_out[step] = dot(outgate_w[1], d_gatepre)
        unit_all[:, here] = unit
        outer_all[:, here] = d_outer
        normed_all[:, here] = normed[step]
        gate_all[:, here] = d_gatepre
        return d_unit * scaled_mid, d_unit

    each_row(rows, 4, body, sums)
    spread_triangle(scr, d_tri_out)
    out_weight_grads(unit_all, outer_all, normed_all, gate_all, weights_out)
    for index in range(2):
        small_out[index : index + 1, :] = as_row(sums[index])


def edge_backward(step, scratch, proj_factor, gate_factor):
    here = scratch[step].astype(F32)
    d_proj = (here * proj_factor[step]).astype(BF16)
    d_gate = (here * gate_factor[step]).astype(BF16)
    return jnp.concatenate([d_proj, d_gate], axis=0)


def middle_kernel(
    d_edge, proj_factor, gate_factor, d_normed_gate, scaled_in, inverse_in, cot, outgate,
    scaled_mid, inverse_mid, normed0, normed1, ngain, mgain, mbias, proj_w, gate_w, out_w,
    outgate_w,
    d_tri_out, grad_out, d_normed_out, out_weights, in_weights, small_out,
    scr, scr_tri, unit_all, outer_all, normed_all, gate_all, upper_all, d_in_all, back, sums,
):
    rows, channels, lanes = cot.shape
    out_t = turned(out_w[0])
    gain = column(ngain, 1, lanes)
    gain_mid, bias_mid = column(mgain, 0, lanes), column(mbias, 0, lanes)
    collect_edges(d_edge, scr)
    sums[...] = jnp.zeros_like(sums)
    load_back_weights(proj_w, gate_w, 1, back)

    def upper(step):
        place = lane_block(step, lanes)
        d_in = edge_backward(step, scr, proj_factor, gate_factor)
        d_in_all[:, place] = d_in
        upper_all[:, place] = normed1[step]
        d_normed = d_normed_gate[step] + dot(back[...], d_in)
        scaled = scaled_in[step]
        grad_out[step] = cot[step] + norm_backward(
            d_normed * gain, scaled, inverse_in[pl.ds(step, 1), :]
        )
        return d_normed * scaled, d_normed

    def lower(step):
        place = lane_block(step, lanes)
        gate = outgate[step]
        gated = grad_out[step] * gate
        d_outer = gated.astype(BF16)
        d_unit = dot(out_w[0], d_outer)
        scaled = scaled_mid[step]
        d_tri = norm_backward(d_unit * gain_mid, scaled, inverse_mid[pl.ds(step, 1), :])
        scr_tri[step] = d_tri.astype(BF16)
        unit = (scaled * gain_mid + bias_mid).astype(BF16)
        outer = dot(out_t, unit)
        d_gatepre = (gated * outer * (1.0 - gate)).astype(BF16)
        d_normed_out[step] = dot(outgate_w[0], d_gatepre)
        unit_all[:, place] = unit
        outer_all[:, place] = d_outer
        normed_all[:, place] = normed0[step]
        gate_all[:, place] = d_gatepre
        return d_unit * scaled, d_unit

    each_row(rows, 4, upper, sums.at[2:4])
    each_row(rows, 4, lower, sums.at[0:2])
    spread_triangle(scr_tri, d_tri_out)
    out_weight_grads(unit_all, outer_all, normed_all, gate_all, out_weights)
    in_weight_grads(upper_all, d_in_all, in_weights)
    for index in range(4):
        small_out[index : index + 1, :] = as_row(sums[index])


def split_cores(all_rows, own_out, other_out, few):
    chips, share, width = own_out.shape
    view = all_rows.reshape(chips // few, 2, few, share, width)
    core = lax.rem(lax.axis_index("row"), 2)
    own_out[...] = view[:, core].reshape(own_out.shape)
    other_out[...] = view[:, 1 - core].reshape(other_out.shape)


def finish_kernel(
    few, d_edge, proj_factor, gate_factor, normed, out0, in1, out1,
    own_out, other_out, d_in_all, scr, normed_all, packed,
):
    rows, half, lanes = proj_factor.shape
    collect_edges(d_edge, scr)

    def body(step):
        place = lane_block(step, lanes)
        d_in_all[:, place] = edge_backward(step, scr, proj_factor, gate_factor)
        normed_all[:, place] = normed[step]

    each_row(rows, 4, body)
    first, second, third = d_in_all.shape[0], out0.shape[0], in1.shape[0]
    in_weight_grads(normed_all, d_in_all, packed.at[0:first])
    packed[first : first + second, :] = out0[...]
    packed[first + second : first + second + third, :] = in1[...]
    packed[first + second + third :, :] = out1[...]
    split_cores(packed, own_out, other_out, few)


def norm_sums_kernel(
    d_in, d_normed_gate, scaled_in, proj_w, gate_w, small_middle, small1,
    d_normed_out, extra_out, back, sums,
):
    rows, channels, lanes = scaled_in.shape
    sums[...] = jnp.zeros_like(sums)
    load_back_weights(proj_w, gate_w, 0, back)

    def body(step):
        d_normed = d_normed_gate[step] + dot(back[...], d_in[:, lane_block(step, lanes)])
        d_normed_out[step] = d_normed
        return d_normed * scaled_in[step], d_normed

    each_row(rows, 4, body, sums)
    small = jnp.concatenate(
        [as_row(sums[0]), as_row(sums[1]), small_middle[0:2], small_middle[2:4], small1[...]],
        axis=0,
    )
    high = small.astype(BF16).astype(F32)
    extra_out[...] = jnp.concatenate([high, small - high], axis=0).astype(BF16)


def add_kernel(first, second, extra, out_ref, extra_out):
    out_ref[...] = (first[...].astype(F32) + second[...].astype(F32)).astype(BF16)
    extra_out[...] = extra[...]


def sum_kernel(parts, extra, shared_out):
    chips, share, width = parts.shape
    own = jnp.sum(parts[...].astype(F32), axis=0).astype(BF16)
    for chip in range(chips):
        shared_out[chip, 0:share] = own
        shared_out[chip, share:] = extra[...]


def grad_pair_kernel(
    share, shared, d_normed, scaled_in, inverse_in, grad, ngain, grad_out, mine_out
):
    rows, channels, lanes = grad.shape
    gain = column(ngain, 0, lanes)
    mine_out[...] = jnp.sum(shared[:, share:].astype(F32), axis=0)

    def body(step):
        total = grad[step] + norm_backward(
            d_normed[step] * gain, scaled_in[step], inverse_in[pl.ds(step, 1), :]
        )
        grad_out[step] = jnp.transpose(total).astype(BF16)

    each_row(rows, 4, body)


def unpack_kernel(
    share, few, own, other, mine, proj_out, gate_out, out_out, outgate_out,
    norm_gain_out, norm_bias_out, mid_gain_out, mid_bias_out, weights,
):
    chips, _, width = own.shape
    core = lax.rem(lax.axis_index("row"), 2)
    view = weights.reshape(chips // few, 2, few, share, width)
    block = (chips // few, few, share, width)
    view[:, core] = own[:, 0:share].astype(F32).reshape(block)
    view[:, 1 - core] = other[:, 0:share].astype(F32).reshape(block)
    total = mine[...] + jnp.sum(other[:, share:].astype(F32), axis=0)
    total = total[0:8] + total[8:16]
    for module in range(2):
        for index, out in enumerate((norm_gain_out, norm_bias_out, mid_gain_out, mid_bias_out)):
            at = 4 * module + index
            out[module : module + 1, :] = total[at : at + 1]
        blocks = [
            weights[(6 * module + part) * width : (6 * module + part + 1) * width, :]
            for part in range(6)
        ]
        for side in range(2):
            proj_out[module, side] = blocks[side]
            gate_out[module, side] = blocks[2 + side]
        out_out[module] = blocks[4]
        outgate_out[module] = blocks[5]


def triangle_kernel(incoming, edge, tri_out):
    many, few, _, group, rows, lanes = edge.shape

    def whole(side, channel):
        parts = [edge[:, c, side, channel].reshape(many * rows, lanes) for c in range(few)]
        return jnp.concatenate(parts, axis=1)

    for channel in range(group):
        left, right = whole(0, channel), whole(1, channel)
        tri = (dot_lt if incoming else dot_rt)(left, right).astype(BF16)
        for c in range(few):
            part = tri[:, c * lanes : (c + 1) * lanes]
            tri_out[:, c, channel] = part.reshape(many, rows, lanes)


def edge_grad_kernel(incoming, edge, d_tri, grad_out):
    many, few, _, group, rows, lanes = edge.shape

    def whole(ref, *index):
        parts = [ref[(slice(None), c) + index].reshape(many * rows, lanes) for c in range(few)]
        return jnp.concatenate(parts, axis=1)

    for channel in range(group):
        left, right = whole(edge, 0, channel), whole(edge, 1, channel)
        grad = whole(d_tri, channel)
        if incoming:
            d_left, d_right = dot_rt(right, grad), dot(left, grad)
        else:
            d_left, d_right = dot(grad, right), dot_lt(grad, left)
        for side, value in ((0, d_left), (1, d_right)):
            value = value.astype(BF16)
            for c in range(few):
                part = value[:, c * lanes : (c + 1) * lanes]
                grad_out[:, c, side, channel] = part.reshape(many, rows, lanes)


SCALARS = pl.BlockSpec(memory_space=pltpu.SMEM)
VECTORS = pl.BlockSpec(memory_space=pltpu.VMEM)
FAR = pl.BlockSpec(memory_space=pltpu.HBM)


def call(kernel, name, outs, args, scratch=(), flops=0, grant=16, specs=None):
    shapes = [jax.ShapeDtypeStruct(shape, dtype) for shape, dtype in outs]
    moved = sum(a.size * a.dtype.itemsize for a in list(args) + shapes)
    return pl.pallas_call(
        kernel,
        name=name,
        out_shape=shapes,
        in_specs=specs or [VECTORS] * len(args),
        out_specs=[VECTORS] * len(shapes),
        scratch_shapes=[
            pltpu.VMEM(*item) if isinstance(item, tuple) else item for item in scratch
        ],
        compiler_params=pltpu.CompilerParams(vmem_limit_bytes=grant * 1024 * 1024),
        cost_estimate=pl.CostEstimate(flops=flops, bytes_accessed=moved, transcendentals=0),
    )(*args)


def exchange(values):
    return lax.all_to_all(values, ("row", "col"), split_axis=0, concat_axis=0, tiled=True)


def swap_cores(values, many, few):
    pairs = [(index, index ^ few) for index in range(many * few)]
    return lax.ppermute(values, ("row", "col"), pairs)


def exchange_chips(values, many, few):
    groups = [
        [row * few + col for row in range(core, many, 2) for col in range(few)] for core in range(2)
    ]
    return lax.all_to_all(
        values, ("row", "col"), split_axis=0, concat_axis=0, axis_index_groups=groups, tiled=True
    )


def grouped_device(
    pair, cotangent, lengths, ngain, nbias, proj_w, gate_w, mgain, mbias, out_w, outgate_w,
    *, many, few,
):
    rows, lanes, channels = pair.shape
    shards = many * few
    group = H // shards
    edge = ((shards, 2, group, rows, lanes), BF16)
    grid = ((many, few, 2, group, rows, lanes), BF16)
    tri = ((shards, group, rows, lanes), BF16)
    tri_grid = ((many, few, group, rows, lanes), BF16)
    tile = ((rows, channels, lanes), BF16)
    wide = ((rows, channels, lanes), F32)
    row = ((rows, lanes), F32)
    factor = ((rows, 2 * H, lanes), F32)
    back = ((channels, 4 * H), BF16)
    wts = ((4 * H, channels), BF16)
    big = ((rows, 2 * H, lanes), BF16)
    mid = ((rows, H, lanes), BF16)
    positions = rows * lanes
    flat = ((H, positions), BF16)
    flat_in = ((4 * H, positions), BF16)
    out_rows = ((2 * H, channels), BF16)
    in_rows = ((4 * H, H), BF16)
    triangle = 2 * group * (many * rows) ** 2 * (few * lanes)
    dense = 2 * positions * channels * H

    def sums(count):
        return ((count, H, lanes), F32)

    def small(count):
        return ((count, H), F32)

    saved = [tile, factor, factor, wide, row]
    far = [
        pltpu.with_memory_space_constraint(item, pltpu.HBM)
        for item in (pair, ngain, nbias, proj_w, gate_w)
    ]
    sent, normed0, *factors0, mask = call(
        start_kernel, "start", [edge, *saved, row], [lengths, *far],
        [(pair.shape, BF16), (ngain.shape, F32), (nbias.shape, F32), (proj_w.shape, BF16),
         (gate_w.shape, BF16), pltpu.SemaphoreType.DMA((5,)), wts, big],
        4 * dense, specs=[SCALARS] + [FAR] * len(far),
    )
    edge0 = exchange(sent).reshape(grid[0])
    (here,) = call(
        functools.partial(triangle_kernel, False), "outgoing", [tri_grid], [edge0], (), triangle,
    )
    tri0 = exchange(here.reshape(tri[0]))
    sent, mid_t, normed1, *factors1, outgate0, scaled_mid0, inverse_mid0 = call(
        between_kernel, "between", [edge, tile, *saved, wide, wide, row],
        [mask, tri0, pair, normed0, ngain, nbias, mgain, mbias, out_w, outgate_w, proj_w,
         gate_w],
        [wts, mid, big], 6 * dense,
    )
    edge1 = exchange(sent).reshape(grid[0])
    (here,) = call(
        functools.partial(triangle_kernel, True), "incoming", [tri_grid], [edge1], (), triangle,
    )
    tri1 = exchange(here.reshape(tri[0]))
    sent, new_pair, cot_t, d_normed_gate1, out_grads1, small1 = call(
        turn_kernel, "turn", [tri, (pair.shape, BF16), wide, wide, out_rows, small(2)],
        [tri1, mid_t, normed1, cotangent, mgain, mbias, out_w, outgate_w],
        [mid, mid, flat, flat, flat, flat, sums(2)], 6 * dense,
    )
    d_tri1 = exchange(sent).reshape(tri_grid[0])
    (sent,) = call(
        functools.partial(edge_grad_kernel, True), "incoming_grad", [grid], [edge1, d_tri1],
        (), 2 * triangle,
    )
    d_edge1 = exchange(sent.reshape(edge[0]))
    proj_factor1, gate_factor1, scaled1, inverse1 = factors1
    sent, grad, d_normed_gate0, out_grads0, in_grads1, small_middle = call(
        middle_kernel, "middle", [tri, wide, wide, out_rows, in_rows, small(4)],
        [d_edge1, proj_factor1, gate_factor1, d_normed_gate1, scaled1, inverse1, cot_t, outgate0,
         scaled_mid0, inverse_mid0, normed0, normed1, ngain, mgain, mbias, proj_w, gate_w, out_w,
         outgate_w],
        [big, mid, flat, flat, flat, flat, flat, flat_in, back, sums(4)], 13 * dense,
    )
    d_tri0 = exchange(sent).reshape(tri_grid[0])
    (sent,) = call(
        functools.partial(edge_grad_kernel, False), "outgoing_grad", [grid], [edge0, d_tri0],
        (), 2 * triangle,
    )
    d_edge0 = exchange(sent.reshape(edge[0]))
    share = 12 * H // shards
    chips = shards // 2
    proj_factor0, gate_factor0, scaled0, inverse0 = factors0
    held = ((chips, share, H), BF16)
    own, other, d_in0 = call(
        functools.partial(finish_kernel, few), "finish", [held, held, flat_in],
        [d_edge0, proj_factor0, gate_factor0, normed0, out_grads0, in_grads1, out_grads1],
        [big, flat, ((12 * H, H), BF16)], 4 * dense,
    )
    other = swap_cores(other, many, few)
    d_normed0, extra = call(
        norm_sums_kernel, "norm_sums", [wide, ((16, H), BF16)],
        [d_in0, d_normed_gate0, scaled0, proj_w, gate_w, small_middle, small1], [back, sums(2)],
        4 * dense,
    )
    own, extra = call(add_kernel, "add_cores", [held, ((16, H), BF16)], [own, other, extra])
    parts = exchange_chips(own, many, few)
    (shared,) = call(
        sum_kernel, "sum_weights", [((chips, share + 16, H), BF16)], [parts, extra]
    )
    shared = exchange_chips(shared, many, few)
    other = swap_cores(shared, many, few)
    grad_pair, mine = call(
        functools.partial(grad_pair_kernel, share), "grad_pair",
        [(pair.shape, BF16), ((16, H), F32)],
        [shared, d_normed0, scaled0, inverse0, grad, ngain],
    )
    grad_proj, grad_gate, grad_out, grad_outgate, *vectors = call(
        functools.partial(unpack_kernel, share, few), "unpack",
        [(proj_w.shape, F32), (gate_w.shape, F32), (out_w.shape, F32), (outgate_w.shape, F32),
         (ngain.shape, F32), (nbias.shape, F32), (mgain.shape, F32), (mbias.shape, F32)],
        [shared, other, mine], [((12 * H, H), F32)],
    )
    return (
        new_pair,
        grad_pair,
        vectors[0],
        vectors[1],
        grad_proj,
        grad_gate,
        vectors[2],
        vectors[3],
        grad_out,
        grad_outgate,
    )


def norm_channels(values):
    average = jnp.mean(values, -1, keepdims=True)
    centred = values - average
    variance = jnp.mean(centred * centred, -1, keepdims=True)
    inverse = lax.rsqrt(variance + EPS)
    return (centred * inverse, inverse)


def forward_module(pair_in, pair_mask, weights, incoming):
    gain_in, bias_in, proj_w, gate_w, gain_mid, bias_mid, out_w, outgate_w = weights
    scaled_in, inverse_in = norm_channels(pair_in.astype(jnp.float32))
    normed = (scaled_in * gain_in + bias_in).astype(jnp.bfloat16)
    projected = product("ijc,sch->shij", normed, proj_w)
    gating = jax.nn.sigmoid(product("ijc,sch->shij", normed, gate_w))
    hidden = (projected * gating * pair_mask).astype(jnp.bfloat16)
    left_side, right_side = (
        lax.all_to_all(hidden[0], "row", split_axis=0, concat_axis=1, tiled=True),
        lax.all_to_all(hidden[1], "row", split_axis=0, concat_axis=1, tiled=True),
    )
    if incoming:
        left_side = jnp.swapaxes(left_side, 1, 2)
        right_side = jnp.swapaxes(right_side, 1, 2)
    else:
        left_side, right_side = (
            lax.all_to_all(left_side, "col", split_axis=1, concat_axis=2, tiled=True),
            lax.all_to_all(right_side, "col", split_axis=1, concat_axis=2, tiled=True),
        )
    triangle = product(
        "cik,cjk->cij", left_side, lax.all_gather(right_side, "col", axis=1, tiled=True)
    ).astype(jnp.bfloat16)
    triangle = lax.all_to_all(
        lax.all_to_all(triangle, "col", split_axis=2, concat_axis=1, tiled=True),
        "row",
        split_axis=1,
        concat_axis=0,
        tiled=True,
    )
    tri_values = triangle.astype(jnp.float32)
    total, squares = lax.psum((jnp.sum(tri_values, 0), jnp.sum(tri_values * tri_values, 0)), "ch")
    average = total / H
    inverse_mid = lax.rsqrt(squares / H - average * average + EPS)
    scaled_mid = (tri_values - average) * inverse_mid
    unit = (scaled_mid * gain_mid[:, None, None] + bias_mid[:, None, None]).astype(jnp.bfloat16)
    unit_full = lax.all_gather(unit, "ch", axis=0, tiled=True)
    outer = product("hij,hc->ijc", unit_full, out_w)
    outgate = jax.nn.sigmoid(product("ijc,cd->ijd", normed, outgate_w))
    result = (pair_in.astype(jnp.float32) + outer * outgate).astype(jnp.bfloat16)
    saved = (
        scaled_in,
        inverse_in,
        normed,
        projected,
        gating,
        left_side,
        right_side,
        scaled_mid,
        inverse_mid,
        unit_full,
        outer,
        outgate,
    )
    return (result, saved)


def backward_module(grad_out, pair_mask, weights, saved, incoming):
    gain_in, bias_in, proj_w, gate_w, gain_mid, bias_mid, out_w, outgate_w = weights
    (
        scaled_in,
        inverse_in,
        normed,
        projected,
        gating,
        left_side,
        right_side,
        scaled_mid,
        inverse_mid,
        unit_full,
        outer,
        outgate,
    ) = saved
    d_outer = (grad_out * outgate).astype(jnp.bfloat16)
    d_gatepre = (grad_out * outer * outgate * (1.0 - outgate)).astype(jnp.bfloat16)
    grad_out_w = product("hij,ijc->hc", unit_full, d_outer)
    grad_outgate_w = product("ijc,ijd->cd", normed, d_gatepre)
    width = gain_mid.shape[0]
    own_rows = lax.dynamic_slice_in_dim(out_w, lax.axis_index("ch") * width, width, 0)
    d_unit = product("ijc,hc->hij", d_outer, own_rows)
    d_normed = product("ijd,cd->ijc", d_gatepre, outgate_w)
    weighted = d_unit * gain_mid[:, None, None]
    grad_gain_mid = jnp.sum(d_unit * scaled_mid, (1, 2))
    grad_bias_mid = jnp.sum(d_unit, (1, 2))
    first_sum, second_sum = lax.psum(
        (jnp.sum(weighted, 0), jnp.sum(weighted * scaled_mid, 0)), "ch"
    )
    d_tri = (inverse_mid * (weighted - first_sum / H - scaled_mid * (second_sum / H))).astype(
        jnp.bfloat16
    )
    grad_rows = lax.all_to_all(d_tri, "row", split_axis=0, concat_axis=1, tiled=True)
    grad_cols = lax.all_to_all(grad_rows, "col", split_axis=1, concat_axis=2, tiled=True)
    d_left = product(
        "cij,cjk->cik", grad_cols, lax.all_gather(right_side, "col", axis=1, tiled=True)
    )
    partial_terms = product("cij,cik->cjk", grad_cols, left_side)
    d_right = lax.psum_scatter(
        partial_terms.astype(jnp.bfloat16), "col", scatter_dimension=1, tiled=True
    ).astype(jnp.float32)
    d_left = d_left.astype(jnp.bfloat16)
    d_right = d_right.astype(jnp.bfloat16)
    if incoming:
        d_left = jnp.swapaxes(d_left, 1, 2)
        d_right = jnp.swapaxes(d_right, 1, 2)
    else:
        d_left, d_right = (
            lax.all_to_all(d_left, "col", split_axis=2, concat_axis=1, tiled=True),
            lax.all_to_all(d_right, "col", split_axis=2, concat_axis=1, tiled=True),
        )
    d_left, d_right = (
        lax.all_to_all(d_left, "row", split_axis=1, concat_axis=0, tiled=True),
        lax.all_to_all(d_right, "row", split_axis=1, concat_axis=0, tiled=True),
    )
    d_hidden = jnp.stack([d_left, d_right]).astype(jnp.float32)
    d_proj = (d_hidden * gating * pair_mask).astype(jnp.bfloat16)
    d_gate = (d_hidden * projected * gating * (1.0 - gating) * pair_mask).astype(jnp.bfloat16)
    grad_proj_w = product("ijc,shij->sch", normed, d_proj)
    grad_gate_w = product("ijc,shij->sch", normed, d_gate)
    partial_input = product("shij,sch->ijc", d_proj, proj_w) + product(
        "shij,sch->ijc", d_gate, gate_w
    )
    d_normed = d_normed + lax.psum(partial_input.astype(jnp.bfloat16), "ch").astype(jnp.float32)
    weighted_in = d_normed * gain_in
    grad_gain_in = jnp.sum(d_normed * scaled_in, (0, 1))
    grad_bias_in = jnp.sum(d_normed, (0, 1))
    d_pair = inverse_in * (
        weighted_in
        - jnp.mean(weighted_in, -1, keepdims=True)
        - scaled_in * jnp.mean(weighted_in * scaled_in, -1, keepdims=True)
    )
    grads = (
        grad_gain_in,
        grad_bias_in,
        grad_proj_w,
        grad_gate_w,
        grad_gain_mid,
        grad_bias_mid,
        grad_out_w,
        grad_outgate_w,
    )
    return (grad_out + d_pair, grads)


def per_device(
    pair,
    cotangent,
    lengths,
    norm_gain,
    norm_bias,
    proj_weight,
    gate_weight,
    mid_gain,
    mid_bias,
    out_weight,
    outgate_weight,
):
    rows_here = pair.shape[0]
    cols_here = pair.shape[1]
    row_ids = lax.axis_index("row") * rows_here + lax.iota(jnp.int32, rows_here)
    col_ids = lax.axis_index("col") * cols_here + lax.iota(jnp.int32, cols_here)
    limit = lengths[0]
    pair_mask = ((row_ids[:, None] < limit) & (col_ids[None, :] < limit)).astype(jnp.float32)
    state = pair
    stash = []
    for layer in range(2):
        weights = (
            norm_gain[layer],
            norm_bias[layer],
            proj_weight[layer],
            gate_weight[layer],
            mid_gain[layer],
            mid_bias[layer],
            out_weight[layer],
            outgate_weight[layer],
        )
        state, saved = forward_module(state, pair_mask, weights, layer == 1)
        stash.append(saved)
    grad_state = cotangent.astype(jnp.float32)
    per_layer = [None, None]
    for layer in (1, 0):
        weights = (
            norm_gain[layer],
            norm_bias[layer],
            proj_weight[layer],
            gate_weight[layer],
            mid_gain[layer],
            mid_bias[layer],
            out_weight[layer],
            outgate_weight[layer],
        )
        grad_state, grads = backward_module(
            grad_state, pair_mask, weights, stash[layer], layer == 1
        )
        per_layer[layer] = grads
    lower = per_layer[0]
    upper = per_layer[1]
    summed = lax.psum(
        (
            lower[0],
            lower[1],
            lower[2],
            lower[3],
            lower[4],
            lower[5],
            lower[6],
            lower[7],
            upper[0],
            upper[1],
            upper[2],
            upper[3],
            upper[4],
            upper[5],
            upper[6],
            upper[7],
        ),
        ("row", "col"),
    )
    per_layer = [summed[0:8], summed[8:16]]
    stacked = [jnp.stack([per_layer[0][index], per_layer[1][index]]) for index in range(8)]
    return (
        state,
        grad_state.astype(jnp.bfloat16),
        stacked[0],
        stacked[1],
        stacked[2],
        stacked[3],
        stacked[4],
        stacked[5],
        stacked[6],
        stacked[7],
    )


def on_device(pair, *rest, many, few, split):
    rows, lanes, channels = pair.shape
    shards = many * few
    whole_channels = split == 1 and H % shards == 0 and BLOCK % (H // shards) == 0
    tiles = rows == BLOCK and lanes % 128 == 0 and channels == H
    if whole_channels and tiles and many % 2 == 0 and few & (few - 1) == 0:
        return grouped_device(pair, *rest, many=many, few=few)
    return per_device(pair, *rest)


def solution(mesh):
    in_specs = (
        P(("grp", "row"), "col", None),
        P(("grp", "row"), "col", None),
        P("grp"),
        P(),
        P(),
        P(None, None, None, "ch"),
        P(None, None, None, "ch"),
        P(None, "ch"),
        P(None, "ch"),
        P(),
        P(),
    )
    out_specs = (
        P(("grp", "row"), "col", None),
        P(("grp", "row"), "col", None),
        P("grp", None),
        P("grp", None),
        P("grp", None, None, "ch"),
        P("grp", None, None, "ch"),
        P("grp", "ch"),
        P("grp", "ch"),
        P("grp", None, None),
        P("grp", None, None),
    )
    body = functools.partial(
        on_device, many=mesh.shape["row"], few=mesh.shape["col"], split=mesh.shape["ch"]
    )
    return jax.shard_map(
        body, mesh=mesh, in_specs=in_specs, out_specs=out_specs, check_vma=False
    )
```

```python
import functools

import jax
import jax.numpy as jnp
from jax import lax
from jax.experimental import pallas as pl
from jax.experimental.pallas import tpu as pltpu
from jax.sharding import PartitionSpec as P

H = 128


EPS = 1e-05


def product(spec, left, right):
    return jnp.einsum(spec, left, right, preferred_element_type=jnp.float32)


F32 = jnp.float32
BF16 = jnp.bfloat16


def dot(left, right):
    return lax.dot_general(left, right, (((1,), (0,)), ((), ())), preferred_element_type=F32)


def dot_rt(left, right):
    return lax.dot_general(left, right, (((1,), (1,)), ((), ())), preferred_element_type=F32)


def dot_lt(left, right):
    return lax.dot_general(left, right, (((0,), (0,)), ((), ())), preferred_element_type=F32)


def sigmoid(values):
    return 0.5 * jnp.tanh(0.5 * values) + 0.5


def norm_rows(values):
    scale = 1.0 / values.shape[0]
    average = jnp.sum(values, 0, keepdims=True) * scale
    centred = values - average
    variance = jnp.sum(centred * centred, 0, keepdims=True) * scale
    inverse = lax.rsqrt(variance + EPS)
    return centred * inverse, inverse


def turned(weight):
    return jnp.transpose(weight.astype(F32)).astype(BF16)


def column(ref, module, lanes):
    row = ref[module : module + 1, :]
    return beside(*[jnp.transpose(jnp.broadcast_to(row, (lanes, row.shape[1])))] * 2)


def beside(left, right):
    return jnp.concatenate([left, right], axis=-1)


def pair_of(ref, step):
    return beside(ref[2 * step], ref[2 * step + 1])


def put_pair(ref, step, values):
    lanes = ref.shape[-1]
    ref[2 * step] = values[:, :lanes]
    ref[2 * step + 1] = values[:, lanes:]


def pair_of_rows(ref, step):
    return beside(ref[2 * step : 2 * step + 1, :], ref[2 * step + 1 : 2 * step + 2, :])


def put_pair_of_rows(ref, step, values):
    lanes = ref.shape[-1]
    ref[2 * step : 2 * step + 1, :] = values[:, :lanes]
    ref[2 * step + 1 : 2 * step + 2, :] = values[:, lanes:]


def turned_pair(ref, step):
    return beside(
        jnp.transpose(ref[2 * step].astype(F32)), jnp.transpose(ref[2 * step + 1].astype(F32))
    )


def put_turned_pair(ref, step, values):
    lanes = ref.shape[1]
    ref[2 * step] = jnp.transpose(values[:, :lanes]).astype(BF16)
    ref[2 * step + 1] = jnp.transpose(values[:, lanes:]).astype(BF16)


def as_row(total):
    return jnp.sum(jnp.transpose(total), 0, keepdims=True)


def row_mask(lengths_ref, step, rows, lanes):
    limit = lengths_ref[0]
    row_id = lax.axis_index("row") * rows + step
    col_id = lax.axis_index("col") * lanes + lax.broadcasted_iota(jnp.int32, (1, lanes), 1)
    return jnp.where((row_id < limit) & (col_id < limit), 1.0, 0.0).astype(F32)


def load_in_weights(proj_ref, gate_ref, module, scratch):
    width = proj_ref.shape[-1]
    for side in range(2):
        scratch[side * width : (side + 1) * width, :] = turned(proj_ref[module, side])
        scratch[(2 + side) * width : (3 + side) * width, :] = turned(gate_ref[module, side])


def load_back_weights(proj_ref, gate_ref, module, scratch):
    width = proj_ref.shape[-1]
    for side in range(2):
        scratch[:, side * width : (side + 1) * width] = proj_ref[module, side]
        scratch[:, (2 + side) * width : (3 + side) * width] = gate_ref[module, side]


BLOCK = 16


def turn_matrix(rows):
    size = BLOCK * rows
    out = lax.broadcasted_iota(jnp.int32, (size, size), 0)
    source = lax.broadcasted_iota(jnp.int32, (size, size), 1)
    return jnp.where(source == (out % rows) * BLOCK + out // rows, 1.0, 0.0).astype(BF16)


def spread_blocks(matrix, scratch, start, group):
    rows, _, lanes = scratch.shape
    blocks = [
        scratch[:, at : at + BLOCK, :].reshape(rows * BLOCK, lanes)
        for at in (start, start + BLOCK)
    ]
    both = dot(matrix, beside(*blocks)).astype(BF16)
    parts = [
        part.reshape(BLOCK // group, group, rows, lanes)
        for part in (both[:, :lanes], both[:, lanes:])
    ]
    return jnp.concatenate(parts, axis=0)


def collect_blocks(matrix, values, scratch, start):
    rows, _, lanes = scratch.shape
    flat = values.reshape(2, BLOCK * rows, lanes)
    both = dot(matrix, beside(flat[0], flat[1])).astype(BF16)
    for at, part in ((start, both[:, :lanes]), (start + BLOCK, both[:, lanes:])):
        scratch[:, at : at + BLOCK, :] = part.reshape(rows, BLOCK, lanes)


def spread_edges(scratch, out_ref):
    shards, sides, group, rows, lanes = out_ref.shape
    matrix, step = turn_matrix(rows), 2 * BLOCK // group
    for side in range(sides):
        for shard in range(0, shards, step):
            start = (side * shards + shard) * group
            out_ref[shard : shard + step, side] = spread_blocks(matrix, scratch, start, group)


def collect_edges(in_ref, scratch):
    shards, sides, group, rows, lanes = in_ref.shape
    matrix, step = turn_matrix(rows), 2 * BLOCK // group
    for side in range(sides):
        for shard in range(0, shards, step):
            start = (side * shards + shard) * group
            collect_blocks(matrix, in_ref[shard : shard + step, side], scratch, start)


def spread_triangle(scratch, out_ref):
    shards, group, rows, lanes = out_ref.shape
    matrix, step = turn_matrix(rows), 2 * BLOCK // group
    for shard in range(0, shards, step):
        out_ref[shard : shard + step] = spread_blocks(matrix, scratch, shard * group, group)


def collect_triangle(in_ref, scratch):
    shards, group, rows, lanes = in_ref.shape
    matrix, step = turn_matrix(rows), 2 * BLOCK // group
    for shard in range(0, shards, step):
        collect_blocks(matrix, in_ref[shard : shard + step], scratch, shard * group)


def each_pair(rows, body, sums=None):
    for block in range(0, rows // 2, 2):
        parts = [body(block + step) for step in range(2)]
        for index in range(0 if sums is None else sums.shape[0]):
            total = parts[0][index] + parts[1][index]
            lanes = sums.shape[-1]
            sums[index] += total[:, :lanes] + total[:, lanes:]


def mid_norm(tri):
    scale = 1.0 / tri.shape[0]
    average = jnp.sum(tri, 0, keepdims=True) * scale
    squares = jnp.sum(tri * tri, 0, keepdims=True) * scale
    inverse = lax.rsqrt(squares - average * average + EPS)
    return (tri - average) * inverse, inverse


def norm_backward(weighted, scaled, inverse):
    scale = 1.0 / weighted.shape[0]
    first = jnp.sum(weighted, 0, keepdims=True) * scale
    second = jnp.sum(weighted * scaled, 0, keepdims=True) * scale
    return inverse * (weighted - first - scaled * second)


def save_norm(step, values, scaled_out, inverse_out):
    scaled, inverse = norm_rows(values)
    put_pair(scaled_out, step, scaled)
    put_pair_of_rows(inverse_out, step, inverse)
    return scaled


def save_edges(step, normed, in_weights, mask, proj_out, gate_out):
    pre = dot(in_weights, normed)
    half = pre.shape[0] // 2
    gating = sigmoid(pre[half:])
    factor = gating * mask
    value = pre[:half] * factor
    put_pair(proj_out, step, factor)
    put_pair(gate_out, step, value * (1.0 - gating))
    return value.astype(BF16)


def start_kernel(
    lengths, pair_far, ngain_far, nbias_far, proj_far, gate_far,
    edge_out, normed_out, proj_out, gate_out, scaled_out, inverse_out, mask_out,
    pair, ngain, nbias, proj_w, gate_w, sems, wts, scr,
):
    far = (proj_far.at[0], gate_far.at[0], ngain_far, nbias_far, pair_far)
    near = (proj_w.at[0], gate_w.at[0], ngain, nbias, pair)
    copies = [
        pltpu.make_async_copy(source, target, sems.at[index])
        for index, (source, target) in enumerate(zip(far, near))
    ]
    for copy in copies:
        copy.start()
    for copy in copies:
        copy.wait()
    rows, lanes, channels = pair.shape
    load_in_weights(proj_w, gate_w, 0, wts)
    gain, bias = column(ngain, 0, lanes), column(nbias, 0, lanes)

    def body(step):
        base = turned_pair(pair, step)
        scaled = save_norm(step, base, scaled_out, inverse_out)
        normed = (scaled * gain + bias).astype(BF16)
        put_pair(normed_out, step, normed)
        mask = beside(*[row_mask(lengths, 2 * step + row, rows, lanes) for row in range(2)])
        put_pair_of_rows(mask_out, step, mask)
        put_pair(scr, step, save_edges(step, normed, wts[...], mask, proj_out, gate_out))

    each_pair(rows, body)
    spread_edges(scr, edge_out)


def between_kernel(
    mask_all, tri, pair, normed0, ngain, nbias, mgain, mbias, out_w, outgate_w, proj_w, gate_w,
    edge_out, mid_out, normed_out, proj_out, gate_out, scaled_out, inverse_out,
    outgate_out, scaled_mid_out, inverse_mid_out, wts, tri_in, scr,
):
    rows, lanes, channels = pair.shape
    load_in_weights(proj_w, gate_w, 1, wts)
    out_t, outgate_t = turned(out_w[0]), turned(outgate_w[0])
    gain, bias = column(ngain, 1, lanes), column(nbias, 1, lanes)
    gain_mid, bias_mid = column(mgain, 0, lanes), column(mbias, 0, lanes)
    collect_triangle(tri, tri_in)

    def body(step):
        scaled_mid, inverse_mid = mid_norm(pair_of(tri_in, step).astype(F32))
        put_pair(scaled_mid_out, step, scaled_mid)
        put_pair_of_rows(inverse_mid_out, step, inverse_mid)
        unit = (scaled_mid * gain_mid + bias_mid).astype(BF16)
        outer = dot(out_t, unit)
        outgate = sigmoid(dot(outgate_t, pair_of(normed0, step)))
        put_pair(outgate_out, step, outgate)
        mid = (turned_pair(pair, step) + outer * outgate).astype(BF16)
        put_pair(mid_out, step, mid)
        scaled = save_norm(step, mid.astype(F32), scaled_out, inverse_out)
        normed = (scaled * gain + bias).astype(BF16)
        put_pair(normed_out, step, normed)
        mask = pair_of_rows(mask_all, step)
        put_pair(scr, step, save_edges(step, normed, wts[...], mask, proj_out, gate_out))

    each_pair(rows, body)
    spread_edges(scr, edge_out)


def out_weight_grads(unit, d_outer, normed, d_gatepre, out_ref):
    width = unit.shape[0]
    out_ref[0:width, :] = dot_rt(unit[...], d_outer[...]).astype(out_ref.dtype)
    out_ref[width:, :] = dot_rt(normed[...], d_gatepre[...]).astype(out_ref.dtype)


def in_weight_grads(normed_all, d_in_all, out_ref):
    width = normed_all.shape[0]
    for part in range(d_in_all.shape[0] // width):
        block = slice(part * width, (part + 1) * width)
        out_ref[block, :] = dot_rt(normed_all[...], d_in_all[block, :]).astype(out_ref.dtype)


def lane_block(step, lanes):
    return pl.ds(2 * step * lanes, 2 * lanes)


def turn_kernel(
    tri, mid, normed, cot, mgain, mbias, out_w, outgate_w,
    d_tri_out, new_out, grad_out, d_normed_out, weights_out, small_out,
    tri_in, scr, unit_all, outer_all, normed_all, gate_all, sums,
):
    rows, channels, lanes = mid.shape
    out_t, outgate_t = turned(out_w[1]), turned(outgate_w[1])
    gain_mid, bias_mid = column(mgain, 1, lanes), column(mbias, 1, lanes)
    collect_triangle(tri, tri_in)
    sums[...] = jnp.zeros_like(sums)

    def body(step):
        here = lane_block(step, lanes)
        grad = turned_pair(cot, step)
        put_pair(grad_out, step, grad)
        here_normed = pair_of(normed, step)
        outgate = sigmoid(dot(outgate_t, here_normed))
        gated = grad * outgate
        d_outer = gated.astype(BF16)
        d_unit = dot(out_w[1], d_outer)
        scaled_mid, inverse_mid = mid_norm(pair_of(tri_in, step).astype(F32))
        d_tri = norm_backward(d_unit * gain_mid, scaled_mid, inverse_mid)
        put_pair(scr, step, d_tri.astype(BF16))
        unit = (scaled_mid * gain_mid + bias_mid).astype(BF16)
        outer = dot(out_t, unit)
        put_turned_pair(new_out, step, pair_of(mid, step).astype(F32) + outer * outgate)
        d_gatepre = (gated * outer * (1.0 - outgate)).astype(BF16)
        put_pair(d_normed_out, step, dot(outgate_w[1], d_gatepre))
        unit_all[:, here] = unit
        outer_all[:, here] = d_outer
        normed_all[:, here] = here_normed
        gate_all[:, here] = d_gatepre
        return d_unit * scaled_mid, d_unit

    each_pair(rows, body, sums)
    spread_triangle(scr, d_tri_out)
    out_weight_grads(unit_all, outer_all, normed_all, gate_all, weights_out)
    for index in range(2):
        small_out[index : index + 1, :] = as_row(sums[index])


def edge_backward(step, scratch, proj_factor, gate_factor):
    here = pair_of(scratch, step).astype(F32)
    d_proj = (here * pair_of(proj_factor, step)).astype(BF16)
    d_gate = (here * pair_of(gate_factor, step)).astype(BF16)
    return jnp.concatenate([d_proj, d_gate], axis=0)


def middle_kernel(
    d_edge, proj_factor, gate_factor, d_normed_gate, scaled_in, inverse_in, cot, outgate,
    scaled_mid, inverse_mid, normed0, normed1, ngain, mgain, mbias, proj_w, gate_w, out_w,
    outgate_w,
    d_tri_out, grad_out, d_normed_out, out_weights, in_weights, small_out,
    scr, scr_tri, unit_all, outer_all, normed_all, gate_all, upper_all, d_in_all, back, sums,
):
    rows, channels, lanes = cot.shape
    out_t = turned(out_w[0])
    gain = column(ngain, 1, lanes)
    gain_mid, bias_mid = column(mgain, 0, lanes), column(mbias, 0, lanes)
    collect_edges(d_edge, scr)
    sums[...] = jnp.zeros_like(sums)
    load_back_weights(proj_w, gate_w, 1, back)

    def upper(step):
        place = lane_block(step, lanes)
        d_in = edge_backward(step, scr, proj_factor, gate_factor)
        d_in_all[:, place] = d_in
        upper_all[:, place] = pair_of(normed1, step)
        d_normed = pair_of(d_normed_gate, step) + dot(back[...], d_in)
        scaled = pair_of(scaled_in, step)
        grad = pair_of(cot, step) + norm_backward(
            d_normed * gain, scaled, pair_of_rows(inverse_in, step)
        )
        put_pair(grad_out, step, grad)
        return d_normed * scaled, d_normed

    def lower(step):
        place = lane_block(step, lanes)
        gate = pair_of(outgate, step)
        gated = pair_of(grad_out, step) * gate
        d_outer = gated.astype(BF16)
        d_unit = dot(out_w[0], d_outer)
        scaled = pair_of(scaled_mid, step)
        d_tri = norm_backward(d_unit * gain_mid, scaled, pair_of_rows(inverse_mid, step))
        put_pair(scr_tri, step, d_tri.astype(BF16))
        unit = (scaled * gain_mid + bias_mid).astype(BF16)
        outer = dot(out_t, unit)
        d_gatepre = (gated * outer * (1.0 - gate)).astype(BF16)
        put_pair(d_normed_out, step, dot(outgate_w[0], d_gatepre))
        unit_all[:, place] = unit
        outer_all[:, place] = d_outer
        normed_all[:, place] = pair_of(normed0, step)
        gate_all[:, place] = d_gatepre
        return d_unit * scaled, d_unit

    each_pair(rows, upper, sums.at[2:4])
    each_pair(rows, lower, sums.at[0:2])
    spread_triangle(scr_tri, d_tri_out)
    out_weight_grads(unit_all, outer_all, normed_all, gate_all, out_weights)
    in_weight_grads(upper_all, d_in_all, in_weights)
    for index in range(4):
        small_out[index : index + 1, :] = as_row(sums[index])


def split_cores(all_rows, own_out, other_out, few):
    chips, share, width = own_out.shape
    view = all_rows.reshape(chips // few, 2, few, share, width)
    core = lax.rem(lax.axis_index("row"), 2)
    own_out[...] = view[:, core].reshape(own_out.shape)
    other_out[...] = view[:, 1 - core].reshape(other_out.shape)


def finish_kernel(
    few, d_edge, proj_factor, gate_factor, normed, out0, in1, out1,
    own_out, other_out, d_in_all, scr, normed_all, packed,
):
    rows, half, lanes = proj_factor.shape
    collect_edges(d_edge, scr)

    def body(step):
        place = lane_block(step, lanes)
        d_in_all[:, place] = edge_backward(step, scr, proj_factor, gate_factor)
        normed_all[:, place] = pair_of(normed, step)

    each_pair(rows, body)
    first, second, third = d_in_all.shape[0], out0.shape[0], in1.shape[0]
    in_weight_grads(normed_all, d_in_all, packed.at[0:first])
    packed[first : first + second, :] = out0[...]
    packed[first + second : first + second + third, :] = in1[...]
    packed[first + second + third :, :] = out1[...]
    split_cores(packed, own_out, other_out, few)


def norm_sums_kernel(
    d_in, d_normed_gate, scaled_in, proj_w, gate_w, small_middle, small1,
    d_normed_out, extra_out, back, sums,
):
    rows, channels, lanes = scaled_in.shape
    sums[...] = jnp.zeros_like(sums)
    load_back_weights(proj_w, gate_w, 0, back)

    def body(step):
        here = d_in[:, lane_block(step, lanes)]
        d_normed = pair_of(d_normed_gate, step) + dot(back[...], here)
        put_pair(d_normed_out, step, d_normed)
        return d_normed * pair_of(scaled_in, step), d_normed

    each_pair(rows, body, sums)
    small = jnp.concatenate(
        [as_row(sums[0]), as_row(sums[1]), small_middle[0:2], small_middle[2:4], small1[...]],
        axis=0,
    )
    high = small.astype(BF16).astype(F32)
    extra_out[...] = jnp.concatenate([high, small - high], axis=0).astype(BF16)


def add_kernel(first, second, extra, out_ref, extra_out):
    out_ref[...] = (first[...].astype(F32) + second[...].astype(F32)).astype(BF16)
    extra_out[...] = extra[...]


def sum_kernel(parts, extra, shared_out):
    chips, share, width = parts.shape
    own = jnp.sum(parts[...].astype(F32), axis=0).astype(BF16)
    for chip in range(chips):
        shared_out[chip, 0:share] = own
        shared_out[chip, share:] = extra[...]


def grad_pair_kernel(
    share, shared, d_normed, scaled_in, inverse_in, grad, ngain, grad_out, mine_out
):
    rows, channels, lanes = grad.shape
    gain = column(ngain, 0, lanes)
    mine_out[...] = jnp.sum(shared[:, share:].astype(F32), axis=0)

    def body(step):
        total = pair_of(grad, step) + norm_backward(
            pair_of(d_normed, step) * gain, pair_of(scaled_in, step),
            pair_of_rows(inverse_in, step),
        )
        put_turned_pair(grad_out, step, total)

    each_pair(rows, body)


def unpack_kernel(
    share, few, own, other, mine, proj_out, gate_out, out_out, outgate_out,
    norm_gain_out, norm_bias_out, mid_gain_out, mid_bias_out, weights,
):
    chips, _, width = own.shape
    core = lax.rem(lax.axis_index("row"), 2)
    view = weights.reshape(chips // few, 2, few, share, width)
    block = (chips // few, few, share, width)
    view[:, core] = own[:, 0:share].astype(F32).reshape(block)
    view[:, 1 - core] = other[:, 0:share].astype(F32).reshape(block)
    total = mine[...] + jnp.sum(other[:, share:].astype(F32), axis=0)
    total = total[0:8] + total[8:16]
    for module in range(2):
        for index, out in enumerate((norm_gain_out, norm_bias_out, mid_gain_out, mid_bias_out)):
            at = 4 * module + index
            out[module : module + 1, :] = total[at : at + 1]
        blocks = [
            weights[(6 * module + part) * width : (6 * module + part + 1) * width, :]
            for part in range(6)
        ]
        for side in range(2):
            proj_out[module, side] = blocks[side]
            gate_out[module, side] = blocks[2 + side]
        out_out[module] = blocks[4]
        outgate_out[module] = blocks[5]


def triangle_kernel(incoming, edge, tri_out):
    many, few, _, group, rows, lanes = edge.shape

    def whole(side, channel):
        parts = [edge[:, c, side, channel].reshape(many * rows, lanes) for c in range(few)]
        return jnp.concatenate(parts, axis=1)

    for channel in range(group):
        left, right = whole(0, channel), whole(1, channel)
        tri = (dot_lt if incoming else dot_rt)(left, right).astype(BF16)
        for c in range(few):
            part = tri[:, c * lanes : (c + 1) * lanes]
            tri_out[:, c, channel] = part.reshape(many, rows, lanes)


def edge_grad_kernel(incoming, edge, d_tri, grad_out):
    many, few, _, group, rows, lanes = edge.shape

    def whole(ref, *index):
        parts = [ref[(slice(None), c) + index].reshape(many * rows, lanes) for c in range(few)]
        return jnp.concatenate(parts, axis=1)

    for channel in range(group):
        left, right = whole(edge, 0, channel), whole(edge, 1, channel)
        grad = whole(d_tri, channel)
        if incoming:
            d_left, d_right = dot_rt(right, grad), dot(left, grad)
        else:
            d_left, d_right = dot(grad, right), dot_lt(grad, left)
        for side, value in ((0, d_left), (1, d_right)):
            value = value.astype(BF16)
            for c in range(few):
                part = value[:, c * lanes : (c + 1) * lanes]
                grad_out[:, c, side, channel] = part.reshape(many, rows, lanes)


SCALARS = pl.BlockSpec(memory_space=pltpu.SMEM)
VECTORS = pl.BlockSpec(memory_space=pltpu.VMEM)
FAR = pl.BlockSpec(memory_space=pltpu.HBM)


def call(kernel, name, outs, args, scratch=(), flops=0, grant=16, specs=None):
    shapes = [jax.ShapeDtypeStruct(shape, dtype) for shape, dtype in outs]
    moved = sum(a.size * a.dtype.itemsize for a in list(args) + shapes)
    return pl.pallas_call(
        kernel,
        name=name,
        out_shape=shapes,
        in_specs=specs or [VECTORS] * len(args),
        out_specs=[VECTORS] * len(shapes),
        scratch_shapes=[
            pltpu.VMEM(*item) if isinstance(item, tuple) else item for item in scratch
        ],
        compiler_params=pltpu.CompilerParams(vmem_limit_bytes=grant * 1024 * 1024),
        cost_estimate=pl.CostEstimate(flops=flops, bytes_accessed=moved, transcendentals=0),
    )(*args)


def exchange(values):
    return lax.all_to_all(values, ("row", "col"), split_axis=0, concat_axis=0, tiled=True)


def swap_cores(values, many, few):
    pairs = [(index, index ^ few) for index in range(many * few)]
    return lax.ppermute(values, ("row", "col"), pairs)


def exchange_chips(values, many, few):
    groups = [
        [row * few + col for row in range(core, many, 2) for col in range(few)] for core in range(2)
    ]
    return lax.all_to_all(
        values, ("row", "col"), split_axis=0, concat_axis=0, axis_index_groups=groups, tiled=True
    )


def grouped_device(
    pair, cotangent, lengths, ngain, nbias, proj_w, gate_w, mgain, mbias, out_w, outgate_w,
    *, many, few,
):
    rows, lanes, channels = pair.shape
    shards = many * few
    group = H // shards
    edge = ((shards, 2, group, rows, lanes), BF16)
    grid = ((many, few, 2, group, rows, lanes), BF16)
    tri = ((shards, group, rows, lanes), BF16)
    tri_grid = ((many, few, group, rows, lanes), BF16)
    tile = ((rows, channels, lanes), BF16)
    wide = ((rows, channels, lanes), F32)
    row = ((rows, lanes), F32)
    factor = ((rows, 2 * H, lanes), F32)
    back = ((channels, 4 * H), BF16)
    wts = ((4 * H, channels), BF16)
    big = ((rows, 2 * H, lanes), BF16)
    mid = ((rows, H, lanes), BF16)
    positions = rows * lanes
    flat = ((H, positions), BF16)
    flat_in = ((4 * H, positions), BF16)
    out_rows = ((2 * H, channels), BF16)
    in_rows = ((4 * H, H), BF16)
    triangle = 2 * group * (many * rows) ** 2 * (few * lanes)
    dense = 2 * positions * channels * H

    def sums(count):
        return ((count, H, lanes), F32)

    def small(count):
        return ((count, H), F32)

    saved = [tile, factor, factor, wide, row]
    far = [
        pltpu.with_memory_space_constraint(item, pltpu.HBM)
        for item in (pair, ngain, nbias, proj_w, gate_w)
    ]
    sent, normed0, *factors0, mask = call(
        start_kernel, "start", [edge, *saved, row], [lengths, *far],
        [(pair.shape, BF16), (ngain.shape, F32), (nbias.shape, F32), (proj_w.shape, BF16),
         (gate_w.shape, BF16), pltpu.SemaphoreType.DMA((5,)), wts, big],
        4 * dense, specs=[SCALARS] + [FAR] * len(far),
    )
    edge0 = exchange(sent).reshape(grid[0])
    (here,) = call(
        functools.partial(triangle_kernel, False), "outgoing", [tri_grid], [edge0], (), triangle,
    )
    tri0 = exchange(here.reshape(tri[0]))
    sent, mid_t, normed1, *factors1, outgate0, scaled_mid0, inverse_mid0 = call(
        between_kernel, "between", [edge, tile, *saved, wide, wide, row],
        [mask, tri0, pair, normed0, ngain, nbias, mgain, mbias, out_w, outgate_w, proj_w,
         gate_w],
        [wts, mid, big], 6 * dense,
    )
    edge1 = exchange(sent).reshape(grid[0])
    (here,) = call(
        functools.partial(triangle_kernel, True), "incoming", [tri_grid], [edge1], (), triangle,
    )
    tri1 = exchange(here.reshape(tri[0]))
    sent, new_pair, cot_t, d_normed_gate1, out_grads1, small1 = call(
        turn_kernel, "turn", [tri, (pair.shape, BF16), wide, wide, out_rows, small(2)],
        [tri1, mid_t, normed1, cotangent, mgain, mbias, out_w, outgate_w],
        [mid, mid, flat, flat, flat, flat, sums(2)], 6 * dense,
    )
    d_tri1 = exchange(sent).reshape(tri_grid[0])
    (sent,) = call(
        functools.partial(edge_grad_kernel, True), "incoming_grad", [grid], [edge1, d_tri1],
        (), 2 * triangle,
    )
    d_edge1 = exchange(sent.reshape(edge[0]))
    proj_factor1, gate_factor1, scaled1, inverse1 = factors1
    sent, grad, d_normed_gate0, out_grads0, in_grads1, small_middle = call(
        middle_kernel, "middle", [tri, wide, wide, out_rows, in_rows, small(4)],
        [d_edge1, proj_factor1, gate_factor1, d_normed_gate1, scaled1, inverse1, cot_t, outgate0,
         scaled_mid0, inverse_mid0, normed0, normed1, ngain, mgain, mbias, proj_w, gate_w, out_w,
         outgate_w],
        [big, mid, flat, flat, flat, flat, flat, flat_in, back, sums(4)], 13 * dense,
    )
    d_tri0 = exchange(sent).reshape(tri_grid[0])
    (sent,) = call(
        functools.partial(edge_grad_kernel, False), "outgoing_grad", [grid], [edge0, d_tri0],
        (), 2 * triangle,
    )
    d_edge0 = exchange(sent.reshape(edge[0]))
    share = 12 * H // shards
    chips = shards // 2
    proj_factor0, gate_factor0, scaled0, inverse0 = factors0
    held = ((chips, share, H), BF16)
    own, other, d_in0 = call(
        functools.partial(finish_kernel, few), "finish", [held, held, flat_in],
        [d_edge0, proj_factor0, gate_factor0, normed0, out_grads0, in_grads1, out_grads1],
        [big, flat, ((12 * H, H), BF16)], 4 * dense,
    )
    other = swap_cores(other, many, few)
    d_normed0, extra = call(
        norm_sums_kernel, "norm_sums", [wide, ((16, H), BF16)],
        [d_in0, d_normed_gate0, scaled0, proj_w, gate_w, small_middle, small1], [back, sums(2)],
        4 * dense,
    )
    own, extra = call(add_kernel, "add_cores", [held, ((16, H), BF16)], [own, other, extra])
    parts = exchange_chips(own, many, few)
    (shared,) = call(
        sum_kernel, "sum_weights", [((chips, share + 16, H), BF16)], [parts, extra]
    )
    shared = exchange_chips(shared, many, few)
    other = swap_cores(shared, many, few)
    grad_pair, mine = call(
        functools.partial(grad_pair_kernel, share), "grad_pair",
        [(pair.shape, BF16), ((16, H), F32)],
        [shared, d_normed0, scaled0, inverse0, grad, ngain],
    )
    grad_proj, grad_gate, grad_out, grad_outgate, *vectors = call(
        functools.partial(unpack_kernel, share, few), "unpack",
        [(proj_w.shape, F32), (gate_w.shape, F32), (out_w.shape, F32), (outgate_w.shape, F32),
         (ngain.shape, F32), (nbias.shape, F32), (mgain.shape, F32), (mbias.shape, F32)],
        [shared, other, mine], [((12 * H, H), F32)],
    )
    return (
        new_pair,
        grad_pair,
        vectors[0],
        vectors[1],
        grad_proj,
        grad_gate,
        vectors[2],
        vectors[3],
        grad_out,
        grad_outgate,
    )


def norm_channels(values):
    average = jnp.mean(values, -1, keepdims=True)
    centred = values - average
    variance = jnp.mean(centred * centred, -1, keepdims=True)
    inverse = lax.rsqrt(variance + EPS)
    return (centred * inverse, inverse)


def forward_module(pair_in, pair_mask, weights, incoming):
    gain_in, bias_in, proj_w, gate_w, gain_mid, bias_mid, out_w, outgate_w = weights
    scaled_in, inverse_in = norm_channels(pair_in.astype(jnp.float32))
    normed = (scaled_in * gain_in + bias_in).astype(jnp.bfloat16)
    projected = product("ijc,sch->shij", normed, proj_w)
    gating = jax.nn.sigmoid(product("ijc,sch->shij", normed, gate_w))
    hidden = (projected * gating * pair_mask).astype(jnp.bfloat16)
    left_side, right_side = (
        lax.all_to_all(hidden[0], "row", split_axis=0, concat_axis=1, tiled=True),
        lax.all_to_all(hidden[1], "row", split_axis=0, concat_axis=1, tiled=True),
    )
    if incoming:
        left_side = jnp.swapaxes(left_side, 1, 2)
        right_side = jnp.swapaxes(right_side, 1, 2)
    else:
        left_side, right_side = (
            lax.all_to_all(left_side, "col", split_axis=1, concat_axis=2, tiled=True),
            lax.all_to_all(right_side, "col", split_axis=1, concat_axis=2, tiled=True),
        )
    triangle = product(
        "cik,cjk->cij", left_side, lax.all_gather(right_side, "col", axis=1, tiled=True)
    ).astype(jnp.bfloat16)
    triangle = lax.all_to_all(
        lax.all_to_all(triangle, "col", split_axis=2, concat_axis=1, tiled=True),
        "row",
        split_axis=1,
        concat_axis=0,
        tiled=True,
    )
    tri_values = triangle.astype(jnp.float32)
    total, squares = lax.psum((jnp.sum(tri_values, 0), jnp.sum(tri_values * tri_values, 0)), "ch")
    average = total / H
    inverse_mid = lax.rsqrt(squares / H - average * average + EPS)
    scaled_mid = (tri_values - average) * inverse_mid
    unit = (scaled_mid * gain_mid[:, None, None] + bias_mid[:, None, None]).astype(jnp.bfloat16)
    unit_full = lax.all_gather(unit, "ch", axis=0, tiled=True)
    outer = product("hij,hc->ijc", unit_full, out_w)
    outgate = jax.nn.sigmoid(product("ijc,cd->ijd", normed, outgate_w))
    result = (pair_in.astype(jnp.float32) + outer * outgate).astype(jnp.bfloat16)
    saved = (
        scaled_in,
        inverse_in,
        normed,
        projected,
        gating,
        left_side,
        right_side,
        scaled_mid,
        inverse_mid,
        unit_full,
        outer,
        outgate,
    )
    return (result, saved)


def backward_module(grad_out, pair_mask, weights, saved, incoming):
    gain_in, bias_in, proj_w, gate_w, gain_mid, bias_mid, out_w, outgate_w = weights
    (
        scaled_in,
        inverse_in,
        normed,
        projected,
        gating,
        left_side,
        right_side,
        scaled_mid,
        inverse_mid,
        unit_full,
        outer,
        outgate,
    ) = saved
    d_outer = (grad_out * outgate).astype(jnp.bfloat16)
    d_gatepre = (grad_out * outer * outgate * (1.0 - outgate)).astype(jnp.bfloat16)
    grad_out_w = product("hij,ijc->hc", unit_full, d_outer)
    grad_outgate_w = product("ijc,ijd->cd", normed, d_gatepre)
    width = gain_mid.shape[0]
    own_rows = lax.dynamic_slice_in_dim(out_w, lax.axis_index("ch") * width, width, 0)
    d_unit = product("ijc,hc->hij", d_outer, own_rows)
    d_normed = product("ijd,cd->ijc", d_gatepre, outgate_w)
    weighted = d_unit * gain_mid[:, None, None]
    grad_gain_mid = jnp.sum(d_unit * scaled_mid, (1, 2))
    grad_bias_mid = jnp.sum(d_unit, (1, 2))
    first_sum, second_sum = lax.psum(
        (jnp.sum(weighted, 0), jnp.sum(weighted * scaled_mid, 0)), "ch"
    )
    d_tri = (inverse_mid * (weighted - first_sum / H - scaled_mid * (second_sum / H))).astype(
        jnp.bfloat16
    )
    grad_rows = lax.all_to_all(d_tri, "row", split_axis=0, concat_axis=1, tiled=True)
    grad_cols = lax.all_to_all(grad_rows, "col", split_axis=1, concat_axis=2, tiled=True)
    d_left = product(
        "cij,cjk->cik", grad_cols, lax.all_gather(right_side, "col", axis=1, tiled=True)
    )
    partial_terms = product("cij,cik->cjk", grad_cols, left_side)
    d_right = lax.psum_scatter(
        partial_terms.astype(jnp.bfloat16), "col", scatter_dimension=1, tiled=True
    ).astype(jnp.float32)
    d_left = d_left.astype(jnp.bfloat16)
    d_right = d_right.astype(jnp.bfloat16)
    if incoming:
        d_left = jnp.swapaxes(d_left, 1, 2)
        d_right = jnp.swapaxes(d_right, 1, 2)
    else:
        d_left, d_right = (
            lax.all_to_all(d_left, "col", split_axis=2, concat_axis=1, tiled=True),
            lax.all_to_all(d_right, "col", split_axis=2, concat_axis=1, tiled=True),
        )
    d_left, d_right = (
        lax.all_to_all(d_left, "row", split_axis=1, concat_axis=0, tiled=True),
        lax.all_to_all(d_right, "row", split_axis=1, concat_axis=0, tiled=True),
    )
    d_hidden = jnp.stack([d_left, d_right]).astype(jnp.float32)
    d_proj = (d_hidden * gating * pair_mask).astype(jnp.bfloat16)
    d_gate = (d_hidden * projected * gating * (1.0 - gating) * pair_mask).astype(jnp.bfloat16)
    grad_proj_w = product("ijc,shij->sch", normed, d_proj)
    grad_gate_w = product("ijc,shij->sch", normed, d_gate)
    partial_input = product("shij,sch->ijc", d_proj, proj_w) + product(
        "shij,sch->ijc", d_gate, gate_w
    )
    d_normed = d_normed + lax.psum(partial_input.astype(jnp.bfloat16), "ch").astype(jnp.float32)
    weighted_in = d_normed * gain_in
    grad_gain_in = jnp.sum(d_normed * scaled_in, (0, 1))
    grad_bias_in = jnp.sum(d_normed, (0, 1))
    d_pair = inverse_in * (
        weighted_in
        - jnp.mean(weighted_in, -1, keepdims=True)
        - scaled_in * jnp.mean(weighted_in * scaled_in, -1, keepdims=True)
    )
    grads = (
        grad_gain_in,
        grad_bias_in,
        grad_proj_w,
        grad_gate_w,
        grad_gain_mid,
        grad_bias_mid,
        grad_out_w,
        grad_outgate_w,
    )
    return (grad_out + d_pair, grads)


def per_device(
    pair,
    cotangent,
    lengths,
    norm_gain,
    norm_bias,
    proj_weight,
    gate_weight,
    mid_gain,
    mid_bias,
    out_weight,
    outgate_weight,
):
    rows_here = pair.shape[0]
    cols_here = pair.shape[1]
    row_ids = lax.axis_index("row") * rows_here + lax.iota(jnp.int32, rows_here)
    col_ids = lax.axis_index("col") * cols_here + lax.iota(jnp.int32, cols_here)
    limit = lengths[0]
    pair_mask = ((row_ids[:, None] < limit) & (col_ids[None, :] < limit)).astype(jnp.float32)
    state = pair
    stash = []
    for layer in range(2):
        weights = (
            norm_gain[layer],
            norm_bias[layer],
            proj_weight[layer],
            gate_weight[layer],
            mid_gain[layer],
            mid_bias[layer],
            out_weight[layer],
            outgate_weight[layer],
        )
        state, saved = forward_module(state, pair_mask, weights, layer == 1)
        stash.append(saved)
    grad_state = cotangent.astype(jnp.float32)
    per_layer = [None, None]
    for layer in (1, 0):
        weights = (
            norm_gain[layer],
            norm_bias[layer],
            proj_weight[layer],
            gate_weight[layer],
            mid_gain[layer],
            mid_bias[layer],
            out_weight[layer],
            outgate_weight[layer],
        )
        grad_state, grads = backward_module(
            grad_state, pair_mask, weights, stash[layer], layer == 1
        )
        per_layer[layer] = grads
    lower = per_layer[0]
    upper = per_layer[1]
    summed = lax.psum(
        (
            lower[0],
            lower[1],
            lower[2],
            lower[3],
            lower[4],
            lower[5],
            lower[6],
            lower[7],
            upper[0],
            upper[1],
            upper[2],
            upper[3],
            upper[4],
            upper[5],
            upper[6],
            upper[7],
        ),
        ("row", "col"),
    )
    per_layer = [summed[0:8], summed[8:16]]
    stacked = [jnp.stack([per_layer[0][index], per_layer[1][index]]) for index in range(8)]
    return (
        state,
        grad_state.astype(jnp.bfloat16),
        stacked[0],
        stacked[1],
        stacked[2],
        stacked[3],
        stacked[4],
        stacked[5],
        stacked[6],
        stacked[7],
    )


def on_device(pair, *rest, many, few, split):
    rows, lanes, channels = pair.shape
    shards = many * few
    whole_channels = split == 1 and H % shards == 0 and BLOCK % (H // shards) == 0 and H % (2 * BLOCK) == 0
    tiles = rows == BLOCK and lanes % 128 == 0 and channels == H
    if whole_channels and tiles and many % 2 == 0 and few & (few - 1) == 0:
        return grouped_device(pair, *rest, many=many, few=few)
    return per_device(pair, *rest)


def solution(mesh):
    in_specs = (
        P(("grp", "row"), "col", None),
        P(("grp", "row"), "col", None),
        P("grp"),
        P(),
        P(),
        P(None, None, None, "ch"),
        P(None, None, None, "ch"),
        P(None, "ch"),
        P(None, "ch"),
        P(),
        P(),
    )
    out_specs = (
        P(("grp", "row"), "col", None),
        P(("grp", "row"), "col", None),
        P("grp", None),
        P("grp", None),
        P("grp", None, None, "ch"),
        P("grp", None, None, "ch"),
        P("grp", "ch"),
        P("grp", "ch"),
        P("grp", None, None),
        P("grp", None, None),
    )
    body = functools.partial(
        on_device, many=mesh.shape["row"], few=mesh.shape["col"], split=mesh.shape["ch"]
    )
    return jax.shard_map(
        body, mesh=mesh, in_specs=in_specs, out_specs=out_specs, check_vma=False
    )
```

```python
import functools

import jax
import jax.numpy as jnp
from jax import lax
from jax.experimental import pallas as pl
from jax.experimental.pallas import tpu as pltpu
from jax.sharding import PartitionSpec as P

H = 128


EPS = 1e-05


def product(spec, left, right):
    return jnp.einsum(spec, left, right, preferred_element_type=jnp.float32)


F32 = jnp.float32
BF16 = jnp.bfloat16


def dot(left, right):
    return lax.dot_general(left, right, (((1,), (0,)), ((), ())), preferred_element_type=F32)


def dot_rt(left, right):
    return lax.dot_general(left, right, (((1,), (1,)), ((), ())), preferred_element_type=F32)


def dot_lt(left, right):
    return lax.dot_general(left, right, (((0,), (0,)), ((), ())), preferred_element_type=F32)


def sigmoid(values):
    return 0.5 * jnp.tanh(0.5 * values) + 0.5


def norm_rows(values):
    scale = 1.0 / values.shape[0]
    average = jnp.sum(values, 0, keepdims=True) * scale
    centred = values - average
    variance = jnp.sum(centred * centred, 0, keepdims=True) * scale
    inverse = lax.rsqrt(variance + EPS)
    return centred * inverse, inverse


def turned(weight):
    return jnp.transpose(weight.astype(F32)).astype(BF16)


def column(ref, module, lanes):
    row = ref[module : module + 1, :]
    return beside(*[jnp.transpose(jnp.broadcast_to(row, (lanes, row.shape[1])))] * 2)


def beside(left, right):
    return jnp.concatenate([left, right], axis=-1)


def pair_of(ref, step):
    return beside(ref[2 * step], ref[2 * step + 1])


def put_pair(ref, step, values):
    lanes = ref.shape[-1]
    ref[2 * step] = values[:, :lanes]
    ref[2 * step + 1] = values[:, lanes:]


def pair_of_rows(ref, step):
    return beside(ref[2 * step : 2 * step + 1, :], ref[2 * step + 1 : 2 * step + 2, :])


def put_pair_of_rows(ref, step, values):
    lanes = ref.shape[-1]
    ref[2 * step : 2 * step + 1, :] = values[:, :lanes]
    ref[2 * step + 1 : 2 * step + 2, :] = values[:, lanes:]


def identity(size):
    down = lax.broadcasted_iota(jnp.int32, (size, size), 0)
    across = lax.broadcasted_iota(jnp.int32, (size, size), 1)
    return jnp.where(down == across, 1.0, 0.0).astype(BF16)


def turned_pair(unit_matrix, ref, step):
    lanes, channels = ref.shape[1:]
    both = ref[2 * step : 2 * step + 2].reshape(2 * lanes, channels)
    return dot_rt(unit_matrix, both)


def put_turned_pair(unit_matrix, ref, step, values):
    lanes = ref.shape[1]
    values = values.astype(BF16)
    ref[2 * step] = dot_rt(unit_matrix, values[:, :lanes]).astype(BF16)
    ref[2 * step + 1] = dot_rt(unit_matrix, values[:, lanes:]).astype(BF16)


def copy_pair_out(near, far, sems, step):
    here = pl.ds(2 * step, 2)
    return pltpu.make_async_copy(near.at[here], far.at[here], sems.at[step])


def as_row(total):
    return jnp.sum(jnp.transpose(total), 0, keepdims=True)


def row_mask(lengths_ref, step, rows, lanes):
    limit = lengths_ref[0]
    row_id = lax.axis_index("row") * rows + step
    col_id = lax.axis_index("col") * lanes + lax.broadcasted_iota(jnp.int32, (1, lanes), 1)
    return jnp.where((row_id < limit) & (col_id < limit), 1.0, 0.0).astype(F32)


def load_in_weights(proj_ref, gate_ref, module, scratch):
    width = proj_ref.shape[-1]
    for side in range(2):
        scratch[side * width : (side + 1) * width, :] = turned(proj_ref[module, side])
        scratch[(2 + side) * width : (3 + side) * width, :] = turned(gate_ref[module, side])


def load_back_weights(proj_ref, gate_ref, module, scratch):
    width = proj_ref.shape[-1]
    for side in range(2):
        scratch[:, side * width : (side + 1) * width] = proj_ref[module, side]
        scratch[:, (2 + side) * width : (3 + side) * width] = gate_ref[module, side]


BLOCK = 16


def turn_matrix(rows):
    size = BLOCK * rows
    out = lax.broadcasted_iota(jnp.int32, (size, size), 0)
    source = lax.broadcasted_iota(jnp.int32, (size, size), 1)
    return jnp.where(source == (out % rows) * BLOCK + out // rows, 1.0, 0.0).astype(BF16)


def spread_blocks(matrix, scratch, start, group):
    rows, _, lanes = scratch.shape
    blocks = [
        scratch[:, at : at + BLOCK, :].reshape(rows * BLOCK, lanes)
        for at in (start, start + BLOCK)
    ]
    both = dot(matrix, beside(*blocks)).astype(BF16)
    parts = [
        part.reshape(BLOCK // group, group, rows, lanes)
        for part in (both[:, :lanes], both[:, lanes:])
    ]
    return jnp.concatenate(parts, axis=0)


def collect_blocks(matrix, values, scratch, start):
    rows, _, lanes = scratch.shape
    flat = values.reshape(2, BLOCK * rows, lanes)
    both = dot(matrix, beside(flat[0], flat[1])).astype(BF16)
    for at, part in ((start, both[:, :lanes]), (start + BLOCK, both[:, lanes:])):
        scratch[:, at : at + BLOCK, :] = part.reshape(rows, BLOCK, lanes)


def spread_edges(scratch, out_ref):
    shards, sides, group, rows, lanes = out_ref.shape
    matrix, step = turn_matrix(rows), 2 * BLOCK // group
    for side in range(sides):
        for shard in range(0, shards, step):
            start = (side * shards + shard) * group
            out_ref[shard : shard + step, side] = spread_blocks(matrix, scratch, start, group)


def collect_edges(in_ref, scratch):
    shards, sides, group, rows, lanes = in_ref.shape
    matrix, step = turn_matrix(rows), 2 * BLOCK // group
    for side in range(sides):
        for shard in range(0, shards, step):
            start = (side * shards + shard) * group
            collect_blocks(matrix, in_ref[shard : shard + step, side], scratch, start)


def spread_triangle(scratch, out_ref):
    shards, group, rows, lanes = out_ref.shape
    matrix, step = turn_matrix(rows), 2 * BLOCK // group
    for shard in range(0, shards, step):
        out_ref[shard : shard + step] = spread_blocks(matrix, scratch, shard * group, group)


def collect_triangle(in_ref, scratch):
    shards, group, rows, lanes = in_ref.shape
    matrix, step = turn_matrix(rows), 2 * BLOCK // group
    for shard in range(0, shards, step):
        collect_blocks(matrix, in_ref[shard : shard + step], scratch, shard * group)


def each_pair(rows, body, sums=None):
    for block in range(0, rows // 2, 2):
        parts = [body(block + step) for step in range(2)]
        for index in range(0 if sums is None else sums.shape[0]):
            total = parts[0][index] + parts[1][index]
            lanes = sums.shape[-1]
            sums[index] += total[:, :lanes] + total[:, lanes:]


def mid_norm(tri):
    scale = 1.0 / tri.shape[0]
    average = jnp.sum(tri, 0, keepdims=True) * scale
    squares = jnp.sum(tri * tri, 0, keepdims=True) * scale
    inverse = lax.rsqrt(squares - average * average + EPS)
    return (tri - average) * inverse, inverse


def norm_backward(weighted, scaled, inverse):
    scale = 1.0 / weighted.shape[0]
    first = jnp.sum(weighted, 0, keepdims=True) * scale
    second = jnp.sum(weighted * scaled, 0, keepdims=True) * scale
    return inverse * (weighted - first - scaled * second)


def save_norm(step, values, scaled_out, inverse_out):
    scaled, inverse = norm_rows(values)
    put_pair(scaled_out, step, scaled)
    put_pair_of_rows(inverse_out, step, inverse)
    return scaled


def save_edges(step, normed, in_weights, mask, proj_out, gate_out):
    pre = dot(in_weights, normed)
    half = pre.shape[0] // 2
    gating = sigmoid(pre[half:])
    factor = gating * mask
    value = pre[:half] * factor
    put_pair(proj_out, step, factor)
    put_pair(gate_out, step, value * (1.0 - gating))
    return value.astype(BF16)


def start_kernel(
    lengths, pair_far, ngain_far, nbias_far, proj_far, gate_far,
    edge_out, normed_out, proj_out, gate_out, scaled_out, inverse_out, mask_out,
    pair, ngain, nbias, proj_w, gate_w, sems, wts, scr,
):
    far = (proj_far.at[0], gate_far.at[0], ngain_far, nbias_far, pair_far)
    near = (proj_w.at[0], gate_w.at[0], ngain, nbias, pair)
    copies = [
        pltpu.make_async_copy(source, target, sems.at[index])
        for index, (source, target) in enumerate(zip(far, near))
    ]
    for copy in copies:
        copy.start()
    for copy in copies:
        copy.wait()
    rows, lanes, channels = pair.shape
    load_in_weights(proj_w, gate_w, 0, wts)
    unit_matrix = identity(channels)
    gain, bias = column(ngain, 0, lanes), column(nbias, 0, lanes)

    def body(step):
        base = turned_pair(unit_matrix, pair, step)
        scaled = save_norm(step, base, scaled_out, inverse_out)
        normed = (scaled * gain + bias).astype(BF16)
        put_pair(normed_out, step, normed)
        mask = beside(*[row_mask(lengths, 2 * step + row, rows, lanes) for row in range(2)])
        put_pair_of_rows(mask_out, step, mask)
        put_pair(scr, step, save_edges(step, normed, wts[...], mask, proj_out, gate_out))

    each_pair(rows, body)
    spread_edges(scr, edge_out)


def between_kernel(
    mask_all, tri, pair, normed0, ngain, nbias, mgain, mbias, out_w, outgate_w, proj_w, gate_w,
    edge_out, mid_out, normed_out, proj_out, gate_out, scaled_out, inverse_out,
    outgate_out, scaled_mid_out, inverse_mid_out, wts, tri_in, scr,
):
    rows, lanes, channels = pair.shape
    load_in_weights(proj_w, gate_w, 1, wts)
    unit_matrix = identity(channels)
    out_t, outgate_t = turned(out_w[0]), turned(outgate_w[0])
    gain, bias = column(ngain, 1, lanes), column(nbias, 1, lanes)
    gain_mid, bias_mid = column(mgain, 0, lanes), column(mbias, 0, lanes)
    collect_triangle(tri, tri_in)

    def body(step):
        scaled_mid, inverse_mid = mid_norm(pair_of(tri_in, step).astype(F32))
        put_pair(scaled_mid_out, step, scaled_mid)
        put_pair_of_rows(inverse_mid_out, step, inverse_mid)
        unit = (scaled_mid * gain_mid + bias_mid).astype(BF16)
        outer = dot(out_t, unit)
        outgate = sigmoid(dot(outgate_t, pair_of(normed0, step)))
        put_pair(outgate_out, step, outgate)
        mid = (turned_pair(unit_matrix, pair, step) + outer * outgate).astype(BF16)
        put_pair(mid_out, step, mid)
        scaled = save_norm(step, mid.astype(F32), scaled_out, inverse_out)
        normed = (scaled * gain + bias).astype(BF16)
        put_pair(normed_out, step, normed)
        mask = pair_of_rows(mask_all, step)
        put_pair(scr, step, save_edges(step, normed, wts[...], mask, proj_out, gate_out))

    each_pair(rows, body)
    spread_edges(scr, edge_out)


def out_weight_grads(unit, d_outer, normed, d_gatepre, out_ref):
    width = unit.shape[0]
    out_ref[0:width, :] = dot_rt(unit[...], d_outer[...]).astype(out_ref.dtype)
    out_ref[width:, :] = dot_rt(normed[...], d_gatepre[...]).astype(out_ref.dtype)


def in_weight_grads(normed_all, d_in_all, out_ref):
    width = normed_all.shape[0]
    for part in range(d_in_all.shape[0] // width):
        block = slice(part * width, (part + 1) * width)
        out_ref[block, :] = dot_rt(normed_all[...], d_in_all[block, :]).astype(out_ref.dtype)


def lane_block(step, lanes):
    return pl.ds(2 * step * lanes, 2 * lanes)


def turn_kernel(
    tri, mid, normed, cot, mgain, mbias, out_w, outgate_w,
    d_tri_out, new_out, grad_out, d_normed_out, weights_out, small_out,
    new_near, sems, tri_in, scr, unit_all, outer_all, normed_all, gate_all, sums,
):
    rows, channels, lanes = mid.shape
    unit_matrix = identity(channels)
    out_t, outgate_t = turned(out_w[1]), turned(outgate_w[1])
    gain_mid, bias_mid = column(mgain, 1, lanes), column(mbias, 1, lanes)
    collect_triangle(tri, tri_in)
    sums[...] = jnp.zeros_like(sums)

    def body(step):
        here = lane_block(step, lanes)
        grad = turned_pair(unit_matrix, cot, step)
        put_pair(grad_out, step, grad)
        here_normed = pair_of(normed, step)
        outgate = sigmoid(dot(outgate_t, here_normed))
        gated = grad * outgate
        d_outer = gated.astype(BF16)
        d_unit = dot(out_w[1], d_outer)
        scaled_mid, inverse_mid = mid_norm(pair_of(tri_in, step).astype(F32))
        d_tri = norm_backward(d_unit * gain_mid, scaled_mid, inverse_mid)
        put_pair(scr, step, d_tri.astype(BF16))
        unit = (scaled_mid * gain_mid + bias_mid).astype(BF16)
        outer = dot(out_t, unit)
        update = pair_of(mid, step).astype(F32) + outer * outgate
        put_turned_pair(unit_matrix, new_near, step, update)
        copy_pair_out(new_near, new_out, sems, step).start()
        d_gatepre = (gated * outer * (1.0 - outgate)).astype(BF16)
        put_pair(d_normed_out, step, dot(outgate_w[1], d_gatepre))
        unit_all[:, here] = unit
        outer_all[:, here] = d_outer
        normed_all[:, here] = here_normed
        gate_all[:, here] = d_gatepre
        return d_unit * scaled_mid, d_unit

    each_pair(rows, body, sums)
    spread_triangle(scr, d_tri_out)
    out_weight_grads(unit_all, outer_all, normed_all, gate_all, weights_out)
    for index in range(2):
        small_out[index : index + 1, :] = as_row(sums[index])
    for step in range(rows // 2):
        copy_pair_out(new_near, new_out, sems, step).wait()


def edge_backward(step, scratch, proj_factor, gate_factor):
    here = pair_of(scratch, step).astype(F32)
    d_proj = (here * pair_of(proj_factor, step)).astype(BF16)
    d_gate = (here * pair_of(gate_factor, step)).astype(BF16)
    return jnp.concatenate([d_proj, d_gate], axis=0)


def middle_kernel(
    d_edge, proj_factor, gate_factor, d_normed_gate, scaled_in, inverse_in, cot, outgate,
    scaled_mid, inverse_mid, normed0, normed1, ngain, mgain, mbias, proj_w, gate_w, out_w,
    outgate_w,
    d_tri_out, grad_out, d_normed_out, out_weights, in_weights, small_out,
    scr, scr_tri, unit_all, outer_all, normed_all, gate_all, upper_all, d_in_all, back, sums,
):
    rows, channels, lanes = cot.shape
    out_t = turned(out_w[0])
    gain = column(ngain, 1, lanes)
    gain_mid, bias_mid = column(mgain, 0, lanes), column(mbias, 0, lanes)
    collect_edges(d_edge, scr)
    sums[...] = jnp.zeros_like(sums)
    load_back_weights(proj_w, gate_w, 1, back)

    def upper(step):
        place = lane_block(step, lanes)
        d_in = edge_backward(step, scr, proj_factor, gate_factor)
        d_in_all[:, place] = d_in
        upper_all[:, place] = pair_of(normed1, step)
        d_normed = pair_of(d_normed_gate, step) + dot(back[...], d_in)
        scaled = pair_of(scaled_in, step)
        grad = pair_of(cot, step) + norm_backward(
            d_normed * gain, scaled, pair_of_rows(inverse_in, step)
        )
        put_pair(grad_out, step, grad)
        return d_normed * scaled, d_normed

    def lower(step):
        place = lane_block(step, lanes)
        gate = pair_of(outgate, step)
        gated = pair_of(grad_out, step) * gate
        d_outer = gated.astype(BF16)
        d_unit = dot(out_w[0], d_outer)
        scaled = pair_of(scaled_mid, step)
        d_tri = norm_backward(d_unit * gain_mid, scaled, pair_of_rows(inverse_mid, step))
        put_pair(scr_tri, step, d_tri.astype(BF16))
        unit = (scaled * gain_mid + bias_mid).astype(BF16)
        outer = dot(out_t, unit)
        d_gatepre = (gated * outer * (1.0 - gate)).astype(BF16)
        put_pair(d_normed_out, step, dot(outgate_w[0], d_gatepre))
        unit_all[:, place] = unit
        outer_all[:, place] = d_outer
        normed_all[:, place] = pair_of(normed0, step)
        gate_all[:, place] = d_gatepre
        return d_unit * scaled, d_unit

    each_pair(rows, upper, sums.at[2:4])
    each_pair(rows, lower, sums.at[0:2])
    spread_triangle(scr_tri, d_tri_out)
    out_weight_grads(unit_all, outer_all, normed_all, gate_all, out_weights)
    in_weight_grads(upper_all, d_in_all, in_weights)
    for index in range(4):
        small_out[index : index + 1, :] = as_row(sums[index])


def split_cores(all_rows, own_out, other_out, few):
    chips, share, width = own_out.shape
    view = all_rows.reshape(chips // few, 2, few, share, width)
    core = lax.rem(lax.axis_index("row"), 2)
    own_out[...] = view[:, core].reshape(own_out.shape)
    other_out[...] = view[:, 1 - core].reshape(other_out.shape)


def finish_kernel(
    few, d_edge, proj_factor, gate_factor, normed, out0, in1, out1,
    own_out, other_out, d_in_all, scr, normed_all, packed,
):
    rows, half, lanes = proj_factor.shape
    collect_edges(d_edge, scr)

    def body(step):
        place = lane_block(step, lanes)
        d_in_all[:, place] = edge_backward(step, scr, proj_factor, gate_factor)
        normed_all[:, place] = pair_of(normed, step)

    each_pair(rows, body)
    first, second, third = d_in_all.shape[0], out0.shape[0], in1.shape[0]
    in_weight_grads(normed_all, d_in_all, packed.at[0:first])
    packed[first : first + second, :] = out0[...]
    packed[first + second : first + second + third, :] = in1[...]
    packed[first + second + third :, :] = out1[...]
    split_cores(packed, own_out, other_out, few)


def norm_sums_kernel(
    d_in, d_normed_gate, scaled_in, proj_w, gate_w, small_middle, small1,
    d_normed_out, extra_out, back, sums,
):
    rows, channels, lanes = scaled_in.shape
    sums[...] = jnp.zeros_like(sums)
    load_back_weights(proj_w, gate_w, 0, back)

    def body(step):
        here = d_in[:, lane_block(step, lanes)]
        d_normed = pair_of(d_normed_gate, step) + dot(back[...], here)
        put_pair(d_normed_out, step, d_normed)
        return d_normed * pair_of(scaled_in, step), d_normed

    each_pair(rows, body, sums)
    small = jnp.concatenate(
        [as_row(sums[0]), as_row(sums[1]), small_middle[0:2], small_middle[2:4], small1[...]],
        axis=0,
    )
    high = small.astype(BF16).astype(F32)
    extra_out[...] = jnp.concatenate([high, small - high], axis=0).astype(BF16)


def add_kernel(first, second, extra, out_ref, extra_out):
    out_ref[...] = (first[...].astype(F32) + second[...].astype(F32)).astype(BF16)
    extra_out[...] = extra[...]


def sum_kernel(parts, extra, shared_out):
    chips, share, width = parts.shape
    own = jnp.sum(parts[...].astype(F32), axis=0).astype(BF16)
    for chip in range(chips):
        shared_out[chip, 0:share] = own
        shared_out[chip, share:] = extra[...]


def grad_pair_kernel(
    share, shared, d_normed, scaled_in, inverse_in, grad, ngain, grad_out, mine_out,
    grad_near, sems,
):
    rows, channels, lanes = grad.shape
    unit_matrix = identity(channels)
    gain = column(ngain, 0, lanes)
    mine_out[...] = jnp.sum(shared[:, share:].astype(F32), axis=0)

    def body(step):
        total = pair_of(grad, step) + norm_backward(
            pair_of(d_normed, step) * gain, pair_of(scaled_in, step),
            pair_of_rows(inverse_in, step),
        )
        put_turned_pair(unit_matrix, grad_near, step, total)
        copy_pair_out(grad_near, grad_out, sems, step).start()

    each_pair(rows, body)
    for step in range(rows // 2):
        copy_pair_out(grad_near, grad_out, sems, step).wait()


def unpack_kernel(
    share, few, own, other, mine, proj_out, gate_out, out_out, outgate_out,
    norm_gain_out, norm_bias_out, mid_gain_out, mid_bias_out, weights,
):
    chips, _, width = own.shape
    core = lax.rem(lax.axis_index("row"), 2)
    view = weights.reshape(chips // few, 2, few, share, width)
    block = (chips // few, few, share, width)
    view[:, core] = own[:, 0:share].astype(F32).reshape(block)
    view[:, 1 - core] = other[:, 0:share].astype(F32).reshape(block)
    total = mine[...] + jnp.sum(other[:, share:].astype(F32), axis=0)
    total = total[0:8] + total[8:16]
    for module in range(2):
        for index, out in enumerate((norm_gain_out, norm_bias_out, mid_gain_out, mid_bias_out)):
            at = 4 * module + index
            out[module : module + 1, :] = total[at : at + 1]
        blocks = [
            weights[(6 * module + part) * width : (6 * module + part + 1) * width, :]
            for part in range(6)
        ]
        for side in range(2):
            proj_out[module, side] = blocks[side]
            gate_out[module, side] = blocks[2 + side]
        out_out[module] = blocks[4]
        outgate_out[module] = blocks[5]


def triangle_kernel(incoming, edge, tri_out):
    many, few, _, group, rows, lanes = edge.shape

    def whole(side, channel):
        parts = [edge[:, c, side, channel].reshape(many * rows, lanes) for c in range(few)]
        return jnp.concatenate(parts, axis=1)

    for channel in range(group):
        left, right = whole(0, channel), whole(1, channel)
        tri = (dot_lt if incoming else dot_rt)(left, right).astype(BF16)
        for c in range(few):
            part = tri[:, c * lanes : (c + 1) * lanes]
            tri_out[:, c, channel] = part.reshape(many, rows, lanes)


def edge_grad_kernel(incoming, edge, d_tri, grad_out):
    many, few, _, group, rows, lanes = edge.shape

    def whole(ref, *index):
        parts = [ref[(slice(None), c) + index].reshape(many * rows, lanes) for c in range(few)]
        return jnp.concatenate(parts, axis=1)

    for channel in range(group):
        left, right = whole(edge, 0, channel), whole(edge, 1, channel)
        grad = whole(d_tri, channel)
        if incoming:
            d_left, d_right = dot_rt(right, grad), dot(left, grad)
        else:
            d_left, d_right = dot(grad, right), dot_lt(grad, left)
        for side, value in ((0, d_left), (1, d_right)):
            value = value.astype(BF16)
            for c in range(few):
                part = value[:, c * lanes : (c + 1) * lanes]
                grad_out[:, c, side, channel] = part.reshape(many, rows, lanes)


SCALARS = pl.BlockSpec(memory_space=pltpu.SMEM)
VECTORS = pl.BlockSpec(memory_space=pltpu.VMEM)
FAR = pl.BlockSpec(memory_space=pltpu.HBM)


def call(kernel, name, outs, args, scratch=(), flops=0, grant=16, specs=None, out_specs=None):
    shapes = [jax.ShapeDtypeStruct(shape, dtype) for shape, dtype in outs]
    moved = sum(a.size * a.dtype.itemsize for a in list(args) + shapes)
    return pl.pallas_call(
        kernel,
        name=name,
        out_shape=shapes,
        in_specs=specs or [VECTORS] * len(args),
        out_specs=out_specs or [VECTORS] * len(shapes),
        scratch_shapes=[
            pltpu.VMEM(*item) if isinstance(item, tuple) else item for item in scratch
        ],
        compiler_params=pltpu.CompilerParams(vmem_limit_bytes=grant * 1024 * 1024),
        cost_estimate=pl.CostEstimate(flops=flops, bytes_accessed=moved, transcendentals=0),
    )(*args)


def exchange(values):
    return lax.all_to_all(values, ("row", "col"), split_axis=0, concat_axis=0, tiled=True)


def swap_cores(values, many, few):
    pairs = [(index, index ^ few) for index in range(many * few)]
    return lax.ppermute(values, ("row", "col"), pairs)


def exchange_chips(values, many, few):
    groups = [
        [row * few + col for row in range(core, many, 2) for col in range(few)] for core in range(2)
    ]
    return lax.all_to_all(
        values, ("row", "col"), split_axis=0, concat_axis=0, axis_index_groups=groups, tiled=True
    )


def grouped_device(
    pair, cotangent, lengths, ngain, nbias, proj_w, gate_w, mgain, mbias, out_w, outgate_w,
    *, many, few,
):
    rows, lanes, channels = pair.shape
    shards = many * few
    group = H // shards
    edge = ((shards, 2, group, rows, lanes), BF16)
    grid = ((many, few, 2, group, rows, lanes), BF16)
    tri = ((shards, group, rows, lanes), BF16)
    tri_grid = ((many, few, group, rows, lanes), BF16)
    tile = ((rows, channels, lanes), BF16)
    wide = ((rows, channels, lanes), F32)
    row = ((rows, lanes), F32)
    factor = ((rows, 2 * H, lanes), F32)
    back = ((channels, 4 * H), BF16)
    wts = ((4 * H, channels), BF16)
    big = ((rows, 2 * H, lanes), BF16)
    mid = ((rows, H, lanes), BF16)
    positions = rows * lanes
    flat = ((H, positions), BF16)
    flat_in = ((4 * H, positions), BF16)
    out_rows = ((2 * H, channels), BF16)
    in_rows = ((4 * H, H), BF16)
    triangle = 2 * group * (many * rows) ** 2 * (few * lanes)
    dense = 2 * positions * channels * H

    def sums(count):
        return ((count, H, lanes), F32)

    def small(count):
        return ((count, H), F32)

    saved = [tile, factor, factor, wide, row]
    far = [
        pltpu.with_memory_space_constraint(item, pltpu.HBM)
        for item in (pair, ngain, nbias, proj_w, gate_w)
    ]
    sent, normed0, *factors0, mask = call(
        start_kernel, "start", [edge, *saved, row], [lengths, *far],
        [(pair.shape, BF16), (ngain.shape, F32), (nbias.shape, F32), (proj_w.shape, BF16),
         (gate_w.shape, BF16), pltpu.SemaphoreType.DMA((5,)), wts, big],
        4 * dense, specs=[SCALARS] + [FAR] * len(far),
    )
    edge0 = exchange(sent).reshape(grid[0])
    (here,) = call(
        functools.partial(triangle_kernel, False), "outgoing", [tri_grid], [edge0], (), triangle,
    )
    tri0 = exchange(here.reshape(tri[0]))
    sent, mid_t, normed1, *factors1, outgate0, scaled_mid0, inverse_mid0 = call(
        between_kernel, "between", [edge, tile, *saved, wide, wide, row],
        [mask, tri0, pair, normed0, ngain, nbias, mgain, mbias, out_w, outgate_w, proj_w,
         gate_w],
        [wts, mid, big], 6 * dense,
    )
    edge1 = exchange(sent).reshape(grid[0])
    (here,) = call(
        functools.partial(triangle_kernel, True), "incoming", [tri_grid], [edge1], (), triangle,
    )
    tri1 = exchange(here.reshape(tri[0]))
    sent, new_pair, cot_t, d_normed_gate1, out_grads1, small1 = call(
        turn_kernel, "turn", [tri, (pair.shape, BF16), wide, wide, out_rows, small(2)],
        [tri1, mid_t, normed1, cotangent, mgain, mbias, out_w, outgate_w],
        [(pair.shape, BF16), pltpu.SemaphoreType.DMA((rows // 2,)), mid, mid, flat, flat, flat,
         flat, sums(2)],
        6 * dense, out_specs=[VECTORS, FAR] + [VECTORS] * 4,
    )
    d_tri1 = exchange(sent).reshape(tri_grid[0])
    (sent,) = call(
        functools.partial(edge_grad_kernel, True), "incoming_grad", [grid], [edge1, d_tri1],
        (), 2 * triangle,
    )
    d_edge1 = exchange(sent.reshape(edge[0]))
    proj_factor1, gate_factor1, scaled1, inverse1 = factors1
    sent, grad, d_normed_gate0, out_grads0, in_grads1, small_middle = call(
        middle_kernel, "middle", [tri, wide, wide, out_rows, in_rows, small(4)],
        [d_edge1, proj_factor1, gate_factor1, d_normed_gate1, scaled1, inverse1, cot_t, outgate0,
         scaled_mid0, inverse_mid0, normed0, normed1, ngain, mgain, mbias, proj_w, gate_w, out_w,
         outgate_w],
        [big, mid, flat, flat, flat, flat, flat, flat_in, back, sums(4)], 13 * dense,
    )
    d_tri0 = exchange(sent).reshape(tri_grid[0])
    (sent,) = call(
        functools.partial(edge_grad_kernel, False), "outgoing_grad", [grid], [edge0, d_tri0],
        (), 2 * triangle,
    )
    d_edge0 = exchange(sent.reshape(edge[0]))
    share = 12 * H // shards
    chips = shards // 2
    proj_factor0, gate_factor0, scaled0, inverse0 = factors0
    held = ((chips, share, H), BF16)
    own, other, d_in0 = call(
        functools.partial(finish_kernel, few), "finish", [held, held, flat_in],
        [d_edge0, proj_factor0, gate_factor0, normed0, out_grads0, in_grads1, out_grads1],
        [big, flat, ((12 * H, H), BF16)], 4 * dense,
    )
    other = swap_cores(other, many, few)
    d_normed0, extra = call(
        norm_sums_kernel, "norm_sums", [wide, ((16, H), BF16)],
        [d_in0, d_normed_gate0, scaled0, proj_w, gate_w, small_middle, small1], [back, sums(2)],
        4 * dense,
    )
    own, extra = call(add_kernel, "add_cores", [held, ((16, H), BF16)], [own, other, extra])
    parts = exchange_chips(own, many, few)
    (shared,) = call(
        sum_kernel, "sum_weights", [((chips, share + 16, H), BF16)], [parts, extra]
    )
    shared = exchange_chips(shared, many, few)
    other = swap_cores(shared, many, few)
    grad_pair, mine = call(
        functools.partial(grad_pair_kernel, share), "grad_pair",
        [(pair.shape, BF16), ((16, H), F32)],
        [shared, d_normed0, scaled0, inverse0, grad, ngain],
        [(pair.shape, BF16), pltpu.SemaphoreType.DMA((rows // 2,))], out_specs=[FAR, VECTORS],
    )
    grad_proj, grad_gate, grad_out, grad_outgate, *vectors = call(
        functools.partial(unpack_kernel, share, few), "unpack",
        [(proj_w.shape, F32), (gate_w.shape, F32), (out_w.shape, F32), (outgate_w.shape, F32),
         (ngain.shape, F32), (nbias.shape, F32), (mgain.shape, F32), (mbias.shape, F32)],
        [shared, other, mine], [((12 * H, H), F32)],
    )
    return (
        new_pair,
        grad_pair,
        vectors[0],
        vectors[1],
        grad_proj,
        grad_gate,
        vectors[2],
        vectors[3],
        grad_out,
        grad_outgate,
    )


def norm_channels(values):
    average = jnp.mean(values, -1, keepdims=True)
    centred = values - average
    variance = jnp.mean(centred * centred, -1, keepdims=True)
    inverse = lax.rsqrt(variance + EPS)
    return (centred * inverse, inverse)


def forward_module(pair_in, pair_mask, weights, incoming):
    gain_in, bias_in, proj_w, gate_w, gain_mid, bias_mid, out_w, outgate_w = weights
    scaled_in, inverse_in = norm_channels(pair_in.astype(jnp.float32))
    normed = (scaled_in * gain_in + bias_in).astype(jnp.bfloat16)
    projected = product("ijc,sch->shij", normed, proj_w)
    gating = jax.nn.sigmoid(product("ijc,sch->shij", normed, gate_w))
    hidden = (projected * gating * pair_mask).astype(jnp.bfloat16)
    left_side, right_side = (
        lax.all_to_all(hidden[0], "row", split_axis=0, concat_axis=1, tiled=True),
        lax.all_to_all(hidden[1], "row", split_axis=0, concat_axis=1, tiled=True),
    )
    if incoming:
        left_side = jnp.swapaxes(left_side, 1, 2)
        right_side = jnp.swapaxes(right_side, 1, 2)
    else:
        left_side, right_side = (
            lax.all_to_all(left_side, "col", split_axis=1, concat_axis=2, tiled=True),
            lax.all_to_all(right_side, "col", split_axis=1, concat_axis=2, tiled=True),
        )
    triangle = product(
        "cik,cjk->cij", left_side, lax.all_gather(right_side, "col", axis=1, tiled=True)
    ).astype(jnp.bfloat16)
    triangle = lax.all_to_all(
        lax.all_to_all(triangle, "col", split_axis=2, concat_axis=1, tiled=True),
        "row",
        split_axis=1,
        concat_axis=0,
        tiled=True,
    )
    tri_values = triangle.astype(jnp.float32)
    total, squares = lax.psum((jnp.sum(tri_values, 0), jnp.sum(tri_values * tri_values, 0)), "ch")
    average = total / H
    inverse_mid = lax.rsqrt(squares / H - average * average + EPS)
    scaled_mid = (tri_values - average) * inverse_mid
    unit = (scaled_mid * gain_mid[:, None, None] + bias_mid[:, None, None]).astype(jnp.bfloat16)
    unit_full = lax.all_gather(unit, "ch", axis=0, tiled=True)
    outer = product("hij,hc->ijc", unit_full, out_w)
    outgate = jax.nn.sigmoid(product("ijc,cd->ijd", normed, outgate_w))
    result = (pair_in.astype(jnp.float32) + outer * outgate).astype(jnp.bfloat16)
    saved = (
        scaled_in,
        inverse_in,
        normed,
        projected,
        gating,
        left_side,
        right_side,
        scaled_mid,
        inverse_mid,
        unit_full,
        outer,
        outgate,
    )
    return (result, saved)


def backward_module(grad_out, pair_mask, weights, saved, incoming):
    gain_in, bias_in, proj_w, gate_w, gain_mid, bias_mid, out_w, outgate_w = weights
    (
        scaled_in,
        inverse_in,
        normed,
        projected,
        gating,
        left_side,
        right_side,
        scaled_mid,
        inverse_mid,
        unit_full,
        outer,
        outgate,
    ) = saved
    d_outer = (grad_out * outgate).astype(jnp.bfloat16)
    d_gatepre = (grad_out * outer * outgate * (1.0 - outgate)).astype(jnp.bfloat16)
    grad_out_w = product("hij,ijc->hc", unit_full, d_outer)
    grad_outgate_w = product("ijc,ijd->cd", normed, d_gatepre)
    width = gain_mid.shape[0]
    own_rows = lax.dynamic_slice_in_dim(out_w, lax.axis_index("ch") * width, width, 0)
    d_unit = product("ijc,hc->hij", d_outer, own_rows)
    d_normed = product("ijd,cd->ijc", d_gatepre, outgate_w)
    weighted = d_unit * gain_mid[:, None, None]
    grad_gain_mid = jnp.sum(d_unit * scaled_mid, (1, 2))
    grad_bias_mid = jnp.sum(d_unit, (1, 2))
    first_sum, second_sum = lax.psum(
        (jnp.sum(weighted, 0), jnp.sum(weighted * scaled_mid, 0)), "ch"
    )
    d_tri = (inverse_mid * (weighted - first_sum / H - scaled_mid * (second_sum / H))).astype(
        jnp.bfloat16
    )
    grad_rows = lax.all_to_all(d_tri, "row", split_axis=0, concat_axis=1, tiled=True)
    grad_cols = lax.all_to_all(grad_rows, "col", split_axis=1, concat_axis=2, tiled=True)
    d_left = product(
        "cij,cjk->cik", grad_cols, lax.all_gather(right_side, "col", axis=1, tiled=True)
    )
    partial_terms = product("cij,cik->cjk", grad_cols, left_side)
    d_right = lax.psum_scatter(
        partial_terms.astype(jnp.bfloat16), "col", scatter_dimension=1, tiled=True
    ).astype(jnp.float32)
    d_left = d_left.astype(jnp.bfloat16)
    d_right = d_right.astype(jnp.bfloat16)
    if incoming:
        d_left = jnp.swapaxes(d_left, 1, 2)
        d_right = jnp.swapaxes(d_right, 1, 2)
    else:
        d_left, d_right = (
            lax.all_to_all(d_left, "col", split_axis=2, concat_axis=1, tiled=True),
            lax.all_to_all(d_right, "col", split_axis=2, concat_axis=1, tiled=True),
        )
    d_left, d_right = (
        lax.all_to_all(d_left, "row", split_axis=1, concat_axis=0, tiled=True),
        lax.all_to_all(d_right, "row", split_axis=1, concat_axis=0, tiled=True),
    )
    d_hidden = jnp.stack([d_left, d_right]).astype(jnp.float32)
    d_proj = (d_hidden * gating * pair_mask).astype(jnp.bfloat16)
    d_gate = (d_hidden * projected * gating * (1.0 - gating) * pair_mask).astype(jnp.bfloat16)
    grad_proj_w = product("ijc,shij->sch", normed, d_proj)
    grad_gate_w = product("ijc,shij->sch", normed, d_gate)
    partial_input = product("shij,sch->ijc", d_proj, proj_w) + product(
        "shij,sch->ijc", d_gate, gate_w
    )
    d_normed = d_normed + lax.psum(partial_input.astype(jnp.bfloat16), "ch").astype(jnp.float32)
    weighted_in = d_normed * gain_in
    grad_gain_in = jnp.sum(d_normed * scaled_in, (0, 1))
    grad_bias_in = jnp.sum(d_normed, (0, 1))
    d_pair = inverse_in * (
        weighted_in
        - jnp.mean(weighted_in, -1, keepdims=True)
        - scaled_in * jnp.mean(weighted_in * scaled_in, -1, keepdims=True)
    )
    grads = (
        grad_gain_in,
        grad_bias_in,
        grad_proj_w,
        grad_gate_w,
        grad_gain_mid,
        grad_bias_mid,
        grad_out_w,
        grad_outgate_w,
    )
    return (grad_out + d_pair, grads)


def per_device(
    pair,
    cotangent,
    lengths,
    norm_gain,
    norm_bias,
    proj_weight,
    gate_weight,
    mid_gain,
    mid_bias,
    out_weight,
    outgate_weight,
):
    rows_here = pair.shape[0]
    cols_here = pair.shape[1]
    row_ids = lax.axis_index("row") * rows_here + lax.iota(jnp.int32, rows_here)
    col_ids = lax.axis_index("col") * cols_here + lax.iota(jnp.int32, cols_here)
    limit = lengths[0]
    pair_mask = ((row_ids[:, None] < limit) & (col_ids[None, :] < limit)).astype(jnp.float32)
    state = pair
    stash = []
    for layer in range(2):
        weights = (
            norm_gain[layer],
            norm_bias[layer],
            proj_weight[layer],
            gate_weight[layer],
            mid_gain[layer],
            mid_bias[layer],
            out_weight[layer],
            outgate_weight[layer],
        )
        state, saved = forward_module(state, pair_mask, weights, layer == 1)
        stash.append(saved)
    grad_state = cotangent.astype(jnp.float32)
    per_layer = [None, None]
    for layer in (1, 0):
        weights = (
            norm_gain[layer],
            norm_bias[layer],
            proj_weight[layer],
            gate_weight[layer],
            mid_gain[layer],
            mid_bias[layer],
            out_weight[layer],
            outgate_weight[layer],
        )
        grad_state, grads = backward_module(
            grad_state, pair_mask, weights, stash[layer], layer == 1
        )
        per_layer[layer] = grads
    lower = per_layer[0]
    upper = per_layer[1]
    summed = lax.psum(
        (
            lower[0],
            lower[1],
            lower[2],
            lower[3],
            lower[4],
            lower[5],
            lower[6],
            lower[7],
            upper[0],
            upper[1],
            upper[2],
            upper[3],
            upper[4],
            upper[5],
            upper[6],
            upper[7],
        ),
        ("row", "col"),
    )
    per_layer = [summed[0:8], summed[8:16]]
    stacked = [jnp.stack([per_layer[0][index], per_layer[1][index]]) for index in range(8)]
    return (
        state,
        grad_state.astype(jnp.bfloat16),
        stacked[0],
        stacked[1],
        stacked[2],
        stacked[3],
        stacked[4],
        stacked[5],
        stacked[6],
        stacked[7],
    )


def on_device(pair, *rest, many, few, split):
    rows, lanes, channels = pair.shape
    shards = many * few
    whole_channels = split == 1 and H % shards == 0 and BLOCK % (H // shards) == 0 and H % (2 * BLOCK) == 0
    tiles = rows == BLOCK and lanes == H and channels == H
    if whole_channels and tiles and many % 2 == 0 and few & (few - 1) == 0:
        return grouped_device(pair, *rest, many=many, few=few)
    return per_device(pair, *rest)


def solution(mesh):
    in_specs = (
        P(("grp", "row"), "col", None),
        P(("grp", "row"), "col", None),
        P("grp"),
        P(),
        P(),
        P(None, None, None, "ch"),
        P(None, None, None, "ch"),
        P(None, "ch"),
        P(None, "ch"),
        P(),
        P(),
    )
    out_specs = (
        P(("grp", "row"), "col", None),
        P(("grp", "row"), "col", None),
        P("grp", None),
        P("grp", None),
        P("grp", None, None, "ch"),
        P("grp", None, None, "ch"),
        P("grp", "ch"),
        P("grp", "ch"),
        P("grp", None, None),
        P("grp", None, None),
    )
    body = functools.partial(
        on_device, many=mesh.shape["row"], few=mesh.shape["col"], split=mesh.shape["ch"]
    )
    return jax.shard_map(
        body, mesh=mesh, in_specs=in_specs, out_specs=out_specs, check_vma=False
    )
```

```python
import functools

import jax
import jax.numpy as jnp
from jax import lax
from jax.experimental import pallas as pl
from jax.experimental.pallas import tpu as pltpu
from jax.sharding import PartitionSpec as P

H = 128


EPS = 1e-05


def product(spec, left, right):
    return jnp.einsum(spec, left, right, preferred_element_type=jnp.float32)


F32 = jnp.float32
BF16 = jnp.bfloat16


def dot(left, right):
    return lax.dot_general(left, right, (((1,), (0,)), ((), ())), preferred_element_type=F32)


def dot_rt(left, right):
    return lax.dot_general(left, right, (((1,), (1,)), ((), ())), preferred_element_type=F32)


def dot_lt(left, right):
    return lax.dot_general(left, right, (((0,), (0,)), ((), ())), preferred_element_type=F32)


def sigmoid(values):
    return 0.5 * jnp.tanh(0.5 * values) + 0.5


def norm_rows(values):
    scale = 1.0 / values.shape[0]
    average = jnp.sum(values, 0, keepdims=True) * scale
    centred = values - average
    variance = jnp.sum(centred * centred, 0, keepdims=True) * scale
    inverse = lax.rsqrt(variance + EPS)
    return centred * inverse, inverse


def turned(weight):
    return jnp.transpose(weight.astype(F32)).astype(BF16)


def column(ref, module, lanes):
    row = ref[module : module + 1, :]
    return beside(*[jnp.transpose(jnp.broadcast_to(row, (lanes, row.shape[1])))] * 2)


def beside(left, right):
    return jnp.concatenate([left, right], axis=-1)


def pair_of(ref, step):
    return beside(ref[2 * step], ref[2 * step + 1])


def put_pair(ref, step, values):
    lanes = ref.shape[-1]
    ref[2 * step] = values[:, :lanes]
    ref[2 * step + 1] = values[:, lanes:]


def pair_of_rows(ref, step):
    return beside(ref[2 * step : 2 * step + 1, :], ref[2 * step + 1 : 2 * step + 2, :])


def put_pair_of_rows(ref, step, values):
    lanes = ref.shape[-1]
    ref[2 * step : 2 * step + 1, :] = values[:, :lanes]
    ref[2 * step + 1 : 2 * step + 2, :] = values[:, lanes:]


def turned_pair(ref, step):
    return beside(
        jnp.transpose(ref[2 * step].astype(F32)), jnp.transpose(ref[2 * step + 1].astype(F32))
    )


def put_turned_pair(ref, step, values):
    lanes = ref.shape[1]
    ref[2 * step] = jnp.transpose(values[:, :lanes]).astype(BF16)
    ref[2 * step + 1] = jnp.transpose(values[:, lanes:]).astype(BF16)


def as_row(total):
    return jnp.sum(jnp.transpose(total), 0, keepdims=True)


def row_mask(lengths_ref, step, rows, lanes):
    limit = lengths_ref[0]
    row_id = lax.axis_index("row") * rows + step
    col_id = lax.axis_index("col") * lanes + lax.broadcasted_iota(jnp.int32, (1, lanes), 1)
    return jnp.where((row_id < limit) & (col_id < limit), 1.0, 0.0).astype(F32)


def load_in_weights(proj_ref, gate_ref, module, scratch):
    width = proj_ref.shape[-1]
    for side in range(2):
        scratch[side * width : (side + 1) * width, :] = turned(proj_ref[module, side])
        scratch[(2 + side) * width : (3 + side) * width, :] = turned(gate_ref[module, side])


def load_back_weights(proj_ref, gate_ref, module, scratch):
    width = proj_ref.shape[-1]
    for side in range(2):
        scratch[:, side * width : (side + 1) * width] = proj_ref[module, side]
        scratch[:, (2 + side) * width : (3 + side) * width] = gate_ref[module, side]


BLOCK = 16


def turn_matrix(rows):
    size = BLOCK * rows
    out = lax.broadcasted_iota(jnp.int32, (size, size), 0)
    source = lax.broadcasted_iota(jnp.int32, (size, size), 1)
    return jnp.where(source == (out % rows) * BLOCK + out // rows, 1.0, 0.0).astype(BF16)


def spread_blocks(matrix, scratch, start, group):
    rows, _, lanes = scratch.shape
    blocks = [
        scratch[:, at : at + BLOCK, :].reshape(rows * BLOCK, lanes)
        for at in (start, start + BLOCK)
    ]
    both = dot(matrix, beside(*blocks)).astype(BF16)
    parts = [
        part.reshape(BLOCK // group, group, rows, lanes)
        for part in (both[:, :lanes], both[:, lanes:])
    ]
    return jnp.concatenate(parts, axis=0)


def collect_blocks(matrix, values, scratch, start):
    rows, _, lanes = scratch.shape
    flat = values.reshape(2, BLOCK * rows, lanes)
    both = dot(matrix, beside(flat[0], flat[1])).astype(BF16)
    for at, part in ((start, both[:, :lanes]), (start + BLOCK, both[:, lanes:])):
        scratch[:, at : at + BLOCK, :] = part.reshape(rows, BLOCK, lanes)


def spread_edges(scratch, out_ref):
    shards, sides, group, rows, lanes = out_ref.shape
    matrix, step = turn_matrix(rows), 2 * BLOCK // group
    for side in range(sides):
        for shard in range(0, shards, step):
            start = (side * shards + shard) * group
            out_ref[shard : shard + step, side] = spread_blocks(matrix, scratch, start, group)


def collect_edges(in_ref, scratch):
    shards, sides, group, rows, lanes = in_ref.shape
    matrix, step = turn_matrix(rows), 2 * BLOCK // group
    for side in range(sides):
        for shard in range(0, shards, step):
            start = (side * shards + shard) * group
            collect_blocks(matrix, in_ref[shard : shard + step, side], scratch, start)


def spread_triangle(scratch, out_ref):
    shards, group, rows, lanes = out_ref.shape
    matrix, step = turn_matrix(rows), 2 * BLOCK // group
    for shard in range(0, shards, step):
        out_ref[shard : shard + step] = spread_blocks(matrix, scratch, shard * group, group)


def collect_triangle(in_ref, scratch):
    shards, group, rows, lanes = in_ref.shape
    matrix, step = turn_matrix(rows), 2 * BLOCK // group
    for shard in range(0, shards, step):
        collect_blocks(matrix, in_ref[shard : shard + step], scratch, shard * group)


def each_pair(rows, body, sums=None):
    for block in range(0, rows // 2, 2):
        parts = [body(block + step) for step in range(2)]
        for index in range(0 if sums is None else sums.shape[0]):
            total = parts[0][index] + parts[1][index]
            lanes = sums.shape[-1]
            sums[index] += total[:, :lanes] + total[:, lanes:]


def mid_norm(tri):
    scale = 1.0 / tri.shape[0]
    average = jnp.sum(tri, 0, keepdims=True) * scale
    squares = jnp.sum(tri * tri, 0, keepdims=True) * scale
    inverse = lax.rsqrt(squares - average * average + EPS)
    return (tri - average) * inverse, inverse


def norm_backward(weighted, scaled, inverse):
    scale = 1.0 / weighted.shape[0]
    first = jnp.sum(weighted, 0, keepdims=True) * scale
    second = jnp.sum(weighted * scaled, 0, keepdims=True) * scale
    return inverse * (weighted - first - scaled * second)


def save_norm(step, values, scaled_out, inverse_out):
    scaled, inverse = norm_rows(values)
    put_pair(scaled_out, step, scaled)
    put_pair_of_rows(inverse_out, step, inverse)
    return scaled


def save_edges(step, normed, in_weights, mask, proj_out, gate_out):
    pre = dot(in_weights, normed)
    half = pre.shape[0] // 2
    gating = sigmoid(pre[half:])
    factor = gating * mask
    value = pre[:half] * factor
    put_pair(proj_out, step, factor)
    put_pair(gate_out, step, value * (1.0 - gating))
    return value.astype(BF16)


def start_kernel(
    lengths, pair_far, ngain_far, nbias_far, proj_far, gate_far,
    edge_out, normed_out, proj_out, gate_out, scaled_out, inverse_out, mask_out,
    pair, ngain, nbias, proj_w, gate_w, sems, wts, scr,
):
    rows, lanes, channels = pair.shape
    blocks = [pl.ds(start, 4) for start in range(0, rows, 4)]
    far = [proj_far.at[0], gate_far.at[0], ngain_far, nbias_far]
    near = [proj_w.at[0], gate_w.at[0], ngain, nbias]
    far += [pair_far.at[block] for block in blocks]
    near += [pair.at[block] for block in blocks]
    copies = [
        pltpu.make_async_copy(source, target, sems.at[index])
        for index, (source, target) in enumerate(zip(far, near))
    ]
    for copy in copies:
        copy.start()
    for copy in copies[:4]:
        copy.wait()
    load_in_weights(proj_w, gate_w, 0, wts)
    gain, bias = column(ngain, 0, lanes), column(nbias, 0, lanes)

    def body(step):
        if step % 2 == 0:
            copies[4 + step // 2].wait()
        base = turned_pair(pair, step)
        scaled = save_norm(step, base, scaled_out, inverse_out)
        normed = (scaled * gain + bias).astype(BF16)
        put_pair(normed_out, step, normed)
        mask = beside(*[row_mask(lengths, 2 * step + row, rows, lanes) for row in range(2)])
        put_pair_of_rows(mask_out, step, mask)
        put_pair(scr, step, save_edges(step, normed, wts[...], mask, proj_out, gate_out))

    each_pair(rows, body)
    spread_edges(scr, edge_out)


def between_kernel(
    mask_all, tri, pair, normed0, ngain, nbias, mgain, mbias, out_w, outgate_w, proj_w, gate_w,
    edge_out, mid_out, normed_out, proj_out, gate_out, scaled_out, inverse_out,
    outgate_out, scaled_mid_out, inverse_mid_out, wts, tri_in, scr,
):
    rows, lanes, channels = pair.shape
    load_in_weights(proj_w, gate_w, 1, wts)
    out_t, outgate_t = turned(out_w[0]), turned(outgate_w[0])
    gain, bias = column(ngain, 1, lanes), column(nbias, 1, lanes)
    gain_mid, bias_mid = column(mgain, 0, lanes), column(mbias, 0, lanes)
    collect_triangle(tri, tri_in)

    def body(step):
        scaled_mid, inverse_mid = mid_norm(pair_of(tri_in, step).astype(F32))
        put_pair(scaled_mid_out, step, scaled_mid)
        put_pair_of_rows(inverse_mid_out, step, inverse_mid)
        unit = (scaled_mid * gain_mid + bias_mid).astype(BF16)
        outer = dot(out_t, unit)
        outgate = sigmoid(dot(outgate_t, pair_of(normed0, step)))
        put_pair(outgate_out, step, outgate)
        mid = (turned_pair(pair, step) + outer * outgate).astype(BF16)
        put_pair(mid_out, step, mid)
        scaled = save_norm(step, mid.astype(F32), scaled_out, inverse_out)
        normed = (scaled * gain + bias).astype(BF16)
        put_pair(normed_out, step, normed)
        mask = pair_of_rows(mask_all, step)
        put_pair(scr, step, save_edges(step, normed, wts[...], mask, proj_out, gate_out))

    each_pair(rows, body)
    spread_edges(scr, edge_out)


def out_weight_grads(unit, d_outer, normed, d_gatepre, out_ref):
    width = unit.shape[0]
    out_ref[0:width, :] = dot_rt(unit[...], d_outer[...]).astype(out_ref.dtype)
    out_ref[width:, :] = dot_rt(normed[...], d_gatepre[...]).astype(out_ref.dtype)


def in_weight_grads(normed_all, d_in_all, out_ref):
    width = normed_all.shape[0]
    for part in range(d_in_all.shape[0] // width):
        block = slice(part * width, (part + 1) * width)
        out_ref[block, :] = dot_rt(normed_all[...], d_in_all[block, :]).astype(out_ref.dtype)


def lane_block(step, lanes):
    return pl.ds(2 * step * lanes, 2 * lanes)


def turn_kernel(
    tri, mid, normed, cot, mgain, mbias, out_w, outgate_w,
    d_tri_out, new_out, grad_out, d_normed_out, weights_out, small_out,
    tri_in, scr, unit_all, outer_all, normed_all, gate_all, sums,
):
    rows, channels, lanes = mid.shape
    out_t, outgate_t = turned(out_w[1]), turned(outgate_w[1])
    gain_mid, bias_mid = column(mgain, 1, lanes), column(mbias, 1, lanes)
    collect_triangle(tri, tri_in)
    sums[...] = jnp.zeros_like(sums)

    def body(step):
        here = lane_block(step, lanes)
        grad = turned_pair(cot, step)
        put_pair(grad_out, step, grad)
        here_normed = pair_of(normed, step)
        outgate = sigmoid(dot(outgate_t, here_normed))
        gated = grad * outgate
        d_outer = gated.astype(BF16)
        d_unit = dot(out_w[1], d_outer)
        scaled_mid, inverse_mid = mid_norm(pair_of(tri_in, step).astype(F32))
        d_tri = norm_backward(d_unit * gain_mid, scaled_mid, inverse_mid)
        put_pair(scr, step, d_tri.astype(BF16))
        unit = (scaled_mid * gain_mid + bias_mid).astype(BF16)
        outer = dot(out_t, unit)
        put_pair(new_out, step, (pair_of(mid, step).astype(F32) + outer * outgate).astype(BF16))
        d_gatepre = (gated * outer * (1.0 - outgate)).astype(BF16)
        put_pair(d_normed_out, step, dot(outgate_w[1], d_gatepre))
        unit_all[:, here] = unit
        outer_all[:, here] = d_outer
        normed_all[:, here] = here_normed
        gate_all[:, here] = d_gatepre
        return d_unit * scaled_mid, d_unit

    each_pair(rows, body, sums)
    spread_triangle(scr, d_tri_out)
    out_weight_grads(unit_all, outer_all, normed_all, gate_all, weights_out)
    for index in range(2):
        small_out[index : index + 1, :] = as_row(sums[index])


def edge_backward(step, scratch, proj_factor, gate_factor):
    here = pair_of(scratch, step).astype(F32)
    d_proj = (here * pair_of(proj_factor, step)).astype(BF16)
    d_gate = (here * pair_of(gate_factor, step)).astype(BF16)
    return jnp.concatenate([d_proj, d_gate], axis=0)


def middle_kernel(
    d_edge, proj_factor, gate_factor, d_normed_gate, scaled_in, inverse_in, cot, outgate,
    scaled_mid, inverse_mid, normed0, normed1, ngain, mgain, mbias, proj_w, gate_w, out_w,
    outgate_w,
    d_tri_out, grad_out, d_normed_out, out_weights, in_weights, small_out,
    scr, scr_tri, unit_all, outer_all, normed_all, gate_all, upper_all, d_in_all, back, sums,
):
    rows, channels, lanes = cot.shape
    out_t = turned(out_w[0])
    gain = column(ngain, 1, lanes)
    gain_mid, bias_mid = column(mgain, 0, lanes), column(mbias, 0, lanes)
    collect_edges(d_edge, scr)
    sums[...] = jnp.zeros_like(sums)
    load_back_weights(proj_w, gate_w, 1, back)

    def upper(step):
        place = lane_block(step, lanes)
        d_in = edge_backward(step, scr, proj_factor, gate_factor)
        d_in_all[:, place] = d_in
        upper_all[:, place] = pair_of(normed1, step)
        d_normed = pair_of(d_normed_gate, step) + dot(back[...], d_in)
        scaled = pair_of(scaled_in, step)
        grad = pair_of(cot, step) + norm_backward(
            d_normed * gain, scaled, pair_of_rows(inverse_in, step)
        )
        put_pair(grad_out, step, grad)
        return d_normed * scaled, d_normed

    def lower(step):
        place = lane_block(step, lanes)
        gate = pair_of(outgate, step)
        gated = pair_of(grad_out, step) * gate
        d_outer = gated.astype(BF16)
        d_unit = dot(out_w[0], d_outer)
        scaled = pair_of(scaled_mid, step)
        d_tri = norm_backward(d_unit * gain_mid, scaled, pair_of_rows(inverse_mid, step))
        put_pair(scr_tri, step, d_tri.astype(BF16))
        unit = (scaled * gain_mid + bias_mid).astype(BF16)
        outer = dot(out_t, unit)
        d_gatepre = (gated * outer * (1.0 - gate)).astype(BF16)
        put_pair(d_normed_out, step, dot(outgate_w[0], d_gatepre))
        unit_all[:, place] = unit
        outer_all[:, place] = d_outer
        normed_all[:, place] = pair_of(normed0, step)
        gate_all[:, place] = d_gatepre
        return d_unit * scaled, d_unit

    each_pair(rows, upper, sums.at[2:4])
    each_pair(rows, lower, sums.at[0:2])
    spread_triangle(scr_tri, d_tri_out)
    out_weight_grads(unit_all, outer_all, normed_all, gate_all, out_weights)
    in_weight_grads(upper_all, d_in_all, in_weights)
    for index in range(4):
        small_out[index : index + 1, :] = as_row(sums[index])


def split_cores(all_rows, own_out, other_out, few):
    chips, share, width = own_out.shape
    view = all_rows.reshape(chips // few, 2, few, share, width)
    core = lax.rem(lax.axis_index("row"), 2)
    own_out[...] = view[:, core].reshape(own_out.shape)
    other_out[...] = view[:, 1 - core].reshape(other_out.shape)


def finish_kernel(
    few, d_edge, proj_factor, gate_factor, normed, out0, in1, out1,
    own_out, other_out, d_in_all, scr, normed_all, packed,
):
    rows, half, lanes = proj_factor.shape
    collect_edges(d_edge, scr)

    def body(step):
        place = lane_block(step, lanes)
        d_in_all[:, place] = edge_backward(step, scr, proj_factor, gate_factor)
        normed_all[:, place] = pair_of(normed, step)

    each_pair(rows, body)
    first, second, third = d_in_all.shape[0], out0.shape[0], in1.shape[0]
    in_weight_grads(normed_all, d_in_all, packed.at[0:first])
    packed[first : first + second, :] = out0[...]
    packed[first + second : first + second + third, :] = in1[...]
    packed[first + second + third :, :] = out1[...]
    split_cores(packed, own_out, other_out, few)


def norm_sums_kernel(
    d_in, d_normed_gate, scaled_in, proj_w, gate_w, small_middle, small1, new_t,
    d_normed_out, small_out, new_out, back, sums,
):
    rows, channels, lanes = scaled_in.shape
    sums[...] = jnp.zeros_like(sums)
    load_back_weights(proj_w, gate_w, 0, back)

    def body(step):
        here = d_in[:, lane_block(step, lanes)]
        d_normed = pair_of(d_normed_gate, step) + dot(back[...], here)
        put_pair(d_normed_out, step, d_normed)
        put_turned_pair(new_out, step, pair_of(new_t, step).astype(F32))
        return d_normed * pair_of(scaled_in, step), d_normed

    each_pair(rows, body, sums)
    small_out[...] = jnp.concatenate(
        [as_row(sums[0]), as_row(sums[1]), small_middle[0:2], small_middle[2:4], small1[...]],
        axis=0,
    )


def add_kernel(first, second, small, out_ref, small_out):
    out_ref[...] = (first[...].astype(F32) + second[...].astype(F32)).astype(BF16)
    small_out[...] = small[...]


def sum_kernel(parts, small, small_other, shared_out):
    chips, share, width = parts.shape
    own = jnp.sum(parts[...].astype(F32), axis=0).astype(BF16)
    both = small[...] + small_other[...]
    high = both.astype(BF16).astype(F32)
    core = lax.rem(lax.axis_index("row"), 2)
    mine = jnp.where(core == 0, high, both - high).astype(BF16)
    for chip in range(chips):
        shared_out[chip, 0:share] = own
        shared_out[chip, share:] = mine


def grad_pair_kernel(
    share, shared, d_normed, scaled_in, inverse_in, grad, ngain, grad_out, mine_out
):
    rows, channels, lanes = grad.shape
    gain = column(ngain, 0, lanes)
    mine_out[...] = jnp.sum(shared[:, share:].astype(F32), axis=0)

    def body(step):
        total = pair_of(grad, step) + norm_backward(
            pair_of(d_normed, step) * gain, pair_of(scaled_in, step),
            pair_of_rows(inverse_in, step),
        )
        put_turned_pair(grad_out, step, total)

    each_pair(rows, body)


def unpack_kernel(
    share, few, own, other, mine, proj_out, gate_out, out_out, outgate_out,
    norm_gain_out, norm_bias_out, mid_gain_out, mid_bias_out, weights,
):
    chips, _, width = own.shape
    core = lax.rem(lax.axis_index("row"), 2)
    view = weights.reshape(chips // few, 2, few, share, width)
    block = (chips // few, few, share, width)
    view[:, core] = own[:, 0:share].astype(F32).reshape(block)
    view[:, 1 - core] = other[:, 0:share].astype(F32).reshape(block)
    total = mine[...] + jnp.sum(other[:, share:].astype(F32), axis=0)
    for module in range(2):
        for index, out in enumerate((norm_gain_out, norm_bias_out, mid_gain_out, mid_bias_out)):
            at = 4 * module + index
            out[module : module + 1, :] = total[at : at + 1]
        blocks = [
            weights[(6 * module + part) * width : (6 * module + part + 1) * width, :]
            for part in range(6)
        ]
        for side in range(2):
            proj_out[module, side] = blocks[side]
            gate_out[module, side] = blocks[2 + side]
        out_out[module] = blocks[4]
        outgate_out[module] = blocks[5]


def triangle_kernel(incoming, edge, tri_out):
    many, few, _, group, rows, lanes = edge.shape

    def whole(side, channel):
        parts = [edge[:, c, side, channel].reshape(many * rows, lanes) for c in range(few)]
        return jnp.concatenate(parts, axis=1)

    for channel in range(group):
        left, right = whole(0, channel), whole(1, channel)
        tri = (dot_lt if incoming else dot_rt)(left, right).astype(BF16)
        for c in range(few):
            part = tri[:, c * lanes : (c + 1) * lanes]
            tri_out[:, c, channel] = part.reshape(many, rows, lanes)


def edge_grad_kernel(incoming, edge, d_tri, grad_out):
    many, few, _, group, rows, lanes = edge.shape

    def whole(ref, *index):
        parts = [ref[(slice(None), c) + index].reshape(many * rows, lanes) for c in range(few)]
        return jnp.concatenate(parts, axis=1)

    for channel in range(group):
        left, right = whole(edge, 0, channel), whole(edge, 1, channel)
        grad = whole(d_tri, channel)
        if incoming:
            d_left, d_right = dot_rt(right, grad), dot(left, grad)
        else:
            d_left, d_right = dot(grad, right), dot_lt(grad, left)
        for side, value in ((0, d_left), (1, d_right)):
            value = value.astype(BF16)
            for c in range(few):
                part = value[:, c * lanes : (c + 1) * lanes]
                grad_out[:, c, side, channel] = part.reshape(many, rows, lanes)


SCALARS = pl.BlockSpec(memory_space=pltpu.SMEM)
VECTORS = pl.BlockSpec(memory_space=pltpu.VMEM)
FAR = pl.BlockSpec(memory_space=pltpu.HBM)


def call(kernel, name, outs, args, scratch=(), flops=0, grant=16, specs=None):
    shapes = [jax.ShapeDtypeStruct(shape, dtype) for shape, dtype in outs]
    moved = sum(a.size * a.dtype.itemsize for a in list(args) + shapes)
    return pl.pallas_call(
        kernel,
        name=name,
        out_shape=shapes,
        in_specs=specs or [VECTORS] * len(args),
        out_specs=[VECTORS] * len(shapes),
        scratch_shapes=[
            pltpu.VMEM(*item) if isinstance(item, tuple) else item for item in scratch
        ],
        compiler_params=pltpu.CompilerParams(vmem_limit_bytes=grant * 1024 * 1024),
        cost_estimate=pl.CostEstimate(flops=flops, bytes_accessed=moved, transcendentals=0),
    )(*args)


def exchange(values):
    return lax.all_to_all(values, ("row", "col"), split_axis=0, concat_axis=0, tiled=True)


def swap_cores(values, many, few):
    pairs = [(index, index ^ few) for index in range(many * few)]
    return lax.ppermute(values, ("row", "col"), pairs)


def exchange_chips(values, many, few):
    groups = [
        [row * few + col for row in range(core, many, 2) for col in range(few)] for core in range(2)
    ]
    return lax.all_to_all(
        values, ("row", "col"), split_axis=0, concat_axis=0, axis_index_groups=groups, tiled=True
    )


def grouped_device(
    pair, cotangent, lengths, ngain, nbias, proj_w, gate_w, mgain, mbias, out_w, outgate_w,
    *, many, few,
):
    rows, lanes, channels = pair.shape
    shards = many * few
    group = H // shards
    edge = ((shards, 2, group, rows, lanes), BF16)
    grid = ((many, few, 2, group, rows, lanes), BF16)
    tri = ((shards, group, rows, lanes), BF16)
    tri_grid = ((many, few, group, rows, lanes), BF16)
    tile = ((rows, channels, lanes), BF16)
    wide = ((rows, channels, lanes), F32)
    row = ((rows, lanes), F32)
    factor = ((rows, 2 * H, lanes), F32)
    back = ((channels, 4 * H), BF16)
    wts = ((4 * H, channels), BF16)
    big = ((rows, 2 * H, lanes), BF16)
    mid = ((rows, H, lanes), BF16)
    positions = rows * lanes
    flat = ((H, positions), BF16)
    flat_in = ((4 * H, positions), BF16)
    out_rows = ((2 * H, channels), BF16)
    in_rows = ((4 * H, H), BF16)
    triangle = 2 * group * (many * rows) ** 2 * (few * lanes)
    dense = 2 * positions * channels * H

    def sums(count):
        return ((count, H, lanes), F32)

    def small(count):
        return ((count, H), F32)

    saved = [tile, factor, factor, wide, row]
    far = [
        pltpu.with_memory_space_constraint(item, pltpu.HBM)
        for item in (pair, ngain, nbias, proj_w, gate_w)
    ]
    sent, normed0, *factors0, mask = call(
        start_kernel, "start", [edge, *saved, row], [lengths, *far],
        [(pair.shape, BF16), (ngain.shape, F32), (nbias.shape, F32), (proj_w.shape, BF16),
         (gate_w.shape, BF16), pltpu.SemaphoreType.DMA((4 + rows // 4,)), wts, big],
        4 * dense, specs=[SCALARS] + [FAR] * len(far),
    )
    edge0 = exchange(sent).reshape(grid[0])
    (here,) = call(
        functools.partial(triangle_kernel, False), "outgoing", [tri_grid], [edge0], (), triangle,
    )
    tri0 = exchange(here.reshape(tri[0]))
    sent, mid_t, normed1, *factors1, outgate0, scaled_mid0, inverse_mid0 = call(
        between_kernel, "between", [edge, tile, *saved, wide, wide, row],
        [mask, tri0, pair, normed0, ngain, nbias, mgain, mbias, out_w, outgate_w, proj_w,
         gate_w],
        [wts, mid, big], 6 * dense,
    )
    edge1 = exchange(sent).reshape(grid[0])
    (here,) = call(
        functools.partial(triangle_kernel, True), "incoming", [tri_grid], [edge1], (), triangle,
    )
    tri1 = exchange(here.reshape(tri[0]))
    sent, new_t, cot_t, d_normed_gate1, out_grads1, small1 = call(
        turn_kernel, "turn", [tri, tile, wide, wide, out_rows, small(2)],
        [tri1, mid_t, normed1, cotangent, mgain, mbias, out_w, outgate_w],
        [mid, mid, flat, flat, flat, flat, sums(2)], 6 * dense,
    )
    d_tri1 = exchange(sent).reshape(tri_grid[0])
    (sent,) = call(
        functools.partial(edge_grad_kernel, True), "incoming_grad", [grid], [edge1, d_tri1],
        (), 2 * triangle,
    )
    d_edge1 = exchange(sent.reshape(edge[0]))
    proj_factor1, gate_factor1, scaled1, inverse1 = factors1
    sent, grad, d_normed_gate0, out_grads0, in_grads1, small_middle = call(
        middle_kernel, "middle", [tri, wide, wide, out_rows, in_rows, small(4)],
        [d_edge1, proj_factor1, gate_factor1, d_normed_gate1, scaled1, inverse1, cot_t, outgate0,
         scaled_mid0, inverse_mid0, normed0, normed1, ngain, mgain, mbias, proj_w, gate_w, out_w,
         outgate_w],
        [big, mid, flat, flat, flat, flat, flat, flat_in, back, sums(4)], 13 * dense,
    )
    d_tri0 = exchange(sent).reshape(tri_grid[0])
    (sent,) = call(
        functools.partial(edge_grad_kernel, False), "outgoing_grad", [grid], [edge0, d_tri0],
        (), 2 * triangle,
    )
    d_edge0 = exchange(sent.reshape(edge[0]))
    share = 12 * H // shards
    chips = shards // 2
    proj_factor0, gate_factor0, scaled0, inverse0 = factors0
    held = ((chips, share, H), BF16)
    own, other, d_in0 = call(
        functools.partial(finish_kernel, few), "finish", [held, held, flat_in],
        [d_edge0, proj_factor0, gate_factor0, normed0, out_grads0, in_grads1, out_grads1],
        [big, flat, ((12 * H, H), BF16)], 4 * dense,
    )
    other = swap_cores(other, many, few)
    d_normed0, sums_here, new_pair = call(
        norm_sums_kernel, "norm_sums", [wide, small(8), (pair.shape, BF16)],
        [d_in0, d_normed_gate0, scaled0, proj_w, gate_w, small_middle, small1, new_t],
        [back, sums(2)],
        4 * dense,
    )
    own, sums_here = call(add_kernel, "add_cores", [held, small(8)], [own, other, sums_here])
    sums_other = swap_cores(sums_here, many, few)
    parts = exchange_chips(own, many, few)
    (shared,) = call(
        sum_kernel, "sum_weights", [((chips, share + 8, H), BF16)],
        [parts, sums_here, sums_other],
    )
    shared = exchange_chips(shared, many, few)
    other = swap_cores(shared, many, few)
    grad_pair, mine = call(
        functools.partial(grad_pair_kernel, share), "grad_pair",
        [(pair.shape, BF16), small(8)],
        [shared, d_normed0, scaled0, inverse0, grad, ngain],
    )
    grad_proj, grad_gate, grad_out, grad_outgate, *vectors = call(
        functools.partial(unpack_kernel, share, few), "unpack",
        [(proj_w.shape, F32), (gate_w.shape, F32), (out_w.shape, F32), (outgate_w.shape, F32),
         (ngain.shape, F32), (nbias.shape, F32), (mgain.shape, F32), (mbias.shape, F32)],
        [shared, other, mine], [((12 * H, H), F32)],
    )
    return (
        new_pair,
        grad_pair,
        vectors[0],
        vectors[1],
        grad_proj,
        grad_gate,
        vectors[2],
        vectors[3],
        grad_out,
        grad_outgate,
    )


def norm_channels(values):
    average = jnp.mean(values, -1, keepdims=True)
    centred = values - average
    variance = jnp.mean(centred * centred, -1, keepdims=True)
    inverse = lax.rsqrt(variance + EPS)
    return (centred * inverse, inverse)


def forward_module(pair_in, pair_mask, weights, incoming):
    gain_in, bias_in, proj_w, gate_w, gain_mid, bias_mid, out_w, outgate_w = weights
    scaled_in, inverse_in = norm_channels(pair_in.astype(jnp.float32))
    normed = (scaled_in * gain_in + bias_in).astype(jnp.bfloat16)
    projected = product("ijc,sch->shij", normed, proj_w)
    gating = jax.nn.sigmoid(product("ijc,sch->shij", normed, gate_w))
    hidden = (projected * gating * pair_mask).astype(jnp.bfloat16)
    left_side, right_side = (
        lax.all_to_all(hidden[0], "row", split_axis=0, concat_axis=1, tiled=True),
        lax.all_to_all(hidden[1], "row", split_axis=0, concat_axis=1, tiled=True),
    )
    if incoming:
        left_side = jnp.swapaxes(left_side, 1, 2)
        right_side = jnp.swapaxes(right_side, 1, 2)
    else:
        left_side, right_side = (
            lax.all_to_all(left_side, "col", split_axis=1, concat_axis=2, tiled=True),
            lax.all_to_all(right_side, "col", split_axis=1, concat_axis=2, tiled=True),
        )
    triangle = product(
        "cik,cjk->cij", left_side, lax.all_gather(right_side, "col", axis=1, tiled=True)
    ).astype(jnp.bfloat16)
    triangle = lax.all_to_all(
        lax.all_to_all(triangle, "col", split_axis=2, concat_axis=1, tiled=True),
        "row",
        split_axis=1,
        concat_axis=0,
        tiled=True,
    )
    tri_values = triangle.astype(jnp.float32)
    total, squares = lax.psum((jnp.sum(tri_values, 0), jnp.sum(tri_values * tri_values, 0)), "ch")
    average = total / H
    inverse_mid = lax.rsqrt(squares / H - average * average + EPS)
    scaled_mid = (tri_values - average) * inverse_mid
    unit = (scaled_mid * gain_mid[:, None, None] + bias_mid[:, None, None]).astype(jnp.bfloat16)
    unit_full = lax.all_gather(unit, "ch", axis=0, tiled=True)
    outer = product("hij,hc->ijc", unit_full, out_w)
    outgate = jax.nn.sigmoid(product("ijc,cd->ijd", normed, outgate_w))
    result = (pair_in.astype(jnp.float32) + outer * outgate).astype(jnp.bfloat16)
    saved = (
        scaled_in,
        inverse_in,
        normed,
        projected,
        gating,
        left_side,
        right_side,
        scaled_mid,
        inverse_mid,
        unit_full,
        outer,
        outgate,
    )
    return (result, saved)


def backward_module(grad_out, pair_mask, weights, saved, incoming):
    gain_in, bias_in, proj_w, gate_w, gain_mid, bias_mid, out_w, outgate_w = weights
    (
        scaled_in,
        inverse_in,
        normed,
        projected,
        gating,
        left_side,
        right_side,
        scaled_mid,
        inverse_mid,
        unit_full,
        outer,
        outgate,
    ) = saved
    d_outer = (grad_out * outgate).astype(jnp.bfloat16)
    d_gatepre = (grad_out * outer * outgate * (1.0 - outgate)).astype(jnp.bfloat16)
    grad_out_w = product("hij,ijc->hc", unit_full, d_outer)
    grad_outgate_w = product("ijc,ijd->cd", normed, d_gatepre)
    width = gain_mid.shape[0]
    own_rows = lax.dynamic_slice_in_dim(out_w, lax.axis_index("ch") * width, width, 0)
    d_unit = product("ijc,hc->hij", d_outer, own_rows)
    d_normed = product("ijd,cd->ijc", d_gatepre, outgate_w)
    weighted = d_unit * gain_mid[:, None, None]
    grad_gain_mid = jnp.sum(d_unit * scaled_mid, (1, 2))
    grad_bias_mid = jnp.sum(d_unit, (1, 2))
    first_sum, second_sum = lax.psum(
        (jnp.sum(weighted, 0), jnp.sum(weighted * scaled_mid, 0)), "ch"
    )
    d_tri = (inverse_mid * (weighted - first_sum / H - scaled_mid * (second_sum / H))).astype(
        jnp.bfloat16
    )
    grad_rows = lax.all_to_all(d_tri, "row", split_axis=0, concat_axis=1, tiled=True)
    grad_cols = lax.all_to_all(grad_rows, "col", split_axis=1, concat_axis=2, tiled=True)
    d_left = product(
        "cij,cjk->cik", grad_cols, lax.all_gather(right_side, "col", axis=1, tiled=True)
    )
    partial_terms = product("cij,cik->cjk", grad_cols, left_side)
    d_right = lax.psum_scatter(
        partial_terms.astype(jnp.bfloat16), "col", scatter_dimension=1, tiled=True
    ).astype(jnp.float32)
    d_left = d_left.astype(jnp.bfloat16)
    d_right = d_right.astype(jnp.bfloat16)
    if incoming:
        d_left = jnp.swapaxes(d_left, 1, 2)
        d_right = jnp.swapaxes(d_right, 1, 2)
    else:
        d_left, d_right = (
            lax.all_to_all(d_left, "col", split_axis=2, concat_axis=1, tiled=True),
            lax.all_to_all(d_right, "col", split_axis=2, concat_axis=1, tiled=True),
        )
    d_left, d_right = (
        lax.all_to_all(d_left, "row", split_axis=1, concat_axis=0, tiled=True),
        lax.all_to_all(d_right, "row", split_axis=1, concat_axis=0, tiled=True),
    )
    d_hidden = jnp.stack([d_left, d_right]).astype(jnp.float32)
    d_proj = (d_hidden * gating * pair_mask).astype(jnp.bfloat16)
    d_gate = (d_hidden * projected * gating * (1.0 - gating) * pair_mask).astype(jnp.bfloat16)
    grad_proj_w = product("ijc,shij->sch", normed, d_proj)
    grad_gate_w = product("ijc,shij->sch", normed, d_gate)
    partial_input = product("shij,sch->ijc", d_proj, proj_w) + product(
        "shij,sch->ijc", d_gate, gate_w
    )
    d_normed = d_normed + lax.psum(partial_input.astype(jnp.bfloat16), "ch").astype(jnp.float32)
    weighted_in = d_normed * gain_in
    grad_gain_in = jnp.sum(d_normed * scaled_in, (0, 1))
    grad_bias_in = jnp.sum(d_normed, (0, 1))
    d_pair = inverse_in * (
        weighted_in
        - jnp.mean(weighted_in, -1, keepdims=True)
        - scaled_in * jnp.mean(weighted_in * scaled_in, -1, keepdims=True)
    )
    grads = (
        grad_gain_in,
        grad_bias_in,
        grad_proj_w,
        grad_gate_w,
        grad_gain_mid,
        grad_bias_mid,
        grad_out_w,
        grad_outgate_w,
    )
    return (grad_out + d_pair, grads)


def per_device(
    pair,
    cotangent,
    lengths,
    norm_gain,
    norm_bias,
    proj_weight,
    gate_weight,
    mid_gain,
    mid_bias,
    out_weight,
    outgate_weight,
):
    rows_here = pair.shape[0]
    cols_here = pair.shape[1]
    row_ids = lax.axis_index("row") * rows_here + lax.iota(jnp.int32, rows_here)
    col_ids = lax.axis_index("col") * cols_here + lax.iota(jnp.int32, cols_here)
    limit = lengths[0]
    pair_mask = ((row_ids[:, None] < limit) & (col_ids[None, :] < limit)).astype(jnp.float32)
    state = pair
    stash = []
    for layer in range(2):
        weights = (
            norm_gain[layer],
            norm_bias[layer],
            proj_weight[layer],
            gate_weight[layer],
            mid_gain[layer],
            mid_bias[layer],
            out_weight[layer],
            outgate_weight[layer],
        )
        state, saved = forward_module(state, pair_mask, weights, layer == 1)
        stash.append(saved)
    grad_state = cotangent.astype(jnp.float32)
    per_layer = [None, None]
    for layer in (1, 0):
        weights = (
            norm_gain[layer],
            norm_bias[layer],
            proj_weight[layer],
            gate_weight[layer],
            mid_gain[layer],
            mid_bias[layer],
            out_weight[layer],
            outgate_weight[layer],
        )
        grad_state, grads = backward_module(
            grad_state, pair_mask, weights, stash[layer], layer == 1
        )
        per_layer[layer] = grads
    lower = per_layer[0]
    upper = per_layer[1]
    summed = lax.psum(
        (
            lower[0],
            lower[1],
            lower[2],
            lower[3],
            lower[4],
            lower[5],
            lower[6],
            lower[7],
            upper[0],
            upper[1],
            upper[2],
            upper[3],
            upper[4],
            upper[5],
            upper[6],
            upper[7],
        ),
        ("row", "col"),
    )
    per_layer = [summed[0:8], summed[8:16]]
    stacked = [jnp.stack([per_layer[0][index], per_layer[1][index]]) for index in range(8)]
    return (
        state,
        grad_state.astype(jnp.bfloat16),
        stacked[0],
        stacked[1],
        stacked[2],
        stacked[3],
        stacked[4],
        stacked[5],
        stacked[6],
        stacked[7],
    )


def on_device(pair, *rest, many, few, split):
    rows, lanes, channels = pair.shape
    shards = many * few
    whole_channels = split == 1 and H % shards == 0 and BLOCK % (H // shards) == 0 and H % (2 * BLOCK) == 0
    tiles = rows == BLOCK and lanes % 128 == 0 and channels == H
    if whole_channels and tiles and many % 2 == 0 and few & (few - 1) == 0:
        return grouped_device(pair, *rest, many=many, few=few)
    return per_device(pair, *rest)


def solution(mesh):
    in_specs = (
        P(("grp", "row"), "col", None),
        P(("grp", "row"), "col", None),
        P("grp"),
        P(),
        P(),
        P(None, None, None, "ch"),
        P(None, None, None, "ch"),
        P(None, "ch"),
        P(None, "ch"),
        P(),
        P(),
    )
    out_specs = (
        P(("grp", "row"), "col", None),
        P(("grp", "row"), "col", None),
        P("grp", None),
        P("grp", None),
        P("grp", None, None, "ch"),
        P("grp", None, None, "ch"),
        P("grp", "ch"),
        P("grp", "ch"),
        P("grp", None, None),
        P("grp", None, None),
    )
    body = functools.partial(
        on_device, many=mesh.shape["row"], few=mesh.shape["col"], split=mesh.shape["ch"]
    )
    return jax.shard_map(
        body, mesh=mesh, in_specs=in_specs, out_specs=out_specs, check_vma=False
    )
```

```python
import functools

import jax
import jax.numpy as jnp
from jax import lax
from jax.experimental import pallas as pl
from jax.experimental.pallas import tpu as pltpu
from jax.sharding import PartitionSpec as P

H = 128


EPS = 1e-05


def product(spec, left, right):
    return jnp.einsum(spec, left, right, preferred_element_type=jnp.float32)


F32 = jnp.float32
BF16 = jnp.bfloat16


def dot(left, right):
    return lax.dot_general(left, right, (((1,), (0,)), ((), ())), preferred_element_type=F32)


def dot_rt(left, right):
    return lax.dot_general(left, right, (((1,), (1,)), ((), ())), preferred_element_type=F32)


def dot_lt(left, right):
    return lax.dot_general(left, right, (((0,), (0,)), ((), ())), preferred_element_type=F32)


def sigmoid(values):
    return 0.5 * jnp.tanh(0.5 * values) + 0.5


def norm_rows(values):
    scale = 1.0 / values.shape[0]
    average = jnp.sum(values, 0, keepdims=True) * scale
    centred = values - average
    variance = jnp.sum(centred * centred, 0, keepdims=True) * scale
    inverse = lax.rsqrt(variance + EPS)
    return centred * inverse, inverse


def turned(weight):
    return jnp.transpose(weight.astype(F32)).astype(BF16)


def column(ref, module, lanes):
    row = ref[module : module + 1, :]
    return beside(*[jnp.transpose(jnp.broadcast_to(row, (lanes, row.shape[1])))] * 2)


def beside(left, right):
    return jnp.concatenate([left, right], axis=-1)


def pair_of(ref, step):
    return beside(ref[2 * step], ref[2 * step + 1])


def put_pair(ref, step, values):
    lanes = ref.shape[-1]
    ref[2 * step] = values[:, :lanes]
    ref[2 * step + 1] = values[:, lanes:]


def pair_of_rows(ref, step):
    return beside(ref[2 * step : 2 * step + 1, :], ref[2 * step + 1 : 2 * step + 2, :])


def put_pair_of_rows(ref, step, values):
    lanes = ref.shape[-1]
    ref[2 * step : 2 * step + 1, :] = values[:, :lanes]
    ref[2 * step + 1 : 2 * step + 2, :] = values[:, lanes:]


def turned_pair(ref, step):
    return beside(
        jnp.transpose(ref[2 * step].astype(F32)), jnp.transpose(ref[2 * step + 1].astype(F32))
    )


def put_turned_pair(ref, step, values):
    lanes = ref.shape[1]
    ref[2 * step] = jnp.transpose(values[:, :lanes]).astype(BF16)
    ref[2 * step + 1] = jnp.transpose(values[:, lanes:]).astype(BF16)


def as_row(total):
    return jnp.sum(jnp.transpose(total), 0, keepdims=True)


def row_mask(lengths_ref, step, rows, lanes):
    limit = lengths_ref[0]
    row_id = lax.axis_index("row") * rows + step
    col_id = lax.axis_index("col") * lanes + lax.broadcasted_iota(jnp.int32, (1, lanes), 1)
    return jnp.where((row_id < limit) & (col_id < limit), 1.0, 0.0).astype(F32)


def load_in_weights(proj_ref, gate_ref, module, scratch):
    width = proj_ref.shape[-1]
    for side in range(2):
        scratch[side * width : (side + 1) * width, :] = turned(proj_ref[module, side])
        scratch[(2 + side) * width : (3 + side) * width, :] = turned(gate_ref[module, side])


def load_back_weights(proj_ref, gate_ref, module, scratch):
    width = proj_ref.shape[-1]
    for side in range(2):
        scratch[:, side * width : (side + 1) * width] = proj_ref[module, side]
        scratch[:, (2 + side) * width : (3 + side) * width] = gate_ref[module, side]


BLOCK = 16


def turn_matrix(rows):
    size = BLOCK * rows
    out = lax.broadcasted_iota(jnp.int32, (size, size), 0)
    source = lax.broadcasted_iota(jnp.int32, (size, size), 1)
    return jnp.where(source == (out % rows) * BLOCK + out // rows, 1.0, 0.0).astype(BF16)


def spread_blocks(matrix, scratch, start, group):
    rows, _, lanes = scratch.shape
    blocks = [
        scratch[:, at : at + BLOCK, :].reshape(rows * BLOCK, lanes)
        for at in (start, start + BLOCK)
    ]
    both = dot(matrix, beside(*blocks)).astype(BF16)
    parts = [
        part.reshape(BLOCK // group, group, rows, lanes)
        for part in (both[:, :lanes], both[:, lanes:])
    ]
    return jnp.concatenate(parts, axis=0)


def collect_blocks(matrix, values, scratch, start):
    rows, _, lanes = scratch.shape
    flat = values.reshape(2, BLOCK * rows, lanes)
    both = dot(matrix, beside(flat[0], flat[1])).astype(BF16)
    for at, part in ((start, both[:, :lanes]), (start + BLOCK, both[:, lanes:])):
        scratch[:, at : at + BLOCK, :] = part.reshape(rows, BLOCK, lanes)


def spread_edges(scratch, out_ref):
    shards, sides, group, rows, lanes = out_ref.shape
    matrix, step = turn_matrix(rows), 2 * BLOCK // group
    for side in range(sides):
        for shard in range(0, shards, step):
            start = (side * shards + shard) * group
            out_ref[shard : shard + step, side] = spread_blocks(matrix, scratch, start, group)


def collect_edges(in_ref, scratch):
    shards, sides, group, rows, lanes = in_ref.shape
    matrix, step = turn_matrix(rows), 2 * BLOCK // group
    for side in range(sides):
        for shard in range(0, shards, step):
            start = (side * shards + shard) * group
            collect_blocks(matrix, in_ref[shard : shard + step, side], scratch, start)


def spread_triangle(scratch, out_ref):
    shards, group, rows, lanes = out_ref.shape
    matrix, step = turn_matrix(rows), 2 * BLOCK // group
    for shard in range(0, shards, step):
        out_ref[shard : shard + step] = spread_blocks(matrix, scratch, shard * group, group)


def collect_triangle(in_ref, scratch):
    shards, group, rows, lanes = in_ref.shape
    matrix, step = turn_matrix(rows), 2 * BLOCK // group
    for shard in range(0, shards, step):
        collect_blocks(matrix, in_ref[shard : shard + step], scratch, shard * group)


def each_pair(rows, body, sums=None):
    for block in range(0, rows // 2, 2):
        parts = [body(block + step) for step in range(2)]
        for index in range(0 if sums is None else sums.shape[0]):
            total = parts[0][index] + parts[1][index]
            lanes = sums.shape[-1]
            sums[index] += total[:, :lanes] + total[:, lanes:]


def mid_norm(tri):
    scale = 1.0 / tri.shape[0]
    average = jnp.sum(tri, 0, keepdims=True) * scale
    squares = jnp.sum(tri * tri, 0, keepdims=True) * scale
    inverse = lax.rsqrt(squares - average * average + EPS)
    return (tri - average) * inverse, inverse


def norm_backward(weighted, scaled, inverse):
    scale = 1.0 / weighted.shape[0]
    first = jnp.sum(weighted, 0, keepdims=True) * scale
    second = jnp.sum(weighted * scaled, 0, keepdims=True) * scale
    return inverse * (weighted - first - scaled * second)


def save_norm(step, values, scaled_out, inverse_out):
    scaled, inverse = norm_rows(values)
    put_pair(scaled_out, step, scaled)
    put_pair_of_rows(inverse_out, step, inverse)
    return scaled


def save_edges(step, normed, in_weights, mask, proj_out, gate_out):
    pre = dot(in_weights, normed)
    half = pre.shape[0] // 2
    gating = sigmoid(pre[half:])
    factor = gating * mask
    value = pre[:half] * factor
    put_pair(proj_out, step, factor)
    put_pair(gate_out, step, value * (1.0 - gating))
    return value.astype(BF16)


def start_kernel(
    lengths, pair_far, ngain_far, nbias_far, proj_far, gate_far,
    edge_out, normed_out, proj_out, gate_out, scaled_out, inverse_out, mask_out,
    pair, ngain, nbias, proj_w, gate_w, sems, wts, scr,
):
    far = (proj_far.at[0], gate_far.at[0], ngain_far, nbias_far, pair_far)
    near = (proj_w.at[0], gate_w.at[0], ngain, nbias, pair)
    copies = [
        pltpu.make_async_copy(source, target, sems.at[index])
        for index, (source, target) in enumerate(zip(far, near))
    ]
    for copy in copies:
        copy.start()
    for copy in copies:
        copy.wait()
    rows, lanes, channels = pair.shape
    load_in_weights(proj_w, gate_w, 0, wts)
    gain, bias = column(ngain, 0, lanes), column(nbias, 0, lanes)

    def body(step):
        base = turned_pair(pair, step)
        scaled = save_norm(step, base, scaled_out, inverse_out)
        normed = (scaled * gain + bias).astype(BF16)
        put_pair(normed_out, step, normed)
        mask = beside(*[row_mask(lengths, 2 * step + row, rows, lanes) for row in range(2)])
        put_pair_of_rows(mask_out, step, mask)
        put_pair(scr, step, save_edges(step, normed, wts[...], mask, proj_out, gate_out))

    each_pair(rows, body)
    spread_edges(scr, edge_out)


def between_kernel(
    mask_all, tri, pair, normed0, ngain, nbias, mgain, mbias, out_w, outgate_w, proj_w, gate_w,
    edge_out, mid_out, normed_out, proj_out, gate_out, scaled_out, inverse_out,
    outgate_out, scaled_mid_out, inverse_mid_out, wts, tri_in, scr,
):
    rows, lanes, channels = pair.shape
    load_in_weights(proj_w, gate_w, 1, wts)
    out_t, outgate_t = turned(out_w[0]), turned(outgate_w[0])
    gain, bias = column(ngain, 1, lanes), column(nbias, 1, lanes)
    gain_mid, bias_mid = column(mgain, 0, lanes), column(mbias, 0, lanes)
    collect_triangle(tri, tri_in)

    def body(step):
        scaled_mid, inverse_mid = mid_norm(pair_of(tri_in, step).astype(F32))
        put_pair(scaled_mid_out, step, scaled_mid)
        put_pair_of_rows(inverse_mid_out, step, inverse_mid)
        unit = (scaled_mid * gain_mid + bias_mid).astype(BF16)
        outer = dot(out_t, unit)
        outgate = sigmoid(dot(outgate_t, pair_of(normed0, step)))
        put_pair(outgate_out, step, outgate)
        mid = (turned_pair(pair, step) + outer * outgate).astype(BF16)
        put_pair(mid_out, step, mid)
        scaled = save_norm(step, mid.astype(F32), scaled_out, inverse_out)
        normed = (scaled * gain + bias).astype(BF16)
        put_pair(normed_out, step, normed)
        mask = pair_of_rows(mask_all, step)
        put_pair(scr, step, save_edges(step, normed, wts[...], mask, proj_out, gate_out))

    each_pair(rows, body)
    spread_edges(scr, edge_out)


def out_weight_grads(unit, d_outer, normed, d_gatepre, out_ref):
    width = unit.shape[0]
    out_ref[0:width, :] = dot_rt(unit[...], d_outer[...]).astype(out_ref.dtype)
    out_ref[width:, :] = dot_rt(normed[...], d_gatepre[...]).astype(out_ref.dtype)


def in_weight_grads(normed_all, d_in_all, out_ref):
    width = normed_all.shape[0]
    for part in range(d_in_all.shape[0] // width):
        block = slice(part * width, (part + 1) * width)
        out_ref[block, :] = dot_rt(normed_all[...], d_in_all[block, :]).astype(out_ref.dtype)


def lane_block(step, lanes):
    return pl.ds(2 * step * lanes, 2 * lanes)


def turn_kernel(
    tri, mid, normed, cot, mgain, mbias, out_w, outgate_w,
    d_tri_out, new_out, grad_out, d_normed_out, weights_out, small_out,
    tri_in, scr, unit_all, outer_all, normed_all, gate_all, sums,
):
    rows, channels, lanes = mid.shape
    out_t, outgate_t = turned(out_w[1]), turned(outgate_w[1])
    gain_mid, bias_mid = column(mgain, 1, lanes), column(mbias, 1, lanes)
    collect_triangle(tri, tri_in)
    sums[...] = jnp.zeros_like(sums)

    def body(step):
        here = lane_block(step, lanes)
        grad = turned_pair(cot, step)
        put_pair(grad_out, step, grad)
        here_normed = pair_of(normed, step)
        outgate = sigmoid(dot(outgate_t, here_normed))
        gated = grad * outgate
        d_outer = gated.astype(BF16)
        d_unit = dot(out_w[1], d_outer)
        scaled_mid, inverse_mid = mid_norm(pair_of(tri_in, step).astype(F32))
        d_tri = norm_backward(d_unit * gain_mid, scaled_mid, inverse_mid)
        put_pair(scr, step, d_tri.astype(BF16))
        unit = (scaled_mid * gain_mid + bias_mid).astype(BF16)
        outer = dot(out_t, unit)
        put_pair(new_out, step, (pair_of(mid, step).astype(F32) + outer * outgate).astype(BF16))
        d_gatepre = (gated * outer * (1.0 - outgate)).astype(BF16)
        put_pair(d_normed_out, step, dot(outgate_w[1], d_gatepre))
        unit_all[:, here] = unit
        outer_all[:, here] = d_outer
        normed_all[:, here] = here_normed
        gate_all[:, here] = d_gatepre
        return d_unit * scaled_mid, d_unit

    each_pair(rows, body, sums)
    spread_triangle(scr, d_tri_out)
    out_weight_grads(unit_all, outer_all, normed_all, gate_all, weights_out)
    for index in range(2):
        small_out[index : index + 1, :] = as_row(sums[index])


def edge_backward(step, scratch, proj_factor, gate_factor):
    here = pair_of(scratch, step).astype(F32)
    d_proj = (here * pair_of(proj_factor, step)).astype(BF16)
    d_gate = (here * pair_of(gate_factor, step)).astype(BF16)
    return jnp.concatenate([d_proj, d_gate], axis=0)


def middle_kernel(
    d_edge, proj_factor, gate_factor, d_normed_gate, scaled_in, inverse_in, cot, outgate,
    scaled_mid, inverse_mid, normed0, normed1, ngain, mgain, mbias, proj_w, gate_w, out_w,
    outgate_w,
    d_tri_out, grad_out, d_normed_out, out_weights, in_weights, small_out,
    scr, scr_tri, unit_all, outer_all, normed_all, gate_all, upper_all, d_in_all, back, sums,
):
    rows, channels, lanes = cot.shape
    out_t = turned(out_w[0])
    gain = column(ngain, 1, lanes)
    gain_mid, bias_mid = column(mgain, 0, lanes), column(mbias, 0, lanes)
    collect_edges(d_edge, scr)
    sums[...] = jnp.zeros_like(sums)
    load_back_weights(proj_w, gate_w, 1, back)

    def upper(step):
        place = lane_block(step, lanes)
        d_in = edge_backward(step, scr, proj_factor, gate_factor)
        d_in_all[:, place] = d_in
        upper_all[:, place] = pair_of(normed1, step)
        d_normed = pair_of(d_normed_gate, step) + dot(back[...], d_in)
        scaled = pair_of(scaled_in, step)
        grad = pair_of(cot, step) + norm_backward(
            d_normed * gain, scaled, pair_of_rows(inverse_in, step)
        )
        put_pair(grad_out, step, grad)
        return d_normed * scaled, d_normed

    def lower(step):
        place = lane_block(step, lanes)
        gate = pair_of(outgate, step)
        gated = pair_of(grad_out, step) * gate
        d_outer = gated.astype(BF16)
        d_unit = dot(out_w[0], d_outer)
        scaled = pair_of(scaled_mid, step)
        d_tri = norm_backward(d_unit * gain_mid, scaled, pair_of_rows(inverse_mid, step))
        put_pair(scr_tri, step, d_tri.astype(BF16))
        unit = (scaled * gain_mid + bias_mid).astype(BF16)
        outer = dot(out_t, unit)
        d_gatepre = (gated * outer * (1.0 - gate)).astype(BF16)
        put_pair(d_normed_out, step, dot(outgate_w[0], d_gatepre))
        unit_all[:, place] = unit
        outer_all[:, place] = d_outer
        normed_all[:, place] = pair_of(normed0, step)
        gate_all[:, place] = d_gatepre
        return d_unit * scaled, d_unit

    each_pair(rows, upper, sums.at[2:4])
    each_pair(rows, lower, sums.at[0:2])
    spread_triangle(scr_tri, d_tri_out)
    out_weight_grads(unit_all, outer_all, normed_all, gate_all, out_weights)
    in_weight_grads(upper_all, d_in_all, in_weights)
    for index in range(4):
        small_out[index : index + 1, :] = as_row(sums[index])


def split_cores(all_rows, own_out, other_out, few):
    chips, share, width = own_out.shape
    view = all_rows.reshape(chips // few, 2, few, share, width)
    core = lax.rem(lax.axis_index("row"), 2)
    own_out[...] = view[:, core].reshape(own_out.shape)
    other_out[...] = view[:, 1 - core].reshape(other_out.shape)


def finish_kernel(
    few, d_edge, proj_factor, gate_factor, normed, out0, in1, out1,
    own_out, other_out, d_in_all, scr, normed_all, packed,
):
    rows, half, lanes = proj_factor.shape
    collect_edges(d_edge, scr)

    def body(step):
        place = lane_block(step, lanes)
        d_in_all[:, place] = edge_backward(step, scr, proj_factor, gate_factor)
        normed_all[:, place] = pair_of(normed, step)

    each_pair(rows, body)
    first, second, third = d_in_all.shape[0], out0.shape[0], in1.shape[0]
    in_weight_grads(normed_all, d_in_all, packed.at[0:first])
    packed[first : first + second, :] = out0[...]
    packed[first + second : first + second + third, :] = in1[...]
    packed[first + second + third :, :] = out1[...]
    split_cores(packed, own_out, other_out, few)


def norm_sums_kernel(
    d_in, d_normed_gate, scaled_in, proj_w, gate_w, small_middle, small1, new_t,
    d_normed_out, extra_out, new_out, back, sums,
):
    rows, channels, lanes = scaled_in.shape
    sums[...] = jnp.zeros_like(sums)
    load_back_weights(proj_w, gate_w, 0, back)

    def body(step):
        here = d_in[:, lane_block(step, lanes)]
        d_normed = pair_of(d_normed_gate, step) + dot(back[...], here)
        put_pair(d_normed_out, step, d_normed)
        put_turned_pair(new_out, step, pair_of(new_t, step).astype(F32))
        return d_normed * pair_of(scaled_in, step), d_normed

    each_pair(rows, body, sums)
    small = jnp.concatenate(
        [as_row(sums[0]), as_row(sums[1]), small_middle[0:2], small_middle[2:4], small1[...]],
        axis=0,
    )
    high = small.astype(BF16).astype(F32)
    extra_out[...] = jnp.concatenate([high, small - high], axis=0).astype(BF16)


def add_kernel(first, second, extra, out_ref, extra_out):
    out_ref[...] = (first[...].astype(F32) + second[...].astype(F32)).astype(BF16)
    extra_out[...] = extra[...]


def sum_kernel(parts, extra, shared_out):
    chips, share, width = parts.shape
    own = jnp.sum(parts[...].astype(F32), axis=0).astype(BF16)
    for chip in range(chips):
        shared_out[chip, 0:share] = own
        shared_out[chip, share:] = extra[...]


def grad_pair_kernel(
    share, shared, d_normed, scaled_in, inverse_in, grad, ngain, grad_out, mine_out
):
    rows, channels, lanes = grad.shape
    gain = column(ngain, 0, lanes)
    mine_out[...] = jnp.sum(shared[:, share:].astype(F32), axis=0)

    def body(step):
        total = pair_of(grad, step) + norm_backward(
            pair_of(d_normed, step) * gain, pair_of(scaled_in, step),
            pair_of_rows(inverse_in, step),
        )
        put_turned_pair(grad_out, step, total)

    each_pair(rows, body)


def unpack_kernel(
    share, few, own, other, mine, proj_out, gate_out, out_out, outgate_out,
    norm_gain_out, norm_bias_out, mid_gain_out, mid_bias_out, weights,
):
    chips, _, width = own.shape
    core = lax.rem(lax.axis_index("row"), 2)
    view = weights.reshape(chips // few, 2, few, share, width)
    block = (chips // few, few, share, width)
    view[:, core] = own[:, 0:share].astype(F32).reshape(block)
    view[:, 1 - core] = other[:, 0:share].astype(F32).reshape(block)
    total = mine[...] + jnp.sum(other[:, share:].astype(F32), axis=0)
    total = total[0:8] + total[8:16]
    for module in range(2):
        for index, out in enumerate((norm_gain_out, norm_bias_out, mid_gain_out, mid_bias_out)):
            at = 4 * module + index
            out[module : module + 1, :] = total[at : at + 1]
        blocks = [
            weights[(6 * module + part) * width : (6 * module + part + 1) * width, :]
            for part in range(6)
        ]
        for side in range(2):
            proj_out[module, side] = blocks[side]
            gate_out[module, side] = blocks[2 + side]
        out_out[module] = blocks[4]
        outgate_out[module] = blocks[5]


def triangle_kernel(incoming, edge, tri_out):
    many, few, _, group, rows, lanes = edge.shape

    def whole(side, channel):
        parts = [edge[:, c, side, channel].reshape(many * rows, lanes) for c in range(few)]
        return jnp.concatenate(parts, axis=1)

    for channel in range(group):
        left, right = whole(0, channel), whole(1, channel)
        tri = (dot_lt if incoming else dot_rt)(left, right).astype(BF16)
        for c in range(few):
            part = tri[:, c * lanes : (c + 1) * lanes]
            tri_out[:, c, channel] = part.reshape(many, rows, lanes)


def edge_grad_kernel(incoming, edge, d_tri, grad_out):
    many, few, _, group, rows, lanes = edge.shape

    def whole(ref, *index):
        parts = [ref[(slice(None), c) + index].reshape(many * rows, lanes) for c in range(few)]
        return jnp.concatenate(parts, axis=1)

    for channel in range(group):
        left, right = whole(edge, 0, channel), whole(edge, 1, channel)
        grad = whole(d_tri, channel)
        if incoming:
            d_left, d_right = dot_rt(right, grad), dot(left, grad)
        else:
            d_left, d_right = dot(grad, right), dot_lt(grad, left)
        for side, value in ((0, d_left), (1, d_right)):
            value = value.astype(BF16)
            for c in range(few):
                part = value[:, c * lanes : (c + 1) * lanes]
                grad_out[:, c, side, channel] = part.reshape(many, rows, lanes)


SCALARS = pl.BlockSpec(memory_space=pltpu.SMEM)
VECTORS = pl.BlockSpec(memory_space=pltpu.VMEM)
FAR = pl.BlockSpec(memory_space=pltpu.HBM)


def call(kernel, name, outs, args, scratch=(), flops=0, grant=16, specs=None):
    shapes = [jax.ShapeDtypeStruct(shape, dtype) for shape, dtype in outs]
    moved = sum(a.size * a.dtype.itemsize for a in list(args) + shapes)
    return pl.pallas_call(
        kernel,
        name=name,
        out_shape=shapes,
        in_specs=specs or [VECTORS] * len(args),
        out_specs=[VECTORS] * len(shapes),
        scratch_shapes=[
            pltpu.VMEM(*item) if isinstance(item, tuple) else item for item in scratch
        ],
        compiler_params=pltpu.CompilerParams(vmem_limit_bytes=grant * 1024 * 1024),
        cost_estimate=pl.CostEstimate(flops=flops, bytes_accessed=moved, transcendentals=0),
    )(*args)


def exchange(values):
    return lax.all_to_all(values, ("row", "col"), split_axis=0, concat_axis=0, tiled=True)


def swap_cores(values, many, few):
    pairs = [(index, index ^ few) for index in range(many * few)]
    return lax.ppermute(values, ("row", "col"), pairs)


def exchange_chips(values, many, few):
    groups = [
        [row * few + col for row in range(core, many, 2) for col in range(few)] for core in range(2)
    ]
    return lax.all_to_all(
        values, ("row", "col"), split_axis=0, concat_axis=0, axis_index_groups=groups, tiled=True
    )


def grouped_device(
    pair, cotangent, lengths, ngain, nbias, proj_w, gate_w, mgain, mbias, out_w, outgate_w,
    *, many, few,
):
    rows, lanes, channels = pair.shape
    shards = many * few
    group = H // shards
    edge = ((shards, 2, group, rows, lanes), BF16)
    grid = ((many, few, 2, group, rows, lanes), BF16)
    tri = ((shards, group, rows, lanes), BF16)
    tri_grid = ((many, few, group, rows, lanes), BF16)
    tile = ((rows, channels, lanes), BF16)
    wide = ((rows, channels, lanes), F32)
    row = ((rows, lanes), F32)
    factor = ((rows, 2 * H, lanes), F32)
    back = ((channels, 4 * H), BF16)
    wts = ((4 * H, channels), BF16)
    big = ((rows, 2 * H, lanes), BF16)
    mid = ((rows, H, lanes), BF16)
    positions = rows * lanes
    flat = ((H, positions), BF16)
    flat_in = ((4 * H, positions), BF16)
    out_rows = ((2 * H, channels), BF16)
    in_rows = ((4 * H, H), BF16)
    triangle = 2 * group * (many * rows) ** 2 * (few * lanes)
    dense = 2 * positions * channels * H

    def sums(count):
        return ((count, H, lanes), F32)

    def small(count):
        return ((count, H), F32)

    saved = [tile, factor, factor, wide, row]
    far = [
        pltpu.with_memory_space_constraint(item, pltpu.HBM)
        for item in (pair, ngain, nbias, proj_w, gate_w)
    ]
    sent, normed0, *factors0, mask = call(
        start_kernel, "start", [edge, *saved, row], [lengths, *far],
        [(pair.shape, BF16), (ngain.shape, F32), (nbias.shape, F32), (proj_w.shape, BF16),
         (gate_w.shape, BF16), pltpu.SemaphoreType.DMA((5,)), wts, big],
        4 * dense, specs=[SCALARS] + [FAR] * len(far),
    )
    edge0 = exchange(sent).reshape(grid[0])
    (here,) = call(
        functools.partial(triangle_kernel, False), "outgoing", [tri_grid], [edge0], (), triangle,
    )
    tri0 = exchange(here.reshape(tri[0]))
    sent, mid_t, normed1, *factors1, outgate0, scaled_mid0, inverse_mid0 = call(
        between_kernel, "between", [edge, tile, *saved, wide, wide, row],
        [mask, tri0, pair, normed0, ngain, nbias, mgain, mbias, out_w, outgate_w, proj_w,
         gate_w],
        [wts, mid, big], 6 * dense,
    )
    edge1 = exchange(sent).reshape(grid[0])
    (here,) = call(
        functools.partial(triangle_kernel, True), "incoming", [tri_grid], [edge1], (), triangle,
    )
    tri1 = exchange(here.reshape(tri[0]))
    sent, new_t, cot_t, d_normed_gate1, out_grads1, small1 = call(
        turn_kernel, "turn", [tri, tile, wide, wide, out_rows, small(2)],
        [tri1, mid_t, normed1, cotangent, mgain, mbias, out_w, outgate_w],
        [mid, mid, flat, flat, flat, flat, sums(2)], 6 * dense,
    )
    d_tri1 = exchange(sent).reshape(tri_grid[0])
    (sent,) = call(
        functools.partial(edge_grad_kernel, True), "incoming_grad", [grid], [edge1, d_tri1],
        (), 2 * triangle,
    )
    d_edge1 = exchange(sent.reshape(edge[0]))
    proj_factor1, gate_factor1, scaled1, inverse1 = factors1
    sent, grad, d_normed_gate0, out_grads0, in_grads1, small_middle = call(
        middle_kernel, "middle", [tri, wide, wide, out_rows, in_rows, small(4)],
        [d_edge1, proj_factor1, gate_factor1, d_normed_gate1, scaled1, inverse1, cot_t, outgate0,
         scaled_mid0, inverse_mid0, normed0, normed1, ngain, mgain, mbias, proj_w, gate_w, out_w,
         outgate_w],
        [big, mid, flat, flat, flat, flat, flat, flat_in, back, sums(4)], 13 * dense,
    )
    d_tri0 = exchange(sent).reshape(tri_grid[0])
    (sent,) = call(
        functools.partial(edge_grad_kernel, False), "outgoing_grad", [grid], [edge0, d_tri0],
        (), 2 * triangle,
    )
    d_edge0 = exchange(sent.reshape(edge[0]))
    share = 12 * H // shards
    chips = shards // 2
    proj_factor0, gate_factor0, scaled0, inverse0 = factors0
    held = ((chips, share, H), BF16)
    own, other, d_in0 = call(
        functools.partial(finish_kernel, few), "finish", [held, held, flat_in],
        [d_edge0, proj_factor0, gate_factor0, normed0, out_grads0, in_grads1, out_grads1],
        [big, flat, ((12 * H, H), BF16)], 4 * dense,
    )
    other = swap_cores(other, many, few)
    d_normed0, extra, new_pair = call(
        norm_sums_kernel, "norm_sums", [wide, ((16, H), BF16), (pair.shape, BF16)],
        [d_in0, d_normed_gate0, scaled0, proj_w, gate_w, small_middle, small1, new_t],
        [back, sums(2)],
        4 * dense,
    )
    own, extra = call(add_kernel, "add_cores", [held, ((16, H), BF16)], [own, other, extra])
    parts = exchange_chips(own, many, few)
    (shared,) = call(
        sum_kernel, "sum_weights", [((chips, share + 16, H), BF16)], [parts, extra]
    )
    shared = exchange_chips(shared, many, few)
    other = swap_cores(shared, many, few)
    grad_pair, mine = call(
        functools.partial(grad_pair_kernel, share), "grad_pair",
        [(pair.shape, BF16), ((16, H), F32)],
        [shared, d_normed0, scaled0, inverse0, grad, ngain],
    )
    grad_proj, grad_gate, grad_out, grad_outgate, *vectors = call(
        functools.partial(unpack_kernel, share, few), "unpack",
        [(proj_w.shape, F32), (gate_w.shape, F32), (out_w.shape, F32), (outgate_w.shape, F32),
         (ngain.shape, F32), (nbias.shape, F32), (mgain.shape, F32), (mbias.shape, F32)],
        [shared, other, mine], [((12 * H, H), F32)],
    )
    return (
        new_pair,
        grad_pair,
        vectors[0],
        vectors[1],
        grad_proj,
        grad_gate,
        vectors[2],
        vectors[3],
        grad_out,
        grad_outgate,
    )


def norm_channels(values):
    average = jnp.mean(values, -1, keepdims=True)
    centred = values - average
    variance = jnp.mean(centred * centred, -1, keepdims=True)
    inverse = lax.rsqrt(variance + EPS)
    return (centred * inverse, inverse)


def forward_module(pair_in, pair_mask, weights, incoming):
    gain_in, bias_in, proj_w, gate_w, gain_mid, bias_mid, out_w, outgate_w = weights
    scaled_in, inverse_in = norm_channels(pair_in.astype(jnp.float32))
    normed = (scaled_in * gain_in + bias_in).astype(jnp.bfloat16)
    projected = product("ijc,sch->shij", normed, proj_w)
    gating = jax.nn.sigmoid(product("ijc,sch->shij", normed, gate_w))
    hidden = (projected * gating * pair_mask).astype(jnp.bfloat16)
    left_side, right_side = (
        lax.all_to_all(hidden[0], "row", split_axis=0, concat_axis=1, tiled=True),
        lax.all_to_all(hidden[1], "row", split_axis=0, concat_axis=1, tiled=True),
    )
    if incoming:
        left_side = jnp.swapaxes(left_side, 1, 2)
        right_side = jnp.swapaxes(right_side, 1, 2)
    else:
        left_side, right_side = (
            lax.all_to_all(left_side, "col", split_axis=1, concat_axis=2, tiled=True),
            lax.all_to_all(right_side, "col", split_axis=1, concat_axis=2, tiled=True),
        )
    triangle = product(
        "cik,cjk->cij", left_side, lax.all_gather(right_side, "col", axis=1, tiled=True)
    ).astype(jnp.bfloat16)
    triangle = lax.all_to_all(
        lax.all_to_all(triangle, "col", split_axis=2, concat_axis=1, tiled=True),
        "row",
        split_axis=1,
        concat_axis=0,
        tiled=True,
    )
    tri_values = triangle.astype(jnp.float32)
    total, squares = lax.psum((jnp.sum(tri_values, 0), jnp.sum(tri_values * tri_values, 0)), "ch")
    average = total / H
    inverse_mid = lax.rsqrt(squares / H - average * average + EPS)
    scaled_mid = (tri_values - average) * inverse_mid
    unit = (scaled_mid * gain_mid[:, None, None] + bias_mid[:, None, None]).astype(jnp.bfloat16)
    unit_full = lax.all_gather(unit, "ch", axis=0, tiled=True)
    outer = product("hij,hc->ijc", unit_full, out_w)
    outgate = jax.nn.sigmoid(product("ijc,cd->ijd", normed, outgate_w))
    result = (pair_in.astype(jnp.float32) + outer * outgate).astype(jnp.bfloat16)
    saved = (
        scaled_in,
        inverse_in,
        normed,
        projected,
        gating,
        left_side,
        right_side,
        scaled_mid,
        inverse_mid,
        unit_full,
        outer,
        outgate,
    )
    return (result, saved)


def backward_module(grad_out, pair_mask, weights, saved, incoming):
    gain_in, bias_in, proj_w, gate_w, gain_mid, bias_mid, out_w, outgate_w = weights
    (
        scaled_in,
        inverse_in,
        normed,
        projected,
        gating,
        left_side,
        right_side,
        scaled_mid,
        inverse_mid,
        unit_full,
        outer,
        outgate,
    ) = saved
    d_outer = (grad_out * outgate).astype(jnp.bfloat16)
    d_gatepre = (grad_out * outer * outgate * (1.0 - outgate)).astype(jnp.bfloat16)
    grad_out_w = product("hij,ijc->hc", unit_full, d_outer)
    grad_outgate_w = product("ijc,ijd->cd", normed, d_gatepre)
    width = gain_mid.shape[0]
    own_rows = lax.dynamic_slice_in_dim(out_w, lax.axis_index("ch") * width, width, 0)
    d_unit = product("ijc,hc->hij", d_outer, own_rows)
    d_normed = product("ijd,cd->ijc", d_gatepre, outgate_w)
    weighted = d_unit * gain_mid[:, None, None]
    grad_gain_mid = jnp.sum(d_unit * scaled_mid, (1, 2))
    grad_bias_mid = jnp.sum(d_unit, (1, 2))
    first_sum, second_sum = lax.psum(
        (jnp.sum(weighted, 0), jnp.sum(weighted * scaled_mid, 0)), "ch"
    )
    d_tri = (inverse_mid * (weighted - first_sum / H - scaled_mid * (second_sum / H))).astype(
        jnp.bfloat16
    )
    grad_rows = lax.all_to_all(d_tri, "row", split_axis=0, concat_axis=1, tiled=True)
    grad_cols = lax.all_to_all(grad_rows, "col", split_axis=1, concat_axis=2, tiled=True)
    d_left = product(
        "cij,cjk->cik", grad_cols, lax.all_gather(right_side, "col", axis=1, tiled=True)
    )
    partial_terms = product("cij,cik->cjk", grad_cols, left_side)
    d_right = lax.psum_scatter(
        partial_terms.astype(jnp.bfloat16), "col", scatter_dimension=1, tiled=True
    ).astype(jnp.float32)
    d_left = d_left.astype(jnp.bfloat16)
    d_right = d_right.astype(jnp.bfloat16)
    if incoming:
        d_left = jnp.swapaxes(d_left, 1, 2)
        d_right = jnp.swapaxes(d_right, 1, 2)
    else:
        d_left, d_right = (
            lax.all_to_all(d_left, "col", split_axis=2, concat_axis=1, tiled=True),
            lax.all_to_all(d_right, "col", split_axis=2, concat_axis=1, tiled=True),
        )
    d_left, d_right = (
        lax.all_to_all(d_left, "row", split_axis=1, concat_axis=0, tiled=True),
        lax.all_to_all(d_right, "row", split_axis=1, concat_axis=0, tiled=True),
    )
    d_hidden = jnp.stack([d_left, d_right]).astype(jnp.float32)
    d_proj = (d_hidden * gating * pair_mask).astype(jnp.bfloat16)
    d_gate = (d_hidden * projected * gating * (1.0 - gating) * pair_mask).astype(jnp.bfloat16)
    grad_proj_w = product("ijc,shij->sch", normed, d_proj)
    grad_gate_w = product("ijc,shij->sch", normed, d_gate)
    partial_input = product("shij,sch->ijc", d_proj, proj_w) + product(
        "shij,sch->ijc", d_gate, gate_w
    )
    d_normed = d_normed + lax.psum(partial_input.astype(jnp.bfloat16), "ch").astype(jnp.float32)
    weighted_in = d_normed * gain_in
    grad_gain_in = jnp.sum(d_normed * scaled_in, (0, 1))
    grad_bias_in = jnp.sum(d_normed, (0, 1))
    d_pair = inverse_in * (
        weighted_in
        - jnp.mean(weighted_in, -1, keepdims=True)
        - scaled_in * jnp.mean(weighted_in * scaled_in, -1, keepdims=True)
    )
    grads = (
        grad_gain_in,
        grad_bias_in,
        grad_proj_w,
        grad_gate_w,
        grad_gain_mid,
        grad_bias_mid,
        grad_out_w,
        grad_outgate_w,
    )
    return (grad_out + d_pair, grads)


def per_device(
    pair,
    cotangent,
    lengths,
    norm_gain,
    norm_bias,
    proj_weight,
    gate_weight,
    mid_gain,
    mid_bias,
    out_weight,
    outgate_weight,
):
    rows_here = pair.shape[0]
    cols_here = pair.shape[1]
    row_ids = lax.axis_index("row") * rows_here + lax.iota(jnp.int32, rows_here)
    col_ids = lax.axis_index("col") * cols_here + lax.iota(jnp.int32, cols_here)
    limit = lengths[0]
    pair_mask = ((row_ids[:, None] < limit) & (col_ids[None, :] < limit)).astype(jnp.float32)
    state = pair
    stash = []
    for layer in range(2):
        weights = (
            norm_gain[layer],
            norm_bias[layer],
            proj_weight[layer],
            gate_weight[layer],
            mid_gain[layer],
            mid_bias[layer],
            out_weight[layer],
            outgate_weight[layer],
        )
        state, saved = forward_module(state, pair_mask, weights, layer == 1)
        stash.append(saved)
    grad_state = cotangent.astype(jnp.float32)
    per_layer = [None, None]
    for layer in (1, 0):
        weights = (
            norm_gain[layer],
            norm_bias[layer],
            proj_weight[layer],
            gate_weight[layer],
            mid_gain[layer],
            mid_bias[layer],
            out_weight[layer],
            outgate_weight[layer],
        )
        grad_state, grads = backward_module(
            grad_state, pair_mask, weights, stash[layer], layer == 1
        )
        per_layer[layer] = grads
    lower = per_layer[0]
    upper = per_layer[1]
    summed = lax.psum(
        (
            lower[0],
            lower[1],
            lower[2],
            lower[3],
            lower[4],
            lower[5],
            lower[6],
            lower[7],
            upper[0],
            upper[1],
            upper[2],
            upper[3],
            upper[4],
            upper[5],
            upper[6],
            upper[7],
        ),
        ("row", "col"),
    )
    per_layer = [summed[0:8], summed[8:16]]
    stacked = [jnp.stack([per_layer[0][index], per_layer[1][index]]) for index in range(8)]
    return (
        state,
        grad_state.astype(jnp.bfloat16),
        stacked[0],
        stacked[1],
        stacked[2],
        stacked[3],
        stacked[4],
        stacked[5],
        stacked[6],
        stacked[7],
    )


def on_device(pair, *rest, many, few, split):
    rows, lanes, channels = pair.shape
    shards = many * few
    whole_channels = split == 1 and H % shards == 0 and BLOCK % (H // shards) == 0 and H % (2 * BLOCK) == 0
    tiles = rows == BLOCK and lanes % 128 == 0 and channels == H
    if whole_channels and tiles and many % 2 == 0 and few & (few - 1) == 0:
        return grouped_device(pair, *rest, many=many, few=few)
    return per_device(pair, *rest)


def solution(mesh):
    in_specs = (
        P(("grp", "row"), "col", None),
        P(("grp", "row"), "col", None),
        P("grp"),
        P(),
        P(),
        P(None, None, None, "ch"),
        P(None, None, None, "ch"),
        P(None, "ch"),
        P(None, "ch"),
        P(),
        P(),
    )
    out_specs = (
        P(("grp", "row"), "col", None),
        P(("grp", "row"), "col", None),
        P("grp", None),
        P("grp", None),
        P("grp", None, None, "ch"),
        P("grp", None, None, "ch"),
        P("grp", "ch"),
        P("grp", "ch"),
        P("grp", None, None),
        P("grp", None, None),
    )
    body = functools.partial(
        on_device, many=mesh.shape["row"], few=mesh.shape["col"], split=mesh.shape["ch"]
    )
    return jax.shard_map(
        body, mesh=mesh, in_specs=in_specs, out_specs=out_specs, check_vma=False
    )
```

```python
import functools

import jax
import jax.numpy as jnp
from jax import lax
from jax.experimental import pallas as pl
from jax.experimental.pallas import tpu as pltpu
from jax.sharding import PartitionSpec as P

H = 128


EPS = 1e-05


def product(spec, left, right):
    return jnp.einsum(spec, left, right, preferred_element_type=jnp.float32)


F32 = jnp.float32
BF16 = jnp.bfloat16


def dot(left, right):
    return lax.dot_general(left, right, (((1,), (0,)), ((), ())), preferred_element_type=F32)


def dot_rt(left, right):
    return lax.dot_general(left, right, (((1,), (1,)), ((), ())), preferred_element_type=F32)


def dot_lt(left, right):
    return lax.dot_general(left, right, (((0,), (0,)), ((), ())), preferred_element_type=F32)


def sigmoid(values):
    return 0.5 * jnp.tanh(0.5 * values) + 0.5


def norm_rows(values):
    scale = 1.0 / values.shape[0]
    average = jnp.sum(values, 0, keepdims=True) * scale
    centred = values - average
    variance = jnp.sum(centred * centred, 0, keepdims=True) * scale
    inverse = lax.rsqrt(variance + EPS)
    return centred * inverse, inverse


def turned(weight):
    return jnp.transpose(weight)


def column(ref, module, lanes):
    row = ref[module : module + 1, :]
    return beside(*[jnp.transpose(jnp.broadcast_to(row, (lanes, row.shape[1])))] * 2)


def beside(left, right):
    return jnp.concatenate([left, right], axis=-1)


def pair_of(ref, step):
    return beside(ref[2 * step], ref[2 * step + 1])


def put_pair(ref, step, values):
    lanes = ref.shape[-1]
    ref[2 * step] = values[:, :lanes]
    ref[2 * step + 1] = values[:, lanes:]


def pair_of_rows(ref, step):
    return beside(ref[2 * step : 2 * step + 1, :], ref[2 * step + 1 : 2 * step + 2, :])


def put_pair_of_rows(ref, step, values):
    lanes = ref.shape[-1]
    ref[2 * step : 2 * step + 1, :] = values[:, :lanes]
    ref[2 * step + 1 : 2 * step + 2, :] = values[:, lanes:]


def turned_pair(ref, step):
    return beside(jnp.transpose(ref[2 * step]), jnp.transpose(ref[2 * step + 1])).astype(F32)


def put_turned_pair(ref, step, values):
    lanes = ref.shape[1]
    values = values.astype(BF16)
    ref[2 * step] = jnp.transpose(values[:, :lanes])
    ref[2 * step + 1] = jnp.transpose(values[:, lanes:])


def as_row(total):
    return jnp.sum(jnp.transpose(total), 0, keepdims=True)


def row_mask(lengths_ref, step, rows, lanes):
    limit = lengths_ref[0]
    row_id = lax.axis_index("row") * rows + step
    col_id = lax.axis_index("col") * lanes + lax.broadcasted_iota(jnp.int32, (1, lanes), 1)
    return jnp.where((row_id < limit) & (col_id < limit), 1.0, 0.0).astype(F32)


def load_in_weights(proj_ref, gate_ref, module, scratch):
    width = proj_ref.shape[-1]
    for side in range(2):
        scratch[side * width : (side + 1) * width, :] = turned(proj_ref[module, side])
        scratch[(2 + side) * width : (3 + side) * width, :] = turned(gate_ref[module, side])


def load_back_weights(proj_ref, gate_ref, module, scratch):
    width = proj_ref.shape[-1]
    for side in range(2):
        scratch[:, side * width : (side + 1) * width] = proj_ref[module, side]
        scratch[:, (2 + side) * width : (3 + side) * width] = gate_ref[module, side]


BLOCK = 16


def turn_matrix(rows):
    size = BLOCK * rows
    out = lax.broadcasted_iota(jnp.int32, (size, size), 0)
    source = lax.broadcasted_iota(jnp.int32, (size, size), 1)
    return jnp.where(source == (out % rows) * BLOCK + out // rows, 1.0, 0.0).astype(BF16)


def spread_blocks(matrix, scratch, start, group):
    rows, _, lanes = scratch.shape
    blocks = [
        scratch[:, at : at + BLOCK, :].reshape(rows * BLOCK, lanes)
        for at in (start, start + BLOCK)
    ]
    both = dot(matrix, beside(*blocks)).astype(BF16)
    parts = [
        part.reshape(BLOCK // group, group, rows, lanes)
        for part in (both[:, :lanes], both[:, lanes:])
    ]
    return jnp.concatenate(parts, axis=0)


def collect_blocks(matrix, values, scratch, start):
    rows, _, lanes = scratch.shape
    flat = values.reshape(2, BLOCK * rows, lanes)
    both = dot(matrix, beside(flat[0], flat[1])).astype(BF16)
    for at, part in ((start, both[:, :lanes]), (start + BLOCK, both[:, lanes:])):
        scratch[:, at : at + BLOCK, :] = part.reshape(rows, BLOCK, lanes)


def spread_edges(scratch, out_ref):
    shards, sides, group, rows, lanes = out_ref.shape
    matrix, step = turn_matrix(rows), 2 * BLOCK // group
    for side in range(sides):
        for shard in range(0, shards, step):
            start = (side * shards + shard) * group
            out_ref[shard : shard + step, side] = spread_blocks(matrix, scratch, start, group)


def collect_edges(in_ref, scratch):
    shards, sides, group, rows, lanes = in_ref.shape
    matrix, step = turn_matrix(rows), 2 * BLOCK // group
    for side in range(sides):
        for shard in range(0, shards, step):
            start = (side * shards + shard) * group
            collect_blocks(matrix, in_ref[shard : shard + step, side], scratch, start)


def spread_triangle(scratch, out_ref):
    shards, group, rows, lanes = out_ref.shape
    matrix, step = turn_matrix(rows), 2 * BLOCK // group
    for shard in range(0, shards, step):
        out_ref[shard : shard + step] = spread_blocks(matrix, scratch, shard * group, group)


def collect_triangle(in_ref, scratch):
    shards, group, rows, lanes = in_ref.shape
    matrix, step = turn_matrix(rows), 2 * BLOCK // group
    for shard in range(0, shards, step):
        collect_blocks(matrix, in_ref[shard : shard + step], scratch, shard * group)


def each_pair(rows, body, sums=None):
    for block in range(0, rows // 2, 2):
        parts = [body(block + step) for step in range(2)]
        for index in range(0 if sums is None else sums.shape[0]):
            total = parts[0][index] + parts[1][index]
            lanes = sums.shape[-1]
            sums[index] += total[:, :lanes] + total[:, lanes:]


def mid_norm(tri):
    scale = 1.0 / tri.shape[0]
    average = jnp.sum(tri, 0, keepdims=True) * scale
    squares = jnp.sum(tri * tri, 0, keepdims=True) * scale
    inverse = lax.rsqrt(squares - average * average + EPS)
    return (tri - average) * inverse, inverse


def norm_backward(weighted, scaled, inverse):
    scale = 1.0 / weighted.shape[0]
    first = jnp.sum(weighted, 0, keepdims=True) * scale
    second = jnp.sum(weighted * scaled, 0, keepdims=True) * scale
    return inverse * (weighted - first - scaled * second)


def save_norm(step, values, scaled_out, inverse_out):
    scaled, inverse = norm_rows(values)
    put_pair(scaled_out, step, scaled)
    put_pair_of_rows(inverse_out, step, inverse)
    return scaled


def save_edges(step, normed, in_weights, mask, proj_out, gate_out):
    pre = dot(in_weights, normed)
    half = pre.shape[0] // 2
    gating = sigmoid(pre[half:])
    factor = gating * mask
    value = pre[:half] * factor
    put_pair(proj_out, step, factor)
    put_pair(gate_out, step, value * (1.0 - gating))
    return value.astype(BF16)


def start_kernel(
    lengths, pair_far, ngain_far, nbias_far, proj_far, gate_far,
    edge_out, normed_out, proj_out, gate_out, scaled_out, inverse_out, mask_out,
    pair, ngain, nbias, proj_w, gate_w, sems, wts, scr,
):
    far = (proj_far.at[0], gate_far.at[0], ngain_far, nbias_far, pair_far)
    near = (proj_w.at[0], gate_w.at[0], ngain, nbias, pair)
    copies = [
        pltpu.make_async_copy(source, target, sems.at[index])
        for index, (source, target) in enumerate(zip(far, near))
    ]
    for copy in copies:
        copy.start()
    for copy in copies:
        copy.wait()
    rows, lanes, channels = pair.shape
    load_in_weights(proj_w, gate_w, 0, wts)
    gain, bias = column(ngain, 0, lanes), column(nbias, 0, lanes)

    def body(step):
        base = turned_pair(pair, step)
        scaled = save_norm(step, base, scaled_out, inverse_out)
        normed = (scaled * gain + bias).astype(BF16)
        put_pair(normed_out, step, normed)
        mask = beside(*[row_mask(lengths, 2 * step + row, rows, lanes) for row in range(2)])
        put_pair_of_rows(mask_out, step, mask)
        put_pair(scr, step, save_edges(step, normed, wts[...], mask, proj_out, gate_out))

    each_pair(rows, body)
    spread_edges(scr, edge_out)


def between_kernel(
    mask_all, tri, pair, normed0, ngain, nbias, mgain, mbias, out_w, outgate_w, proj_w, gate_w,
    edge_out, mid_out, normed_out, proj_out, gate_out, scaled_out, inverse_out,
    outgate_out, scaled_mid_out, inverse_mid_out, wts, tri_in, scr,
):
    rows, lanes, channels = pair.shape
    load_in_weights(proj_w, gate_w, 1, wts)
    out_t, outgate_t = turned(out_w[0]), turned(outgate_w[0])
    gain, bias = column(ngain, 1, lanes), column(nbias, 1, lanes)
    gain_mid, bias_mid = column(mgain, 0, lanes), column(mbias, 0, lanes)
    collect_triangle(tri, tri_in)

    def body(step):
        scaled_mid, inverse_mid = mid_norm(pair_of(tri_in, step).astype(F32))
        put_pair(scaled_mid_out, step, scaled_mid)
        put_pair_of_rows(inverse_mid_out, step, inverse_mid)
        unit = (scaled_mid * gain_mid + bias_mid).astype(BF16)
        outer = dot(out_t, unit)
        outgate = sigmoid(dot(outgate_t, pair_of(normed0, step)))
        put_pair(outgate_out, step, outgate)
        mid = (turned_pair(pair, step) + outer * outgate).astype(BF16)
        put_pair(mid_out, step, mid)
        scaled = save_norm(step, mid.astype(F32), scaled_out, inverse_out)
        normed = (scaled * gain + bias).astype(BF16)
        put_pair(normed_out, step, normed)
        mask = pair_of_rows(mask_all, step)
        put_pair(scr, step, save_edges(step, normed, wts[...], mask, proj_out, gate_out))

    each_pair(rows, body)
    spread_edges(scr, edge_out)


def out_weight_grads(unit, d_outer, normed, d_gatepre, out_ref):
    width = unit.shape[0]
    out_ref[0:width, :] = dot_rt(unit[...], d_outer[...]).astype(out_ref.dtype)
    out_ref[width:, :] = dot_rt(normed[...], d_gatepre[...]).astype(out_ref.dtype)


def in_weight_grads(normed_all, d_in_all, out_ref):
    width = normed_all.shape[0]
    for part in range(d_in_all.shape[0] // width):
        block = slice(part * width, (part + 1) * width)
        out_ref[block, :] = dot_rt(normed_all[...], d_in_all[block, :]).astype(out_ref.dtype)


def lane_block(step, lanes):
    return pl.ds(2 * step * lanes, 2 * lanes)


def turn_kernel(
    tri, mid, normed, cot, mgain, mbias, out_w, outgate_w,
    d_tri_out, new_out, grad_out, d_normed_out, weights_out, small_out,
    tri_in, scr, unit_all, outer_all, normed_all, gate_all, sums,
):
    rows, channels, lanes = mid.shape
    out_t, outgate_t = turned(out_w[1]), turned(outgate_w[1])
    gain_mid, bias_mid = column(mgain, 1, lanes), column(mbias, 1, lanes)
    collect_triangle(tri, tri_in)
    sums[...] = jnp.zeros_like(sums)

    def body(step):
        here = lane_block(step, lanes)
        grad = turned_pair(cot, step)
        put_pair(grad_out, step, grad)
        here_normed = pair_of(normed, step)
        outgate = sigmoid(dot(outgate_t, here_normed))
        gated = grad * outgate
        d_outer = gated.astype(BF16)
        d_unit = dot(out_w[1], d_outer)
        scaled_mid, inverse_mid = mid_norm(pair_of(tri_in, step).astype(F32))
        d_tri = norm_backward(d_unit * gain_mid, scaled_mid, inverse_mid)
        put_pair(scr, step, d_tri.astype(BF16))
        unit = (scaled_mid * gain_mid + bias_mid).astype(BF16)
        outer = dot(out_t, unit)
        put_pair(new_out, step, (pair_of(mid, step).astype(F32) + outer * outgate).astype(BF16))
        d_gatepre = (gated * outer * (1.0 - outgate)).astype(BF16)
        put_pair(d_normed_out, step, dot(outgate_w[1], d_gatepre))
        unit_all[:, here] = unit
        outer_all[:, here] = d_outer
        normed_all[:, here] = here_normed
        gate_all[:, here] = d_gatepre
        return d_unit * scaled_mid, d_unit

    each_pair(rows, body, sums)
    spread_triangle(scr, d_tri_out)
    out_weight_grads(unit_all, outer_all, normed_all, gate_all, weights_out)
    for index in range(2):
        small_out[index : index + 1, :] = as_row(sums[index])


def edge_backward(step, scratch, proj_factor, gate_factor):
    here = pair_of(scratch, step).astype(F32)
    d_proj = (here * pair_of(proj_factor, step)).astype(BF16)
    d_gate = (here * pair_of(gate_factor, step)).astype(BF16)
    return jnp.concatenate([d_proj, d_gate], axis=0)


def middle_kernel(
    d_edge, proj_factor, gate_factor, d_normed_gate, scaled_in, inverse_in, cot, outgate,
    scaled_mid, inverse_mid, normed0, normed1, ngain, mgain, mbias, proj_w, gate_w, out_w,
    outgate_w,
    d_tri_out, grad_out, d_normed_out, out_weights, in_weights, small_out,
    scr, scr_tri, unit_all, outer_all, normed_all, gate_all, upper_all, d_in_all, back, sums,
):
    rows, channels, lanes = cot.shape
    out_t = turned(out_w[0])
    gain = column(ngain, 1, lanes)
    gain_mid, bias_mid = column(mgain, 0, lanes), column(mbias, 0, lanes)
    collect_edges(d_edge, scr)
    sums[...] = jnp.zeros_like(sums)
    load_back_weights(proj_w, gate_w, 1, back)

    def upper(step):
        place = lane_block(step, lanes)
        d_in = edge_backward(step, scr, proj_factor, gate_factor)
        d_in_all[:, place] = d_in
        upper_all[:, place] = pair_of(normed1, step)
        d_normed = pair_of(d_normed_gate, step) + dot(back[...], d_in)
        scaled = pair_of(scaled_in, step)
        grad = pair_of(cot, step) + norm_backward(
            d_normed * gain, scaled, pair_of_rows(inverse_in, step)
        )
        put_pair(grad_out, step, grad)
        return d_normed * scaled, d_normed

    def lower(step):
        place = lane_block(step, lanes)
        gate = pair_of(outgate, step)
        gated = pair_of(grad_out, step) * gate
        d_outer = gated.astype(BF16)
        d_unit = dot(out_w[0], d_outer)
        scaled = pair_of(scaled_mid, step)
        d_tri = norm_backward(d_unit * gain_mid, scaled, pair_of_rows(inverse_mid, step))
        put_pair(scr_tri, step, d_tri.astype(BF16))
        unit = (scaled * gain_mid + bias_mid).astype(BF16)
        outer = dot(out_t, unit)
        d_gatepre = (gated * outer * (1.0 - gate)).astype(BF16)
        put_pair(d_normed_out, step, dot(outgate_w[0], d_gatepre))
        unit_all[:, place] = unit
        outer_all[:, place] = d_outer
        normed_all[:, place] = pair_of(normed0, step)
        gate_all[:, place] = d_gatepre
        return d_unit * scaled, d_unit

    each_pair(rows, upper, sums.at[2:4])
    each_pair(rows, lower, sums.at[0:2])
    spread_triangle(scr_tri, d_tri_out)
    out_weight_grads(unit_all, outer_all, normed_all, gate_all, out_weights)
    in_weight_grads(upper_all, d_in_all, in_weights)
    for index in range(4):
        small_out[index : index + 1, :] = as_row(sums[index])


def split_cores(all_rows, own_out, other_out, few):
    chips, share, width = own_out.shape
    view = all_rows.reshape(chips // few, 2, few, share, width)
    core = lax.rem(lax.axis_index("row"), 2)
    own_out[...] = view[:, core].reshape(own_out.shape)
    other_out[...] = view[:, 1 - core].reshape(other_out.shape)


def finish_kernel(
    few, d_edge, proj_factor, gate_factor, normed, out0, in1, out1,
    own_out, other_out, d_in_all, scr, normed_all, packed,
):
    rows, half, lanes = proj_factor.shape
    collect_edges(d_edge, scr)

    def body(step):
        place = lane_block(step, lanes)
        d_in_all[:, place] = edge_backward(step, scr, proj_factor, gate_factor)
        normed_all[:, place] = pair_of(normed, step)

    each_pair(rows, body)
    first, second, third = d_in_all.shape[0], out0.shape[0], in1.shape[0]
    in_weight_grads(normed_all, d_in_all, packed.at[0:first])
    packed[first : first + second, :] = out0[...]
    packed[first + second : first + second + third, :] = in1[...]
    packed[first + second + third :, :] = out1[...]
    split_cores(packed, own_out, other_out, few)


def norm_sums_kernel(
    d_in, d_normed_gate, scaled_in, proj_w, gate_w, small_middle, small1, new_t,
    d_normed_out, extra_out, new_out, back, sums,
):
    rows, channels, lanes = scaled_in.shape
    sums[...] = jnp.zeros_like(sums)
    load_back_weights(proj_w, gate_w, 0, back)

    def body(step):
        here = d_in[:, lane_block(step, lanes)]
        d_normed = pair_of(d_normed_gate, step) + dot(back[...], here)
        put_pair(d_normed_out, step, d_normed)
        put_turned_pair(new_out, step, pair_of(new_t, step))
        return d_normed * pair_of(scaled_in, step), d_normed

    each_pair(rows, body, sums)
    small = jnp.concatenate(
        [as_row(sums[0]), as_row(sums[1]), small_middle[0:2], small_middle[2:4], small1[...]],
        axis=0,
    )
    high = small.astype(BF16).astype(F32)
    extra_out[...] = jnp.concatenate([high, small - high], axis=0).astype(BF16)


def add_kernel(first, second, extra, out_ref, extra_out):
    out_ref[...] = (first[...].astype(F32) + second[...].astype(F32)).astype(BF16)
    extra_out[...] = extra[...]


def sum_kernel(parts, extra, shared_out):
    chips, share, width = parts.shape
    own = jnp.sum(parts[...].astype(F32), axis=0).astype(BF16)
    for chip in range(chips):
        shared_out[chip, 0:share] = own
        shared_out[chip, share:] = extra[...]


def grad_pair_kernel(
    share, shared, d_normed, scaled_in, inverse_in, grad, ngain, grad_out, mine_out
):
    rows, channels, lanes = grad.shape
    gain = column(ngain, 0, lanes)
    mine_out[...] = jnp.sum(shared[:, share:].astype(F32), axis=0)

    def body(step):
        total = pair_of(grad, step) + norm_backward(
            pair_of(d_normed, step) * gain, pair_of(scaled_in, step),
            pair_of_rows(inverse_in, step),
        )
        put_turned_pair(grad_out, step, total)

    each_pair(rows, body)


def unpack_kernel(
    share, few, own, other, mine, proj_out, gate_out, out_out, outgate_out,
    norm_gain_out, norm_bias_out, mid_gain_out, mid_bias_out, weights,
):
    chips, _, width = own.shape
    core = lax.rem(lax.axis_index("row"), 2)
    view = weights.reshape(chips // few, 2, few, share, width)
    block = (chips // few, few, share, width)
    view[:, core] = own[:, 0:share].astype(F32).reshape(block)
    view[:, 1 - core] = other[:, 0:share].astype(F32).reshape(block)
    total = mine[...] + jnp.sum(other[:, share:].astype(F32), axis=0)
    total = total[0:8] + total[8:16]
    for module in range(2):
        for index, out in enumerate((norm_gain_out, norm_bias_out, mid_gain_out, mid_bias_out)):
            at = 4 * module + index
            out[module : module + 1, :] = total[at : at + 1]
        blocks = [
            weights[(6 * module + part) * width : (6 * module + part + 1) * width, :]
            for part in range(6)
        ]
        for side in range(2):
            proj_out[module, side] = blocks[side]
            gate_out[module, side] = blocks[2 + side]
        out_out[module] = blocks[4]
        outgate_out[module] = blocks[5]


def triangle_kernel(incoming, edge, tri_out):
    many, few, _, group, rows, lanes = edge.shape

    def whole(side, channel):
        parts = [edge[:, c, side, channel].reshape(many * rows, lanes) for c in range(few)]
        return jnp.concatenate(parts, axis=1)

    for channel in range(group):
        left, right = whole(0, channel), whole(1, channel)
        tri = (dot_lt if incoming else dot_rt)(left, right).astype(BF16)
        for c in range(few):
            part = tri[:, c * lanes : (c + 1) * lanes]
            tri_out[:, c, channel] = part.reshape(many, rows, lanes)


def edge_grad_kernel(incoming, edge, d_tri, grad_out):
    many, few, _, group, rows, lanes = edge.shape

    def whole(ref, *index):
        parts = [ref[(slice(None), c) + index].reshape(many * rows, lanes) for c in range(few)]
        return jnp.concatenate(parts, axis=1)

    for channel in range(group):
        left, right = whole(edge, 0, channel), whole(edge, 1, channel)
        grad = whole(d_tri, channel)
        if incoming:
            d_left, d_right = dot_rt(right, grad), dot(left, grad)
        else:
            d_left, d_right = dot(grad, right), dot_lt(grad, left)
        for side, value in ((0, d_left), (1, d_right)):
            value = value.astype(BF16)
            for c in range(few):
                part = value[:, c * lanes : (c + 1) * lanes]
                grad_out[:, c, side, channel] = part.reshape(many, rows, lanes)


SCALARS = pl.BlockSpec(memory_space=pltpu.SMEM)
VECTORS = pl.BlockSpec(memory_space=pltpu.VMEM)
FAR = pl.BlockSpec(memory_space=pltpu.HBM)


def call(kernel, name, outs, args, scratch=(), flops=0, grant=16, specs=None):
    shapes = [jax.ShapeDtypeStruct(shape, dtype) for shape, dtype in outs]
    moved = sum(a.size * a.dtype.itemsize for a in list(args) + shapes)
    return pl.pallas_call(
        kernel,
        name=name,
        out_shape=shapes,
        in_specs=specs or [VECTORS] * len(args),
        out_specs=[VECTORS] * len(shapes),
        scratch_shapes=[
            pltpu.VMEM(*item) if isinstance(item, tuple) else item for item in scratch
        ],
        compiler_params=pltpu.CompilerParams(vmem_limit_bytes=grant * 1024 * 1024),
        cost_estimate=pl.CostEstimate(flops=flops, bytes_accessed=moved, transcendentals=0),
    )(*args)


def exchange(values):
    return lax.all_to_all(values, ("row", "col"), split_axis=0, concat_axis=0, tiled=True)


def swap_cores(values, many, few):
    pairs = [(index, index ^ few) for index in range(many * few)]
    return lax.ppermute(values, ("row", "col"), pairs)


def exchange_chips(values, many, few):
    groups = [
        [row * few + col for row in range(core, many, 2) for col in range(few)] for core in range(2)
    ]
    return lax.all_to_all(
        values, ("row", "col"), split_axis=0, concat_axis=0, axis_index_groups=groups, tiled=True
    )


def grouped_device(
    pair, cotangent, lengths, ngain, nbias, proj_w, gate_w, mgain, mbias, out_w, outgate_w,
    *, many, few,
):
    rows, lanes, channels = pair.shape
    shards = many * few
    group = H // shards
    edge = ((shards, 2, group, rows, lanes), BF16)
    grid = ((many, few, 2, group, rows, lanes), BF16)
    tri = ((shards, group, rows, lanes), BF16)
    tri_grid = ((many, few, group, rows, lanes), BF16)
    tile = ((rows, channels, lanes), BF16)
    wide = ((rows, channels, lanes), F32)
    row = ((rows, lanes), F32)
    factor = ((rows, 2 * H, lanes), F32)
    back = ((channels, 4 * H), BF16)
    wts = ((4 * H, channels), BF16)
    big = ((rows, 2 * H, lanes), BF16)
    mid = ((rows, H, lanes), BF16)
    positions = rows * lanes
    flat = ((H, positions), BF16)
    flat_in = ((4 * H, positions), BF16)
    out_rows = ((2 * H, channels), BF16)
    in_rows = ((4 * H, H), BF16)
    triangle = 2 * group * (many * rows) ** 2 * (few * lanes)
    dense = 2 * positions * channels * H

    def sums(count):
        return ((count, H, lanes), F32)

    def small(count):
        return ((count, H), F32)

    saved = [tile, factor, factor, wide, row]
    far = [
        pltpu.with_memory_space_constraint(item, pltpu.HBM)
        for item in (pair, ngain, nbias, proj_w, gate_w)
    ]
    sent, normed0, *factors0, mask = call(
        start_kernel, "start", [edge, *saved, row], [lengths, *far],
        [(pair.shape, BF16), (ngain.shape, F32), (nbias.shape, F32), (proj_w.shape, BF16),
         (gate_w.shape, BF16), pltpu.SemaphoreType.DMA((5,)), wts, big],
        4 * dense, specs=[SCALARS] + [FAR] * len(far),
    )
    edge0 = exchange(sent).reshape(grid[0])
    (here,) = call(
        functools.partial(triangle_kernel, False), "outgoing", [tri_grid], [edge0], (), triangle,
    )
    tri0 = exchange(here.reshape(tri[0]))
    sent, mid_t, normed1, *factors1, outgate0, scaled_mid0, inverse_mid0 = call(
        between_kernel, "between", [edge, tile, *saved, wide, wide, row],
        [mask, tri0, pair, normed0, ngain, nbias, mgain, mbias, out_w, outgate_w, proj_w,
         gate_w],
        [wts, mid, big], 6 * dense,
    )
    edge1 = exchange(sent).reshape(grid[0])
    (here,) = call(
        functools.partial(triangle_kernel, True), "incoming", [tri_grid], [edge1], (), triangle,
    )
    tri1 = exchange(here.reshape(tri[0]))
    sent, new_t, cot_t, d_normed_gate1, out_grads1, small1 = call(
        turn_kernel, "turn", [tri, tile, wide, wide, out_rows, small(2)],
        [tri1, mid_t, normed1, cotangent, mgain, mbias, out_w, outgate_w],
        [mid, mid, flat, flat, flat, flat, sums(2)], 6 * dense,
    )
    d_tri1 = exchange(sent).reshape(tri_grid[0])
    (sent,) = call(
        functools.partial(edge_grad_kernel, True), "incoming_grad", [grid], [edge1, d_tri1],
        (), 2 * triangle,
    )
    d_edge1 = exchange(sent.reshape(edge[0]))
    proj_factor1, gate_factor1, scaled1, inverse1 = factors1
    sent, grad, d_normed_gate0, out_grads0, in_grads1, small_middle = call(
        middle_kernel, "middle", [tri, wide, wide, out_rows, in_rows, small(4)],
        [d_edge1, proj_factor1, gate_factor1, d_normed_gate1, scaled1, inverse1, cot_t, outgate0,
         scaled_mid0, inverse_mid0, normed0, normed1, ngain, mgain, mbias, proj_w, gate_w, out_w,
         outgate_w],
        [big, mid, flat, flat, flat, flat, flat, flat_in, back, sums(4)], 13 * dense,
    )
    d_tri0 = exchange(sent).reshape(tri_grid[0])
    (sent,) = call(
        functools.partial(edge_grad_kernel, False), "outgoing_grad", [grid], [edge0, d_tri0],
        (), 2 * triangle,
    )
    d_edge0 = exchange(sent.reshape(edge[0]))
    share = 12 * H // shards
    chips = shards // 2
    proj_factor0, gate_factor0, scaled0, inverse0 = factors0
    held = ((chips, share, H), BF16)
    own, other, d_in0 = call(
        functools.partial(finish_kernel, few), "finish", [held, held, flat_in],
        [d_edge0, proj_factor0, gate_factor0, normed0, out_grads0, in_grads1, out_grads1],
        [big, flat, ((12 * H, H), BF16)], 4 * dense,
    )
    other = swap_cores(other, many, few)
    d_normed0, extra, new_pair = call(
        norm_sums_kernel, "norm_sums", [wide, ((16, H), BF16), (pair.shape, BF16)],
        [d_in0, d_normed_gate0, scaled0, proj_w, gate_w, small_middle, small1, new_t],
        [back, sums(2)],
        4 * dense,
    )
    own, extra = call(add_kernel, "add_cores", [held, ((16, H), BF16)], [own, other, extra])
    parts = exchange_chips(own, many, few)
    (shared,) = call(
        sum_kernel, "sum_weights", [((chips, share + 16, H), BF16)], [parts, extra]
    )
    shared = exchange_chips(shared, many, few)
    other = swap_cores(shared, many, few)
    grad_pair, mine = call(
        functools.partial(grad_pair_kernel, share), "grad_pair",
        [(pair.shape, BF16), ((16, H), F32)],
        [shared, d_normed0, scaled0, inverse0, grad, ngain],
    )
    grad_proj, grad_gate, grad_out, grad_outgate, *vectors = call(
        functools.partial(unpack_kernel, share, few), "unpack",
        [(proj_w.shape, F32), (gate_w.shape, F32), (out_w.shape, F32), (outgate_w.shape, F32),
         (ngain.shape, F32), (nbias.shape, F32), (mgain.shape, F32), (mbias.shape, F32)],
        [shared, other, mine], [((12 * H, H), F32)],
    )
    return (
        new_pair,
        grad_pair,
        vectors[0],
        vectors[1],
        grad_proj,
        grad_gate,
        vectors[2],
        vectors[3],
        grad_out,
        grad_outgate,
    )


def norm_channels(values):
    average = jnp.mean(values, -1, keepdims=True)
    centred = values - average
    variance = jnp.mean(centred * centred, -1, keepdims=True)
    inverse = lax.rsqrt(variance + EPS)
    return (centred * inverse, inverse)


def forward_module(pair_in, pair_mask, weights, incoming):
    gain_in, bias_in, proj_w, gate_w, gain_mid, bias_mid, out_w, outgate_w = weights
    scaled_in, inverse_in = norm_channels(pair_in.astype(jnp.float32))
    normed = (scaled_in * gain_in + bias_in).astype(jnp.bfloat16)
    projected = product("ijc,sch->shij", normed, proj_w)
    gating = jax.nn.sigmoid(product("ijc,sch->shij", normed, gate_w))
    hidden = (projected * gating * pair_mask).astype(jnp.bfloat16)
    left_side, right_side = (
        lax.all_to_all(hidden[0], "row", split_axis=0, concat_axis=1, tiled=True),
        lax.all_to_all(hidden[1], "row", split_axis=0, concat_axis=1, tiled=True),
    )
    if incoming:
        left_side = jnp.swapaxes(left_side, 1, 2)
        right_side = jnp.swapaxes(right_side, 1, 2)
    else:
        left_side, right_side = (
            lax.all_to_all(left_side, "col", split_axis=1, concat_axis=2, tiled=True),
            lax.all_to_all(right_side, "col", split_axis=1, concat_axis=2, tiled=True),
        )
    triangle = product(
        "cik,cjk->cij", left_side, lax.all_gather(right_side, "col", axis=1, tiled=True)
    ).astype(jnp.bfloat16)
    triangle = lax.all_to_all(
        lax.all_to_all(triangle, "col", split_axis=2, concat_axis=1, tiled=True),
        "row",
        split_axis=1,
        concat_axis=0,
        tiled=True,
    )
    tri_values = triangle.astype(jnp.float32)
    total, squares = lax.psum((jnp.sum(tri_values, 0), jnp.sum(tri_values * tri_values, 0)), "ch")
    average = total / H
    inverse_mid = lax.rsqrt(squares / H - average * average + EPS)
    scaled_mid = (tri_values - average) * inverse_mid
    unit = (scaled_mid * gain_mid[:, None, None] + bias_mid[:, None, None]).astype(jnp.bfloat16)
    unit_full = lax.all_gather(unit, "ch", axis=0, tiled=True)
    outer = product("hij,hc->ijc", unit_full, out_w)
    outgate = jax.nn.sigmoid(product("ijc,cd->ijd", normed, outgate_w))
    result = (pair_in.astype(jnp.float32) + outer * outgate).astype(jnp.bfloat16)
    saved = (
        scaled_in,
        inverse_in,
        normed,
        projected,
        gating,
        left_side,
        right_side,
        scaled_mid,
        inverse_mid,
        unit_full,
        outer,
        outgate,
    )
    return (result, saved)


def backward_module(grad_out, pair_mask, weights, saved, incoming):
    gain_in, bias_in, proj_w, gate_w, gain_mid, bias_mid, out_w, outgate_w = weights
    (
        scaled_in,
        inverse_in,
        normed,
        projected,
        gating,
        left_side,
        right_side,
        scaled_mid,
        inverse_mid,
        unit_full,
        outer,
        outgate,
    ) = saved
    d_outer = (grad_out * outgate).astype(jnp.bfloat16)
    d_gatepre = (grad_out * outer * outgate * (1.0 - outgate)).astype(jnp.bfloat16)
    grad_out_w = product("hij,ijc->hc", unit_full, d_outer)
    grad_outgate_w = product("ijc,ijd->cd", normed, d_gatepre)
    width = gain_mid.shape[0]
    own_rows = lax.dynamic_slice_in_dim(out_w, lax.axis_index("ch") * width, width, 0)
    d_unit = product("ijc,hc->hij", d_outer, own_rows)
    d_normed = product("ijd,cd->ijc", d_gatepre, outgate_w)
    weighted = d_unit * gain_mid[:, None, None]
    grad_gain_mid = jnp.sum(d_unit * scaled_mid, (1, 2))
    grad_bias_mid = jnp.sum(d_unit, (1, 2))
    first_sum, second_sum = lax.psum(
        (jnp.sum(weighted, 0), jnp.sum(weighted * scaled_mid, 0)), "ch"
    )
    d_tri = (inverse_mid * (weighted - first_sum / H - scaled_mid * (second_sum / H))).astype(
        jnp.bfloat16
    )
    grad_rows = lax.all_to_all(d_tri, "row", split_axis=0, concat_axis=1, tiled=True)
    grad_cols = lax.all_to_all(grad_rows, "col", split_axis=1, concat_axis=2, tiled=True)
    d_left = product(
        "cij,cjk->cik", grad_cols, lax.all_gather(right_side, "col", axis=1, tiled=True)
    )
    partial_terms = product("cij,cik->cjk", grad_cols, left_side)
    d_right = lax.psum_scatter(
        partial_terms.astype(jnp.bfloat16), "col", scatter_dimension=1, tiled=True
    ).astype(jnp.float32)
    d_left = d_left.astype(jnp.bfloat16)
    d_right = d_right.astype(jnp.bfloat16)
    if incoming:
        d_left = jnp.swapaxes(d_left, 1, 2)
        d_right = jnp.swapaxes(d_right, 1, 2)
    else:
        d_left, d_right = (
            lax.all_to_all(d_left, "col", split_axis=2, concat_axis=1, tiled=True),
            lax.all_to_all(d_right, "col", split_axis=2, concat_axis=1, tiled=True),
        )
    d_left, d_right = (
        lax.all_to_all(d_left, "row", split_axis=1, concat_axis=0, tiled=True),
        lax.all_to_all(d_right, "row", split_axis=1, concat_axis=0, tiled=True),
    )
    d_hidden = jnp.stack([d_left, d_right]).astype(jnp.float32)
    d_proj = (d_hidden * gating * pair_mask).astype(jnp.bfloat16)
    d_gate = (d_hidden * projected * gating * (1.0 - gating) * pair_mask).astype(jnp.bfloat16)
    grad_proj_w = product("ijc,shij->sch", normed, d_proj)
    grad_gate_w = product("ijc,shij->sch", normed, d_gate)
    partial_input = product("shij,sch->ijc", d_proj, proj_w) + product(
        "shij,sch->ijc", d_gate, gate_w
    )
    d_normed = d_normed + lax.psum(partial_input.astype(jnp.bfloat16), "ch").astype(jnp.float32)
    weighted_in = d_normed * gain_in
    grad_gain_in = jnp.sum(d_normed * scaled_in, (0, 1))
    grad_bias_in = jnp.sum(d_normed, (0, 1))
    d_pair = inverse_in * (
        weighted_in
        - jnp.mean(weighted_in, -1, keepdims=True)
        - scaled_in * jnp.mean(weighted_in * scaled_in, -1, keepdims=True)
    )
    grads = (
        grad_gain_in,
        grad_bias_in,
        grad_proj_w,
        grad_gate_w,
        grad_gain_mid,
        grad_bias_mid,
        grad_out_w,
        grad_outgate_w,
    )
    return (grad_out + d_pair, grads)


def per_device(
    pair,
    cotangent,
    lengths,
    norm_gain,
    norm_bias,
    proj_weight,
    gate_weight,
    mid_gain,
    mid_bias,
    out_weight,
    outgate_weight,
):
    rows_here = pair.shape[0]
    cols_here = pair.shape[1]
    row_ids = lax.axis_index("row") * rows_here + lax.iota(jnp.int32, rows_here)
    col_ids = lax.axis_index("col") * cols_here + lax.iota(jnp.int32, cols_here)
    limit = lengths[0]
    pair_mask = ((row_ids[:, None] < limit) & (col_ids[None, :] < limit)).astype(jnp.float32)
    state = pair
    stash = []
    for layer in range(2):
        weights = (
            norm_gain[layer],
            norm_bias[layer],
            proj_weight[layer],
            gate_weight[layer],
            mid_gain[layer],
            mid_bias[layer],
            out_weight[layer],
            outgate_weight[layer],
        )
        state, saved = forward_module(state, pair_mask, weights, layer == 1)
        stash.append(saved)
    grad_state = cotangent.astype(jnp.float32)
    per_layer = [None, None]
    for layer in (1, 0):
        weights = (
            norm_gain[layer],
            norm_bias[layer],
            proj_weight[layer],
            gate_weight[layer],
            mid_gain[layer],
            mid_bias[layer],
            out_weight[layer],
            outgate_weight[layer],
        )
        grad_state, grads = backward_module(
            grad_state, pair_mask, weights, stash[layer], layer == 1
        )
        per_layer[layer] = grads
    lower = per_layer[0]
    upper = per_layer[1]
    summed = lax.psum(
        (
            lower[0],
            lower[1],
            lower[2],
            lower[3],
            lower[4],
            lower[5],
            lower[6],
            lower[7],
            upper[0],
            upper[1],
            upper[2],
            upper[3],
            upper[4],
            upper[5],
            upper[6],
            upper[7],
        ),
        ("row", "col"),
    )
    per_layer = [summed[0:8], summed[8:16]]
    stacked = [jnp.stack([per_layer[0][index], per_layer[1][index]]) for index in range(8)]
    return (
        state,
        grad_state.astype(jnp.bfloat16),
        stacked[0],
        stacked[1],
        stacked[2],
        stacked[3],
        stacked[4],
        stacked[5],
        stacked[6],
        stacked[7],
    )


def on_device(pair, *rest, many, few, split):
    rows, lanes, channels = pair.shape
    shards = many * few
    whole_channels = split == 1 and H % shards == 0 and BLOCK % (H // shards) == 0 and H % (2 * BLOCK) == 0
    tiles = rows == BLOCK and lanes % 128 == 0 and channels == H
    if whole_channels and tiles and many % 2 == 0 and few & (few - 1) == 0:
        return grouped_device(pair, *rest, many=many, few=few)
    return per_device(pair, *rest)


def solution(mesh):
    in_specs = (
        P(("grp", "row"), "col", None),
        P(("grp", "row"), "col", None),
        P("grp"),
        P(),
        P(),
        P(None, None, None, "ch"),
        P(None, None, None, "ch"),
        P(None, "ch"),
        P(None, "ch"),
        P(),
        P(),
    )
    out_specs = (
        P(("grp", "row"), "col", None),
        P(("grp", "row"), "col", None),
        P("grp", None),
        P("grp", None),
        P("grp", None, None, "ch"),
        P("grp", None, None, "ch"),
        P("grp", "ch"),
        P("grp", "ch"),
        P("grp", None, None),
        P("grp", None, None),
    )
    body = functools.partial(
        on_device, many=mesh.shape["row"], few=mesh.shape["col"], split=mesh.shape["ch"]
    )
    return jax.shard_map(
        body, mesh=mesh, in_specs=in_specs, out_specs=out_specs, check_vma=False
    )
```

```python
import functools

import jax
import jax.numpy as jnp
from jax import lax
from jax.experimental import pallas as pl
from jax.experimental.pallas import tpu as pltpu
from jax.sharding import PartitionSpec as P

H = 128


EPS = 1e-05


def product(spec, left, right):
    return jnp.einsum(spec, left, right, preferred_element_type=jnp.float32)


F32 = jnp.float32
BF16 = jnp.bfloat16


def dot(left, right):
    return lax.dot_general(left, right, (((1,), (0,)), ((), ())), preferred_element_type=F32)


def dot_rt(left, right):
    return lax.dot_general(left, right, (((1,), (1,)), ((), ())), preferred_element_type=F32)


def dot_lt(left, right):
    return lax.dot_general(left, right, (((0,), (0,)), ((), ())), preferred_element_type=F32)


def sigmoid_of_minus(values):
    return 1.0 / (1.0 + jnp.exp(values))


def norm_rows(values):
    scale = 1.0 / values.shape[0]
    average = jnp.sum(values, 0, keepdims=True) * scale
    centred = values - average
    variance = jnp.sum(centred * centred, 0, keepdims=True) * scale
    inverse = lax.rsqrt(variance + EPS)
    return centred * inverse, inverse


def turned(weight):
    return jnp.transpose(weight)


def column(ref, module, lanes):
    row = ref[module : module + 1, :]
    return beside(*[jnp.transpose(jnp.broadcast_to(row, (lanes, row.shape[1])))] * 2)


def beside(left, right):
    return jnp.concatenate([left, right], axis=-1)


def pair_of(ref, step):
    return beside(ref[2 * step], ref[2 * step + 1])


def put_pair(ref, step, values):
    lanes = ref.shape[-1]
    ref[2 * step] = values[:, :lanes]
    ref[2 * step + 1] = values[:, lanes:]


def pair_of_rows(ref, step):
    return beside(ref[2 * step : 2 * step + 1, :], ref[2 * step + 1 : 2 * step + 2, :])


def put_pair_of_rows(ref, step, values):
    lanes = ref.shape[-1]
    ref[2 * step : 2 * step + 1, :] = values[:, :lanes]
    ref[2 * step + 1 : 2 * step + 2, :] = values[:, lanes:]


def turned_pair(ref, step):
    return beside(jnp.transpose(ref[2 * step]), jnp.transpose(ref[2 * step + 1])).astype(F32)


def put_turned_pair(ref, step, values):
    lanes = ref.shape[1]
    values = values.astype(BF16)
    ref[2 * step] = jnp.transpose(values[:, :lanes])
    ref[2 * step + 1] = jnp.transpose(values[:, lanes:])


def as_row(total):
    return jnp.sum(jnp.transpose(total), 0, keepdims=True)


def row_mask(lengths_ref, step, rows, lanes):
    limit = lengths_ref[0]
    row_id = lax.axis_index("row") * rows + step
    col_id = lax.axis_index("col") * lanes + lax.broadcasted_iota(jnp.int32, (1, lanes), 1)
    return jnp.where((row_id < limit) & (col_id < limit), 1.0, 0.0).astype(F32)


def load_in_weights(proj_ref, gate_ref, module, scratch):
    width = proj_ref.shape[-1]
    for side in range(2):
        scratch[side * width : (side + 1) * width, :] = turned(proj_ref[module, side])
        scratch[(2 + side) * width : (3 + side) * width, :] = -turned(gate_ref[module, side])


def load_back_weights(proj_ref, gate_ref, module, scratch):
    width = proj_ref.shape[-1]
    for side in range(2):
        scratch[:, side * width : (side + 1) * width] = proj_ref[module, side]
        scratch[:, (2 + side) * width : (3 + side) * width] = gate_ref[module, side]


BLOCK = 16


def turn_matrix(rows):
    size = BLOCK * rows
    out = lax.broadcasted_iota(jnp.int32, (size, size), 0)
    source = lax.broadcasted_iota(jnp.int32, (size, size), 1)
    return jnp.where(source == (out % rows) * BLOCK + out // rows, 1.0, 0.0).astype(BF16)


def spread_blocks(matrix, scratch, start, group):
    rows, _, lanes = scratch.shape
    blocks = [
        scratch[:, at : at + BLOCK, :].reshape(rows * BLOCK, lanes)
        for at in (start, start + BLOCK)
    ]
    both = dot(matrix, beside(*blocks)).astype(BF16)
    parts = [
        part.reshape(BLOCK // group, group, rows, lanes)
        for part in (both[:, :lanes], both[:, lanes:])
    ]
    return jnp.concatenate(parts, axis=0)


def collect_blocks(matrix, values, scratch, start):
    rows, _, lanes = scratch.shape
    flat = values.reshape(2, BLOCK * rows, lanes)
    both = dot(matrix, beside(flat[0], flat[1])).astype(BF16)
    for at, part in ((start, both[:, :lanes]), (start + BLOCK, both[:, lanes:])):
        scratch[:, at : at + BLOCK, :] = part.reshape(rows, BLOCK, lanes)


def spread_edges(scratch, out_ref):
    shards, sides, group, rows, lanes = out_ref.shape
    matrix, step = turn_matrix(rows), 2 * BLOCK // group
    for side in range(sides):
        for shard in range(0, shards, step):
            start = (side * shards + shard) * group
            out_ref[shard : shard + step, side] = spread_blocks(matrix, scratch, start, group)


def collect_edges(in_ref, scratch):
    shards, sides, group, rows, lanes = in_ref.shape
    matrix, step = turn_matrix(rows), 2 * BLOCK // group
    for side in range(sides):
        for shard in range(0, shards, step):
            start = (side * shards + shard) * group
            collect_blocks(matrix, in_ref[shard : shard + step, side], scratch, start)


def spread_triangle(scratch, out_ref):
    shards, group, rows, lanes = out_ref.shape
    matrix, step = turn_matrix(rows), 2 * BLOCK // group
    for shard in range(0, shards, step):
        out_ref[shard : shard + step] = spread_blocks(matrix, scratch, shard * group, group)


def collect_triangle(in_ref, scratch):
    shards, group, rows, lanes = in_ref.shape
    matrix, step = turn_matrix(rows), 2 * BLOCK // group
    for shard in range(0, shards, step):
        collect_blocks(matrix, in_ref[shard : shard + step], scratch, shard * group)


def each_pair(rows, body, sums=None):
    for block in range(0, rows // 2, 2):
        parts = [body(block + step) for step in range(2)]
        for index in range(0 if sums is None else sums.shape[0]):
            total = parts[0][index] + parts[1][index]
            lanes = sums.shape[-1]
            sums[index] += total[:, :lanes] + total[:, lanes:]


def mid_norm(tri):
    scale = 1.0 / tri.shape[0]
    average = jnp.sum(tri, 0, keepdims=True) * scale
    squares = jnp.sum(tri * tri, 0, keepdims=True) * scale
    inverse = lax.rsqrt(squares - average * average + EPS)
    return (tri - average) * inverse, inverse


def norm_backward(weighted, scaled, inverse):
    scale = 1.0 / weighted.shape[0]
    first = jnp.sum(weighted, 0, keepdims=True) * scale
    second = jnp.sum(weighted * scaled, 0, keepdims=True) * scale
    return inverse * (weighted - first - scaled * second)


def save_norm(step, values, scaled_out, inverse_out):
    scaled, inverse = norm_rows(values)
    put_pair(scaled_out, step, scaled)
    put_pair_of_rows(inverse_out, step, inverse)
    return scaled


def save_edges(step, normed, in_weights, mask, proj_out, gate_out):
    pre = dot(in_weights, normed)
    half = pre.shape[0] // 2
    gating = sigmoid_of_minus(pre[half:])
    factor = gating * mask
    value = pre[:half] * factor
    put_pair(proj_out, step, factor)
    put_pair(gate_out, step, value * (1.0 - gating))
    return value.astype(BF16)


def start_kernel(
    lengths, pair_far, ngain_far, nbias_far, proj_far, gate_far,
    edge_out, normed_out, proj_out, gate_out, scaled_out, inverse_out, mask_out,
    pair, ngain, nbias, proj_w, gate_w, sems, wts, scr,
):
    far = (proj_far.at[0], gate_far.at[0], ngain_far, nbias_far, pair_far)
    near = (proj_w.at[0], gate_w.at[0], ngain, nbias, pair)
    copies = [
        pltpu.make_async_copy(source, target, sems.at[index])
        for index, (source, target) in enumerate(zip(far, near))
    ]
    for copy in copies:
        copy.start()
    for copy in copies:
        copy.wait()
    rows, lanes, channels = pair.shape
    load_in_weights(proj_w, gate_w, 0, wts)
    gain, bias = column(ngain, 0, lanes), column(nbias, 0, lanes)

    def body(step):
        base = turned_pair(pair, step)
        scaled = save_norm(step, base, scaled_out, inverse_out)
        normed = (scaled * gain + bias).astype(BF16)
        put_pair(normed_out, step, normed)
        mask = beside(*[row_mask(lengths, 2 * step + row, rows, lanes) for row in range(2)])
        put_pair_of_rows(mask_out, step, mask)
        put_pair(scr, step, save_edges(step, normed, wts[...], mask, proj_out, gate_out))

    each_pair(rows, body)
    spread_edges(scr, edge_out)


def between_kernel(
    mask_all, tri, pair, normed0, ngain, nbias, mgain, mbias, out_w, outgate_w, proj_w, gate_w,
    edge_out, mid_out, normed_out, proj_out, gate_out, scaled_out, inverse_out,
    outgate_out, scaled_mid_out, inverse_mid_out, wts, tri_in, scr,
):
    rows, lanes, channels = pair.shape
    load_in_weights(proj_w, gate_w, 1, wts)
    out_t, outgate_t = turned(out_w[0]), -turned(outgate_w[0])
    gain, bias = column(ngain, 1, lanes), column(nbias, 1, lanes)
    gain_mid, bias_mid = column(mgain, 0, lanes), column(mbias, 0, lanes)
    collect_triangle(tri, tri_in)

    def body(step):
        scaled_mid, inverse_mid = mid_norm(pair_of(tri_in, step).astype(F32))
        put_pair(scaled_mid_out, step, scaled_mid)
        put_pair_of_rows(inverse_mid_out, step, inverse_mid)
        unit = (scaled_mid * gain_mid + bias_mid).astype(BF16)
        outer = dot(out_t, unit)
        outgate = sigmoid_of_minus(dot(outgate_t, pair_of(normed0, step)))
        put_pair(outgate_out, step, outgate)
        mid = (turned_pair(pair, step) + outer * outgate).astype(BF16)
        put_pair(mid_out, step, mid)
        scaled = save_norm(step, mid.astype(F32), scaled_out, inverse_out)
        normed = (scaled * gain + bias).astype(BF16)
        put_pair(normed_out, step, normed)
        mask = pair_of_rows(mask_all, step)
        put_pair(scr, step, save_edges(step, normed, wts[...], mask, proj_out, gate_out))

    each_pair(rows, body)
    spread_edges(scr, edge_out)


def out_weight_grads(unit, d_outer, normed, d_gatepre, out_ref):
    width = unit.shape[0]
    out_ref[0:width, :] = dot_rt(unit[...], d_outer[...]).astype(out_ref.dtype)
    out_ref[width:, :] = dot_rt(normed[...], d_gatepre[...]).astype(out_ref.dtype)


def in_weight_grads(normed_all, d_in_all, out_ref):
    width = normed_all.shape[0]
    for part in range(d_in_all.shape[0] // width):
        block = slice(part * width, (part + 1) * width)
        out_ref[block, :] = dot_rt(normed_all[...], d_in_all[block, :]).astype(out_ref.dtype)


def lane_block(step, lanes):
    return pl.ds(2 * step * lanes, 2 * lanes)


def turn_kernel(
    tri, mid, normed, cot, mgain, mbias, out_w, outgate_w,
    d_tri_out, new_out, grad_out, d_normed_out, weights_out, small_out,
    tri_in, scr, unit_all, outer_all, normed_all, gate_all, sums,
):
    rows, channels, lanes = mid.shape
    out_t, outgate_t = turned(out_w[1]), -turned(outgate_w[1])
    gain_mid, bias_mid = column(mgain, 1, lanes), column(mbias, 1, lanes)
    collect_triangle(tri, tri_in)
    sums[...] = jnp.zeros_like(sums)

    def body(step):
        here = lane_block(step, lanes)
        grad = turned_pair(cot, step)
        put_pair(grad_out, step, grad)
        here_normed = pair_of(normed, step)
        outgate = sigmoid_of_minus(dot(outgate_t, here_normed))
        gated = grad * outgate
        d_outer = gated.astype(BF16)
        d_unit = dot(out_w[1], d_outer)
        scaled_mid, inverse_mid = mid_norm(pair_of(tri_in, step).astype(F32))
        d_tri = norm_backward(d_unit * gain_mid, scaled_mid, inverse_mid)
        put_pair(scr, step, d_tri.astype(BF16))
        unit = (scaled_mid * gain_mid + bias_mid).astype(BF16)
        outer = dot(out_t, unit)
        put_pair(new_out, step, (pair_of(mid, step).astype(F32) + outer * outgate).astype(BF16))
        d_gatepre = (gated * outer * (1.0 - outgate)).astype(BF16)
        put_pair(d_normed_out, step, dot(outgate_w[1], d_gatepre))
        unit_all[:, here] = unit
        outer_all[:, here] = d_outer
        normed_all[:, here] = here_normed
        gate_all[:, here] = d_gatepre
        return d_unit * scaled_mid, d_unit

    each_pair(rows, body, sums)
    spread_triangle(scr, d_tri_out)
    out_weight_grads(unit_all, outer_all, normed_all, gate_all, weights_out)
    for index in range(2):
        small_out[index : index + 1, :] = as_row(sums[index])


def edge_backward(step, scratch, proj_factor, gate_factor):
    here = pair_of(scratch, step).astype(F32)
    d_proj = (here * pair_of(proj_factor, step)).astype(BF16)
    d_gate = (here * pair_of(gate_factor, step)).astype(BF16)
    return jnp.concatenate([d_proj, d_gate], axis=0)


def middle_kernel(
    d_edge, proj_factor, gate_factor, d_normed_gate, scaled_in, inverse_in, cot, outgate,
    scaled_mid, inverse_mid, normed0, normed1, ngain, mgain, mbias, proj_w, gate_w, out_w,
    outgate_w,
    d_tri_out, grad_out, d_normed_out, out_weights, in_weights, small_out,
    scr, scr_tri, unit_all, outer_all, normed_all, gate_all, upper_all, d_in_all, back, sums,
):
    rows, channels, lanes = cot.shape
    out_t = turned(out_w[0])
    gain = column(ngain, 1, lanes)
    gain_mid, bias_mid = column(mgain, 0, lanes), column(mbias, 0, lanes)
    collect_edges(d_edge, scr)
    sums[...] = jnp.zeros_like(sums)
    load_back_weights(proj_w, gate_w, 1, back)

    def upper(step):
        place = lane_block(step, lanes)
        d_in = edge_backward(step, scr, proj_factor, gate_factor)
        d_in_all[:, place] = d_in
        upper_all[:, place] = pair_of(normed1, step)
        d_normed = pair_of(d_normed_gate, step) + dot(back[...], d_in)
        scaled = pair_of(scaled_in, step)
        grad = pair_of(cot, step) + norm_backward(
            d_normed * gain, scaled, pair_of_rows(inverse_in, step)
        )
        put_pair(grad_out, step, grad)
        return d_normed * scaled, d_normed

    def lower(step):
        place = lane_block(step, lanes)
        gate = pair_of(outgate, step)
        gated = pair_of(grad_out, step) * gate
        d_outer = gated.astype(BF16)
        d_unit = dot(out_w[0], d_outer)
        scaled = pair_of(scaled_mid, step)
        d_tri = norm_backward(d_unit * gain_mid, scaled, pair_of_rows(inverse_mid, step))
        put_pair(scr_tri, step, d_tri.astype(BF16))
        unit = (scaled * gain_mid + bias_mid).astype(BF16)
        outer = dot(out_t, unit)
        d_gatepre = (gated * outer * (1.0 - gate)).astype(BF16)
        put_pair(d_normed_out, step, dot(outgate_w[0], d_gatepre))
        unit_all[:, place] = unit
        outer_all[:, place] = d_outer
        normed_all[:, place] = pair_of(normed0, step)
        gate_all[:, place] = d_gatepre
        return d_unit * scaled, d_unit

    each_pair(rows, upper, sums.at[2:4])
    each_pair(rows, lower, sums.at[0:2])
    spread_triangle(scr_tri, d_tri_out)
    out_weight_grads(unit_all, outer_all, normed_all, gate_all, out_weights)
    in_weight_grads(upper_all, d_in_all, in_weights)
    for index in range(4):
        small_out[index : index + 1, :] = as_row(sums[index])


def split_cores(all_rows, own_out, other_out, few):
    chips, share, width = own_out.shape
    view = all_rows.reshape(chips // few, 2, few, share, width)
    core = lax.rem(lax.axis_index("row"), 2)
    own_out[...] = view[:, core].reshape(own_out.shape)
    other_out[...] = view[:, 1 - core].reshape(other_out.shape)


def finish_kernel(
    few, d_edge, proj_factor, gate_factor, normed, out0, in1, out1,
    own_out, other_out, d_in_all, scr, normed_all, packed,
):
    rows, half, lanes = proj_factor.shape
    collect_edges(d_edge, scr)

    def body(step):
        place = lane_block(step, lanes)
        d_in_all[:, place] = edge_backward(step, scr, proj_factor, gate_factor)
        normed_all[:, place] = pair_of(normed, step)

    each_pair(rows, body)
    first, second, third = d_in_all.shape[0], out0.shape[0], in1.shape[0]
    in_weight_grads(normed_all, d_in_all, packed.at[0:first])
    packed[first : first + second, :] = out0[...]
    packed[first + second : first + second + third, :] = in1[...]
    packed[first + second + third :, :] = out1[...]
    split_cores(packed, own_out, other_out, few)


def norm_sums_kernel(
    d_in, d_normed_gate, scaled_in, proj_w, gate_w, small_middle, small1, new_t,
    d_normed_out, extra_out, new_out, back, sums,
):
    rows, channels, lanes = scaled_in.shape
    sums[...] = jnp.zeros_like(sums)
    load_back_weights(proj_w, gate_w, 0, back)

    def body(step):
        here = d_in[:, lane_block(step, lanes)]
        d_normed = pair_of(d_normed_gate, step) + dot(back[...], here)
        put_pair(d_normed_out, step, d_normed)
        put_turned_pair(new_out, step, pair_of(new_t, step))
        return d_normed * pair_of(scaled_in, step), d_normed

    each_pair(rows, body, sums)
    small = jnp.concatenate(
        [as_row(sums[0]), as_row(sums[1]), small_middle[0:2], small_middle[2:4], small1[...]],
        axis=0,
    )
    high = small.astype(BF16).astype(F32)
    extra_out[...] = jnp.concatenate([high, small - high], axis=0).astype(BF16)


def add_kernel(first, second, extra, out_ref, extra_out):
    out_ref[...] = (first[...].astype(F32) + second[...].astype(F32)).astype(BF16)
    extra_out[...] = extra[...]


def sum_kernel(parts, extra, shared_out):
    chips, share, width = parts.shape
    own = jnp.sum(parts[...].astype(F32), axis=0).astype(BF16)
    for chip in range(chips):
        shared_out[chip, 0:share] = own
        shared_out[chip, share:] = extra[...]


def grad_pair_kernel(
    share, shared, d_normed, scaled_in, inverse_in, grad, ngain, grad_out, mine_out
):
    rows, channels, lanes = grad.shape
    gain = column(ngain, 0, lanes)
    mine_out[...] = jnp.sum(shared[:, share:].astype(F32), axis=0)

    def body(step):
        total = pair_of(grad, step) + norm_backward(
            pair_of(d_normed, step) * gain, pair_of(scaled_in, step),
            pair_of_rows(inverse_in, step),
        )
        put_turned_pair(grad_out, step, total)

    each_pair(rows, body)


def unpack_kernel(
    share, few, own, other, mine, proj_out, gate_out, out_out, outgate_out,
    norm_gain_out, norm_bias_out, mid_gain_out, mid_bias_out, weights,
):
    chips, _, width = own.shape
    core = lax.rem(lax.axis_index("row"), 2)
    view = weights.reshape(chips // few, 2, few, share, width)
    block = (chips // few, few, share, width)
    view[:, core] = own[:, 0:share].astype(F32).reshape(block)
    view[:, 1 - core] = other[:, 0:share].astype(F32).reshape(block)
    total = mine[...] + jnp.sum(other[:, share:].astype(F32), axis=0)
    total = total[0:8] + total[8:16]
    for module in range(2):
        for index, out in enumerate((norm_gain_out, norm_bias_out, mid_gain_out, mid_bias_out)):
            at = 4 * module + index
            out[module : module + 1, :] = total[at : at + 1]
        blocks = [
            weights[(6 * module + part) * width : (6 * module + part + 1) * width, :]
            for part in range(6)
        ]
        for side in range(2):
            proj_out[module, side] = blocks[side]
            gate_out[module, side] = blocks[2 + side]
        out_out[module] = blocks[4]
        outgate_out[module] = blocks[5]


def triangle_kernel(incoming, edge, tri_out):
    many, few, _, group, rows, lanes = edge.shape

    def whole(side, channel):
        parts = [edge[:, c, side, channel].reshape(many * rows, lanes) for c in range(few)]
        return jnp.concatenate(parts, axis=1)

    for channel in range(group):
        left, right = whole(0, channel), whole(1, channel)
        tri = (dot_lt if incoming else dot_rt)(left, right).astype(BF16)
        for c in range(few):
            part = tri[:, c * lanes : (c + 1) * lanes]
            tri_out[:, c, channel] = part.reshape(many, rows, lanes)


def edge_grad_kernel(incoming, edge, d_tri, grad_out):
    many, few, _, group, rows, lanes = edge.shape

    def whole(ref, *index):
        parts = [ref[(slice(None), c) + index].reshape(many * rows, lanes) for c in range(few)]
        return jnp.concatenate(parts, axis=1)

    for channel in range(group):
        left, right = whole(edge, 0, channel), whole(edge, 1, channel)
        grad = whole(d_tri, channel)
        if incoming:
            d_left, d_right = dot_rt(right, grad), dot(left, grad)
        else:
            d_left, d_right = dot(grad, right), dot_lt(grad, left)
        for side, value in ((0, d_left), (1, d_right)):
            value = value.astype(BF16)
            for c in range(few):
                part = value[:, c * lanes : (c + 1) * lanes]
                grad_out[:, c, side, channel] = part.reshape(many, rows, lanes)


SCALARS = pl.BlockSpec(memory_space=pltpu.SMEM)
VECTORS = pl.BlockSpec(memory_space=pltpu.VMEM)
FAR = pl.BlockSpec(memory_space=pltpu.HBM)


def call(kernel, name, outs, args, scratch=(), flops=0, grant=16, specs=None):
    shapes = [jax.ShapeDtypeStruct(shape, dtype) for shape, dtype in outs]
    moved = sum(a.size * a.dtype.itemsize for a in list(args) + shapes)
    return pl.pallas_call(
        kernel,
        name=name,
        out_shape=shapes,
        in_specs=specs or [VECTORS] * len(args),
        out_specs=[VECTORS] * len(shapes),
        scratch_shapes=[
            pltpu.VMEM(*item) if isinstance(item, tuple) else item for item in scratch
        ],
        compiler_params=pltpu.CompilerParams(vmem_limit_bytes=grant * 1024 * 1024),
        cost_estimate=pl.CostEstimate(flops=flops, bytes_accessed=moved, transcendentals=0),
    )(*args)


def exchange(values):
    return lax.all_to_all(values, ("row", "col"), split_axis=0, concat_axis=0, tiled=True)


def swap_cores(values, many, few):
    pairs = [(index, index ^ few) for index in range(many * few)]
    return lax.ppermute(values, ("row", "col"), pairs)


def exchange_chips(values, many, few):
    groups = [
        [row * few + col for row in range(core, many, 2) for col in range(few)] for core in range(2)
    ]
    return lax.all_to_all(
        values, ("row", "col"), split_axis=0, concat_axis=0, axis_index_groups=groups, tiled=True
    )


def grouped_device(
    pair, cotangent, lengths, ngain, nbias, proj_w, gate_w, mgain, mbias, out_w, outgate_w,
    *, many, few,
):
    rows, lanes, channels = pair.shape
    shards = many * few
    group = H // shards
    edge = ((shards, 2, group, rows, lanes), BF16)
    grid = ((many, few, 2, group, rows, lanes), BF16)
    tri = ((shards, group, rows, lanes), BF16)
    tri_grid = ((many, few, group, rows, lanes), BF16)
    tile = ((rows, channels, lanes), BF16)
    wide = ((rows, channels, lanes), F32)
    row = ((rows, lanes), F32)
    factor = ((rows, 2 * H, lanes), F32)
    back = ((channels, 4 * H), BF16)
    wts = ((4 * H, channels), BF16)
    big = ((rows, 2 * H, lanes), BF16)
    mid = ((rows, H, lanes), BF16)
    positions = rows * lanes
    flat = ((H, positions), BF16)
    flat_in = ((4 * H, positions), BF16)
    out_rows = ((2 * H, channels), BF16)
    in_rows = ((4 * H, H), BF16)
    triangle = 2 * group * (many * rows) ** 2 * (few * lanes)
    dense = 2 * positions * channels * H

    def sums(count):
        return ((count, H, lanes), F32)

    def small(count):
        return ((count, H), F32)

    saved = [tile, factor, factor, wide, row]
    far = [
        pltpu.with_memory_space_constraint(item, pltpu.HBM)
        for item in (pair, ngain, nbias, proj_w, gate_w)
    ]
    sent, normed0, *factors0, mask = call(
        start_kernel, "start", [edge, *saved, row], [lengths, *far],
        [(pair.shape, BF16), (ngain.shape, F32), (nbias.shape, F32), (proj_w.shape, BF16),
         (gate_w.shape, BF16), pltpu.SemaphoreType.DMA((5,)), wts, big],
        4 * dense, specs=[SCALARS] + [FAR] * len(far),
    )
    edge0 = exchange(sent).reshape(grid[0])
    (here,) = call(
        functools.partial(triangle_kernel, False), "outgoing", [tri_grid], [edge0], (), triangle,
    )
    tri0 = exchange(here.reshape(tri[0]))
    sent, mid_t, normed1, *factors1, outgate0, scaled_mid0, inverse_mid0 = call(
        between_kernel, "between", [edge, tile, *saved, wide, wide, row],
        [mask, tri0, pair, normed0, ngain, nbias, mgain, mbias, out_w, outgate_w, proj_w,
         gate_w],
        [wts, mid, big], 6 * dense,
    )
    edge1 = exchange(sent).reshape(grid[0])
    (here,) = call(
        functools.partial(triangle_kernel, True), "incoming", [tri_grid], [edge1], (), triangle,
    )
    tri1 = exchange(here.reshape(tri[0]))
    sent, new_t, cot_t, d_normed_gate1, out_grads1, small1 = call(
        turn_kernel, "turn", [tri, tile, wide, wide, out_rows, small(2)],
        [tri1, mid_t, normed1, cotangent, mgain, mbias, out_w, outgate_w],
        [mid, mid, flat, flat, flat, flat, sums(2)], 6 * dense,
    )
    d_tri1 = exchange(sent).reshape(tri_grid[0])
    (sent,) = call(
        functools.partial(edge_grad_kernel, True), "incoming_grad", [grid], [edge1, d_tri1],
        (), 2 * triangle,
    )
    d_edge1 = exchange(sent.reshape(edge[0]))
    proj_factor1, gate_factor1, scaled1, inverse1 = factors1
    sent, grad, d_normed_gate0, out_grads0, in_grads1, small_middle = call(
        middle_kernel, "middle", [tri, wide, wide, out_rows, in_rows, small(4)],
        [d_edge1, proj_factor1, gate_factor1, d_normed_gate1, scaled1, inverse1, cot_t, outgate0,
         scaled_mid0, inverse_mid0, normed0, normed1, ngain, mgain, mbias, proj_w, gate_w, out_w,
         outgate_w],
        [big, mid, flat, flat, flat, flat, flat, flat_in, back, sums(4)], 13 * dense,
    )
    d_tri0 = exchange(sent).reshape(tri_grid[0])
    (sent,) = call(
        functools.partial(edge_grad_kernel, False), "outgoing_grad", [grid], [edge0, d_tri0],
        (), 2 * triangle,
    )
    d_edge0 = exchange(sent.reshape(edge[0]))
    share = 12 * H // shards
    chips = shards // 2
    proj_factor0, gate_factor0, scaled0, inverse0 = factors0
    held = ((chips, share, H), BF16)
    own, other, d_in0 = call(
        functools.partial(finish_kernel, few), "finish", [held, held, flat_in],
        [d_edge0, proj_factor0, gate_factor0, normed0, out_grads0, in_grads1, out_grads1],
        [big, flat, ((12 * H, H), BF16)], 4 * dense,
    )
    other = swap_cores(other, many, few)
    d_normed0, extra, new_pair = call(
        norm_sums_kernel, "norm_sums", [wide, ((16, H), BF16), (pair.shape, BF16)],
        [d_in0, d_normed_gate0, scaled0, proj_w, gate_w, small_middle, small1, new_t],
        [back, sums(2)],
        4 * dense,
    )
    own, extra = call(add_kernel, "add_cores", [held, ((16, H), BF16)], [own, other, extra])
    parts = exchange_chips(own, many, few)
    (shared,) = call(
        sum_kernel, "sum_weights", [((chips, share + 16, H), BF16)], [parts, extra]
    )
    shared = exchange_chips(shared, many, few)
    other = swap_cores(shared, many, few)
    grad_pair, mine = call(
        functools.partial(grad_pair_kernel, share), "grad_pair",
        [(pair.shape, BF16), ((16, H), F32)],
        [shared, d_normed0, scaled0, inverse0, grad, ngain],
    )
    grad_proj, grad_gate, grad_out, grad_outgate, *vectors = call(
        functools.partial(unpack_kernel, share, few), "unpack",
        [(proj_w.shape, F32), (gate_w.shape, F32), (out_w.shape, F32), (outgate_w.shape, F32),
         (ngain.shape, F32), (nbias.shape, F32), (mgain.shape, F32), (mbias.shape, F32)],
        [shared, other, mine], [((12 * H, H), F32)],
    )
    return (
        new_pair,
        grad_pair,
        vectors[0],
        vectors[1],
        grad_proj,
        grad_gate,
        vectors[2],
        vectors[3],
        grad_out,
        grad_outgate,
    )


def norm_channels(values):
    average = jnp.mean(values, -1, keepdims=True)
    centred = values - average
    variance = jnp.mean(centred * centred, -1, keepdims=True)
    inverse = lax.rsqrt(variance + EPS)
    return (centred * inverse, inverse)


def forward_module(pair_in, pair_mask, weights, incoming):
    gain_in, bias_in, proj_w, gate_w, gain_mid, bias_mid, out_w, outgate_w = weights
    scaled_in, inverse_in = norm_channels(pair_in.astype(jnp.float32))
    normed = (scaled_in * gain_in + bias_in).astype(jnp.bfloat16)
    projected = product("ijc,sch->shij", normed, proj_w)
    gating = jax.nn.sigmoid(product("ijc,sch->shij", normed, gate_w))
    hidden = (projected * gating * pair_mask).astype(jnp.bfloat16)
    left_side, right_side = (
        lax.all_to_all(hidden[0], "row", split_axis=0, concat_axis=1, tiled=True),
        lax.all_to_all(hidden[1], "row", split_axis=0, concat_axis=1, tiled=True),
    )
    if incoming:
        left_side = jnp.swapaxes(left_side, 1, 2)
        right_side = jnp.swapaxes(right_side, 1, 2)
    else:
        left_side, right_side = (
            lax.all_to_all(left_side, "col", split_axis=1, concat_axis=2, tiled=True),
            lax.all_to_all(right_side, "col", split_axis=1, concat_axis=2, tiled=True),
        )
    triangle = product(
        "cik,cjk->cij", left_side, lax.all_gather(right_side, "col", axis=1, tiled=True)
    ).astype(jnp.bfloat16)
    triangle = lax.all_to_all(
        lax.all_to_all(triangle, "col", split_axis=2, concat_axis=1, tiled=True),
        "row",
        split_axis=1,
        concat_axis=0,
        tiled=True,
    )
    tri_values = triangle.astype(jnp.float32)
    total, squares = lax.psum((jnp.sum(tri_values, 0), jnp.sum(tri_values * tri_values, 0)), "ch")
    average = total / H
    inverse_mid = lax.rsqrt(squares / H - average * average + EPS)
    scaled_mid = (tri_values - average) * inverse_mid
    unit = (scaled_mid * gain_mid[:, None, None] + bias_mid[:, None, None]).astype(jnp.bfloat16)
    unit_full = lax.all_gather(unit, "ch", axis=0, tiled=True)
    outer = product("hij,hc->ijc", unit_full, out_w)
    outgate = jax.nn.sigmoid(product("ijc,cd->ijd", normed, outgate_w))
    result = (pair_in.astype(jnp.float32) + outer * outgate).astype(jnp.bfloat16)
    saved = (
        scaled_in,
        inverse_in,
        normed,
        projected,
        gating,
        left_side,
        right_side,
        scaled_mid,
        inverse_mid,
        unit_full,
        outer,
        outgate,
    )
    return (result, saved)


def backward_module(grad_out, pair_mask, weights, saved, incoming):
    gain_in, bias_in, proj_w, gate_w, gain_mid, bias_mid, out_w, outgate_w = weights
    (
        scaled_in,
        inverse_in,
        normed,
        projected,
        gating,
        left_side,
        right_side,
        scaled_mid,
        inverse_mid,
        unit_full,
        outer,
        outgate,
    ) = saved
    d_outer = (grad_out * outgate).astype(jnp.bfloat16)
    d_gatepre = (grad_out * outer * outgate * (1.0 - outgate)).astype(jnp.bfloat16)
    grad_out_w = product("hij,ijc->hc", unit_full, d_outer)
    grad_outgate_w = product("ijc,ijd->cd", normed, d_gatepre)
    width = gain_mid.shape[0]
    own_rows = lax.dynamic_slice_in_dim(out_w, lax.axis_index("ch") * width, width, 0)
    d_unit = product("ijc,hc->hij", d_outer, own_rows)
    d_normed = product("ijd,cd->ijc", d_gatepre, outgate_w)
    weighted = d_unit * gain_mid[:, None, None]
    grad_gain_mid = jnp.sum(d_unit * scaled_mid, (1, 2))
    grad_bias_mid = jnp.sum(d_unit, (1, 2))
    first_sum, second_sum = lax.psum(
        (jnp.sum(weighted, 0), jnp.sum(weighted * scaled_mid, 0)), "ch"
    )
    d_tri = (inverse_mid * (weighted - first_sum / H - scaled_mid * (second_sum / H))).astype(
        jnp.bfloat16
    )
    grad_rows = lax.all_to_all(d_tri, "row", split_axis=0, concat_axis=1, tiled=True)
    grad_cols = lax.all_to_all(grad_rows, "col", split_axis=1, concat_axis=2, tiled=True)
    d_left = product(
        "cij,cjk->cik", grad_cols, lax.all_gather(right_side, "col", axis=1, tiled=True)
    )
    partial_terms = product("cij,cik->cjk", grad_cols, left_side)
    d_right = lax.psum_scatter(
        partial_terms.astype(jnp.bfloat16), "col", scatter_dimension=1, tiled=True
    ).astype(jnp.float32)
    d_left = d_left.astype(jnp.bfloat16)
    d_right = d_right.astype(jnp.bfloat16)
    if incoming:
        d_left = jnp.swapaxes(d_left, 1, 2)
        d_right = jnp.swapaxes(d_right, 1, 2)
    else:
        d_left, d_right = (
            lax.all_to_all(d_left, "col", split_axis=2, concat_axis=1, tiled=True),
            lax.all_to_all(d_right, "col", split_axis=2, concat_axis=1, tiled=True),
        )
    d_left, d_right = (
        lax.all_to_all(d_left, "row", split_axis=1, concat_axis=0, tiled=True),
        lax.all_to_all(d_right, "row", split_axis=1, concat_axis=0, tiled=True),
    )
    d_hidden = jnp.stack([d_left, d_right]).astype(jnp.float32)
    d_proj = (d_hidden * gating * pair_mask).astype(jnp.bfloat16)
    d_gate = (d_hidden * projected * gating * (1.0 - gating) * pair_mask).astype(jnp.bfloat16)
    grad_proj_w = product("ijc,shij->sch", normed, d_proj)
    grad_gate_w = product("ijc,shij->sch", normed, d_gate)
    partial_input = product("shij,sch->ijc", d_proj, proj_w) + product(
        "shij,sch->ijc", d_gate, gate_w
    )
    d_normed = d_normed + lax.psum(partial_input.astype(jnp.bfloat16), "ch").astype(jnp.float32)
    weighted_in = d_normed * gain_in
    grad_gain_in = jnp.sum(d_normed * scaled_in, (0, 1))
    grad_bias_in = jnp.sum(d_normed, (0, 1))
    d_pair = inverse_in * (
        weighted_in
        - jnp.mean(weighted_in, -1, keepdims=True)
        - scaled_in * jnp.mean(weighted_in * scaled_in, -1, keepdims=True)
    )
    grads = (
        grad_gain_in,
        grad_bias_in,
        grad_proj_w,
        grad_gate_w,
        grad_gain_mid,
        grad_bias_mid,
        grad_out_w,
        grad_outgate_w,
    )
    return (grad_out + d_pair, grads)


def per_device(
    pair,
    cotangent,
    lengths,
    norm_gain,
    norm_bias,
    proj_weight,
    gate_weight,
    mid_gain,
    mid_bias,
    out_weight,
    outgate_weight,
):
    rows_here = pair.shape[0]
    cols_here = pair.shape[1]
    row_ids = lax.axis_index("row") * rows_here + lax.iota(jnp.int32, rows_here)
    col_ids = lax.axis_index("col") * cols_here + lax.iota(jnp.int32, cols_here)
    limit = lengths[0]
    pair_mask = ((row_ids[:, None] < limit) & (col_ids[None, :] < limit)).astype(jnp.float32)
    state = pair
    stash = []
    for layer in range(2):
        weights = (
            norm_gain[layer],
            norm_bias[layer],
            proj_weight[layer],
            gate_weight[layer],
            mid_gain[layer],
            mid_bias[layer],
            out_weight[layer],
            outgate_weight[layer],
        )
        state, saved = forward_module(state, pair_mask, weights, layer == 1)
        stash.append(saved)
    grad_state = cotangent.astype(jnp.float32)
    per_layer = [None, None]
    for layer in (1, 0):
        weights = (
            norm_gain[layer],
            norm_bias[layer],
            proj_weight[layer],
            gate_weight[layer],
            mid_gain[layer],
            mid_bias[layer],
            out_weight[layer],
            outgate_weight[layer],
        )
        grad_state, grads = backward_module(
            grad_state, pair_mask, weights, stash[layer], layer == 1
        )
        per_layer[layer] = grads
    lower = per_layer[0]
    upper = per_layer[1]
    summed = lax.psum(
        (
            lower[0],
            lower[1],
            lower[2],
            lower[3],
            lower[4],
            lower[5],
            lower[6],
            lower[7],
            upper[0],
            upper[1],
            upper[2],
            upper[3],
            upper[4],
            upper[5],
            upper[6],
            upper[7],
        ),
        ("row", "col"),
    )
    per_layer = [summed[0:8], summed[8:16]]
    stacked = [jnp.stack([per_layer[0][index], per_layer[1][index]]) for index in range(8)]
    return (
        state,
        grad_state.astype(jnp.bfloat16),
        stacked[0],
        stacked[1],
        stacked[2],
        stacked[3],
        stacked[4],
        stacked[5],
        stacked[6],
        stacked[7],
    )


def on_device(pair, *rest, many, few, split):
    rows, lanes, channels = pair.shape
    shards = many * few
    whole_channels = split == 1 and H % shards == 0 and BLOCK % (H // shards) == 0 and H % (2 * BLOCK) == 0
    tiles = rows == BLOCK and lanes % 128 == 0 and channels == H
    if whole_channels and tiles and many % 2 == 0 and few & (few - 1) == 0:
        return grouped_device(pair, *rest, many=many, few=few)
    return per_device(pair, *rest)


def solution(mesh):
    in_specs = (
        P(("grp", "row"), "col", None),
        P(("grp", "row"), "col", None),
        P("grp"),
        P(),
        P(),
        P(None, None, None, "ch"),
        P(None, None, None, "ch"),
        P(None, "ch"),
        P(None, "ch"),
        P(),
        P(),
    )
    out_specs = (
        P(("grp", "row"), "col", None),
        P(("grp", "row"), "col", None),
        P("grp", None),
        P("grp", None),
        P("grp", None, None, "ch"),
        P("grp", None, None, "ch"),
        P("grp", "ch"),
        P("grp", "ch"),
        P("grp", None, None),
        P("grp", None, None),
    )
    body = functools.partial(
        on_device, many=mesh.shape["row"], few=mesh.shape["col"], split=mesh.shape["ch"]
    )
    return jax.shard_map(
        body, mesh=mesh, in_specs=in_specs, out_specs=out_specs, check_vma=False
    )
```

```python
import functools

import jax
import jax.numpy as jnp
from jax import lax
from jax.experimental import pallas as pl
from jax.experimental.pallas import tpu as pltpu
from jax.sharding import PartitionSpec as P

H = 128


EPS = 1e-05


def product(spec, left, right):
    return jnp.einsum(spec, left, right, preferred_element_type=jnp.float32)


F32 = jnp.float32
BF16 = jnp.bfloat16


def dot(left, right):
    return lax.dot_general(left, right, (((1,), (0,)), ((), ())), preferred_element_type=F32)


def dot_rt(left, right):
    return lax.dot_general(left, right, (((1,), (1,)), ((), ())), preferred_element_type=F32)


def dot_lt(left, right):
    return lax.dot_general(left, right, (((0,), (0,)), ((), ())), preferred_element_type=F32)


def sigmoid_of_minus(values):
    return 1.0 / (1.0 + jnp.exp(values))


def norm_rows(values):
    scale = 1.0 / values.shape[0]
    average = jnp.sum(values, 0, keepdims=True) * scale
    centred = values - average
    variance = jnp.sum(centred * centred, 0, keepdims=True) * scale
    inverse = lax.rsqrt(variance + EPS)
    return centred * inverse, inverse


def turned(weight):
    return jnp.transpose(weight)


def column(ref, module, lanes):
    row = ref[module : module + 1, :]
    return beside(*[jnp.transpose(jnp.broadcast_to(row, (lanes, row.shape[1])))] * 2)


def beside(left, right):
    return jnp.concatenate([left, right], axis=-1)


def pair_of(ref, step):
    return beside(ref[2 * step], ref[2 * step + 1])


def put_pair(ref, step, values):
    lanes = ref.shape[-1]
    ref[2 * step] = values[:, :lanes]
    ref[2 * step + 1] = values[:, lanes:]


def pair_of_rows(ref, step):
    return beside(ref[2 * step : 2 * step + 1, :], ref[2 * step + 1 : 2 * step + 2, :])


def put_pair_of_rows(ref, step, values):
    lanes = ref.shape[-1]
    ref[2 * step : 2 * step + 1, :] = values[:, :lanes]
    ref[2 * step + 1 : 2 * step + 2, :] = values[:, lanes:]


def turned_pair(ref, step):
    return beside(jnp.transpose(ref[2 * step]), jnp.transpose(ref[2 * step + 1])).astype(F32)


def put_turned_pair(ref, step, values):
    lanes = ref.shape[1]
    values = values.astype(BF16)
    ref[2 * step] = jnp.transpose(values[:, :lanes])
    ref[2 * step + 1] = jnp.transpose(values[:, lanes:])


def as_row(total):
    return jnp.sum(jnp.transpose(total), 0, keepdims=True)


def row_mask(lengths_ref, step, rows, lanes):
    limit = lengths_ref[0]
    row_id = lax.axis_index("row") * rows + step
    col_id = lax.axis_index("col") * lanes + lax.broadcasted_iota(jnp.int32, (1, lanes), 1)
    return jnp.where((row_id < limit) & (col_id < limit), 1.0, 0.0).astype(F32)


def load_in_weights(proj_ref, gate_ref, module, scratch):
    width = proj_ref.shape[-1]
    for side in range(2):
        scratch[side * width : (side + 1) * width, :] = turned(proj_ref[module, side])
        scratch[(2 + side) * width : (3 + side) * width, :] = -turned(gate_ref[module, side])


def load_back_weights(proj_ref, gate_ref, module, scratch):
    width = proj_ref.shape[-1]
    for side in range(2):
        scratch[:, side * width : (side + 1) * width] = proj_ref[module, side]
        scratch[:, (2 + side) * width : (3 + side) * width] = gate_ref[module, side]


BLOCK = 16


def turn_matrix(rows):
    size = BLOCK * rows
    out = lax.broadcasted_iota(jnp.int32, (size, size), 0)
    source = lax.broadcasted_iota(jnp.int32, (size, size), 1)
    return jnp.where(source == (out % rows) * BLOCK + out // rows, 1.0, 0.0).astype(BF16)


def spread_blocks(matrix, scratch, start, group):
    rows, _, lanes = scratch.shape
    blocks = [
        scratch[:, at : at + BLOCK, :].reshape(rows * BLOCK, lanes)
        for at in (start, start + BLOCK)
    ]
    both = dot(matrix, beside(*blocks)).astype(BF16)
    parts = [
        part.reshape(BLOCK // group, group, rows, lanes)
        for part in (both[:, :lanes], both[:, lanes:])
    ]
    return jnp.concatenate(parts, axis=0)


def collect_blocks(matrix, values, scratch, start):
    rows, _, lanes = scratch.shape
    flat = values.reshape(2, BLOCK * rows, lanes)
    both = dot(matrix, beside(flat[0], flat[1])).astype(BF16)
    for at, part in ((start, both[:, :lanes]), (start + BLOCK, both[:, lanes:])):
        scratch[:, at : at + BLOCK, :] = part.reshape(rows, BLOCK, lanes)


def spread_edges(scratch, out_ref):
    shards, sides, group, rows, lanes = out_ref.shape
    matrix, step = turn_matrix(rows), 2 * BLOCK // group
    for side in range(sides):
        for shard in range(0, shards, step):
            start = (side * shards + shard) * group
            out_ref[shard : shard + step, side] = spread_blocks(matrix, scratch, start, group)


def collect_edges(in_ref, scratch):
    shards, sides, group, rows, lanes = in_ref.shape
    matrix, step = turn_matrix(rows), 2 * BLOCK // group
    for side in range(sides):
        for shard in range(0, shards, step):
            start = (side * shards + shard) * group
            collect_blocks(matrix, in_ref[shard : shard + step, side], scratch, start)


def spread_triangle(scratch, out_ref):
    shards, group, rows, lanes = out_ref.shape
    matrix, step = turn_matrix(rows), 2 * BLOCK // group
    for shard in range(0, shards, step):
        out_ref[shard : shard + step] = spread_blocks(matrix, scratch, shard * group, group)


def collect_triangle(in_ref, scratch):
    shards, group, rows, lanes = in_ref.shape
    matrix, step = turn_matrix(rows), 2 * BLOCK // group
    for shard in range(0, shards, step):
        collect_blocks(matrix, in_ref[shard : shard + step], scratch, shard * group)


def each_pair(rows, body, sums=None):
    for block in range(0, rows // 2, 2):
        parts = [body(block + step) for step in range(2)]
        for index in range(0 if sums is None else sums.shape[0]):
            total = parts[0][index] + parts[1][index]
            lanes = sums.shape[-1]
            sums[index] += total[:, :lanes] + total[:, lanes:]


def mid_norm(tri):
    scale = 1.0 / tri.shape[0]
    average = jnp.sum(tri, 0, keepdims=True) * scale
    squares = jnp.sum(tri * tri, 0, keepdims=True) * scale
    inverse = lax.rsqrt(squares - average * average + EPS)
    return (tri - average) * inverse, inverse


def norm_backward(weighted, scaled, inverse):
    scale = 1.0 / weighted.shape[0]
    first = jnp.sum(weighted, 0, keepdims=True) * scale
    second = jnp.sum(weighted * scaled, 0, keepdims=True) * scale
    return inverse * (weighted - first - scaled * second)


def save_norm(step, values, scaled_out, inverse_out):
    scaled, inverse = norm_rows(values)
    put_pair(scaled_out, step, scaled)
    put_pair_of_rows(inverse_out, step, inverse)
    return scaled


def save_edges(step, normed, in_weights, mask, proj_out, gate_out):
    pre = dot(in_weights, normed)
    half = pre.shape[0] // 2
    gating = sigmoid_of_minus(pre[half:])
    factor = gating * mask
    value = pre[:half] * factor
    put_pair(proj_out, step, factor)
    put_pair(gate_out, step, value * (1.0 - gating))
    return value.astype(BF16)


def start_kernel(
    lengths, pair_far, ngain_far, nbias_far, proj_far, gate_far,
    edge_out, normed_out, proj_out, gate_out, scaled_out, inverse_out, mask_out,
    pair, ngain, nbias, proj_w, gate_w, sems, wts, scr,
):
    far = (proj_far.at[0], gate_far.at[0], ngain_far, nbias_far, pair_far)
    near = (proj_w.at[0], gate_w.at[0], ngain, nbias, pair)
    copies = [
        pltpu.make_async_copy(source, target, sems.at[index])
        for index, (source, target) in enumerate(zip(far, near))
    ]
    for copy in copies:
        copy.start()
    for copy in copies:
        copy.wait()
    rows, lanes, channels = pair.shape
    load_in_weights(proj_w, gate_w, 0, wts)
    gain, bias = column(ngain, 0, lanes), column(nbias, 0, lanes)

    def body(step):
        base = turned_pair(pair, step)
        scaled = save_norm(step, base, scaled_out, inverse_out)
        normed = (scaled * gain + bias).astype(BF16)
        put_pair(normed_out, step, normed)
        mask = beside(*[row_mask(lengths, 2 * step + row, rows, lanes) for row in range(2)])
        put_pair_of_rows(mask_out, step, mask)
        put_pair(scr, step, save_edges(step, normed, wts[...], mask, proj_out, gate_out))

    each_pair(rows, body)
    spread_edges(scr, edge_out)


def between_kernel(
    mask_all, tri, pair, normed0, ngain, nbias, mgain, mbias, out_w, outgate_w, proj_w, gate_w,
    edge_out, mid_out, normed_out, proj_out, gate_out, scaled_out, inverse_out,
    outgate_out, scaled_mid_out, inverse_mid_out, wts, tri_in, scr,
):
    rows, lanes, channels = pair.shape
    load_in_weights(proj_w, gate_w, 1, wts)
    out_t, outgate_t = turned(out_w[0]), -turned(outgate_w[0])
    gain, bias = column(ngain, 1, lanes), column(nbias, 1, lanes)
    gain_mid, bias_mid = column(mgain, 0, lanes), column(mbias, 0, lanes)
    collect_triangle(tri, tri_in)

    def body(step):
        scaled_mid, inverse_mid = mid_norm(pair_of(tri_in, step).astype(F32))
        put_pair(scaled_mid_out, step, scaled_mid)
        put_pair_of_rows(inverse_mid_out, step, inverse_mid)
        unit = (scaled_mid * gain_mid + bias_mid).astype(BF16)
        outer = dot(out_t, unit)
        outgate = sigmoid_of_minus(dot(outgate_t, pair_of(normed0, step)))
        put_pair(outgate_out, step, outgate)
        mid = (turned_pair(pair, step) + outer * outgate).astype(BF16)
        put_pair(mid_out, step, mid)
        scaled = save_norm(step, mid.astype(F32), scaled_out, inverse_out)
        normed = (scaled * gain + bias).astype(BF16)
        put_pair(normed_out, step, normed)
        mask = pair_of_rows(mask_all, step)
        put_pair(scr, step, save_edges(step, normed, wts[...], mask, proj_out, gate_out))

    each_pair(rows, body)
    spread_edges(scr, edge_out)


def out_weight_grads(unit, d_outer, normed, d_gatepre, out_ref):
    width = unit.shape[0]
    out_ref[0:width, :] = dot_rt(unit[...], d_outer[...]).astype(out_ref.dtype)
    out_ref[width:, :] = dot_rt(normed[...], d_gatepre[...]).astype(out_ref.dtype)


def in_weight_grads(normed_all, d_in_all, out_ref):
    width = normed_all.shape[0]
    grads = dot_rt(normed_all[...], d_in_all[...]).astype(out_ref.dtype)
    for part in range(d_in_all.shape[0] // width):
        block = slice(part * width, (part + 1) * width)
        out_ref[block, :] = grads[:, block]


def lane_block(step, lanes):
    return pl.ds(2 * step * lanes, 2 * lanes)


def turn_kernel(
    tri, mid, normed, cot, mgain, mbias, out_w, outgate_w,
    d_tri_out, new_out, grad_out, d_normed_out, weights_out, small_out,
    tri_in, scr, unit_all, outer_all, normed_all, gate_all, sums,
):
    rows, channels, lanes = mid.shape
    out_t, outgate_t = turned(out_w[1]), -turned(outgate_w[1])
    gain_mid, bias_mid = column(mgain, 1, lanes), column(mbias, 1, lanes)
    collect_triangle(tri, tri_in)
    sums[...] = jnp.zeros_like(sums)

    def body(step):
        here = lane_block(step, lanes)
        grad = turned_pair(cot, step)
        put_pair(grad_out, step, grad)
        here_normed = pair_of(normed, step)
        outgate = sigmoid_of_minus(dot(outgate_t, here_normed))
        gated = grad * outgate
        d_outer = gated.astype(BF16)
        d_unit = dot(out_w[1], d_outer)
        scaled_mid, inverse_mid = mid_norm(pair_of(tri_in, step).astype(F32))
        d_tri = norm_backward(d_unit * gain_mid, scaled_mid, inverse_mid)
        put_pair(scr, step, d_tri.astype(BF16))
        unit = (scaled_mid * gain_mid + bias_mid).astype(BF16)
        outer = dot(out_t, unit)
        put_pair(new_out, step, (pair_of(mid, step).astype(F32) + outer * outgate).astype(BF16))
        d_gatepre = (gated * outer * (1.0 - outgate)).astype(BF16)
        put_pair(d_normed_out, step, dot(outgate_w[1], d_gatepre))
        unit_all[:, here] = unit
        outer_all[:, here] = d_outer
        normed_all[:, here] = here_normed
        gate_all[:, here] = d_gatepre
        return d_unit * scaled_mid, d_unit

    each_pair(rows, body, sums)
    spread_triangle(scr, d_tri_out)
    out_weight_grads(unit_all, outer_all, normed_all, gate_all, weights_out)
    for index in range(2):
        small_out[index : index + 1, :] = as_row(sums[index])


def edge_backward(step, scratch, proj_factor, gate_factor):
    here = pair_of(scratch, step).astype(F32)
    d_proj = (here * pair_of(proj_factor, step)).astype(BF16)
    d_gate = (here * pair_of(gate_factor, step)).astype(BF16)
    return jnp.concatenate([d_proj, d_gate], axis=0)


def middle_kernel(
    d_edge, proj_factor, gate_factor, d_normed_gate, scaled_in, inverse_in, cot, outgate,
    scaled_mid, inverse_mid, normed0, normed1, ngain, mgain, mbias, proj_w, gate_w, out_w,
    outgate_w,
    d_tri_out, grad_out, d_normed_out, out_weights, in_weights, small_out,
    scr, scr_tri, unit_all, outer_all, normed_all, gate_all, upper_all, d_in_all, back, sums,
):
    rows, channels, lanes = cot.shape
    out_t = turned(out_w[0])
    gain = column(ngain, 1, lanes)
    gain_mid, bias_mid = column(mgain, 0, lanes), column(mbias, 0, lanes)
    collect_edges(d_edge, scr)
    sums[...] = jnp.zeros_like(sums)
    load_back_weights(proj_w, gate_w, 1, back)

    def upper(step):
        place = lane_block(step, lanes)
        d_in = edge_backward(step, scr, proj_factor, gate_factor)
        d_in_all[:, place] = d_in
        upper_all[:, place] = pair_of(normed1, step)
        d_normed = pair_of(d_normed_gate, step) + dot(back[...], d_in)
        scaled = pair_of(scaled_in, step)
        grad = pair_of(cot, step) + norm_backward(
            d_normed * gain, scaled, pair_of_rows(inverse_in, step)
        )
        put_pair(grad_out, step, grad)
        return d_normed * scaled, d_normed

    def lower(step):
        place = lane_block(step, lanes)
        gate = pair_of(outgate, step)
        gated = pair_of(grad_out, step) * gate
        d_outer = gated.astype(BF16)
        d_unit = dot(out_w[0], d_outer)
        scaled = pair_of(scaled_mid, step)
        d_tri = norm_backward(d_unit * gain_mid, scaled, pair_of_rows(inverse_mid, step))
        put_pair(scr_tri, step, d_tri.astype(BF16))
        unit = (scaled * gain_mid + bias_mid).astype(BF16)
        outer = dot(out_t, unit)
        d_gatepre = (gated * outer * (1.0 - gate)).astype(BF16)
        put_pair(d_normed_out, step, dot(outgate_w[0], d_gatepre))
        unit_all[:, place] = unit
        outer_all[:, place] = d_outer
        normed_all[:, place] = pair_of(normed0, step)
        gate_all[:, place] = d_gatepre
        return d_unit * scaled, d_unit

    def both(step):
        last = rows // 2 - 1
        above = upper(step) if step <= last else None
        below = lower(step - 1) if step > 0 else None
        return above, below

    totals = [None, None, None, None]
    for step in range(rows // 2 + 1):
        above, below = both(step)
        for first, parts in ((2, above), (0, below)):
            for index in range(0 if parts is None else 2):
                at = first + index
                part = parts[index][:, :lanes] + parts[index][:, lanes:]
                totals[at] = part if totals[at] is None else totals[at] + part
        if step % 2 == 1 or step == rows // 2:
            for at in range(4):
                if totals[at] is not None:
                    sums[at] += totals[at]
            totals = [None, None, None, None]
    spread_triangle(scr_tri, d_tri_out)
    out_weight_grads(unit_all, outer_all, normed_all, gate_all, out_weights)
    in_weight_grads(upper_all, d_in_all, in_weights)
    for index in range(4):
        small_out[index : index + 1, :] = as_row(sums[index])


def split_cores(all_rows, own_out, other_out, few):
    chips, share, width = own_out.shape
    view = all_rows.reshape(chips // few, 2, few, share, width)
    core = lax.rem(lax.axis_index("row"), 2)
    own_out[...] = view[:, core].reshape(own_out.shape)
    other_out[...] = view[:, 1 - core].reshape(other_out.shape)


def finish_kernel(
    few, d_edge, proj_factor, gate_factor, normed, out0, in1, out1,
    own_out, other_out, d_in_all, scr, normed_all, packed,
):
    rows, half, lanes = proj_factor.shape
    collect_edges(d_edge, scr)

    def body(step):
        place = lane_block(step, lanes)
        d_in_all[:, place] = edge_backward(step, scr, proj_factor, gate_factor)
        normed_all[:, place] = pair_of(normed, step)

    each_pair(rows, body)
    first, second, third = d_in_all.shape[0], out0.shape[0], in1.shape[0]
    in_weight_grads(normed_all, d_in_all, packed.at[0:first])
    packed[first : first + second, :] = out0[...]
    packed[first + second : first + second + third, :] = in1[...]
    packed[first + second + third :, :] = out1[...]
    split_cores(packed, own_out, other_out, few)


def norm_sums_kernel(
    d_in, d_normed_gate, scaled_in, proj_w, gate_w, small_middle, small1, new_t,
    d_normed_out, extra_out, new_out, back, sums,
):
    rows, channels, lanes = scaled_in.shape
    sums[...] = jnp.zeros_like(sums)
    load_back_weights(proj_w, gate_w, 0, back)

    def body(step):
        here = d_in[:, lane_block(step, lanes)]
        d_normed = pair_of(d_normed_gate, step) + dot(back[...], here)
        put_pair(d_normed_out, step, d_normed)
        put_turned_pair(new_out, step, pair_of(new_t, step))
        return d_normed * pair_of(scaled_in, step), d_normed

    each_pair(rows, body, sums)
    small = jnp.concatenate(
        [as_row(sums[0]), as_row(sums[1]), small_middle[0:2], small_middle[2:4], small1[...]],
        axis=0,
    )
    high = small.astype(BF16).astype(F32)
    extra_out[...] = jnp.concatenate([high, small - high], axis=0).astype(BF16)


def add_kernel(first, second, extra, out_ref, extra_out):
    out_ref[...] = (first[...].astype(F32) + second[...].astype(F32)).astype(BF16)
    extra_out[...] = extra[...]


def sum_kernel(parts, extra, shared_out):
    chips, share, width = parts.shape
    own = jnp.sum(parts[...].astype(F32), axis=0).astype(BF16)
    for chip in range(chips):
        shared_out[chip, 0:share] = own
        shared_out[chip, share:] = extra[...]


def grad_pair_kernel(
    share, shared, d_normed, scaled_in, inverse_in, grad, ngain, grad_out, mine_out
):
    rows, channels, lanes = grad.shape
    gain = column(ngain, 0, lanes)
    mine_out[...] = jnp.sum(shared[:, share:].astype(F32), axis=0)

    def body(step):
        total = pair_of(grad, step) + norm_backward(
            pair_of(d_normed, step) * gain, pair_of(scaled_in, step),
            pair_of_rows(inverse_in, step),
        )
        put_turned_pair(grad_out, step, total)

    each_pair(rows, body)


def unpack_kernel(
    share, few, own, other, mine, proj_out, gate_out, out_out, outgate_out,
    norm_gain_out, norm_bias_out, mid_gain_out, mid_bias_out, weights,
):
    chips, _, width = own.shape
    core = lax.rem(lax.axis_index("row"), 2)
    view = weights.reshape(chips // few, 2, few, share, width)
    block = (chips // few, few, share, width)
    view[:, core] = own[:, 0:share].astype(F32).reshape(block)
    view[:, 1 - core] = other[:, 0:share].astype(F32).reshape(block)
    total = mine[...] + jnp.sum(other[:, share:].astype(F32), axis=0)
    total = total[0:8] + total[8:16]
    for module in range(2):
        for index, out in enumerate((norm_gain_out, norm_bias_out, mid_gain_out, mid_bias_out)):
            at = 4 * module + index
            out[module : module + 1, :] = total[at : at + 1]
        blocks = [
            weights[(6 * module + part) * width : (6 * module + part + 1) * width, :]
            for part in range(6)
        ]
        for side in range(2):
            proj_out[module, side] = blocks[side]
            gate_out[module, side] = blocks[2 + side]
        out_out[module] = blocks[4]
        outgate_out[module] = blocks[5]


def triangle_kernel(incoming, edge, tri_out):
    many, few, _, group, rows, lanes = edge.shape

    def whole(side, channel):
        parts = [edge[:, c, side, channel].reshape(many * rows, lanes) for c in range(few)]
        return jnp.concatenate(parts, axis=1)

    for channel in range(group):
        left, right = whole(0, channel), whole(1, channel)
        tri = (dot_lt if incoming else dot_rt)(left, right).astype(BF16)
        for c in range(few):
            part = tri[:, c * lanes : (c + 1) * lanes]
            tri_out[:, c, channel] = part.reshape(many, rows, lanes)


def edge_grad_kernel(incoming, edge, d_tri, grad_out):
    many, few, _, group, rows, lanes = edge.shape

    def whole(ref, *index):
        parts = [ref[(slice(None), c) + index].reshape(many * rows, lanes) for c in range(few)]
        return jnp.concatenate(parts, axis=1)

    for channel in range(group):
        left, right = whole(edge, 0, channel), whole(edge, 1, channel)
        grad = whole(d_tri, channel)
        if incoming:
            d_left, d_right = dot_rt(right, grad), dot(left, grad)
        else:
            d_left, d_right = dot(grad, right), dot_lt(grad, left)
        for side, value in ((0, d_left), (1, d_right)):
            value = value.astype(BF16)
            for c in range(few):
                part = value[:, c * lanes : (c + 1) * lanes]
                grad_out[:, c, side, channel] = part.reshape(many, rows, lanes)


SCALARS = pl.BlockSpec(memory_space=pltpu.SMEM)
VECTORS = pl.BlockSpec(memory_space=pltpu.VMEM)
FAR = pl.BlockSpec(memory_space=pltpu.HBM)


def call(kernel, name, outs, args, scratch=(), flops=0, grant=16, specs=None):
    shapes = [jax.ShapeDtypeStruct(shape, dtype) for shape, dtype in outs]
    moved = sum(a.size * a.dtype.itemsize for a in list(args) + shapes)
    return pl.pallas_call(
        kernel,
        name=name,
        out_shape=shapes,
        in_specs=specs or [VECTORS] * len(args),
        out_specs=[VECTORS] * len(shapes),
        scratch_shapes=[
            pltpu.VMEM(*item) if isinstance(item, tuple) else item for item in scratch
        ],
        compiler_params=pltpu.CompilerParams(vmem_limit_bytes=grant * 1024 * 1024),
        cost_estimate=pl.CostEstimate(flops=flops, bytes_accessed=moved, transcendentals=0),
    )(*args)


def exchange(values):
    return lax.all_to_all(values, ("row", "col"), split_axis=0, concat_axis=0, tiled=True)


def swap_cores(values, many, few):
    pairs = [(index, index ^ few) for index in range(many * few)]
    return lax.ppermute(values, ("row", "col"), pairs)


def exchange_chips(values, many, few):
    groups = [
        [row * few + col for row in range(core, many, 2) for col in range(few)] for core in range(2)
    ]
    return lax.all_to_all(
        values, ("row", "col"), split_axis=0, concat_axis=0, axis_index_groups=groups, tiled=True
    )


def grouped_device(
    pair, cotangent, lengths, ngain, nbias, proj_w, gate_w, mgain, mbias, out_w, outgate_w,
    *, many, few,
):
    rows, lanes, channels = pair.shape
    shards = many * few
    group = H // shards
    edge = ((shards, 2, group, rows, lanes), BF16)
    grid = ((many, few, 2, group, rows, lanes), BF16)
    tri = ((shards, group, rows, lanes), BF16)
    tri_grid = ((many, few, group, rows, lanes), BF16)
    tile = ((rows, channels, lanes), BF16)
    wide = ((rows, channels, lanes), F32)
    row = ((rows, lanes), F32)
    factor = ((rows, 2 * H, lanes), F32)
    back = ((channels, 4 * H), BF16)
    wts = ((4 * H, channels), BF16)
    big = ((rows, 2 * H, lanes), BF16)
    mid = ((rows, H, lanes), BF16)
    positions = rows * lanes
    flat = ((H, positions), BF16)
    flat_in = ((4 * H, positions), BF16)
    out_rows = ((2 * H, channels), BF16)
    in_rows = ((4 * H, H), BF16)
    triangle = 2 * group * (many * rows) ** 2 * (few * lanes)
    dense = 2 * positions * channels * H

    def sums(count):
        return ((count, H, lanes), F32)

    def small(count):
        return ((count, H), F32)

    saved = [tile, factor, factor, wide, row]
    far = [
        pltpu.with_memory_space_constraint(item, pltpu.HBM)
        for item in (pair, ngain, nbias, proj_w, gate_w)
    ]
    sent, normed0, *factors0, mask = call(
        start_kernel, "start", [edge, *saved, row], [lengths, *far],
        [(pair.shape, BF16), (ngain.shape, F32), (nbias.shape, F32), (proj_w.shape, BF16),
         (gate_w.shape, BF16), pltpu.SemaphoreType.DMA((5,)), wts, big],
        4 * dense, specs=[SCALARS] + [FAR] * len(far),
    )
    edge0 = exchange(sent).reshape(grid[0])
    (here,) = call(
        functools.partial(triangle_kernel, False), "outgoing", [tri_grid], [edge0], (), triangle,
    )
    tri0 = exchange(here.reshape(tri[0]))
    sent, mid_t, normed1, *factors1, outgate0, scaled_mid0, inverse_mid0 = call(
        between_kernel, "between", [edge, tile, *saved, wide, wide, row],
        [mask, tri0, pair, normed0, ngain, nbias, mgain, mbias, out_w, outgate_w, proj_w,
         gate_w],
        [wts, mid, big], 6 * dense,
    )
    edge1 = exchange(sent).reshape(grid[0])
    (here,) = call(
        functools.partial(triangle_kernel, True), "incoming", [tri_grid], [edge1], (), triangle,
    )
    tri1 = exchange(here.reshape(tri[0]))
    sent, new_t, cot_t, d_normed_gate1, out_grads1, small1 = call(
        turn_kernel, "turn", [tri, tile, wide, wide, out_rows, small(2)],
        [tri1, mid_t, normed1, cotangent, mgain, mbias, out_w, outgate_w],
        [mid, mid, flat, flat, flat, flat, sums(2)], 6 * dense,
    )
    d_tri1 = exchange(sent).reshape(tri_grid[0])
    (sent,) = call(
        functools.partial(edge_grad_kernel, True), "incoming_grad", [grid], [edge1, d_tri1],
        (), 2 * triangle,
    )
    d_edge1 = exchange(sent.reshape(edge[0]))
    proj_factor1, gate_factor1, scaled1, inverse1 = factors1
    sent, grad, d_normed_gate0, out_grads0, in_grads1, small_middle = call(
        middle_kernel, "middle", [tri, wide, wide, out_rows, in_rows, small(4)],
        [d_edge1, proj_factor1, gate_factor1, d_normed_gate1, scaled1, inverse1, cot_t, outgate0,
         scaled_mid0, inverse_mid0, normed0, normed1, ngain, mgain, mbias, proj_w, gate_w, out_w,
         outgate_w],
        [big, mid, flat, flat, flat, flat, flat, flat_in, back, sums(4)], 13 * dense,
    )
    d_tri0 = exchange(sent).reshape(tri_grid[0])
    (sent,) = call(
        functools.partial(edge_grad_kernel, False), "outgoing_grad", [grid], [edge0, d_tri0],
        (), 2 * triangle,
    )
    d_edge0 = exchange(sent.reshape(edge[0]))
    share = 12 * H // shards
    chips = shards // 2
    proj_factor0, gate_factor0, scaled0, inverse0 = factors0
    held = ((chips, share, H), BF16)
    own, other, d_in0 = call(
        functools.partial(finish_kernel, few), "finish", [held, held, flat_in],
        [d_edge0, proj_factor0, gate_factor0, normed0, out_grads0, in_grads1, out_grads1],
        [big, flat, ((12 * H, H), BF16)], 4 * dense,
    )
    other = swap_cores(other, many, few)
    d_normed0, extra, new_pair = call(
        norm_sums_kernel, "norm_sums", [wide, ((16, H), BF16), (pair.shape, BF16)],
        [d_in0, d_normed_gate0, scaled0, proj_w, gate_w, small_middle, small1, new_t],
        [back, sums(2)],
        4 * dense,
    )
    own, extra = call(add_kernel, "add_cores", [held, ((16, H), BF16)], [own, other, extra])
    parts = exchange_chips(own, many, few)
    (shared,) = call(
        sum_kernel, "sum_weights", [((chips, share + 16, H), BF16)], [parts, extra]
    )
    shared = exchange_chips(shared, many, few)
    other = swap_cores(shared, many, few)
    grad_pair, mine = call(
        functools.partial(grad_pair_kernel, share), "grad_pair",
        [(pair.shape, BF16), ((16, H), F32)],
        [shared, d_normed0, scaled0, inverse0, grad, ngain],
    )
    grad_proj, grad_gate, grad_out, grad_outgate, *vectors = call(
        functools.partial(unpack_kernel, share, few), "unpack",
        [(proj_w.shape, F32), (gate_w.shape, F32), (out_w.shape, F32), (outgate_w.shape, F32),
         (ngain.shape, F32), (nbias.shape, F32), (mgain.shape, F32), (mbias.shape, F32)],
        [shared, other, mine], [((12 * H, H), F32)],
    )
    return (
        new_pair,
        grad_pair,
        vectors[0],
        vectors[1],
        grad_proj,
        grad_gate,
        vectors[2],
        vectors[3],
        grad_out,
        grad_outgate,
    )


def norm_channels(values):
    average = jnp.mean(values, -1, keepdims=True)
    centred = values - average
    variance = jnp.mean(centred * centred, -1, keepdims=True)
    inverse = lax.rsqrt(variance + EPS)
    return (centred * inverse, inverse)


def forward_module(pair_in, pair_mask, weights, incoming):
    gain_in, bias_in, proj_w, gate_w, gain_mid, bias_mid, out_w, outgate_w = weights
    scaled_in, inverse_in = norm_channels(pair_in.astype(jnp.float32))
    normed = (scaled_in * gain_in + bias_in).astype(jnp.bfloat16)
    projected = product("ijc,sch->shij", normed, proj_w)
    gating = jax.nn.sigmoid(product("ijc,sch->shij", normed, gate_w))
    hidden = (projected * gating * pair_mask).astype(jnp.bfloat16)
    left_side, right_side = (
        lax.all_to_all(hidden[0], "row", split_axis=0, concat_axis=1, tiled=True),
        lax.all_to_all(hidden[1], "row", split_axis=0, concat_axis=1, tiled=True),
    )
    if incoming:
        left_side = jnp.swapaxes(left_side, 1, 2)
        right_side = jnp.swapaxes(right_side, 1, 2)
    else:
        left_side, right_side = (
            lax.all_to_all(left_side, "col", split_axis=1, concat_axis=2, tiled=True),
            lax.all_to_all(right_side, "col", split_axis=1, concat_axis=2, tiled=True),
        )
    triangle = product(
        "cik,cjk->cij", left_side, lax.all_gather(right_side, "col", axis=1, tiled=True)
    ).astype(jnp.bfloat16)
    triangle = lax.all_to_all(
        lax.all_to_all(triangle, "col", split_axis=2, concat_axis=1, tiled=True),
        "row",
        split_axis=1,
        concat_axis=0,
        tiled=True,
    )
    tri_values = triangle.astype(jnp.float32)
    total, squares = lax.psum((jnp.sum(tri_values, 0), jnp.sum(tri_values * tri_values, 0)), "ch")
    average = total / H
    inverse_mid = lax.rsqrt(squares / H - average * average + EPS)
    scaled_mid = (tri_values - average) * inverse_mid
    unit = (scaled_mid * gain_mid[:, None, None] + bias_mid[:, None, None]).astype(jnp.bfloat16)
    unit_full = lax.all_gather(unit, "ch", axis=0, tiled=True)
    outer = product("hij,hc->ijc", unit_full, out_w)
    outgate = jax.nn.sigmoid(product("ijc,cd->ijd", normed, outgate_w))
    result = (pair_in.astype(jnp.float32) + outer * outgate).astype(jnp.bfloat16)
    saved = (
        scaled_in,
        inverse_in,
        normed,
        projected,
        gating,
        left_side,
        right_side,
        scaled_mid,
        inverse_mid,
        unit_full,
        outer,
        outgate,
    )
    return (result, saved)


def backward_module(grad_out, pair_mask, weights, saved, incoming):
    gain_in, bias_in, proj_w, gate_w, gain_mid, bias_mid, out_w, outgate_w = weights
    (
        scaled_in,
        inverse_in,
        normed,
        projected,
        gating,
        left_side,
        right_side,
        scaled_mid,
        inverse_mid,
        unit_full,
        outer,
        outgate,
    ) = saved
    d_outer = (grad_out * outgate).astype(jnp.bfloat16)
    d_gatepre = (grad_out * outer * outgate * (1.0 - outgate)).astype(jnp.bfloat16)
    grad_out_w = product("hij,ijc->hc", unit_full, d_outer)
    grad_outgate_w = product("ijc,ijd->cd", normed, d_gatepre)
    width = gain_mid.shape[0]
    own_rows = lax.dynamic_slice_in_dim(out_w, lax.axis_index("ch") * width, width, 0)
    d_unit = product("ijc,hc->hij", d_outer, own_rows)
    d_normed = product("ijd,cd->ijc", d_gatepre, outgate_w)
    weighted = d_unit * gain_mid[:, None, None]
    grad_gain_mid = jnp.sum(d_unit * scaled_mid, (1, 2))
    grad_bias_mid = jnp.sum(d_unit, (1, 2))
    first_sum, second_sum = lax.psum(
        (jnp.sum(weighted, 0), jnp.sum(weighted * scaled_mid, 0)), "ch"
    )
    d_tri = (inverse_mid * (weighted - first_sum / H - scaled_mid * (second_sum / H))).astype(
        jnp.bfloat16
    )
    grad_rows = lax.all_to_all(d_tri, "row", split_axis=0, concat_axis=1, tiled=True)
    grad_cols = lax.all_to_all(grad_rows, "col", split_axis=1, concat_axis=2, tiled=True)
    d_left = product(
        "cij,cjk->cik", grad_cols, lax.all_gather(right_side, "col", axis=1, tiled=True)
    )
    partial_terms = product("cij,cik->cjk", grad_cols, left_side)
    d_right = lax.psum_scatter(
        partial_terms.astype(jnp.bfloat16), "col", scatter_dimension=1, tiled=True
    ).astype(jnp.float32)
    d_left = d_left.astype(jnp.bfloat16)
    d_right = d_right.astype(jnp.bfloat16)
    if incoming:
        d_left = jnp.swapaxes(d_left, 1, 2)
        d_right = jnp.swapaxes(d_right, 1, 2)
    else:
        d_left, d_right = (
            lax.all_to_all(d_left, "col", split_axis=2, concat_axis=1, tiled=True),
            lax.all_to_all(d_right, "col", split_axis=2, concat_axis=1, tiled=True),
        )
    d_left, d_right = (
        lax.all_to_all(d_left, "row", split_axis=1, concat_axis=0, tiled=True),
        lax.all_to_all(d_right, "row", split_axis=1, concat_axis=0, tiled=True),
    )
    d_hidden = jnp.stack([d_left, d_right]).astype(jnp.float32)
    d_proj = (d_hidden * gating * pair_mask).astype(jnp.bfloat16)
    d_gate = (d_hidden * projected * gating * (1.0 - gating) * pair_mask).astype(jnp.bfloat16)
    grad_proj_w = product("ijc,shij->sch", normed, d_proj)
    grad_gate_w = product("ijc,shij->sch", normed, d_gate)
    partial_input = product("shij,sch->ijc", d_proj, proj_w) + product(
        "shij,sch->ijc", d_gate, gate_w
    )
    d_normed = d_normed + lax.psum(partial_input.astype(jnp.bfloat16), "ch").astype(jnp.float32)
    weighted_in = d_normed * gain_in
    grad_gain_in = jnp.sum(d_normed * scaled_in, (0, 1))
    grad_bias_in = jnp.sum(d_normed, (0, 1))
    d_pair = inverse_in * (
        weighted_in
        - jnp.mean(weighted_in, -1, keepdims=True)
        - scaled_in * jnp.mean(weighted_in * scaled_in, -1, keepdims=True)
    )
    grads = (
        grad_gain_in,
        grad_bias_in,
        grad_proj_w,
        grad_gate_w,
        grad_gain_mid,
        grad_bias_mid,
        grad_out_w,
        grad_outgate_w,
    )
    return (grad_out + d_pair, grads)


def per_device(
    pair,
    cotangent,
    lengths,
    norm_gain,
    norm_bias,
    proj_weight,
    gate_weight,
    mid_gain,
    mid_bias,
    out_weight,
    outgate_weight,
):
    rows_here = pair.shape[0]
    cols_here = pair.shape[1]
    row_ids = lax.axis_index("row") * rows_here + lax.iota(jnp.int32, rows_here)
    col_ids = lax.axis_index("col") * cols_here + lax.iota(jnp.int32, cols_here)
    limit = lengths[0]
    pair_mask = ((row_ids[:, None] < limit) & (col_ids[None, :] < limit)).astype(jnp.float32)
    state = pair
    stash = []
    for layer in range(2):
        weights = (
            norm_gain[layer],
            norm_bias[layer],
            proj_weight[layer],
            gate_weight[layer],
            mid_gain[layer],
            mid_bias[layer],
            out_weight[layer],
            outgate_weight[layer],
        )
        state, saved = forward_module(state, pair_mask, weights, layer == 1)
        stash.append(saved)
    grad_state = cotangent.astype(jnp.float32)
    per_layer = [None, None]
    for layer in (1, 0):
        weights = (
            norm_gain[layer],
            norm_bias[layer],
            proj_weight[layer],
            gate_weight[layer],
            mid_gain[layer],
            mid_bias[layer],
            out_weight[layer],
            outgate_weight[layer],
        )
        grad_state, grads = backward_module(
            grad_state, pair_mask, weights, stash[layer], layer == 1
        )
        per_layer[layer] = grads
    lower = per_layer[0]
    upper = per_layer[1]
    summed = lax.psum(
        (
            lower[0],
            lower[1],
            lower[2],
            lower[3],
            lower[4],
            lower[5],
            lower[6],
            lower[7],
            upper[0],
            upper[1],
            upper[2],
            upper[3],
            upper[4],
            upper[5],
            upper[6],
            upper[7],
        ),
        ("row", "col"),
    )
    per_layer = [summed[0:8], summed[8:16]]
    stacked = [jnp.stack([per_layer[0][index], per_layer[1][index]]) for index in range(8)]
    return (
        state,
        grad_state.astype(jnp.bfloat16),
        stacked[0],
        stacked[1],
        stacked[2],
        stacked[3],
        stacked[4],
        stacked[5],
        stacked[6],
        stacked[7],
    )


def on_device(pair, *rest, many, few, split):
    rows, lanes, channels = pair.shape
    shards = many * few
    whole_channels = split == 1 and H % shards == 0 and BLOCK % (H // shards) == 0 and H % (2 * BLOCK) == 0
    tiles = rows == BLOCK and lanes % 128 == 0 and channels == H
    if whole_channels and tiles and many % 2 == 0 and few & (few - 1) == 0:
        return grouped_device(pair, *rest, many=many, few=few)
    return per_device(pair, *rest)


def solution(mesh):
    in_specs = (
        P(("grp", "row"), "col", None),
        P(("grp", "row"), "col", None),
        P("grp"),
        P(),
        P(),
        P(None, None, None, "ch"),
        P(None, None, None, "ch"),
        P(None, "ch"),
        P(None, "ch"),
        P(),
        P(),
    )
    out_specs = (
        P(("grp", "row"), "col", None),
        P(("grp", "row"), "col", None),
        P("grp", None),
        P("grp", None),
        P("grp", None, None, "ch"),
        P("grp", None, None, "ch"),
        P("grp", "ch"),
        P("grp", "ch"),
        P("grp", None, None),
        P("grp", None, None),
    )
    body = functools.partial(
        on_device, many=mesh.shape["row"], few=mesh.shape["col"], split=mesh.shape["ch"]
    )
    return jax.shard_map(
        body, mesh=mesh, in_specs=in_specs, out_specs=out_specs, check_vma=False
    )
```

```python
import functools

import jax
import jax.numpy as jnp
from jax import lax
from jax.experimental import pallas as pl
from jax.experimental.pallas import tpu as pltpu
from jax.sharding import PartitionSpec as P

H = 128


EPS = 1e-05


def product(spec, left, right):
    return jnp.einsum(spec, left, right, preferred_element_type=jnp.float32)


F32 = jnp.float32
BF16 = jnp.bfloat16


def dot(left, right):
    return lax.dot_general(left, right, (((1,), (0,)), ((), ())), preferred_element_type=F32)


def dot_rt(left, right):
    return lax.dot_general(left, right, (((1,), (1,)), ((), ())), preferred_element_type=F32)


def dot_lt(left, right):
    return lax.dot_general(left, right, (((0,), (0,)), ((), ())), preferred_element_type=F32)


def sigmoid_of_minus(values):
    return 1.0 / (1.0 + jnp.exp(values))


def norm_rows(values):
    scale = 1.0 / values.shape[0]
    average = jnp.sum(values, 0, keepdims=True) * scale
    centred = values - average
    variance = jnp.sum(centred * centred, 0, keepdims=True) * scale
    inverse = lax.rsqrt(variance + EPS)
    return centred * inverse, inverse


def turned(weight):
    return jnp.transpose(weight)


def column(ref, module, lanes):
    row = ref[module : module + 1, :]
    return beside(*[jnp.transpose(jnp.broadcast_to(row, (lanes, row.shape[1])))] * 2)


def beside(left, right):
    return jnp.concatenate([left, right], axis=-1)


def pair_of(ref, step):
    return beside(ref[2 * step], ref[2 * step + 1])


def put_pair(ref, step, values):
    lanes = ref.shape[-1]
    ref[2 * step] = values[:, :lanes]
    ref[2 * step + 1] = values[:, lanes:]


def pair_of_rows(ref, step):
    return beside(ref[2 * step : 2 * step + 1, :], ref[2 * step + 1 : 2 * step + 2, :])


def put_pair_of_rows(ref, step, values):
    lanes = ref.shape[-1]
    ref[2 * step : 2 * step + 1, :] = values[:, :lanes]
    ref[2 * step + 1 : 2 * step + 2, :] = values[:, lanes:]


def turned_pair(ref, step):
    return beside(jnp.transpose(ref[2 * step]), jnp.transpose(ref[2 * step + 1])).astype(F32)


def put_turned_pair(ref, step, values):
    lanes = ref.shape[1]
    values = values.astype(BF16)
    ref[2 * step] = jnp.transpose(values[:, :lanes])
    ref[2 * step + 1] = jnp.transpose(values[:, lanes:])


def as_row(total):
    return jnp.sum(jnp.transpose(total), 0, keepdims=True)


def row_mask(lengths_ref, step, rows, lanes):
    limit = lengths_ref[0]
    row_id = lax.axis_index("row") * rows + step
    col_id = lax.axis_index("col") * lanes + lax.broadcasted_iota(jnp.int32, (1, lanes), 1)
    return jnp.where((row_id < limit) & (col_id < limit), 1.0, 0.0).astype(F32)


def load_in_weights(proj_ref, gate_ref, module, scratch):
    width = proj_ref.shape[-1]
    for side in range(2):
        scratch[side * width : (side + 1) * width, :] = turned(proj_ref[module, side])
        scratch[(2 + side) * width : (3 + side) * width, :] = -turned(gate_ref[module, side])


def load_back_weights(proj_ref, gate_ref, module, scratch):
    width = proj_ref.shape[-1]
    for side in range(2):
        scratch[:, side * width : (side + 1) * width] = proj_ref[module, side]
        scratch[:, (2 + side) * width : (3 + side) * width] = gate_ref[module, side]


BLOCK = 16


def turn_matrix(rows):
    size = BLOCK * rows
    out = lax.broadcasted_iota(jnp.int32, (size, size), 0)
    source = lax.broadcasted_iota(jnp.int32, (size, size), 1)
    return jnp.where(source == (out % rows) * BLOCK + out // rows, 1.0, 0.0).astype(BF16)


def spread_blocks(matrix, scratch, start, group):
    rows, _, lanes = scratch.shape
    blocks = [
        scratch[:, at : at + BLOCK, :].reshape(rows * BLOCK, lanes)
        for at in (start, start + BLOCK)
    ]
    both = dot(matrix, beside(*blocks)).astype(BF16)
    parts = [
        part.reshape(BLOCK // group, group, rows, lanes)
        for part in (both[:, :lanes], both[:, lanes:])
    ]
    return jnp.concatenate(parts, axis=0)


def collect_blocks(matrix, values, scratch, start):
    rows, _, lanes = scratch.shape
    flat = values.reshape(2, BLOCK * rows, lanes)
    both = dot(matrix, beside(flat[0], flat[1])).astype(BF16)
    for at, part in ((start, both[:, :lanes]), (start + BLOCK, both[:, lanes:])):
        scratch[:, at : at + BLOCK, :] = part.reshape(rows, BLOCK, lanes)


def spread_edges(scratch, out_ref):
    shards, sides, group, rows, lanes = out_ref.shape
    matrix, step = turn_matrix(rows), 2 * BLOCK // group
    for side in range(sides):
        for shard in range(0, shards, step):
            start = (side * shards + shard) * group
            out_ref[shard : shard + step, side] = spread_blocks(matrix, scratch, start, group)


def collect_edges(in_ref, scratch):
    shards, sides, group, rows, lanes = in_ref.shape
    matrix, step = turn_matrix(rows), 2 * BLOCK // group
    for side in range(sides):
        for shard in range(0, shards, step):
            start = (side * shards + shard) * group
            collect_blocks(matrix, in_ref[shard : shard + step, side], scratch, start)


def spread_triangle(scratch, out_ref):
    shards, group, rows, lanes = out_ref.shape
    matrix, step = turn_matrix(rows), 2 * BLOCK // group
    for shard in range(0, shards, step):
        out_ref[shard : shard + step] = spread_blocks(matrix, scratch, shard * group, group)


def collect_triangle(in_ref, scratch):
    shards, group, rows, lanes = in_ref.shape
    matrix, step = turn_matrix(rows), 2 * BLOCK // group
    for shard in range(0, shards, step):
        collect_blocks(matrix, in_ref[shard : shard + step], scratch, shard * group)


def each_pair(rows, body, sums=None):
    for block in range(0, rows // 2, 2):
        parts = [body(block + step) for step in range(2)]
        for index in range(0 if sums is None else sums.shape[0]):
            total = parts[0][index] + parts[1][index]
            lanes = sums.shape[-1]
            sums[index] += total[:, :lanes] + total[:, lanes:]


def mid_norm(tri):
    scale = 1.0 / tri.shape[0]
    average = jnp.sum(tri, 0, keepdims=True) * scale
    squares = jnp.sum(tri * tri, 0, keepdims=True) * scale
    inverse = lax.rsqrt(squares - average * average + EPS)
    return (tri - average) * inverse, inverse


def norm_backward(weighted, scaled, inverse):
    scale = 1.0 / weighted.shape[0]
    first = jnp.sum(weighted, 0, keepdims=True) * scale
    second = jnp.sum(weighted * scaled, 0, keepdims=True) * scale
    return inverse * (weighted - first - scaled * second)


def save_norm(step, values, scaled_out, inverse_out):
    scaled, inverse = norm_rows(values)
    put_pair(scaled_out, step, scaled)
    put_pair_of_rows(inverse_out, step, inverse)
    return scaled


def save_edges(step, normed, in_weights, mask, proj_out, gate_out):
    pre = dot(in_weights, normed)
    half = pre.shape[0] // 2
    gating = sigmoid_of_minus(pre[half:])
    factor = gating * mask
    value = pre[:half] * factor
    put_pair(proj_out, step, factor.astype(BF16))
    put_pair(gate_out, step, (value * (1.0 - gating)).astype(BF16))
    return value.astype(BF16)


def start_kernel(
    lengths, pair_far, ngain_far, nbias_far, proj_far, gate_far,
    edge_out, normed_out, proj_out, gate_out, scaled_out, inverse_out, mask_out,
    pair, ngain, nbias, proj_w, gate_w, sems, wts, scr,
):
    far = (proj_far.at[0], gate_far.at[0], ngain_far, nbias_far, pair_far)
    near = (proj_w.at[0], gate_w.at[0], ngain, nbias, pair)
    copies = [
        pltpu.make_async_copy(source, target, sems.at[index])
        for index, (source, target) in enumerate(zip(far, near))
    ]
    for copy in copies:
        copy.start()
    for copy in copies:
        copy.wait()
    rows, lanes, channels = pair.shape
    load_in_weights(proj_w, gate_w, 0, wts)
    gain, bias = column(ngain, 0, lanes), column(nbias, 0, lanes)

    def body(step):
        base = turned_pair(pair, step)
        scaled = save_norm(step, base, scaled_out, inverse_out)
        normed = (scaled * gain + bias).astype(BF16)
        put_pair(normed_out, step, normed)
        mask = beside(*[row_mask(lengths, 2 * step + row, rows, lanes) for row in range(2)])
        put_pair_of_rows(mask_out, step, mask)
        put_pair(scr, step, save_edges(step, normed, wts[...], mask, proj_out, gate_out))

    each_pair(rows, body)
    spread_edges(scr, edge_out)


def between_kernel(
    mask_all, tri, pair, normed0, ngain, nbias, mgain, mbias, out_w, outgate_w, proj_w, gate_w,
    edge_out, mid_out, normed_out, proj_out, gate_out, scaled_out, inverse_out,
    outgate_out, scaled_mid_out, inverse_mid_out, wts, tri_in, scr,
):
    rows, lanes, channels = pair.shape
    load_in_weights(proj_w, gate_w, 1, wts)
    out_t, outgate_t = turned(out_w[0]), -turned(outgate_w[0])
    gain, bias = column(ngain, 1, lanes), column(nbias, 1, lanes)
    gain_mid, bias_mid = column(mgain, 0, lanes), column(mbias, 0, lanes)
    collect_triangle(tri, tri_in)

    def body(step):
        scaled_mid, inverse_mid = mid_norm(pair_of(tri_in, step).astype(F32))
        put_pair(scaled_mid_out, step, scaled_mid)
        put_pair_of_rows(inverse_mid_out, step, inverse_mid)
        unit = (scaled_mid * gain_mid + bias_mid).astype(BF16)
        outer = dot(out_t, unit)
        outgate = sigmoid_of_minus(dot(outgate_t, pair_of(normed0, step)))
        put_pair(outgate_out, step, outgate)
        mid = (turned_pair(pair, step) + outer * outgate).astype(BF16)
        put_pair(mid_out, step, mid)
        scaled = save_norm(step, mid.astype(F32), scaled_out, inverse_out)
        normed = (scaled * gain + bias).astype(BF16)
        put_pair(normed_out, step, normed)
        mask = pair_of_rows(mask_all, step)
        put_pair(scr, step, save_edges(step, normed, wts[...], mask, proj_out, gate_out))

    each_pair(rows, body)
    spread_edges(scr, edge_out)


def out_weight_grads(unit, d_outer, normed, d_gatepre, out_ref):
    width = unit.shape[0]
    out_ref[0:width, :] = dot_rt(unit[...], d_outer[...]).astype(out_ref.dtype)
    out_ref[width:, :] = dot_rt(normed[...], d_gatepre[...]).astype(out_ref.dtype)


def in_weight_grads(normed_all, d_in_all, out_ref):
    width = normed_all.shape[0]
    for part in range(d_in_all.shape[0] // width):
        block = slice(part * width, (part + 1) * width)
        out_ref[block, :] = dot_rt(normed_all[...], d_in_all[block, :]).astype(out_ref.dtype)


def lane_block(step, lanes):
    return pl.ds(2 * step * lanes, 2 * lanes)


def turn_kernel(
    tri, mid, normed, cot, mgain, mbias, out_w, outgate_w,
    d_tri_out, new_out, grad_out, d_normed_out, weights_out, small_out,
    tri_in, scr, unit_all, outer_all, normed_all, gate_all, sums,
):
    rows, channels, lanes = mid.shape
    out_t, outgate_t = turned(out_w[1]), -turned(outgate_w[1])
    gain_mid, bias_mid = column(mgain, 1, lanes), column(mbias, 1, lanes)
    collect_triangle(tri, tri_in)
    sums[...] = jnp.zeros_like(sums)

    def body(step):
        here = lane_block(step, lanes)
        grad = turned_pair(cot, step)
        put_pair(grad_out, step, grad)
        here_normed = pair_of(normed, step)
        outgate = sigmoid_of_minus(dot(outgate_t, here_normed))
        gated = grad * outgate
        d_outer = gated.astype(BF16)
        d_unit = dot(out_w[1], d_outer)
        scaled_mid, inverse_mid = mid_norm(pair_of(tri_in, step).astype(F32))
        d_tri = norm_backward(d_unit * gain_mid, scaled_mid, inverse_mid)
        put_pair(scr, step, d_tri.astype(BF16))
        unit = (scaled_mid * gain_mid + bias_mid).astype(BF16)
        outer = dot(out_t, unit)
        put_pair(new_out, step, (pair_of(mid, step).astype(F32) + outer * outgate).astype(BF16))
        d_gatepre = (gated * outer * (1.0 - outgate)).astype(BF16)
        put_pair(d_normed_out, step, dot(outgate_w[1], d_gatepre))
        unit_all[:, here] = unit
        outer_all[:, here] = d_outer
        normed_all[:, here] = here_normed
        gate_all[:, here] = d_gatepre
        return d_unit * scaled_mid, d_unit

    each_pair(rows, body, sums)
    spread_triangle(scr, d_tri_out)
    out_weight_grads(unit_all, outer_all, normed_all, gate_all, weights_out)
    for index in range(2):
        small_out[index : index + 1, :] = as_row(sums[index])


def edge_backward(step, scratch, proj_factor, gate_factor):
    here = pair_of(scratch, step).astype(F32)
    d_proj = (here * pair_of(proj_factor, step).astype(F32)).astype(BF16)
    d_gate = (here * pair_of(gate_factor, step).astype(F32)).astype(BF16)
    return jnp.concatenate([d_proj, d_gate], axis=0)


def middle_kernel(
    d_edge, proj_factor, gate_factor, d_normed_gate, scaled_in, inverse_in, cot, outgate,
    scaled_mid, inverse_mid, normed0, normed1, ngain, mgain, mbias, proj_w, gate_w, out_w,
    outgate_w,
    d_tri_out, grad_out, d_normed_out, out_weights, in_weights, small_out,
    scr, scr_tri, unit_all, outer_all, normed_all, gate_all, upper_all, d_in_all, back, sums,
):
    rows, channels, lanes = cot.shape
    out_t = turned(out_w[0])
    gain = column(ngain, 1, lanes)
    gain_mid, bias_mid = column(mgain, 0, lanes), column(mbias, 0, lanes)
    collect_edges(d_edge, scr)
    sums[...] = jnp.zeros_like(sums)
    load_back_weights(proj_w, gate_w, 1, back)

    def upper(step):
        place = lane_block(step, lanes)
        d_in = edge_backward(step, scr, proj_factor, gate_factor)
        d_in_all[:, place] = d_in
        upper_all[:, place] = pair_of(normed1, step)
        d_normed = pair_of(d_normed_gate, step) + dot(back[...], d_in)
        scaled = pair_of(scaled_in, step)
        grad = pair_of(cot, step) + norm_backward(
            d_normed * gain, scaled, pair_of_rows(inverse_in, step)
        )
        put_pair(grad_out, step, grad)
        return d_normed * scaled, d_normed

    def lower(step):
        place = lane_block(step, lanes)
        gate = pair_of(outgate, step)
        gated = pair_of(grad_out, step) * gate
        d_outer = gated.astype(BF16)
        d_unit = dot(out_w[0], d_outer)
        scaled = pair_of(scaled_mid, step)
        d_tri = norm_backward(d_unit * gain_mid, scaled, pair_of_rows(inverse_mid, step))
        put_pair(scr_tri, step, d_tri.astype(BF16))
        unit = (scaled * gain_mid + bias_mid).astype(BF16)
        outer = dot(out_t, unit)
        d_gatepre = (gated * outer * (1.0 - gate)).astype(BF16)
        put_pair(d_normed_out, step, dot(outgate_w[0], d_gatepre))
        unit_all[:, place] = unit
        outer_all[:, place] = d_outer
        normed_all[:, place] = pair_of(normed0, step)
        gate_all[:, place] = d_gatepre
        return d_unit * scaled, d_unit

    each_pair(rows, upper, sums.at[2:4])
    each_pair(rows, lower, sums.at[0:2])
    spread_triangle(scr_tri, d_tri_out)
    out_weight_grads(unit_all, outer_all, normed_all, gate_all, out_weights)
    in_weight_grads(upper_all, d_in_all, in_weights)
    for index in range(4):
        small_out[index : index + 1, :] = as_row(sums[index])


def split_cores(all_rows, own_out, other_out, few):
    chips, share, width = own_out.shape
    view = all_rows.reshape(chips // few, 2, few, share, width)
    core = lax.rem(lax.axis_index("row"), 2)
    own_out[...] = view[:, core].reshape(own_out.shape)
    other_out[...] = view[:, 1 - core].reshape(other_out.shape)


def finish_kernel(
    few, d_edge, proj_factor, gate_factor, normed, out0, in1, out1,
    own_out, other_out, d_in_all, scr, normed_all, packed,
):
    rows, half, lanes = proj_factor.shape
    collect_edges(d_edge, scr)

    def body(step):
        place = lane_block(step, lanes)
        d_in_all[:, place] = edge_backward(step, scr, proj_factor, gate_factor)
        normed_all[:, place] = pair_of(normed, step)

    each_pair(rows, body)
    first, second, third = d_in_all.shape[0], out0.shape[0], in1.shape[0]
    in_weight_grads(normed_all, d_in_all, packed.at[0:first])
    packed[first : first + second, :] = out0[...]
    packed[first + second : first + second + third, :] = in1[...]
    packed[first + second + third :, :] = out1[...]
    split_cores(packed, own_out, other_out, few)


def norm_sums_kernel(
    d_in, d_normed_gate, scaled_in, proj_w, gate_w, small_middle, small1, new_t,
    d_normed_out, extra_out, new_out, back, sums,
):
    rows, channels, lanes = scaled_in.shape
    sums[...] = jnp.zeros_like(sums)
    load_back_weights(proj_w, gate_w, 0, back)

    def body(step):
        here = d_in[:, lane_block(step, lanes)]
        d_normed = pair_of(d_normed_gate, step) + dot(back[...], here)
        put_pair(d_normed_out, step, d_normed)
        put_turned_pair(new_out, step, pair_of(new_t, step))
        return d_normed * pair_of(scaled_in, step), d_normed

    each_pair(rows, body, sums)
    small = jnp.concatenate(
        [as_row(sums[0]), as_row(sums[1]), small_middle[0:2], small_middle[2:4], small1[...]],
        axis=0,
    )
    high = small.astype(BF16).astype(F32)
    extra_out[...] = jnp.concatenate([high, small - high], axis=0).astype(BF16)


def add_kernel(first, second, extra, out_ref, extra_out):
    out_ref[...] = (first[...].astype(F32) + second[...].astype(F32)).astype(BF16)
    extra_out[...] = extra[...]


def sum_kernel(parts, extra, shared_out):
    chips, share, width = parts.shape
    own = jnp.sum(parts[...].astype(F32), axis=0).astype(BF16)
    for chip in range(chips):
        shared_out[chip, 0:share] = own
        shared_out[chip, share:] = extra[...]


def grad_pair_kernel(
    share, shared, d_normed, scaled_in, inverse_in, grad, ngain, grad_out, mine_out
):
    rows, channels, lanes = grad.shape
    gain = column(ngain, 0, lanes)
    mine_out[...] = jnp.sum(shared[:, share:].astype(F32), axis=0)

    def body(step):
        total = pair_of(grad, step) + norm_backward(
            pair_of(d_normed, step) * gain, pair_of(scaled_in, step),
            pair_of_rows(inverse_in, step),
        )
        put_turned_pair(grad_out, step, total)

    each_pair(rows, body)


def unpack_kernel(
    share, few, own, other, mine, proj_out, gate_out, out_out, outgate_out,
    norm_gain_out, norm_bias_out, mid_gain_out, mid_bias_out, weights,
):
    chips, _, width = own.shape
    core = lax.rem(lax.axis_index("row"), 2)
    view = weights.reshape(chips // few, 2, few, share, width)
    block = (chips // few, few, share, width)
    view[:, core] = own[:, 0:share].astype(F32).reshape(block)
    view[:, 1 - core] = other[:, 0:share].astype(F32).reshape(block)
    total = mine[...] + jnp.sum(other[:, share:].astype(F32), axis=0)
    total = total[0:8] + total[8:16]
    for module in range(2):
        for index, out in enumerate((norm_gain_out, norm_bias_out, mid_gain_out, mid_bias_out)):
            at = 4 * module + index
            out[module : module + 1, :] = total[at : at + 1]
        blocks = [
            weights[(6 * module + part) * width : (6 * module + part + 1) * width, :]
            for part in range(6)
        ]
        for side in range(2):
            proj_out[module, side] = blocks[side]
            gate_out[module, side] = blocks[2 + side]
        out_out[module] = blocks[4]
        outgate_out[module] = blocks[5]


def triangle_kernel(incoming, edge, tri_out):
    many, few, _, group, rows, lanes = edge.shape

    def whole(side, channel):
        parts = [edge[:, c, side, channel].reshape(many * rows, lanes) for c in range(few)]
        return jnp.concatenate(parts, axis=1)

    for channel in range(group):
        left, right = whole(0, channel), whole(1, channel)
        tri = (dot_lt if incoming else dot_rt)(left, right).astype(BF16)
        for c in range(few):
            part = tri[:, c * lanes : (c + 1) * lanes]
            tri_out[:, c, channel] = part.reshape(many, rows, lanes)


def edge_grad_kernel(incoming, edge, d_tri, grad_out):
    many, few, _, group, rows, lanes = edge.shape

    def whole(ref, *index):
        parts = [ref[(slice(None), c) + index].reshape(many * rows, lanes) for c in range(few)]
        return jnp.concatenate(parts, axis=1)

    for channel in range(group):
        left, right = whole(edge, 0, channel), whole(edge, 1, channel)
        grad = whole(d_tri, channel)
        if incoming:
            d_left, d_right = dot_rt(right, grad), dot(left, grad)
        else:
            d_left, d_right = dot(grad, right), dot_lt(grad, left)
        for side, value in ((0, d_left), (1, d_right)):
            value = value.astype(BF16)
            for c in range(few):
                part = value[:, c * lanes : (c + 1) * lanes]
                grad_out[:, c, side, channel] = part.reshape(many, rows, lanes)


SCALARS = pl.BlockSpec(memory_space=pltpu.SMEM)
VECTORS = pl.BlockSpec(memory_space=pltpu.VMEM)
FAR = pl.BlockSpec(memory_space=pltpu.HBM)


def call(kernel, name, outs, args, scratch=(), flops=0, grant=16, specs=None):
    shapes = [jax.ShapeDtypeStruct(shape, dtype) for shape, dtype in outs]
    moved = sum(a.size * a.dtype.itemsize for a in list(args) + shapes)
    return pl.pallas_call(
        kernel,
        name=name,
        out_shape=shapes,
        in_specs=specs or [VECTORS] * len(args),
        out_specs=[VECTORS] * len(shapes),
        scratch_shapes=[
            pltpu.VMEM(*item) if isinstance(item, tuple) else item for item in scratch
        ],
        compiler_params=pltpu.CompilerParams(vmem_limit_bytes=grant * 1024 * 1024),
        cost_estimate=pl.CostEstimate(flops=flops, bytes_accessed=moved, transcendentals=0),
    )(*args)


def exchange(values):
    return lax.all_to_all(values, ("row", "col"), split_axis=0, concat_axis=0, tiled=True)


def swap_cores(values, many, few):
    pairs = [(index, index ^ few) for index in range(many * few)]
    return lax.ppermute(values, ("row", "col"), pairs)


def exchange_chips(values, many, few):
    groups = [
        [row * few + col for row in range(core, many, 2) for col in range(few)] for core in range(2)
    ]
    return lax.all_to_all(
        values, ("row", "col"), split_axis=0, concat_axis=0, axis_index_groups=groups, tiled=True
    )


def grouped_device(
    pair, cotangent, lengths, ngain, nbias, proj_w, gate_w, mgain, mbias, out_w, outgate_w,
    *, many, few,
):
    rows, lanes, channels = pair.shape
    shards = many * few
    group = H // shards
    edge = ((shards, 2, group, rows, lanes), BF16)
    grid = ((many, few, 2, group, rows, lanes), BF16)
    tri = ((shards, group, rows, lanes), BF16)
    tri_grid = ((many, few, group, rows, lanes), BF16)
    tile = ((rows, channels, lanes), BF16)
    wide = ((rows, channels, lanes), F32)
    row = ((rows, lanes), F32)
    factor = ((rows, 2 * H, lanes), BF16)
    back = ((channels, 4 * H), BF16)
    wts = ((4 * H, channels), BF16)
    big = ((rows, 2 * H, lanes), BF16)
    mid = ((rows, H, lanes), BF16)
    positions = rows * lanes
    flat = ((H, positions), BF16)
    flat_in = ((4 * H, positions), BF16)
    out_rows = ((2 * H, channels), BF16)
    in_rows = ((4 * H, H), BF16)
    triangle = 2 * group * (many * rows) ** 2 * (few * lanes)
    dense = 2 * positions * channels * H

    def sums(count):
        return ((count, H, lanes), F32)

    def small(count):
        return ((count, H), F32)

    saved = [tile, factor, factor, wide, row]
    far = [
        pltpu.with_memory_space_constraint(item, pltpu.HBM)
        for item in (pair, ngain, nbias, proj_w, gate_w)
    ]
    sent, normed0, *factors0, mask = call(
        start_kernel, "start", [edge, *saved, row], [lengths, *far],
        [(pair.shape, BF16), (ngain.shape, F32), (nbias.shape, F32), (proj_w.shape, BF16),
         (gate_w.shape, BF16), pltpu.SemaphoreType.DMA((5,)), wts, big],
        4 * dense, specs=[SCALARS] + [FAR] * len(far),
    )
    edge0 = exchange(sent).reshape(grid[0])
    (here,) = call(
        functools.partial(triangle_kernel, False), "outgoing", [tri_grid], [edge0], (), triangle,
    )
    tri0 = exchange(here.reshape(tri[0]))
    sent, mid_t, normed1, *factors1, outgate0, scaled_mid0, inverse_mid0 = call(
        between_kernel, "between", [edge, tile, *saved, wide, wide, row],
        [mask, tri0, pair, normed0, ngain, nbias, mgain, mbias, out_w, outgate_w, proj_w,
         gate_w],
        [wts, mid, big], 6 * dense,
    )
    edge1 = exchange(sent).reshape(grid[0])
    (here,) = call(
        functools.partial(triangle_kernel, True), "incoming", [tri_grid], [edge1], (), triangle,
    )
    tri1 = exchange(here.reshape(tri[0]))
    sent, new_t, cot_t, d_normed_gate1, out_grads1, small1 = call(
        turn_kernel, "turn", [tri, tile, wide, wide, out_rows, small(2)],
        [tri1, mid_t, normed1, cotangent, mgain, mbias, out_w, outgate_w],
        [mid, mid, flat, flat, flat, flat, sums(2)], 6 * dense,
    )
    d_tri1 = exchange(sent).reshape(tri_grid[0])
    (sent,) = call(
        functools.partial(edge_grad_kernel, True), "incoming_grad", [grid], [edge1, d_tri1],
        (), 2 * triangle,
    )
    d_edge1 = exchange(sent.reshape(edge[0]))
    proj_factor1, gate_factor1, scaled1, inverse1 = factors1
    sent, grad, d_normed_gate0, out_grads0, in_grads1, small_middle = call(
        middle_kernel, "middle", [tri, wide, wide, out_rows, in_rows, small(4)],
        [d_edge1, proj_factor1, gate_factor1, d_normed_gate1, scaled1, inverse1, cot_t, outgate0,
         scaled_mid0, inverse_mid0, normed0, normed1, ngain, mgain, mbias, proj_w, gate_w, out_w,
         outgate_w],
        [big, mid, flat, flat, flat, flat, flat, flat_in, back, sums(4)], 13 * dense,
    )
    d_tri0 = exchange(sent).reshape(tri_grid[0])
    (sent,) = call(
        functools.partial(edge_grad_kernel, False), "outgoing_grad", [grid], [edge0, d_tri0],
        (), 2 * triangle,
    )
    d_edge0 = exchange(sent.reshape(edge[0]))
    share = 12 * H // shards
    chips = shards // 2
    proj_factor0, gate_factor0, scaled0, inverse0 = factors0
    held = ((chips, share, H), BF16)
    own, other, d_in0 = call(
        functools.partial(finish_kernel, few), "finish", [held, held, flat_in],
        [d_edge0, proj_factor0, gate_factor0, normed0, out_grads0, in_grads1, out_grads1],
        [big, flat, ((12 * H, H), BF16)], 4 * dense,
    )
    other = swap_cores(other, many, few)
    d_normed0, extra, new_pair = call(
        norm_sums_kernel, "norm_sums", [wide, ((16, H), BF16), (pair.shape, BF16)],
        [d_in0, d_normed_gate0, scaled0, proj_w, gate_w, small_middle, small1, new_t],
        [back, sums(2)],
        4 * dense,
    )
    own, extra = call(add_kernel, "add_cores", [held, ((16, H), BF16)], [own, other, extra])
    parts = exchange_chips(own, many, few)
    (shared,) = call(
        sum_kernel, "sum_weights", [((chips, share + 16, H), BF16)], [parts, extra]
    )
    shared = exchange_chips(shared, many, few)
    other = swap_cores(shared, many, few)
    grad_pair, mine = call(
        functools.partial(grad_pair_kernel, share), "grad_pair",
        [(pair.shape, BF16), ((16, H), F32)],
        [shared, d_normed0, scaled0, inverse0, grad, ngain],
    )
    grad_proj, grad_gate, grad_out, grad_outgate, *vectors = call(
        functools.partial(unpack_kernel, share, few), "unpack",
        [(proj_w.shape, F32), (gate_w.shape, F32), (out_w.shape, F32), (outgate_w.shape, F32),
         (ngain.shape, F32), (nbias.shape, F32), (mgain.shape, F32), (mbias.shape, F32)],
        [shared, other, mine], [((12 * H, H), F32)],
    )
    return (
        new_pair,
        grad_pair,
        vectors[0],
        vectors[1],
        grad_proj,
        grad_gate,
        vectors[2],
        vectors[3],
        grad_out,
        grad_outgate,
    )


def norm_channels(values):
    average = jnp.mean(values, -1, keepdims=True)
    centred = values - average
    variance = jnp.mean(centred * centred, -1, keepdims=True)
    inverse = lax.rsqrt(variance + EPS)
    return (centred * inverse, inverse)


def forward_module(pair_in, pair_mask, weights, incoming):
    gain_in, bias_in, proj_w, gate_w, gain_mid, bias_mid, out_w, outgate_w = weights
    scaled_in, inverse_in = norm_channels(pair_in.astype(jnp.float32))
    normed = (scaled_in * gain_in + bias_in).astype(jnp.bfloat16)
    projected = product("ijc,sch->shij", normed, proj_w)
    gating = jax.nn.sigmoid(product("ijc,sch->shij", normed, gate_w))
    hidden = (projected * gating * pair_mask).astype(jnp.bfloat16)
    left_side, right_side = (
        lax.all_to_all(hidden[0], "row", split_axis=0, concat_axis=1, tiled=True),
        lax.all_to_all(hidden[1], "row", split_axis=0, concat_axis=1, tiled=True),
    )
    if incoming:
        left_side = jnp.swapaxes(left_side, 1, 2)
        right_side = jnp.swapaxes(right_side, 1, 2)
    else:
        left_side, right_side = (
            lax.all_to_all(left_side, "col", split_axis=1, concat_axis=2, tiled=True),
            lax.all_to_all(right_side, "col", split_axis=1, concat_axis=2, tiled=True),
        )
    triangle = product(
        "cik,cjk->cij", left_side, lax.all_gather(right_side, "col", axis=1, tiled=True)
    ).astype(jnp.bfloat16)
    triangle = lax.all_to_all(
        lax.all_to_all(triangle, "col", split_axis=2, concat_axis=1, tiled=True),
        "row",
        split_axis=1,
        concat_axis=0,
        tiled=True,
    )
    tri_values = triangle.astype(jnp.float32)
    total, squares = lax.psum((jnp.sum(tri_values, 0), jnp.sum(tri_values * tri_values, 0)), "ch")
    average = total / H
    inverse_mid = lax.rsqrt(squares / H - average * average + EPS)
    scaled_mid = (tri_values - average) * inverse_mid
    unit = (scaled_mid * gain_mid[:, None, None] + bias_mid[:, None, None]).astype(jnp.bfloat16)
    unit_full = lax.all_gather(unit, "ch", axis=0, tiled=True)
    outer = product("hij,hc->ijc", unit_full, out_w)
    outgate = jax.nn.sigmoid(product("ijc,cd->ijd", normed, outgate_w))
    result = (pair_in.astype(jnp.float32) + outer * outgate).astype(jnp.bfloat16)
    saved = (
        scaled_in,
        inverse_in,
        normed,
        projected,
        gating,
        left_side,
        right_side,
        scaled_mid,
        inverse_mid,
        unit_full,
        outer,
        outgate,
    )
    return (result, saved)


def backward_module(grad_out, pair_mask, weights, saved, incoming):
    gain_in, bias_in, proj_w, gate_w, gain_mid, bias_mid, out_w, outgate_w = weights
    (
        scaled_in,
        inverse_in,
        normed,
        projected,
        gating,
        left_side,
        right_side,
        scaled_mid,
        inverse_mid,
        unit_full,
        outer,
        outgate,
    ) = saved
    d_outer = (grad_out * outgate).astype(jnp.bfloat16)
    d_gatepre = (grad_out * outer * outgate * (1.0 - outgate)).astype(jnp.bfloat16)
    grad_out_w = product("hij,ijc->hc", unit_full, d_outer)
    grad_outgate_w = product("ijc,ijd->cd", normed, d_gatepre)
    width = gain_mid.shape[0]
    own_rows = lax.dynamic_slice_in_dim(out_w, lax.axis_index("ch") * width, width, 0)
    d_unit = product("ijc,hc->hij", d_outer, own_rows)
    d_normed = product("ijd,cd->ijc", d_gatepre, outgate_w)
    weighted = d_unit * gain_mid[:, None, None]
    grad_gain_mid = jnp.sum(d_unit * scaled_mid, (1, 2))
    grad_bias_mid = jnp.sum(d_unit, (1, 2))
    first_sum, second_sum = lax.psum(
        (jnp.sum(weighted, 0), jnp.sum(weighted * scaled_mid, 0)), "ch"
    )
    d_tri = (inverse_mid * (weighted - first_sum / H - scaled_mid * (second_sum / H))).astype(
        jnp.bfloat16
    )
    grad_rows = lax.all_to_all(d_tri, "row", split_axis=0, concat_axis=1, tiled=True)
    grad_cols = lax.all_to_all(grad_rows, "col", split_axis=1, concat_axis=2, tiled=True)
    d_left = product(
        "cij,cjk->cik", grad_cols, lax.all_gather(right_side, "col", axis=1, tiled=True)
    )
    partial_terms = product("cij,cik->cjk", grad_cols, left_side)
    d_right = lax.psum_scatter(
        partial_terms.astype(jnp.bfloat16), "col", scatter_dimension=1, tiled=True
    ).astype(jnp.float32)
    d_left = d_left.astype(jnp.bfloat16)
    d_right = d_right.astype(jnp.bfloat16)
    if incoming:
        d_left = jnp.swapaxes(d_left, 1, 2)
        d_right = jnp.swapaxes(d_right, 1, 2)
    else:
        d_left, d_right = (
            lax.all_to_all(d_left, "col", split_axis=2, concat_axis=1, tiled=True),
            lax.all_to_all(d_right, "col", split_axis=2, concat_axis=1, tiled=True),
        )
    d_left, d_right = (
        lax.all_to_all(d_left, "row", split_axis=1, concat_axis=0, tiled=True),
        lax.all_to_all(d_right, "row", split_axis=1, concat_axis=0, tiled=True),
    )
    d_hidden = jnp.stack([d_left, d_right]).astype(jnp.float32)
    d_proj = (d_hidden * gating * pair_mask).astype(jnp.bfloat16)
    d_gate = (d_hidden * projected * gating * (1.0 - gating) * pair_mask).astype(jnp.bfloat16)
    grad_proj_w = product("ijc,shij->sch", normed, d_proj)
    grad_gate_w = product("ijc,shij->sch", normed, d_gate)
    partial_input = product("shij,sch->ijc", d_proj, proj_w) + product(
        "shij,sch->ijc", d_gate, gate_w
    )
    d_normed = d_normed + lax.psum(partial_input.astype(jnp.bfloat16), "ch").astype(jnp.float32)
    weighted_in = d_normed * gain_in
    grad_gain_in = jnp.sum(d_normed * scaled_in, (0, 1))
    grad_bias_in = jnp.sum(d_normed, (0, 1))
    d_pair = inverse_in * (
        weighted_in
        - jnp.mean(weighted_in, -1, keepdims=True)
        - scaled_in * jnp.mean(weighted_in * scaled_in, -1, keepdims=True)
    )
    grads = (
        grad_gain_in,
        grad_bias_in,
        grad_proj_w,
        grad_gate_w,
        grad_gain_mid,
        grad_bias_mid,
        grad_out_w,
        grad_outgate_w,
    )
    return (grad_out + d_pair, grads)


def per_device(
    pair,
    cotangent,
    lengths,
    norm_gain,
    norm_bias,
    proj_weight,
    gate_weight,
    mid_gain,
    mid_bias,
    out_weight,
    outgate_weight,
):
    rows_here = pair.shape[0]
    cols_here = pair.shape[1]
    row_ids = lax.axis_index("row") * rows_here + lax.iota(jnp.int32, rows_here)
    col_ids = lax.axis_index("col") * cols_here + lax.iota(jnp.int32, cols_here)
    limit = lengths[0]
    pair_mask = ((row_ids[:, None] < limit) & (col_ids[None, :] < limit)).astype(jnp.float32)
    state = pair
    stash = []
    for layer in range(2):
        weights = (
            norm_gain[layer],
            norm_bias[layer],
            proj_weight[layer],
            gate_weight[layer],
            mid_gain[layer],
            mid_bias[layer],
            out_weight[layer],
            outgate_weight[layer],
        )
        state, saved = forward_module(state, pair_mask, weights, layer == 1)
        stash.append(saved)
    grad_state = cotangent.astype(jnp.float32)
    per_layer = [None, None]
    for layer in (1, 0):
        weights = (
            norm_gain[layer],
            norm_bias[layer],
            proj_weight[layer],
            gate_weight[layer],
            mid_gain[layer],
            mid_bias[layer],
            out_weight[layer],
            outgate_weight[layer],
        )
        grad_state, grads = backward_module(
            grad_state, pair_mask, weights, stash[layer], layer == 1
        )
        per_layer[layer] = grads
    lower = per_layer[0]
    upper = per_layer[1]
    summed = lax.psum(
        (
            lower[0],
            lower[1],
            lower[2],
            lower[3],
            lower[4],
            lower[5],
            lower[6],
            lower[7],
            upper[0],
            upper[1],
            upper[2],
            upper[3],
            upper[4],
            upper[5],
            upper[6],
            upper[7],
        ),
        ("row", "col"),
    )
    per_layer = [summed[0:8], summed[8:16]]
    stacked = [jnp.stack([per_layer[0][index], per_layer[1][index]]) for index in range(8)]
    return (
        state,
        grad_state.astype(jnp.bfloat16),
        stacked[0],
        stacked[1],
        stacked[2],
        stacked[3],
        stacked[4],
        stacked[5],
        stacked[6],
        stacked[7],
    )


def on_device(pair, *rest, many, few, split):
    rows, lanes, channels = pair.shape
    shards = many * few
    whole_channels = split == 1 and H % shards == 0 and BLOCK % (H // shards) == 0 and H % (2 * BLOCK) == 0
    tiles = rows == BLOCK and lanes % 128 == 0 and channels == H
    if whole_channels and tiles and many % 2 == 0 and few & (few - 1) == 0:
        return grouped_device(pair, *rest, many=many, few=few)
    return per_device(pair, *rest)


def solution(mesh):
    in_specs = (
        P(("grp", "row"), "col", None),
        P(("grp", "row"), "col", None),
        P("grp"),
        P(),
        P(),
        P(None, None, None, "ch"),
        P(None, None, None, "ch"),
        P(None, "ch"),
        P(None, "ch"),
        P(),
        P(),
    )
    out_specs = (
        P(("grp", "row"), "col", None),
        P(("grp", "row"), "col", None),
        P("grp", None),
        P("grp", None),
        P("grp", None, None, "ch"),
        P("grp", None, None, "ch"),
        P("grp", "ch"),
        P("grp", "ch"),
        P("grp", None, None),
        P("grp", None, None),
    )
    body = functools.partial(
        on_device, many=mesh.shape["row"], few=mesh.shape["col"], split=mesh.shape["ch"]
    )
    return jax.shard_map(
        body, mesh=mesh, in_specs=in_specs, out_specs=out_specs, check_vma=False
    )
```

```python
import functools

import jax
import jax.numpy as jnp
from jax import lax
from jax.experimental import pallas as pl
from jax.experimental.pallas import tpu as pltpu
from jax.sharding import PartitionSpec as P

H = 128


EPS = 1e-05


def product(spec, left, right):
    return jnp.einsum(spec, left, right, preferred_element_type=jnp.float32)


F32 = jnp.float32
BF16 = jnp.bfloat16


def dot(left, right):
    return lax.dot_general(left, right, (((1,), (0,)), ((), ())), preferred_element_type=F32)


def dot_rt(left, right):
    return lax.dot_general(left, right, (((1,), (1,)), ((), ())), preferred_element_type=F32)


def dot_lt(left, right):
    return lax.dot_general(left, right, (((0,), (0,)), ((), ())), preferred_element_type=F32)


def sigmoid_of_minus(values):
    return 1.0 / (1.0 + jnp.exp(values))


def norm_rows(values):
    scale = 1.0 / values.shape[0]
    average = jnp.sum(values, 0, keepdims=True) * scale
    centred = values - average
    variance = jnp.sum(centred * centred, 0, keepdims=True) * scale
    inverse = lax.rsqrt(variance + EPS)
    return centred * inverse, inverse


def turned(weight):
    return jnp.transpose(weight)


def column(ref, module, lanes):
    row = ref[module : module + 1, :]
    return beside(*[jnp.transpose(jnp.broadcast_to(row, (lanes, row.shape[1])))] * 2)


def beside(left, right):
    return jnp.concatenate([left, right], axis=-1)


def pair_of(ref, step):
    return beside(ref[2 * step], ref[2 * step + 1])


def put_pair(ref, step, values):
    lanes = ref.shape[-1]
    ref[2 * step] = values[:, :lanes]
    ref[2 * step + 1] = values[:, lanes:]


def pair_of_rows(ref, step):
    return beside(ref[2 * step : 2 * step + 1, :], ref[2 * step + 1 : 2 * step + 2, :])


def put_pair_of_rows(ref, step, values):
    lanes = ref.shape[-1]
    ref[2 * step : 2 * step + 1, :] = values[:, :lanes]
    ref[2 * step + 1 : 2 * step + 2, :] = values[:, lanes:]


def turned_pair(ref, step):
    return beside(jnp.transpose(ref[2 * step]), jnp.transpose(ref[2 * step + 1])).astype(F32)


def put_turned_pair(ref, step, values):
    lanes = ref.shape[1]
    values = values.astype(BF16)
    ref[2 * step] = jnp.transpose(values[:, :lanes])
    ref[2 * step + 1] = jnp.transpose(values[:, lanes:])


def as_row(total):
    return jnp.sum(jnp.transpose(total), 0, keepdims=True)


def row_mask(lengths_ref, step, rows, lanes):
    limit = lengths_ref[0]
    row_id = lax.axis_index("row") * rows + step
    col_id = lax.axis_index("col") * lanes + lax.broadcasted_iota(jnp.int32, (1, lanes), 1)
    return jnp.where((row_id < limit) & (col_id < limit), 1.0, 0.0).astype(F32)


def load_in_weights(proj_ref, gate_ref, module, scratch):
    width = proj_ref.shape[-1]
    for side in range(2):
        scratch[side * width : (side + 1) * width, :] = turned(proj_ref[module, side])
        scratch[(2 + side) * width : (3 + side) * width, :] = -turned(gate_ref[module, side])


def load_back_weights(proj_ref, gate_ref, module, scratch):
    width = proj_ref.shape[-1]
    for side in range(2):
        scratch[:, side * width : (side + 1) * width] = proj_ref[module, side]
        scratch[:, (2 + side) * width : (3 + side) * width] = gate_ref[module, side]


BLOCK = 16


def turn_matrix(rows):
    size = BLOCK * rows
    out = lax.broadcasted_iota(jnp.int32, (size, size), 0)
    source = lax.broadcasted_iota(jnp.int32, (size, size), 1)
    return jnp.where(source == (out % rows) * BLOCK + out // rows, 1.0, 0.0).astype(BF16)


def spread_blocks(matrix, scratch, start, group):
    rows, _, lanes = scratch.shape
    blocks = [
        scratch[:, at : at + BLOCK, :].reshape(rows * BLOCK, lanes)
        for at in (start, start + BLOCK)
    ]
    both = dot(matrix, beside(*blocks)).astype(BF16)
    parts = [
        part.reshape(BLOCK // group, group, rows, lanes)
        for part in (both[:, :lanes], both[:, lanes:])
    ]
    return jnp.concatenate(parts, axis=0)


def collect_blocks(matrix, values, scratch, start):
    rows, _, lanes = scratch.shape
    flat = values.reshape(2, BLOCK * rows, lanes)
    both = dot(matrix, beside(flat[0], flat[1])).astype(BF16)
    for at, part in ((start, both[:, :lanes]), (start + BLOCK, both[:, lanes:])):
        scratch[:, at : at + BLOCK, :] = part.reshape(rows, BLOCK, lanes)


def spread_edges(scratch, out_ref):
    shards, sides, group, rows, lanes = out_ref.shape
    matrix, step = turn_matrix(rows), 2 * BLOCK // group
    for side in range(sides):
        for shard in range(0, shards, step):
            start = (side * shards + shard) * group
            out_ref[shard : shard + step, side] = spread_blocks(matrix, scratch, start, group)


def collect_edges(in_ref, scratch):
    shards, sides, group, rows, lanes = in_ref.shape
    matrix, step = turn_matrix(rows), 2 * BLOCK // group
    for side in range(sides):
        for shard in range(0, shards, step):
            start = (side * shards + shard) * group
            collect_blocks(matrix, in_ref[shard : shard + step, side], scratch, start)


def spread_triangle(scratch, out_ref):
    shards, group, rows, lanes = out_ref.shape
    matrix, step = turn_matrix(rows), 2 * BLOCK // group
    for shard in range(0, shards, step):
        out_ref[shard : shard + step] = spread_blocks(matrix, scratch, shard * group, group)


def collect_triangle(in_ref, scratch):
    shards, group, rows, lanes = in_ref.shape
    matrix, step = turn_matrix(rows), 2 * BLOCK // group
    for shard in range(0, shards, step):
        collect_blocks(matrix, in_ref[shard : shard + step], scratch, shard * group)


def each_pair(rows, body, sums=None):
    for block in range(0, rows // 2, 4):
        parts = [body(block + step) for step in range(4)]
        for index in range(0 if sums is None else sums.shape[0]):
            total = (parts[0][index] + parts[1][index]) + (parts[2][index] + parts[3][index])
            lanes = sums.shape[-1]
            sums[index] += total[:, :lanes] + total[:, lanes:]


def mid_norm(tri):
    scale = 1.0 / tri.shape[0]
    average = jnp.sum(tri, 0, keepdims=True) * scale
    squares = jnp.sum(tri * tri, 0, keepdims=True) * scale
    inverse = lax.rsqrt(squares - average * average + EPS)
    return (tri - average) * inverse, inverse


def norm_backward(weighted, scaled, inverse):
    scale = 1.0 / weighted.shape[0]
    first = jnp.sum(weighted, 0, keepdims=True) * scale
    second = jnp.sum(weighted * scaled, 0, keepdims=True) * scale
    return inverse * (weighted - first - scaled * second)


def save_norm(step, values, scaled_out, inverse_out):
    scaled, inverse = norm_rows(values)
    put_pair(scaled_out, step, scaled)
    put_pair_of_rows(inverse_out, step, inverse)
    return scaled


def save_edges(step, normed, in_weights, mask, proj_out, gate_out):
    pre = dot(in_weights, normed)
    half = pre.shape[0] // 2
    gating = sigmoid_of_minus(pre[half:])
    factor = gating * mask
    value = pre[:half] * factor
    put_pair(proj_out, step, factor)
    put_pair(gate_out, step, value * (1.0 - gating))
    return value.astype(BF16)


def start_kernel(
    lengths, pair_far, ngain_far, nbias_far, proj_far, gate_far,
    edge_out, normed_out, proj_out, gate_out, scaled_out, inverse_out, mask_out,
    pair, ngain, nbias, proj_w, gate_w, sems, wts, scr,
):
    far = (proj_far.at[0], gate_far.at[0], ngain_far, nbias_far, pair_far)
    near = (proj_w.at[0], gate_w.at[0], ngain, nbias, pair)
    copies = [
        pltpu.make_async_copy(source, target, sems.at[index])
        for index, (source, target) in enumerate(zip(far, near))
    ]
    for copy in copies:
        copy.start()
    for copy in copies:
        copy.wait()
    rows, lanes, channels = pair.shape
    load_in_weights(proj_w, gate_w, 0, wts)
    gain, bias = column(ngain, 0, lanes), column(nbias, 0, lanes)

    def body(step):
        base = turned_pair(pair, step)
        scaled = save_norm(step, base, scaled_out, inverse_out)
        normed = (scaled * gain + bias).astype(BF16)
        put_pair(normed_out, step, normed)
        mask = beside(*[row_mask(lengths, 2 * step + row, rows, lanes) for row in range(2)])
        put_pair_of_rows(mask_out, step, mask)
        put_pair(scr, step, save_edges(step, normed, wts[...], mask, proj_out, gate_out))

    each_pair(rows, body)
    spread_edges(scr, edge_out)


def between_kernel(
    mask_all, tri, pair, normed0, ngain, nbias, mgain, mbias, out_w, outgate_w, proj_w, gate_w,
    edge_out, mid_out, normed_out, proj_out, gate_out, scaled_out, inverse_out,
    outgate_out, scaled_mid_out, inverse_mid_out, wts, tri_in, scr,
):
    rows, lanes, channels = pair.shape
    load_in_weights(proj_w, gate_w, 1, wts)
    out_t, outgate_t = turned(out_w[0]), -turned(outgate_w[0])
    gain, bias = column(ngain, 1, lanes), column(nbias, 1, lanes)
    gain_mid, bias_mid = column(mgain, 0, lanes), column(mbias, 0, lanes)
    collect_triangle(tri, tri_in)

    def body(step):
        scaled_mid, inverse_mid = mid_norm(pair_of(tri_in, step).astype(F32))
        put_pair(scaled_mid_out, step, scaled_mid)
        put_pair_of_rows(inverse_mid_out, step, inverse_mid)
        unit = (scaled_mid * gain_mid + bias_mid).astype(BF16)
        outer = dot(out_t, unit)
        outgate = sigmoid_of_minus(dot(outgate_t, pair_of(normed0, step)))
        put_pair(outgate_out, step, outgate)
        mid = (turned_pair(pair, step) + outer * outgate).astype(BF16)
        put_pair(mid_out, step, mid)
        scaled = save_norm(step, mid.astype(F32), scaled_out, inverse_out)
        normed = (scaled * gain + bias).astype(BF16)
        put_pair(normed_out, step, normed)
        mask = pair_of_rows(mask_all, step)
        put_pair(scr, step, save_edges(step, normed, wts[...], mask, proj_out, gate_out))

    each_pair(rows, body)
    spread_edges(scr, edge_out)


def out_weight_grads(unit, d_outer, normed, d_gatepre, out_ref):
    width = unit.shape[0]
    out_ref[0:width, :] = dot_rt(unit[...], d_outer[...]).astype(out_ref.dtype)
    out_ref[width:, :] = dot_rt(normed[...], d_gatepre[...]).astype(out_ref.dtype)


def in_weight_grads(normed_all, d_in_all, out_ref):
    width = normed_all.shape[0]
    for part in range(d_in_all.shape[0] // width):
        block = slice(part * width, (part + 1) * width)
        out_ref[block, :] = dot_rt(normed_all[...], d_in_all[block, :]).astype(out_ref.dtype)


def lane_block(step, lanes):
    return pl.ds(2 * step * lanes, 2 * lanes)


def turn_kernel(
    tri, mid, normed, cot, mgain, mbias, out_w, outgate_w,
    d_tri_out, new_out, grad_out, d_normed_out, weights_out, small_out,
    tri_in, scr, unit_all, outer_all, normed_all, gate_all, sums,
):
    rows, channels, lanes = mid.shape
    out_t, outgate_t = turned(out_w[1]), -turned(outgate_w[1])
    gain_mid, bias_mid = column(mgain, 1, lanes), column(mbias, 1, lanes)
    collect_triangle(tri, tri_in)
    sums[...] = jnp.zeros_like(sums)

    def body(step):
        here = lane_block(step, lanes)
        grad = turned_pair(cot, step)
        put_pair(grad_out, step, grad)
        here_normed = pair_of(normed, step)
        outgate = sigmoid_of_minus(dot(outgate_t, here_normed))
        gated = grad * outgate
        d_outer = gated.astype(BF16)
        d_unit = dot(out_w[1], d_outer)
        scaled_mid, inverse_mid = mid_norm(pair_of(tri_in, step).astype(F32))
        d_tri = norm_backward(d_unit * gain_mid, scaled_mid, inverse_mid)
        put_pair(scr, step, d_tri.astype(BF16))
        unit = (scaled_mid * gain_mid + bias_mid).astype(BF16)
        outer = dot(out_t, unit)
        put_pair(new_out, step, (pair_of(mid, step).astype(F32) + outer * outgate).astype(BF16))
        d_gatepre = (gated * outer * (1.0 - outgate)).astype(BF16)
        put_pair(d_normed_out, step, dot(outgate_w[1], d_gatepre))
        unit_all[:, here] = unit
        outer_all[:, here] = d_outer
        normed_all[:, here] = here_normed
        gate_all[:, here] = d_gatepre
        return d_unit * scaled_mid, d_unit

    each_pair(rows, body, sums)
    spread_triangle(scr, d_tri_out)
    out_weight_grads(unit_all, outer_all, normed_all, gate_all, weights_out)
    for index in range(2):
        small_out[index : index + 1, :] = as_row(sums[index])


def edge_backward(step, scratch, proj_factor, gate_factor):
    here = pair_of(scratch, step).astype(F32)
    d_proj = (here * pair_of(proj_factor, step)).astype(BF16)
    d_gate = (here * pair_of(gate_factor, step)).astype(BF16)
    return jnp.concatenate([d_proj, d_gate], axis=0)


def middle_kernel(
    d_edge, proj_factor, gate_factor, d_normed_gate, scaled_in, inverse_in, cot, outgate,
    scaled_mid, inverse_mid, normed0, normed1, ngain, mgain, mbias, proj_w, gate_w, out_w,
    outgate_w,
    d_tri_out, grad_out, d_normed_out, out_weights, in_weights, small_out,
    scr, scr_tri, unit_all, outer_all, normed_all, gate_all, upper_all, d_in_all, back, sums,
):
    rows, channels, lanes = cot.shape
    out_t = turned(out_w[0])
    gain = column(ngain, 1, lanes)
    gain_mid, bias_mid = column(mgain, 0, lanes), column(mbias, 0, lanes)
    collect_edges(d_edge, scr)
    sums[...] = jnp.zeros_like(sums)
    load_back_weights(proj_w, gate_w, 1, back)

    def upper(step):
        place = lane_block(step, lanes)
        d_in = edge_backward(step, scr, proj_factor, gate_factor)
        d_in_all[:, place] = d_in
        upper_all[:, place] = pair_of(normed1, step)
        d_normed = pair_of(d_normed_gate, step) + dot(back[...], d_in)
        scaled = pair_of(scaled_in, step)
        grad = pair_of(cot, step) + norm_backward(
            d_normed * gain, scaled, pair_of_rows(inverse_in, step)
        )
        put_pair(grad_out, step, grad)
        return d_normed * scaled, d_normed

    def lower(step):
        place = lane_block(step, lanes)
        gate = pair_of(outgate, step)
        gated = pair_of(grad_out, step) * gate
        d_outer = gated.astype(BF16)
        d_unit = dot(out_w[0], d_outer)
        scaled = pair_of(scaled_mid, step)
        d_tri = norm_backward(d_unit * gain_mid, scaled, pair_of_rows(inverse_mid, step))
        put_pair(scr_tri, step, d_tri.astype(BF16))
        unit = (scaled * gain_mid + bias_mid).astype(BF16)
        outer = dot(out_t, unit)
        d_gatepre = (gated * outer * (1.0 - gate)).astype(BF16)
        put_pair(d_normed_out, step, dot(outgate_w[0], d_gatepre))
        unit_all[:, place] = unit
        outer_all[:, place] = d_outer
        normed_all[:, place] = pair_of(normed0, step)
        gate_all[:, place] = d_gatepre
        return d_unit * scaled, d_unit

    each_pair(rows, upper, sums.at[2:4])
    each_pair(rows, lower, sums.at[0:2])
    spread_triangle(scr_tri, d_tri_out)
    out_weight_grads(unit_all, outer_all, normed_all, gate_all, out_weights)
    in_weight_grads(upper_all, d_in_all, in_weights)
    for index in range(4):
        small_out[index : index + 1, :] = as_row(sums[index])


def split_cores(all_rows, own_out, other_out, few):
    chips, share, width = own_out.shape
    view = all_rows.reshape(chips // few, 2, few, share, width)
    core = lax.rem(lax.axis_index("row"), 2)
    own_out[...] = view[:, core].reshape(own_out.shape)
    other_out[...] = view[:, 1 - core].reshape(other_out.shape)


def finish_kernel(
    few, d_edge, proj_factor, gate_factor, normed, out0, in1, out1,
    own_out, other_out, d_in_all, scr, normed_all, packed,
):
    rows, half, lanes = proj_factor.shape
    collect_edges(d_edge, scr)

    def body(step):
        place = lane_block(step, lanes)
        d_in_all[:, place] = edge_backward(step, scr, proj_factor, gate_factor)
        normed_all[:, place] = pair_of(normed, step)

    each_pair(rows, body)
    first, second, third = d_in_all.shape[0], out0.shape[0], in1.shape[0]
    in_weight_grads(normed_all, d_in_all, packed.at[0:first])
    packed[first : first + second, :] = out0[...]
    packed[first + second : first + second + third, :] = in1[...]
    packed[first + second + third :, :] = out1[...]
    split_cores(packed, own_out, other_out, few)


def norm_sums_kernel(
    d_in, d_normed_gate, scaled_in, proj_w, gate_w, small_middle, small1, new_t,
    d_normed_out, extra_out, new_out, back, sums,
):
    rows, channels, lanes = scaled_in.shape
    sums[...] = jnp.zeros_like(sums)
    load_back_weights(proj_w, gate_w, 0, back)

    def body(step):
        here = d_in[:, lane_block(step, lanes)]
        d_normed = pair_of(d_normed_gate, step) + dot(back[...], here)
        put_pair(d_normed_out, step, d_normed)
        put_turned_pair(new_out, step, pair_of(new_t, step))
        return d_normed * pair_of(scaled_in, step), d_normed

    each_pair(rows, body, sums)
    small = jnp.concatenate(
        [as_row(sums[0]), as_row(sums[1]), small_middle[0:2], small_middle[2:4], small1[...]],
        axis=0,
    )
    high = small.astype(BF16).astype(F32)
    extra_out[...] = jnp.concatenate([high, small - high], axis=0).astype(BF16)


def add_kernel(first, second, extra, out_ref, extra_out):
    out_ref[...] = (first[...].astype(F32) + second[...].astype(F32)).astype(BF16)
    extra_out[...] = extra[...]


def sum_kernel(parts, extra, shared_out):
    chips, share, width = parts.shape
    own = jnp.sum(parts[...].astype(F32), axis=0).astype(BF16)
    for chip in range(chips):
        shared_out[chip, 0:share] = own
        shared_out[chip, share:] = extra[...]


def grad_pair_kernel(
    share, shared, d_normed, scaled_in, inverse_in, grad, ngain, grad_out, mine_out
):
    rows, channels, lanes = grad.shape
    gain = column(ngain, 0, lanes)
    mine_out[...] = jnp.sum(shared[:, share:].astype(F32), axis=0)

    def body(step):
        total = pair_of(grad, step) + norm_backward(
            pair_of(d_normed, step) * gain, pair_of(scaled_in, step),
            pair_of_rows(inverse_in, step),
        )
        put_turned_pair(grad_out, step, total)

    each_pair(rows, body)


def unpack_kernel(
    share, few, own, other, mine, proj_out, gate_out, out_out, outgate_out,
    norm_gain_out, norm_bias_out, mid_gain_out, mid_bias_out, weights,
):
    chips, _, width = own.shape
    core = lax.rem(lax.axis_index("row"), 2)
    view = weights.reshape(chips // few, 2, few, share, width)
    block = (chips // few, few, share, width)
    view[:, core] = own[:, 0:share].astype(F32).reshape(block)
    view[:, 1 - core] = other[:, 0:share].astype(F32).reshape(block)
    total = mine[...] + jnp.sum(other[:, share:].astype(F32), axis=0)
    total = total[0:8] + total[8:16]
    for module in range(2):
        for index, out in enumerate((norm_gain_out, norm_bias_out, mid_gain_out, mid_bias_out)):
            at = 4 * module + index
            out[module : module + 1, :] = total[at : at + 1]
        blocks = [
            weights[(6 * module + part) * width : (6 * module + part + 1) * width, :]
            for part in range(6)
        ]
        for side in range(2):
            proj_out[module, side] = blocks[side]
            gate_out[module, side] = blocks[2 + side]
        out_out[module] = blocks[4]
        outgate_out[module] = blocks[5]


def triangle_kernel(incoming, edge, tri_out):
    many, few, _, group, rows, lanes = edge.shape

    def whole(side, channel):
        parts = [edge[:, c, side, channel].reshape(many * rows, lanes) for c in range(few)]
        return jnp.concatenate(parts, axis=1)

    for channel in range(group):
        left, right = whole(0, channel), whole(1, channel)
        tri = (dot_lt if incoming else dot_rt)(left, right).astype(BF16)
        for c in range(few):
            part = tri[:, c * lanes : (c + 1) * lanes]
            tri_out[:, c, channel] = part.reshape(many, rows, lanes)


def edge_grad_kernel(incoming, edge, d_tri, grad_out):
    many, few, _, group, rows, lanes = edge.shape

    def whole(ref, *index):
        parts = [ref[(slice(None), c) + index].reshape(many * rows, lanes) for c in range(few)]
        return jnp.concatenate(parts, axis=1)

    for channel in range(group):
        left, right = whole(edge, 0, channel), whole(edge, 1, channel)
        grad = whole(d_tri, channel)
        if incoming:
            d_left, d_right = dot_rt(right, grad), dot(left, grad)
        else:
            d_left, d_right = dot(grad, right), dot_lt(grad, left)
        for side, value in ((0, d_left), (1, d_right)):
            value = value.astype(BF16)
            for c in range(few):
                part = value[:, c * lanes : (c + 1) * lanes]
                grad_out[:, c, side, channel] = part.reshape(many, rows, lanes)


SCALARS = pl.BlockSpec(memory_space=pltpu.SMEM)
VECTORS = pl.BlockSpec(memory_space=pltpu.VMEM)
FAR = pl.BlockSpec(memory_space=pltpu.HBM)


def call(kernel, name, outs, args, scratch=(), flops=0, grant=16, specs=None):
    shapes = [jax.ShapeDtypeStruct(shape, dtype) for shape, dtype in outs]
    moved = sum(a.size * a.dtype.itemsize for a in list(args) + shapes)
    return pl.pallas_call(
        kernel,
        name=name,
        out_shape=shapes,
        in_specs=specs or [VECTORS] * len(args),
        out_specs=[VECTORS] * len(shapes),
        scratch_shapes=[
            pltpu.VMEM(*item) if isinstance(item, tuple) else item for item in scratch
        ],
        compiler_params=pltpu.CompilerParams(vmem_limit_bytes=grant * 1024 * 1024),
        cost_estimate=pl.CostEstimate(flops=flops, bytes_accessed=moved, transcendentals=0),
    )(*args)


def exchange(values):
    return lax.all_to_all(values, ("row", "col"), split_axis=0, concat_axis=0, tiled=True)


def swap_cores(values, many, few):
    pairs = [(index, index ^ few) for index in range(many * few)]
    return lax.ppermute(values, ("row", "col"), pairs)


def exchange_chips(values, many, few):
    groups = [
        [row * few + col for row in range(core, many, 2) for col in range(few)] for core in range(2)
    ]
    return lax.all_to_all(
        values, ("row", "col"), split_axis=0, concat_axis=0, axis_index_groups=groups, tiled=True
    )


def grouped_device(
    pair, cotangent, lengths, ngain, nbias, proj_w, gate_w, mgain, mbias, out_w, outgate_w,
    *, many, few,
):
    rows, lanes, channels = pair.shape
    shards = many * few
    group = H // shards
    edge = ((shards, 2, group, rows, lanes), BF16)
    grid = ((many, few, 2, group, rows, lanes), BF16)
    tri = ((shards, group, rows, lanes), BF16)
    tri_grid = ((many, few, group, rows, lanes), BF16)
    tile = ((rows, channels, lanes), BF16)
    wide = ((rows, channels, lanes), F32)
    row = ((rows, lanes), F32)
    factor = ((rows, 2 * H, lanes), F32)
    back = ((channels, 4 * H), BF16)
    wts = ((4 * H, channels), BF16)
    big = ((rows, 2 * H, lanes), BF16)
    mid = ((rows, H, lanes), BF16)
    positions = rows * lanes
    flat = ((H, positions), BF16)
    flat_in = ((4 * H, positions), BF16)
    out_rows = ((2 * H, channels), BF16)
    in_rows = ((4 * H, H), BF16)
    triangle = 2 * group * (many * rows) ** 2 * (few * lanes)
    dense = 2 * positions * channels * H

    def sums(count):
        return ((count, H, lanes), F32)

    def small(count):
        return ((count, H), F32)

    saved = [tile, factor, factor, wide, row]
    far = [
        pltpu.with_memory_space_constraint(item, pltpu.HBM)
        for item in (pair, ngain, nbias, proj_w, gate_w)
    ]
    sent, normed0, *factors0, mask = call(
        start_kernel, "start", [edge, *saved, row], [lengths, *far],
        [(pair.shape, BF16), (ngain.shape, F32), (nbias.shape, F32), (proj_w.shape, BF16),
         (gate_w.shape, BF16), pltpu.SemaphoreType.DMA((5,)), wts, big],
        4 * dense, specs=[SCALARS] + [FAR] * len(far),
    )
    edge0 = exchange(sent).reshape(grid[0])
    (here,) = call(
        functools.partial(triangle_kernel, False), "outgoing", [tri_grid], [edge0], (), triangle,
    )
    tri0 = exchange(here.reshape(tri[0]))
    sent, mid_t, normed1, *factors1, outgate0, scaled_mid0, inverse_mid0 = call(
        between_kernel, "between", [edge, tile, *saved, wide, wide, row],
        [mask, tri0, pair, normed0, ngain, nbias, mgain, mbias, out_w, outgate_w, proj_w,
         gate_w],
        [wts, mid, big], 6 * dense,
    )
    edge1 = exchange(sent).reshape(grid[0])
    (here,) = call(
        functools.partial(triangle_kernel, True), "incoming", [tri_grid], [edge1], (), triangle,
    )
    tri1 = exchange(here.reshape(tri[0]))
    sent, new_t, cot_t, d_normed_gate1, out_grads1, small1 = call(
        turn_kernel, "turn", [tri, tile, wide, wide, out_rows, small(2)],
        [tri1, mid_t, normed1, cotangent, mgain, mbias, out_w, outgate_w],
        [mid, mid, flat, flat, flat, flat, sums(2)], 6 * dense,
    )
    d_tri1 = exchange(sent).reshape(tri_grid[0])
    (sent,) = call(
        functools.partial(edge_grad_kernel, True), "incoming_grad", [grid], [edge1, d_tri1],
        (), 2 * triangle,
    )
    d_edge1 = exchange(sent.reshape(edge[0]))
    proj_factor1, gate_factor1, scaled1, inverse1 = factors1
    sent, grad, d_normed_gate0, out_grads0, in_grads1, small_middle = call(
        middle_kernel, "middle", [tri, wide, wide, out_rows, in_rows, small(4)],
        [d_edge1, proj_factor1, gate_factor1, d_normed_gate1, scaled1, inverse1, cot_t, outgate0,
         scaled_mid0, inverse_mid0, normed0, normed1, ngain, mgain, mbias, proj_w, gate_w, out_w,
         outgate_w],
        [big, mid, flat, flat, flat, flat, flat, flat_in, back, sums(4)], 13 * dense,
    )
    d_tri0 = exchange(sent).reshape(tri_grid[0])
    (sent,) = call(
        functools.partial(edge_grad_kernel, False), "outgoing_grad", [grid], [edge0, d_tri0],
        (), 2 * triangle,
    )
    d_edge0 = exchange(sent.reshape(edge[0]))
    share = 12 * H // shards
    chips = shards // 2
    proj_factor0, gate_factor0, scaled0, inverse0 = factors0
    held = ((chips, share, H), BF16)
    own, other, d_in0 = call(
        functools.partial(finish_kernel, few), "finish", [held, held, flat_in],
        [d_edge0, proj_factor0, gate_factor0, normed0, out_grads0, in_grads1, out_grads1],
        [big, flat, ((12 * H, H), BF16)], 4 * dense,
    )
    other = swap_cores(other, many, few)
    d_normed0, extra, new_pair = call(
        norm_sums_kernel, "norm_sums", [wide, ((16, H), BF16), (pair.shape, BF16)],
        [d_in0, d_normed_gate0, scaled0, proj_w, gate_w, small_middle, small1, new_t],
        [back, sums(2)],
        4 * dense,
    )
    own, extra = call(add_kernel, "add_cores", [held, ((16, H), BF16)], [own, other, extra])
    parts = exchange_chips(own, many, few)
    (shared,) = call(
        sum_kernel, "sum_weights", [((chips, share + 16, H), BF16)], [parts, extra]
    )
    shared = exchange_chips(shared, many, few)
    other = swap_cores(shared, many, few)
    grad_pair, mine = call(
        functools.partial(grad_pair_kernel, share), "grad_pair",
        [(pair.shape, BF16), ((16, H), F32)],
        [shared, d_normed0, scaled0, inverse0, grad, ngain],
    )
    grad_proj, grad_gate, grad_out, grad_outgate, *vectors = call(
        functools.partial(unpack_kernel, share, few), "unpack",
        [(proj_w.shape, F32), (gate_w.shape, F32), (out_w.shape, F32), (outgate_w.shape, F32),
         (ngain.shape, F32), (nbias.shape, F32), (mgain.shape, F32), (mbias.shape, F32)],
        [shared, other, mine], [((12 * H, H), F32)],
    )
    return (
        new_pair,
        grad_pair,
        vectors[0],
        vectors[1],
        grad_proj,
        grad_gate,
        vectors[2],
        vectors[3],
        grad_out,
        grad_outgate,
    )


def norm_channels(values):
    average = jnp.mean(values, -1, keepdims=True)
    centred = values - average
    variance = jnp.mean(centred * centred, -1, keepdims=True)
    inverse = lax.rsqrt(variance + EPS)
    return (centred * inverse, inverse)


def forward_module(pair_in, pair_mask, weights, incoming):
    gain_in, bias_in, proj_w, gate_w, gain_mid, bias_mid, out_w, outgate_w = weights
    scaled_in, inverse_in = norm_channels(pair_in.astype(jnp.float32))
    normed = (scaled_in * gain_in + bias_in).astype(jnp.bfloat16)
    projected = product("ijc,sch->shij", normed, proj_w)
    gating = jax.nn.sigmoid(product("ijc,sch->shij", normed, gate_w))
    hidden = (projected * gating * pair_mask).astype(jnp.bfloat16)
    left_side, right_side = (
        lax.all_to_all(hidden[0], "row", split_axis=0, concat_axis=1, tiled=True),
        lax.all_to_all(hidden[1], "row", split_axis=0, concat_axis=1, tiled=True),
    )
    if incoming:
        left_side = jnp.swapaxes(left_side, 1, 2)
        right_side = jnp.swapaxes(right_side, 1, 2)
    else:
        left_side, right_side = (
            lax.all_to_all(left_side, "col", split_axis=1, concat_axis=2, tiled=True),
            lax.all_to_all(right_side, "col", split_axis=1, concat_axis=2, tiled=True),
        )
    triangle = product(
        "cik,cjk->cij", left_side, lax.all_gather(right_side, "col", axis=1, tiled=True)
    ).astype(jnp.bfloat16)
    triangle = lax.all_to_all(
        lax.all_to_all(triangle, "col", split_axis=2, concat_axis=1, tiled=True),
        "row",
        split_axis=1,
        concat_axis=0,
        tiled=True,
    )
    tri_values = triangle.astype(jnp.float32)
    total, squares = lax.psum((jnp.sum(tri_values, 0), jnp.sum(tri_values * tri_values, 0)), "ch")
    average = total / H
    inverse_mid = lax.rsqrt(squares / H - average * average + EPS)
    scaled_mid = (tri_values - average) * inverse_mid
    unit = (scaled_mid * gain_mid[:, None, None] + bias_mid[:, None, None]).astype(jnp.bfloat16)
    unit_full = lax.all_gather(unit, "ch", axis=0, tiled=True)
    outer = product("hij,hc->ijc", unit_full, out_w)
    outgate = jax.nn.sigmoid(product("ijc,cd->ijd", normed, outgate_w))
    result = (pair_in.astype(jnp.float32) + outer * outgate).astype(jnp.bfloat16)
    saved = (
        scaled_in,
        inverse_in,
        normed,
        projected,
        gating,
        left_side,
        right_side,
        scaled_mid,
        inverse_mid,
        unit_full,
        outer,
        outgate,
    )
    return (result, saved)


def backward_module(grad_out, pair_mask, weights, saved, incoming):
    gain_in, bias_in, proj_w, gate_w, gain_mid, bias_mid, out_w, outgate_w = weights
    (
        scaled_in,
        inverse_in,
        normed,
        projected,
        gating,
        left_side,
        right_side,
        scaled_mid,
        inverse_mid,
        unit_full,
        outer,
        outgate,
    ) = saved
    d_outer = (grad_out * outgate).astype(jnp.bfloat16)
    d_gatepre = (grad_out * outer * outgate * (1.0 - outgate)).astype(jnp.bfloat16)
    grad_out_w = product("hij,ijc->hc", unit_full, d_outer)
    grad_outgate_w = product("ijc,ijd->cd", normed, d_gatepre)
    width = gain_mid.shape[0]
    own_rows = lax.dynamic_slice_in_dim(out_w, lax.axis_index("ch") * width, width, 0)
    d_unit = product("ijc,hc->hij", d_outer, own_rows)
    d_normed = product("ijd,cd->ijc", d_gatepre, outgate_w)
    weighted = d_unit * gain_mid[:, None, None]
    grad_gain_mid = jnp.sum(d_unit * scaled_mid, (1, 2))
    grad_bias_mid = jnp.sum(d_unit, (1, 2))
    first_sum, second_sum = lax.psum(
        (jnp.sum(weighted, 0), jnp.sum(weighted * scaled_mid, 0)), "ch"
    )
    d_tri = (inverse_mid * (weighted - first_sum / H - scaled_mid * (second_sum / H))).astype(
        jnp.bfloat16
    )
    grad_rows = lax.all_to_all(d_tri, "row", split_axis=0, concat_axis=1, tiled=True)
    grad_cols = lax.all_to_all(grad_rows, "col", split_axis=1, concat_axis=2, tiled=True)
    d_left = product(
        "cij,cjk->cik", grad_cols, lax.all_gather(right_side, "col", axis=1, tiled=True)
    )
    partial_terms = product("cij,cik->cjk", grad_cols, left_side)
    d_right = lax.psum_scatter(
        partial_terms.astype(jnp.bfloat16), "col", scatter_dimension=1, tiled=True
    ).astype(jnp.float32)
    d_left = d_left.astype(jnp.bfloat16)
    d_right = d_right.astype(jnp.bfloat16)
    if incoming:
        d_left = jnp.swapaxes(d_left, 1, 2)
        d_right = jnp.swapaxes(d_right, 1, 2)
    else:
        d_left, d_right = (
            lax.all_to_all(d_left, "col", split_axis=2, concat_axis=1, tiled=True),
            lax.all_to_all(d_right, "col", split_axis=2, concat_axis=1, tiled=True),
        )
    d_left, d_right = (
        lax.all_to_all(d_left, "row", split_axis=1, concat_axis=0, tiled=True),
        lax.all_to_all(d_right, "row", split_axis=1, concat_axis=0, tiled=True),
    )
    d_hidden = jnp.stack([d_left, d_right]).astype(jnp.float32)
    d_proj = (d_hidden * gating * pair_mask).astype(jnp.bfloat16)
    d_gate = (d_hidden * projected * gating * (1.0 - gating) * pair_mask).astype(jnp.bfloat16)
    grad_proj_w = product("ijc,shij->sch", normed, d_proj)
    grad_gate_w = product("ijc,shij->sch", normed, d_gate)
    partial_input = product("shij,sch->ijc", d_proj, proj_w) + product(
        "shij,sch->ijc", d_gate, gate_w
    )
    d_normed = d_normed + lax.psum(partial_input.astype(jnp.bfloat16), "ch").astype(jnp.float32)
    weighted_in = d_normed * gain_in
    grad_gain_in = jnp.sum(d_normed * scaled_in, (0, 1))
    grad_bias_in = jnp.sum(d_normed, (0, 1))
    d_pair = inverse_in * (
        weighted_in
        - jnp.mean(weighted_in, -1, keepdims=True)
        - scaled_in * jnp.mean(weighted_in * scaled_in, -1, keepdims=True)
    )
    grads = (
        grad_gain_in,
        grad_bias_in,
        grad_proj_w,
        grad_gate_w,
        grad_gain_mid,
        grad_bias_mid,
        grad_out_w,
        grad_outgate_w,
    )
    return (grad_out + d_pair, grads)


def per_device(
    pair,
    cotangent,
    lengths,
    norm_gain,
    norm_bias,
    proj_weight,
    gate_weight,
    mid_gain,
    mid_bias,
    out_weight,
    outgate_weight,
):
    rows_here = pair.shape[0]
    cols_here = pair.shape[1]
    row_ids = lax.axis_index("row") * rows_here + lax.iota(jnp.int32, rows_here)
    col_ids = lax.axis_index("col") * cols_here + lax.iota(jnp.int32, cols_here)
    limit = lengths[0]
    pair_mask = ((row_ids[:, None] < limit) & (col_ids[None, :] < limit)).astype(jnp.float32)
    state = pair
    stash = []
    for layer in range(2):
        weights = (
            norm_gain[layer],
            norm_bias[layer],
            proj_weight[layer],
            gate_weight[layer],
            mid_gain[layer],
            mid_bias[layer],
            out_weight[layer],
            outgate_weight[layer],
        )
        state, saved = forward_module(state, pair_mask, weights, layer == 1)
        stash.append(saved)
    grad_state = cotangent.astype(jnp.float32)
    per_layer = [None, None]
    for layer in (1, 0):
        weights = (
            norm_gain[layer],
            norm_bias[layer],
            proj_weight[layer],
            gate_weight[layer],
            mid_gain[layer],
            mid_bias[layer],
            out_weight[layer],
            outgate_weight[layer],
        )
        grad_state, grads = backward_module(
            grad_state, pair_mask, weights, stash[layer], layer == 1
        )
        per_layer[layer] = grads
    lower = per_layer[0]
    upper = per_layer[1]
    summed = lax.psum(
        (
            lower[0],
            lower[1],
            lower[2],
            lower[3],
            lower[4],
            lower[5],
            lower[6],
            lower[7],
            upper[0],
            upper[1],
            upper[2],
            upper[3],
            upper[4],
            upper[5],
            upper[6],
            upper[7],
        ),
        ("row", "col"),
    )
    per_layer = [summed[0:8], summed[8:16]]
    stacked = [jnp.stack([per_layer[0][index], per_layer[1][index]]) for index in range(8)]
    return (
        state,
        grad_state.astype(jnp.bfloat16),
        stacked[0],
        stacked[1],
        stacked[2],
        stacked[3],
        stacked[4],
        stacked[5],
        stacked[6],
        stacked[7],
    )


def on_device(pair, *rest, many, few, split):
    rows, lanes, channels = pair.shape
    shards = many * few
    whole_channels = split == 1 and H % shards == 0 and BLOCK % (H // shards) == 0 and H % (2 * BLOCK) == 0
    tiles = rows == BLOCK and lanes % 128 == 0 and channels == H
    if whole_channels and tiles and many % 2 == 0 and few & (few - 1) == 0:
        return grouped_device(pair, *rest, many=many, few=few)
    return per_device(pair, *rest)


def solution(mesh):
    in_specs = (
        P(("grp", "row"), "col", None),
        P(("grp", "row"), "col", None),
        P("grp"),
        P(),
        P(),
        P(None, None, None, "ch"),
        P(None, None, None, "ch"),
        P(None, "ch"),
        P(None, "ch"),
        P(),
        P(),
    )
    out_specs = (
        P(("grp", "row"), "col", None),
        P(("grp", "row"), "col", None),
        P("grp", None),
        P("grp", None),
        P("grp", None, None, "ch"),
        P("grp", None, None, "ch"),
        P("grp", "ch"),
        P("grp", "ch"),
        P("grp", None, None),
        P("grp", None, None),
    )
    body = functools.partial(
        on_device, many=mesh.shape["row"], few=mesh.shape["col"], split=mesh.shape["ch"]
    )
    return jax.shard_map(
        body, mesh=mesh, in_specs=in_specs, out_specs=out_specs, check_vma=False
    )
```
